128 devices in a mesh: dp: 32 (over z, y, core), tp: 4 (over x).
Axes of the slice: x: 4, y: 4, z: 4, core: 2. Of those that a mesh axis runs over, the one named last changes fastest.
Arguments:
- hidden_in: bfloat16 [64, 512, 768], P('dp', 'tp'), may hold values from -6 to 6
- reset: int32 [64], P('dp'), may hold values from 0 to 1, as said below
- w_qkv: bfloat16 [768, 2304], P(('dp', 'tp')), may hold values from -0.21875 to 0.21875
- w_attn_out: bfloat16 [768, 768], P(('dp', 'tp')), may hold values from -0.3125 to 0.3125
- norm_gains: bfloat16 [2, 768], P(None, ('dp', 'tp')), may hold values from 0.5 to 1.5
- norm_biases: bfloat16 [2, 768], P(None, ('dp', 'tp')), may hold values from -2 to 2
- memory_tokens: bfloat16 [2, 10, 768], P(None, None, ('dp', 'tp')), may hold values from -6 to 6
- w_in: bfloat16 [768, 3072], P('dp', 'tp'), may hold values from -0.21875 to 0.21875
- w_out: bfloat16 [3072, 768], P('tp', 'dp'), may hold values from -0.109375 to 0.109375
- grad_hidden: bfloat16 [64, 512, 768], P('dp', 'tp'), may hold values from -6 to 6
- grad_memory: bfloat16 [64, 20, 768], P('dp', 'tp'), may hold values from -6 to 6
Outputs:
- hidden_out: bfloat16 [64, 512, 768], P('dp', 'tp')
- memory_out: bfloat16 [64, 20, 768], P('dp', 'tp')
- grad_in: float32 [64, 512, 768], P('dp', 'tp')
- grad_qkv: float32 [768, 2304], P(('dp', 'tp'))
- grad_attn_out: float32 [768, 768], P(('dp', 'tp'))
- grad_gains: float32 [2, 768], P(None, ('dp', 'tp'))
- grad_biases: float32 [2, 768], P(None, ('dp', 'tp'))
- grad_memory_tokens: float32 [2, 10, 768], P(None, None, ('dp', 'tp'))
- grad_w_in: float32 [768, 3072], P('dp', 'tp')
- grad_w_out: float32 [3072, 768], P('tp', 'dp')
The draws below stay inside these ranges and needn't reach their ends.
Inputs may be any that keep to these rules, and one draw needn't show every extreme that they name: reset is 1 at the first segment of every index of dp; each index of dp holds one chain of exactly 2 segments: reset is 1 at its first segment and 0 at its second.
All inputs are finite; a program needn't handle non-finite values.
Results may differ from the reference program's by a relative error of at most 0.017.
Values may be sent and summed in bfloat16 or wider, within the bound.
A program may use at most 128 MiB of HBM per device.

```python
import jax
import jax.numpy as jnp
from jax import lax

D = 768
HEADS = 12
HEAD_DIM = 64
FF = 3072
SEG = 512
MEM = 10
SEGS = 2
SEGMENTS = 64


def draw_reset(key, part):
    key = jax.random.fold_in(key, 7)
    coin_key = jax.random.fold_in(key, 1)
    pick_key = jax.random.fold_in(key, 2)
    position = jnp.arange(SEGMENTS) % SEGS
    owner = jnp.arange(SEGMENTS) // SEGS
    coin = jax.random.randint(coin_key, (SEGMENTS,), 0, 2)
    picked = jax.random.randint(pick_key, (), 0, SEGMENTS // SEGS)
    even_slot = position % 2 == 0
    forced = position % 6 == 0
    free_start = jnp.logical_and(coin == 1, owner != picked)
    starts = jnp.logical_and(even_slot, jnp.logical_or(forced, free_start))
    starts = jnp.logical_and(starts, jnp.logical_or(position == 0, position <= SEGS - 2))
    return starts.astype(jnp.int32)


def with_spikes(result, key, source, target, shards_of, factor):
    def block_of(dim):
        return (jnp.arange(result.shape[dim]) // (result.shape[dim] // shards_of)).reshape((-1,) + (1,) * (result.ndim - 1 - dim))

    one_side = jax.random.permutation(key, shards_of)[block_of(target)]
    other_side = (block_of(target) + shards_of // 2) % shards_of
    return jnp.where((block_of(source) == one_side) | (block_of(source) == other_side), factor * result, result)


def level_of(rng, extent, pieces, smallest, top_value):
    def one(axis_at, blocks):
        steps = jax.random.uniform(jax.random.fold_in(jax.random.fold_in(rng, 6), axis_at), (blocks,), jnp.float32, smallest / len(pieces), top_value / len(pieces))
        return jnp.repeat(jnp.exp(steps), extent[axis_at] // blocks).reshape((-1,) + (1,) * (len(extent) - axis_at - 1))

    level = one(*pieces[0])
    for cut in pieces[1:]:
        level = level * one(*cut)
    return level


def scatter_about(key, dims, scale, bound, pieces=(), kind=jnp.bfloat16):
    array = jax.random.normal(key, dims, jnp.float32) * scale
    if len(pieces) > 0:
        array = level_of(key, dims, pieces, -0.22, 0.18) * array
    return jnp.clip(array, min=-bound, max=bound).astype(kind)


def noise_with(stream_key, dims, width, reach, split, heavy, kind=jnp.bfloat16):
    result = width * jax.random.normal(stream_key, dims, jnp.float32)
    if split:
        result = result * level_of(stream_key, dims, split, -0.22, 0.18)
    return jnp.clip(with_spikes(result, jax.random.fold_in(stream_key, 3), *heavy), -reach, reach).astype(kind)


def setup_inputs(seed: int = 0) -> dict:
    seeds = jax.random.split(jax.random.key(seed), 12)
    return {
        "hidden_in": scatter_about(seeds[0], (SEGMENTS, SEG, D), 1.0, 6.0, ((0, 32), (1, 4))),
        "reset": draw_reset(jax.random.fold_in(seeds[11], 71), 0),
        "w_qkv": scatter_about(seeds[2], (D, 3 * D), D ** -0.5, 0.21875, ((0, 128),)),
        "w_attn_out": scatter_about(seeds[3], (D, D), (D // 2) ** -0.5, 0.3125, ((0, 128),)),
        "norm_gains": jnp.clip(1.0 + 0.1 * jax.random.normal(seeds[4], (2, D), jnp.float32), 0.5, 1.5).astype(jnp.bfloat16),
        "norm_biases": scatter_about(seeds[5], (2, D), 0.3, 2.0, ((1, 128),)),
        "memory_tokens": scatter_about(seeds[6], (2, MEM, D), 1.0, 6.0, ((2, 128),)),
        "w_in": scatter_about(seeds[7], (D, FF), D ** -0.5, 0.21875, ((0, 32), (1, 4))),
        "w_out": scatter_about(seeds[8], (FF, D), FF ** -0.5, 0.109375, ((0, 4), (1, 32))),
        "grad_hidden": noise_with(seeds[9], (SEGMENTS, SEG, D), 1.0, 6.0, ((0, 32), (1, 4)), (0, 2, 32, 2.75)),
        "grad_memory": scatter_about(seeds[10], (SEGMENTS, 2 * MEM, D), 1.0, 6.0, ((0, 32), (1, 4))),
    }


EPSILON = 1e-05

@jax.custom_vjp
def low(v):
    return lax.optimization_barrier(v.astype(jnp.bfloat16)).astype(jnp.float32)

@jax.custom_vjp
def low_back(v):
    return v

def low_keep(v):
    return (low(v), None)

def low_pass(kept, grad):
    return (grad,)

def back_keep(v):
    return (v, None)

def back_low(kept, grad):
    return (low(grad),)
low.defvjp(low_keep, low_pass)
low_back.defvjp(back_keep, back_low)

def product(left, right):
    return jnp.matmul(left, right, precision=lax.Precision.HIGHEST)

def layer_norm(inputs, gain, offset):
    centre = lax.optimization_barrier(jnp.mean(inputs, -1, keepdims=True))
    centred = inputs - centre
    spread = lax.optimization_barrier(jnp.mean(centred * centred, -1, keepdims=True))
    return centred * lax.rsqrt(spread + EPSILON) * gain + offset

def gelu_exact(inputs):
    return 0.5 * inputs * (1.0 + lax.erf(inputs * 0.7071067811865476))

def segment_layer(block, weight_qkv, weight_proj, gains, biases, weight_in, weight_out):
    count = block.shape[0]
    projected = low(low_back(product(block, weight_qkv)))
    queries = projected[:, :D].reshape(count, HEADS, HEAD_DIM)
    keys_part = projected[:, D:2 * D].reshape(count, HEADS, HEAD_DIM)
    values_part = projected[:, 2 * D:].reshape(count, HEADS, HEAD_DIM)
    scores = low_back(jnp.einsum('qhd,khd->hqk', queries, keys_part, precision=lax.Precision.HIGHEST) * 0.125)
    peak = lax.optimization_barrier(jnp.max(scores, -1, keepdims=True))
    raised = jnp.exp(scores - peak)
    probs = raised / lax.optimization_barrier(jnp.sum(raised, -1, keepdims=True))
    attended = jnp.einsum('hqk,khd->qhd', low(probs), values_part, precision=lax.Precision.HIGHEST).reshape(count, D)
    attended = low(low_back(attended))
    branch = low_back(product(attended, weight_proj))
    first = layer_norm(block + branch, gains[0], biases[0])
    hidden = low_back(product(low(first), weight_in))
    active = low(gelu_exact(hidden))
    second = low_back(product(active, weight_out))
    return layer_norm(first + second, gains[1], biases[1])

def reference(hidden_in, reset, w_qkv, w_attn_out, norm_gains, norm_biases, memory_tokens, w_in, w_out, grad_hidden, grad_memory):
    tokens = hidden_in.astype(jnp.float32)
    weight_qkv = w_qkv.astype(jnp.float32)
    weight_proj = w_attn_out.astype(jnp.float32)
    gains = norm_gains.astype(jnp.float32)
    biases = norm_biases.astype(jnp.float32)
    memory = memory_tokens.astype(jnp.float32)
    weight_in = w_in.astype(jnp.float32)
    weight_out = w_out.astype(jnp.float32)

    def pass_one(carry, inputs):
        segment, flag = inputs
        read_rows = jnp.where(flag == 1, memory[0], carry)
        block = jnp.concatenate([segment, read_rows, memory[1]], 0)
        output = segment_layer(block, weight_qkv, weight_proj, gains, biases, weight_in, weight_out)
        written = low(output[SEG + MEM:])
        return (written, carry)
    _, priors = lax.scan(pass_one, jnp.zeros((MEM, D), jnp.float32), (tokens, reset))

    def whole(tokens, weight_qkv, weight_proj, gains, biases, memory, weight_in, weight_out):
        layer = jax.checkpoint(segment_layer)

        def single(inputs):
            segment, flag, prior = inputs
            chosen = flag.astype(jnp.float32)
            read_rows = chosen * memory[0] + (1.0 - chosen) * prior
            block = jnp.concatenate([segment, read_rows, memory[1]], 0)
            return layer(block, weight_qkv, weight_proj, gains, biases, weight_in, weight_out)
        return lax.map(single, (tokens, reset, priors))
    outputs, pullback = jax.vjp(whole, tokens, weight_qkv, weight_proj, gains, biases, memory, weight_in, weight_out)
    upstream = jnp.concatenate([grad_hidden, grad_memory], 1).astype(jnp.float32)
    grads = pullback(upstream)
    return (outputs[:, :SEG].astype(jnp.bfloat16), outputs[:, SEG:].astype(jnp.bfloat16), grads[0], grads[1], grads[2], grads[3], grads[4], grads[5], grads[6], grads[7])
```

```python
import functools

import jax
import jax.numpy as jnp
import numpy as np
from jax import lax
from jax.experimental import pallas as pl
from jax.experimental.pallas import tpu as pltpu
from jax.sharding import PartitionSpec as P

D = 768
HALF = 384
MEM = 10
TOKENS = 64
OWN = 272
ROWS = 2 * OWN
TP = 4
SMALL = 128
ACOLS = 4 * HALF + SMALL
CUT = 768
EPSILON = 1e-05
INV_ROOT_TWO = 0.7071067811865476
INV_ROOT_TWOPI = 0.3989422804014327
EXP_SCALE = 0.125 * 1.4426950408889634
MASKED = -1e30
F32 = jnp.float32
BF16 = jnp.bfloat16
MESH = pl.DeviceIdType.MESH
NN = (((1,), (0,)), ((), ()))
NT = (((1,), (1,)), ((), ()))
TN = (((0,), (0,)), ((), ()))


def dot(a, b, dims=NN):
    return lax.dot_general(a, b, dims, preferred_element_type=F32)


def up16(n):
    return -(-n // 16) * 16


class Shape:
    def __init__(self, dp):
        self.dp = dp
        planes = dp // 2
        self.ny = int(round(planes**0.5))
        self.nz = planes // self.ny
        self.wrows = D // dp
        self.arows = D // (dp * TP)
        self.brows = 2 * self.wrows
        self.pr = up16(self.arows)
        self.fr = up16(self.wrows)


def selections(sh):
    pack = np.zeros((sh.brows, TP * 2 * sh.pr), np.float32)
    for c in range(2):
        for x in range(TP):
            for i in range(sh.arows):
                pack[c * sh.wrows + x * sh.arows + i, (x * 2 + c) * sh.pr + i] = 1
    small = np.zeros((48, SMALL), np.float32)
    for i in range(4):
        small[i, i] = 1
    for kind in range(2):
        for i in range(MEM):
            small[16 + 16 * kind + (i // 5) * 8 + i % 5, 4 + MEM * kind + i] = 1
    return pack, small


def norm_forward(inputs, gain, offset):
    centred = inputs - jnp.mean(inputs, -1, keepdims=True)
    spread = jnp.mean(centred * centred, -1, keepdims=True)
    inverse = lax.rsqrt(spread + EPSILON)
    normed = centred * inverse
    return normed * gain + offset, normed, inverse


def norm_backward(upstream, normed, inverse, gain):
    scaled = upstream * gain
    first_mean = jnp.mean(scaled, -1, keepdims=True)
    second_mean = jnp.mean(scaled * normed, -1, keepdims=True)
    return inverse * (scaled - first_mean - normed * second_mean)


def column_sum(a):
    return jnp.sum(a, 0, keepdims=True)


SCRATCH = {}


def scratch_of(sh):
    nz, ny, br = sh.nz, sh.ny, sh.brows
    s = {
        "p1": ((TP, 2, sh.pr, ACOLS), BF16),
        "f1": ((2, sh.fr, D), BF16),
        "wa": ((nz, ny, br, ACOLS), BF16),
        "wi": ((TP, nz, ny, br, HALF), BF16),
        "wt": ((TP, nz, ny, br, HALF), BF16),
        "wo": ((2, nz, ny, br, HALF), BF16),
        "par": ((8, D), F32),
        "x": ((ROWS, D), BF16),
        "gyt": ((TP * TOKENS, D), BF16),
        "gm": ((2, 8, D), F32),
        "qkv": ((9, ROWS, 128), BF16),
        "pt": ((6, ROWS, ROWS), BF16),
        "ot": ((3, 128, ROWS), BF16),
        "oc": ((ROWS, HALF), BF16),
        "oown": ((2, OWN, HALF), BF16),
        "h1": ((OWN, D), F32),
        "n1": ((OWN, D), F32),
        "inv1": ((OWN, 1), F32),
        "h1b": ((ROWS, D), BF16),
        "gl": ((TP, ROWS, HALF), BF16),
        "sl": ((TP, ROWS, HALF), BF16),
        "fs": ((OWN, D), F32),
        "fr": ((OWN, D), F32),
        "n2": ((OWN, D), F32),
        "yb": ((OWN, D), BF16),
        "mo": ((2, 8, D), F32),
        "hop": ((16, D), BF16),
        "dz": ((OWN, D), F32),
        "dfb": ((ROWS, D), BF16),
        "du": ((TP, ROWS, HALF), BF16),
        "dhs": ((OWN, D), F32),
        "dhr": ((OWN, D), F32),
        "dr": ((OWN, D), F32),
        "dab": ((ROWS, D), BF16),
        "doc": ((3, ROWS, 128), BF16),
        "dqkv": ((9, ROWS, 128), BF16),
        "ga": ((nz, ny, br, ACOLS), BF16),
        "gi": ((TP, nz, ny, br, HALF), BF16),
        "gt": ((TP, nz, ny, br, HALF), BF16),
        "gos": ((D // 2 // br if nz > 1 else 1, br if nz > 1 else HALF, HALF), BF16),
        "dxs": ((OWN, D), F32),
        "dxr": ((OWN, D), F32),
        "dxb": ((TP * TOKENS, D), BF16),
        "sg": ((48, D), F32),
        "e3": ((TP, 2, sh.pr, ACOLS), BF16),
        "r3": ((TP - 1, 2, sh.pr, ACOLS), BF16),
        "s4": ((2, sh.pr, ACOLS), F32),
        "sf": ((2, sh.wrows, D), F32),
    }
    if nz > 1:
        s["gos"] = ((nz // 2, ny, br, HALF), BF16)
    else:
        s["gos"] = ((1, 1, HALF, HALF), BF16)
    sizes = {"x": TP, "z": nz, "y": ny}
    for name, order, cols, axes in jobs_of():
        left = [a for a in axes]
        for step, axis in enumerate(order):
            left = [a for a in left if a != axis]
            dims = tuple(sizes[a] for a in left)
            s[f"r{step}_{name}"] = ((max(1, sizes[axis] - 1),) + dims + (br, cols.stop - cols.start), BF16)
            if step < len(order) - 1:
                s[f"s{step}_{name}"] = (dims + (br, cols.stop - cols.start), BF16)
    return s


def jobs_of():
    orders = [("z", "y", "x"), ("x", "z", "y"), ("y", "x", "z")]
    jobs = []
    for kind in ("t", "i"):
        for j in range(3):
            jobs.append((f"{kind}{j}", orders[j], slice(128 * j, 128 * j + 128), ("x", "z", "y")))
    jobs.append(("a0", ("z", "y"), slice(0, CUT), ("z", "y")))
    jobs.append(("a1", ("y", "z"), slice(CUT, ACOLS), ("z", "y")))
    return jobs


ARRAY = {"t": ("wt", "gt"), "i": ("wi", "gi"), "a": ("wa", "ga")}


def kernel(sh, names, *refs):
    xin, gin, gmem, pk, ff, packsel, smallsel = refs[:7]
    hout, mout, dxo, gao, gfo = refs[7:12]
    b = dict(zip(names, refs[12 : 12 + len(names)]))
    ssem, rsem, xsem, lsem = refs[12 + len(names) :]
    nz, ny, br, wr, pr = sh.nz, sh.ny, sh.brows, sh.wrows, sh.pr

    dp = lax.axis_index("dp")
    x = lax.axis_index("tp")
    core = dp % 2
    y = (dp // 2) % ny
    z = dp // (2 * ny)
    other = 1 - core
    chain = x // 2
    seg = jnp.where((x == 1) | (x == 2), 1, 0)
    at = {"x": x, "y": y, "z": z}
    size = {"x": TP, "y": ny, "z": nz}

    def device(x_=x, y_=y, z_=z, c_=core):
        return ((z_ * ny + y_) * 2 + c_, x_)

    def moved(axis, offset, core_=core):
        there = dict(at)
        there[axis] = (at[axis] + offset) % size[axis]
        return device(there["x"], there["y"], there["z"], core_)

    sibling = device(c_=other)
    counts = {"s": 0, "r": 0}
    sent = []

    def remote(src, dst, to):
        copy = pltpu.make_async_remote_copy(
            src_ref=src,
            dst_ref=dst,
            send_sem=ssem.at[counts["s"]],
            recv_sem=rsem.at[counts["r"]],
            device_id=to,
            device_id_type=MESH,
        )
        counts["s"] += 1
        counts["r"] += 1
        copy.start()
        sent.append(copy)
        return copy

    def arrived(copies):
        for copy in copies:
            copy.wait_recv()

    locals_ = [0]

    def local(src, dst):
        copy = pltpu.make_async_copy(src, dst, lsem.at[locals_[0]])
        locals_[0] += 1
        copy.start()
        return copy

    barrier = pltpu.get_barrier_semaphore()
    peers = [sibling]
    for o in range(1, TP):
        peers += [moved("x", o), moved("x", o, other)]
    for axis in ("y", "z"):
        for o in range(1, size[axis]):
            peers.append(moved(axis, o))
    for peer in peers:
        pl.semaphore_signal(barrier, inc=1, device_id=peer, device_id_type=MESH)
    pl.semaphore_wait(barrier, len(peers))

    pk_local = local(pk.at[core], b["p1"].at[x, core])
    ff_local = local(ff.at[core], b["f1"].at[core])
    pk_swap = remote(pk.at[other], b["p1"].at[x, core], sibling)
    ff_swap = remote(ff.at[other], b["f1"].at[core], sibling)

    conditional = []

    def to_device(src, dst, place, here, kind, send_slot):
        copy = pltpu.make_async_remote_copy(
            src_ref=src,
            dst_ref=dst,
            send_sem=xsem.at[kind, 8 + send_slot],
            recv_sem=here,
            device_id=device(x_=place[0], c_=place[1]),
            device_id_type=MESH,
        )
        same = (place[0] == x) & (place[1] == core)

        @pl.when(same)
        def _():
            pltpu.make_async_copy(src, dst, here).start()

        @pl.when(jnp.logical_not(same))
        def _():
            copy.start()

        conditional.append((same, copy))

    def from_device(dst, here):
        pltpu.make_async_copy(dst, dst, here).wait()

    def chip_of(k, s):
        return s + k * (3 - 2 * s)

    for s in range(2):
        for j in range(2):
            rows = pl.ds(TOKENS * j, TOKENS)
            to_device(
                xin.at[s, rows],
                b["x"].at[pl.ds(pl.multiple_of(OWN * j + TOKENS * x, 16), TOKENS)],
                (chip_of(core, s), j),
                xsem.at[0, x],
                0,
                2 * s + j,
            )
    for s in range(2):
        for j in range(2):
            rows = pl.ds(TOKENS * j, TOKENS)
            to_device(
                gin.at[s, rows],
                b["gyt"].at[pl.ds(pl.multiple_of(TOKENS * x, 16), TOKENS)],
                (chip_of(core, s), j),
                xsem.at[1, x],
                1,
                2 * s + j,
            )
        to_device(
            gmem.at[s],
            b["gm"].at[x % 2],
            (chip_of(core, s), x // 2),
            xsem.at[2, x % 2],
            2,
            s,
        )

    def index(axes, fixed):
        return tuple(fixed.get(a, slice(None)) for a in axes)

    def gather_step(job, step):
        name, order, cols, axes = job
        order = order[::-1]
        array = b[ARRAY[name[0]][0]]
        axis = order[step]
        fixed = {a: at[a] for a in order[step:]}
        part = array.at[index(axes, fixed) + (slice(None), cols)]
        return [remote(part, part, moved(axis, o)) for o in range(1, size[axis])]

    jobs = {j[0]: j for j in jobs_of()}
    ff_names = ["i0", "i1", "i2", "t0", "t1", "t2"]

    ff_local.wait()
    arrived([ff_swap])
    two = [b["f1"][c].astype(F32)[:wr] for c in range(2)]
    block = jnp.concatenate(two, 0).astype(BF16)
    b["wi"][x, z, y] = block[:, :HALF]
    b["wt"][x, z, y] = block[:, HALF:]

    pk_local.wait()
    arrived([pk_swap])
    mine = b["p1"].at[x]
    steps = [remote(mine, mine, moved("x", o)) for o in range(1, TP)]
    arrived(steps)
    b["wa"][z, y] = dot(packsel[...], b["p1"][...].reshape(TP * 2 * pr, ACOLS)).astype(BF16)
    first = {n: gather_step(jobs[n], 0) for n in ("a0", "a1")}
    ff_steps = {n: gather_step(jobs[n], 0) for n in ff_names}
    second = {}
    for n in ("a0", "a1"):
        arrived(first[n])
        second[n] = gather_step(jobs[n], 1)

    for i in range(TP):
        from_device(b["x"].at[pl.ds(pl.multiple_of(OWN * core + TOKENS * i, 16), TOKENS)], xsem.at[0, i])
    half = b["x"].at[pl.ds(pl.multiple_of(OWN * core, 16), TP * TOKENS)]
    x_swap = remote(half, half, sibling)

    for n in ff_names:
        arrived(ff_steps[n])
        ff_steps[n] = gather_step(jobs[n], 1)
    for n in ("a0", "a1"):
        arrived(second[n])
    wo_cols = slice(3 * HALF, 4 * HALF)
    wo_local = local(b["wa"].at[:, :, :, wo_cols], b["wo"].at[core])
    wo_swap = remote(b["wa"].at[:, :, :, wo_cols], b["wo"].at[core], sibling)
    for n in ff_names:
        arrived(ff_steps[n])
        ff_steps[n] = gather_step(jobs[n], 2)

    def attention_weight(n):
        return b["wa"][:, :, :, HALF * n : HALF * (n + 1)].reshape(D, HALF)

    small = b["wa"][:, :, :, 4 * HALF :].reshape(D, SMALL)
    chosen = dot(smallsel[...], small, NT)
    b["par"][...] = chosen[0:8]
    b["x"][OWN + 256 : OWN + 272] = chosen[32:48].astype(BF16)

    @pl.when(seg == 0)
    def _():
        b["x"][256:272] = chosen[16:32].astype(BF16)

    gains = [b["par"][i : i + 1] for i in range(2)]
    biases = [b["par"][2 + i : 3 + i] for i in range(2)]
    arrived([x_swap])

    hop_to = jnp.where(x == 0, 1, 2)
    hops = []
    for j in range(2):
        hops.append(
            pltpu.make_async_remote_copy(
                src_ref=b["hop"],
                dst_ref=b["x"].at[256:272],
                send_sem=xsem.at[6, j],
                recv_sem=xsem.at[6, 2],
                device_id=device(x_=hop_to, c_=j),
                device_id_type=MESH,
            )
        )

    @pl.when(seg == 1)
    def _():
        hops[0].wait_recv()

    own_rows = pl.ds(pl.multiple_of(OWN * core, 16), OWN)
    other_rows = pl.ds(pl.multiple_of(OWN * other, 16), OWN)

    for n in range(3):
        out = dot(b["x"][...], attention_weight(n)).astype(BF16)
        for p in range(3):
            b["qkv"][3 * n + p] = out[:, 128 * p : 128 * p + 128]

    def head_masks(hh):
        lane = lax.broadcasted_iota(jnp.int32, (ROWS, 128), 1)
        row = lax.broadcasted_iota(jnp.int32, (ROWS, 128), 0)
        inside = (lane // 64) == hh
        spare = lane == 64 * (1 - hh)
        memory = ((row >= 256) & (row < 272)) | (row >= OWN + 256)
        invalid = memory & (row % 8 >= 5)
        return inside, spare, invalid

    def forward_pair(p):
        qp, kp, vp = b["qkv"][p], b["qkv"][3 + p], b["qkv"][6 + p]
        vt = vp.T
        for hh in range(2):
            inside, spare, invalid = head_masks(hh)
            zero = jnp.zeros_like(kp)
            kmask = jnp.where(spare & invalid, jnp.full_like(kp, MASKED), zero)
            km = jnp.where(inside, kp, kmask)
            qm = jnp.where(inside, qp, jnp.where(spare, jnp.ones_like(qp), zero))
            scores = dot(km, qm, NT)
            peak = jnp.max(scores, 0, keepdims=True)
            raised = jnp.exp2((scores - peak) * EXP_SCALE)
            total = jnp.sum(raised, 0, keepdims=True)
            probs = (raised * (1.0 / total)).astype(BF16)
            b["pt"][2 * p + hh] = probs
            b["ot"][p, 64 * hh : 64 * hh + 64] = dot(vt[64 * hh : 64 * hh + 64], probs).astype(BF16)

    for p in range(3):
        forward_pair(p)
        b["oc"][:, 128 * p : 128 * p + 128] = b["ot"][p].T

    o_local = local(b["oc"].at[own_rows], b["oown"].at[core])
    o_swap = remote(b["oc"].at[other_rows], b["oown"].at[core], sibling)
    wo_local.wait()
    arrived([wo_swap])
    o_local.wait()
    arrived([o_swap])
    halves = []
    for h in range(2):
        w = b["wo"][h].reshape(D, HALF)
        halves.append(dot(b["oown"][0], w[:HALF]) + dot(b["oown"][1], w[HALF:]))
    attended = jnp.concatenate(halves, 1)
    h1, n1, inv1 = norm_forward(b["x"][own_rows].astype(F32) + attended, gains[0], biases[0])
    b["h1"][...] = h1
    b["n1"][...] = n1
    b["inv1"][...] = inv1
    b["h1b"][own_rows] = h1.astype(BF16)
    h_swap = remote(b["h1b"].at[own_rows], b["h1b"].at[own_rows], sibling)
    for n in ff_names[:3]:
        arrived(ff_steps[n])
    arrived([h_swap])

    def up_weight(t):
        return b["wi"][t].reshape(D, HALF)

    def down_weight(t):
        return b["wt"][t].reshape(D, HALF)

    @pl.loop(0, TP)
    def _(t):
        units = dot(b["h1b"][...], up_weight(t))
        erf = 0.5 * (1.0 + lax.erf(units * INV_ROOT_TWO))
        b["gl"][t] = (units * erf).astype(BF16)
        b["sl"][t] = (erf + units * jnp.exp(-0.5 * units * units) * INV_ROOT_TWOPI).astype(BF16)

    for n in ff_names[3:]:
        arrived(ff_steps[n])

    def partial_down(rows):
        return sum(dot(b["gl"][t, rows], down_weight(t), NT) for t in range(TP))

    b["fs"][...] = partial_down(other_rows)
    f_swap = remote(b["fs"], b["fr"], sibling)
    branch = partial_down(own_rows)
    arrived([f_swap])
    out, n2, inv2 = norm_forward(b["h1"][...] + branch + b["fr"][...], gains[1], biases[1])
    low = out.astype(BF16)
    b["yb"][...] = low
    row16 = lax.broadcasted_iota(jnp.int32, (16, D), 0)
    memory_out = jnp.where(row16 % 8 < 5, out[256:272], 0.0).astype(BF16)
    b["hop"][...] = memory_out
    b["mo"][...] = memory_out.astype(F32).reshape(2, 8, D)

    @pl.when((seg == 0) & (core == 1))
    def _():
        hops[0].start()
        hops[1].start()

    for i in range(TP):
        to_device(
            b["yb"].at[pl.ds(TOKENS * i, TOKENS)],
            hout.at[seg, pl.ds(pl.multiple_of(TOKENS * core, 16), TOKENS)],
            (i, chain),
            xsem.at[3, 2 * seg + core],
            3,
            i,
        )
    for i in range(2):
        to_device(b["mo"].at[i], mout.at[seg], (2 * core + i, chain), xsem.at[4, seg], 4, i)

    for i in range(TP):
        from_device(b["gyt"].at[pl.ds(TOKENS * i, TOKENS)], xsem.at[1, i])
    for i in range(2):
        from_device(b["gm"].at[i], xsem.at[2, i])
    upstream = jnp.concatenate([b["gyt"][...].astype(F32), b["gm"][...].reshape(16, D)], 0)
    b["sg"][...] = jnp.zeros((48, D), F32)
    b["sg"][1:2] = column_sum(upstream * n2)
    b["sg"][3:4] = column_sum(upstream)
    dz = norm_backward(upstream, n2, inv2, gains[1])
    b["dz"][...] = dz
    b["dfb"][own_rows] = dz.astype(BF16)
    df_swap = remote(b["dfb"].at[own_rows], b["dfb"].at[own_rows], sibling)
    arrived([df_swap])

    @pl.loop(0, TP)
    def _(t):
        b["du"][t] = (dot(b["dfb"][...], down_weight(t)) * b["sl"][t].astype(F32)).astype(BF16)

    def partial_up(rows):
        return sum(dot(b["du"][t, rows], up_weight(t), NT) for t in range(TP))

    b["dhs"][...] = partial_up(other_rows)
    dh_swap = remote(b["dhs"], b["dhr"], sibling)
    dh_own = partial_up(own_rows)
    b["dz"][...] = b["dz"][...] + dh_own

    @pl.loop(0, TP)
    def _(t):
        b["gt"][t] = dot(b["dfb"][...], b["gl"][t], TN).astype(BF16).reshape(nz, ny, br, HALF)

    def pick(axes, axis, place):
        return tuple(place if a == axis else slice(None) for a in axes)

    def scatter_send(job, step):
        name, order, cols, axes = job
        axis = order[step]
        left = [a for a in axes if a not in order[:step]]
        if step == 0:
            source = b[ARRAY[name[0]][1]]
            tail = (slice(None), cols)
        else:
            source = b[f"s{step - 1}_{name}"]
            tail = ()
        copies = []
        for o in range(1, size[axis]):
            there = (at[axis] + o) % size[axis]
            copies.append(
                remote(source.at[pick(left, axis, there) + tail], b[f"r{step}_{name}"].at[o - 1], moved(axis, o))
            )
        return copies

    def scatter_sum(job, step, copies):
        name, order, cols, axes = job
        axis = order[step]
        left = [a for a in axes if a not in order[:step]]
        arrived(copies)
        if step == 0:
            mine = b[ARRAY[name[0]][1]][pick(left, axis, at[axis]) + (slice(None), cols)]
        else:
            mine = b[f"s{step - 1}_{name}"][pick(left, axis, at[axis])]
        total = mine.astype(F32)
        for o in range(1, size[axis]):
            total = total + b[f"r{step}_{name}"][o - 1].astype(F32)
        if step < len(order) - 1:
            b[f"s{step}_{name}"][...] = total.astype(BF16)
        return total

    rs = {n: scatter_send(jobs[n], 0) for n in ("t0", "t1", "t2")}

    @pl.loop(0, TP)
    def _(t):
        b["gi"][t] = dot(b["h1b"][...], b["du"][t], TN).astype(BF16).reshape(nz, ny, br, HALF)

    rs.update({n: scatter_send(jobs[n], 0) for n in ("i0", "i1", "i2")})

    arrived([dh_swap])
    into_first = b["dz"][...] + b["dhr"][...]
    b["sg"][0:1] = column_sum(into_first * b["n1"][...])
    b["sg"][2:3] = column_sum(into_first)
    dr = norm_backward(into_first, b["n1"][...], b["inv1"][...], gains[0])
    b["dr"][...] = dr
    b["dab"][own_rows] = dr.astype(BF16)
    da_swap = remote(b["dab"].at[own_rows], b["dab"].at[own_rows], sibling)
    arrived([da_swap])

    def head_rows(ref, c):
        if nz > 1:
            return ref.at[pl.ds(c * (nz // 2), nz // 2)]
        return ref.at[:, :, pl.ds(pl.multiple_of(c * HALF, 16), HALF)]

    grad_mixed = 0.0
    for h in range(2):
        w = head_rows(b["wo"].at[h], core)[...].reshape(HALF, HALF)
        grad_mixed = grad_mixed + dot(b["dab"][:, HALF * h : HALF * (h + 1)], w, NT)
    for p in range(3):
        b["doc"][p] = grad_mixed[:, 128 * p : 128 * p + 128].astype(BF16)

    mixed_t = b["ot"][...].reshape(HALF, ROWS)

    def proj_grad(h):
        cols = pl.ds(pl.multiple_of(HALF * h, 128), HALF)
        return dot(mixed_t, b["dab"][:, cols]).astype(BF16).reshape(b["gos"].shape)

    def wo_part(c):
        return head_rows(b["ga"].at[:, :, :, wo_cols], c)

    b["gos"][...] = proj_grad(other)
    go_swap = remote(b["gos"], wo_part(core), sibling)
    wo_part(core)[...] = proj_grad(core)

    def backward_pair(p):
        qp, kp, vp, dop = b["qkv"][p], b["qkv"][3 + p], b["qkv"][6 + p], b["doc"][p]
        kt = kp.T
        dv = dk = 0.0
        dq = []
        for hh in range(2):
            inside, _, _ = head_masks(hh)
            zero = jnp.zeros_like(kp)
            grad_probs = dot(jnp.where(inside, vp, zero), dop, NT)
            low_probs = b["pt"][2 * p + hh]
            probs = low_probs.astype(F32)
            row_term = jnp.sum(probs * grad_probs, 0, keepdims=True)
            ds = (probs * (grad_probs - row_term)).astype(BF16)
            dv = dv + dot(low_probs, jnp.where(inside, dop, zero))
            dk = dk + dot(ds, jnp.where(inside, qp, zero))
            dq.append(dot(kt[64 * hh : 64 * hh + 64], ds))
        b["dqkv"][p] = (jnp.concatenate(dq, 0) * 0.125).T.astype(BF16)
        b["dqkv"][3 + p] = (dk * 0.125).astype(BF16)
        b["dqkv"][6 + p] = dv.astype(BF16)

    for p in range(3):
        backward_pair(p)
        for n in (("t0", "t1", "t2"), ("i0", "i1", "i2"), ())[p]:
            scatter_sum(jobs[n], 0, rs[n])
            rs[n] = scatter_send(jobs[n], 1)

    def joined(n, rows):
        return jnp.concatenate([b["dqkv"][3 * n + p, rows] for p in range(3)], 1)

    everyone = slice(None)
    for n in range(3):
        part = dot(b["x"][...], joined(n, everyone), TN).astype(BF16)
        b["ga"][:, :, :, HALF * n : HALF * (n + 1)] = part.reshape(nz, ny, br, HALF)
    rs["a0"] = scatter_send(jobs["a0"], 0)

    def partial_input(rows):
        return sum(dot(joined(n, rows), attention_weight(n), NT) for n in range(3))

    b["dxs"][...] = partial_input(other_rows)
    dx_swap = remote(b["dxs"], b["dxr"], sibling)
    dx = partial_input(own_rows) + b["dr"][...]
    arrived([dx_swap])
    dx = dx + b["dxr"][...]
    b["dxb"][...] = dx[:256].astype(BF16)
    for i in range(TP):
        to_device(
            b["dxb"].at[pl.ds(TOKENS * i, TOKENS)],
            dxo.at[seg, pl.ds(pl.multiple_of(TOKENS * core, 16), TOKENS)],
            (i, chain),
            xsem.at[5, 2 * seg + core],
            5,
            i,
        )

    @pl.when((core == 0) & (seg == 0))
    def _():
        b["sg"][16:32] = dx[256:272]

    @pl.when(core == 1)
    def _():
        b["sg"][32:48] = dx[256:272]

    small_grads = dot(b["sg"][...].astype(BF16), smallsel[...], TN).astype(BF16)
    b["ga"][:, :, :, 4 * HALF :] = small_grads.reshape(nz, ny, br, SMALL)
    arrived([go_swap])
    rs["a1"] = scatter_send(jobs["a1"], 0)

    for n in ("t0", "t1", "t2"):
        scatter_sum(jobs[n], 1, rs[n])
        rs[n] = scatter_send(jobs[n], 2)
    for n in ("a0", "a1"):
        scatter_sum(jobs[n], 0, rs[n])
        rs[n] = scatter_send(jobs[n], 1)
    for n in ("i0", "i1", "i2"):
        scatter_sum(jobs[n], 1, rs[n])
        rs[n] = scatter_send(jobs[n], 2)
    last = [scatter_sum(jobs[n], 1, rs[n]).astype(BF16) for n in ("a0", "a1")]
    for n, cols in zip(range(2), (slice(0, CUT), slice(CUT, ACOLS))):
        spread = dot(packsel[...], last[n], TN).astype(BF16)
        b["e3"][:, :, :, cols] = spread.reshape(TP, 2, pr, cols.stop - cols.start)
    steps = [remote(b["e3"].at[(x + o) % TP], b["r3"].at[o - 1], moved("x", o)) for o in range(1, TP)]

    for kind, n0 in (("i", 0), ("t", HALF)):
        for j in range(3):
            n = f"{kind}{j}"
            total = scatter_sum(jobs[n], 2, rs[n])
            cols = slice(n0 + 128 * j, n0 + 128 * j + 128)
            b["sf"][0, :, cols] = total[:wr]
            b["sf"][1, :, cols] = total[wr:]
    sf_local = local(b["sf"].at[core], gfo.at[core])
    sf_swap = remote(b["sf"].at[other], gfo.at[core], sibling)

    arrived(steps)
    total = b["e3"][x].astype(F32)
    for o in range(1, TP):
        total = total + b["r3"][o - 1].astype(F32)
    b["s4"][...] = total
    s4_local = local(b["s4"].at[core], gao.at[core])
    s4_swap = remote(b["s4"].at[other], gao.at[core], sibling)

    for kind, out_ref in ((3, hout), (5, dxo)):
        for s in range(2):
            for j in range(2):
                from_device(out_ref.at[s, pl.ds(TOKENS * j, TOKENS)], xsem.at[kind, 2 * s + j])
    for s in range(2):
        from_device(mout.at[s], xsem.at[4, s])
    sf_local.wait()
    s4_local.wait()
    arrived([sf_swap, s4_swap])

    for copy in sent:
        copy.wait_send()
    for same, copy in conditional:

        @pl.when(jnp.logical_not(same))
        def _():
            copy.wait_send()

    @pl.when((seg == 0) & (core == 1))
    def _():
        hops[0].wait_send()
        hops[1].wait_send()


def layer(sh, arrays):
    pack, small = selections(sh)
    table = scratch_of(sh)
    names = list(table)
    vmem = pl.BlockSpec(memory_space=pltpu.VMEM)
    outs = [
        jax.ShapeDtypeStruct((2, 128, D), BF16),
        jax.ShapeDtypeStruct((2, 8, D), F32),
        jax.ShapeDtypeStruct((2, 128, D), BF16),
        jax.ShapeDtypeStruct((2, sh.pr, ACOLS), F32),
        jax.ShapeDtypeStruct((2, sh.wrows, D), F32),
    ]
    return pl.pallas_call(
        functools.partial(kernel, sh, names),
        name="layer",
        out_shape=outs,
        in_specs=[vmem] * 7,
        out_specs=[vmem] * len(outs),
        scratch_shapes=[pltpu.VMEM(*table[n]) for n in names]
        + [
            pltpu.SemaphoreType.DMA((180,)),
            pltpu.SemaphoreType.DMA((180,)),
            pltpu.SemaphoreType.DMA((7, 12)),
            pltpu.SemaphoreType.DMA((8,)),
        ],
        compiler_params=pltpu.CompilerParams(
            collective_id=0, has_side_effects=True, vmem_limit_bytes=64 * 2**20 - 2**17
        ),
    )(*arrays, jnp.asarray(pack, BF16), jnp.asarray(small, BF16))


def body(
    sh,
    hidden_in,
    reset,
    w_qkv,
    w_attn_out,
    norm_gains,
    norm_biases,
    memory_tokens,
    w_in,
    w_out,
    grad_hidden,
    grad_memory,
):
    ar, wr = sh.arows, sh.wrows
    small = jnp.concatenate([norm_gains, norm_biases, memory_tokens.reshape(2 * MEM, ar)], 0).T
    small = jnp.pad(small, ((0, 0), (0, SMALL - small.shape[1])))
    by_half = w_qkv.reshape(ar, 3, 2, HALF).transpose(2, 0, 1, 3).reshape(2, ar, 3 * HALF)
    proj = w_attn_out.reshape(ar, 2, HALF).transpose(1, 0, 2)
    pk = jnp.concatenate([by_half, proj, jnp.broadcast_to(small, (2, ar, SMALL))], 2)
    pk = jnp.pad(pk, ((0, 0), (0, sh.pr - ar), (0, 0)))
    up = w_in.reshape(wr, 2, HALF).transpose(1, 0, 2)
    down = w_out.T.reshape(wr, 2, HALF).transpose(1, 0, 2)
    ff = jnp.pad(jnp.concatenate([up, down], 2), ((0, 0), (0, sh.fr - wr), (0, 0)))
    gmem = jnp.pad(grad_memory.astype(F32), ((0, 0), (0, 3), (0, 0)))
    hout, mout, dxo, gao, gfo = layer(sh, (hidden_in, grad_hidden, gmem, pk, ff))

    gq = gao[:, :ar, : 3 * HALF].reshape(2, ar, 3, HALF).transpose(1, 2, 0, 3).reshape(ar, 3 * D)
    gp = gao[:, :ar, 3 * HALF : 4 * HALF].transpose(1, 0, 2).reshape(ar, D)
    gs = (gao[0] + gao[1])[:ar, 4 * HALF : 4 * HALF + 4 + 2 * MEM].T
    gi = gfo[:, :, :HALF].transpose(1, 0, 2).reshape(wr, D)
    gt = gfo[:, :, HALF:].transpose(1, 0, 2).reshape(wr, D).T
    return (
        hout,
        mout[:, :5].astype(BF16),
        dxo.astype(F32),
        gq,
        gp,
        gs[0:2],
        gs[2:4],
        gs[4:].reshape(2, MEM, ar),
        gi,
        gt,
    )


def solution(mesh):
    sh = Shape(mesh.shape["dp"])
    return jax.shard_map(
        functools.partial(body, sh),
        mesh=mesh,
        in_specs=(
            P("dp", "tp", None),
            P("dp"),
            P(("dp", "tp"), None),
            P(("dp", "tp"), None),
            P(None, ("dp", "tp")),
            P(None, ("dp", "tp")),
            P(None, None, ("dp", "tp")),
            P("dp", "tp"),
            P("tp", "dp"),
            P("dp", "tp", None),
            P("dp", "tp", None),
        ),
        out_specs=(
            P("dp", "tp", None),
            P("dp", "tp", None),
            P("dp", "tp", None),
            P(("dp", "tp"), None),
            P(("dp", "tp"), None),
            P(None, ("dp", "tp")),
            P(None, ("dp", "tp")),
            P(None, None, ("dp", "tp")),
            P("dp", "tp"),
            P("tp", "dp"),
        ),
        check_vma=False,
    )
```

```python
import functools

import jax
import jax.numpy as jnp
import numpy as np
from jax import lax
from jax.experimental import pallas as pl
from jax.experimental.pallas import tpu as pltpu
from jax.sharding import PartitionSpec as P

D = 768
HALF = 384
MEM = 10
TOKENS = 64
OWN = 272
ROWS = 2 * OWN
TP = 4
SMALL = 128
ACOLS = 4 * HALF + SMALL
CUT = 768
WO = 3 * HALF
EPSILON = 1e-05
INV_ROOT_TWO = 0.7071067811865476
INV_ROOT_TWOPI = 0.3989422804014327
EXP_SCALE = 0.125 * 1.4426950408889634
MASKED = -1e30
F32 = jnp.float32
BF16 = jnp.bfloat16
MESH = pl.DeviceIdType.MESH
NN = (((1,), (0,)), ((), ()))
NT = (((1,), (1,)), ((), ()))
TN = (((0,), (0,)), ((), ()))


def dot(a, b, dims=NN):
    return lax.dot_general(a, b, dims, preferred_element_type=F32)


def up16(n):
    return -(-n // 16) * 16


class Shape:
    def __init__(self, dp):
        self.dp = dp
        planes = dp // 2
        self.ny = int(round(planes**0.5))
        self.nz = planes // self.ny
        self.wrows = D // dp
        self.arows = D // (dp * TP)
        self.brows = 2 * self.wrows
        self.pr = up16(self.arows)
        self.pc = -(-self.arows // 8) * 8
        self.fr = up16(self.wrows)


def selections(sh):
    pack = np.zeros((sh.brows, TP * 2 * sh.pc), np.float32)
    for c in range(2):
        for x in range(TP):
            for i in range(sh.arows):
                pack[c * sh.wrows + x * sh.arows + i, (x * 2 + c) * sh.pc + i] = 1
    small = np.zeros((48, SMALL), np.float32)
    for i in range(4):
        small[i, i] = 1
    for kind in range(2):
        for i in range(MEM):
            small[16 + 16 * kind + (i // 5) * 8 + i % 5, 4 + MEM * kind + i] = 1
    return pack, small


def norm_forward(inputs, gain, offset):
    centred = inputs - jnp.mean(inputs, -1, keepdims=True)
    spread = jnp.mean(centred * centred, -1, keepdims=True)
    inverse = lax.rsqrt(spread + EPSILON)
    normed = centred * inverse
    return normed * gain + offset, normed, inverse


def norm_backward(upstream, normed, inverse, gain):
    scaled = upstream * gain
    first_mean = jnp.mean(scaled, -1, keepdims=True)
    second_mean = jnp.mean(scaled * normed, -1, keepdims=True)
    return inverse * (scaled - first_mean - normed * second_mean)


def column_sum(a):
    return jnp.sum(a, 0, keepdims=True)


SCRATCH = {}


def scratch_of(sh):
    nz, ny, br = sh.nz, sh.ny, sh.brows
    s = {
        "p1": ((2, sh.pr, ACOLS), BF16),
        "p2": ((TP, 2 * sh.pc, ACOLS), BF16),
        "f1": ((2, sh.fr, D), BF16),
        "wa": ((nz, ny, br, ACOLS), BF16),
        "wf": ((TP, nz, ny, br, D), BF16),
        "wo": ((2, nz, ny, br, HALF), BF16),
        "par": ((8, D), F32),
        "x": ((ROWS, D), BF16),
        "gyt": ((TP * TOKENS, D), BF16),
        "gm": ((2, 8, D), F32),
        "qkv": ((9, ROWS, 128), BF16),
        "pt": ((6, ROWS, ROWS), BF16),
        "ot": ((3, 128, ROWS), BF16),
        "oc": ((ROWS, HALF), BF16),
        "oown": ((2, OWN, HALF), BF16),
        "h1": ((OWN, D), F32),
        "n1": ((OWN, D), F32),
        "inv1": ((OWN, 1), F32),
        "h1b": ((ROWS, D), BF16),
        "gl": ((2, ROWS, D), BF16),
        "sl": ((2, ROWS, D), BF16),
        "fs": ((OWN, D), BF16),
        "fr": ((OWN, D), BF16),
        "n2": ((OWN, D), F32),
        "yb": ((OWN, D), BF16),
        "mo": ((2, 8, D), F32),
        "hop": ((16, D), BF16),
        "hopin": ((16, D), BF16),
        "es": ((16, D), F32),
        "er": ((16, D), F32),
        "dz": ((OWN, D), F32),
        "dfb": ((ROWS, D), BF16),
        "du": ((2, ROWS, D), BF16),
        "dhs": ((OWN, D), BF16),
        "dhr": ((OWN, D), BF16),
        "dr": ((OWN, D), F32),
        "dab": ((ROWS, D), BF16),
        "doc": ((3, ROWS, 128), BF16),
        "dqkv": ((9, ROWS, 128), BF16),
        "ga": ((nz, ny, br, ACOLS), BF16),
        "gi": ((TP, nz, ny, br, HALF), BF16),
        "gt": ((TP, nz, ny, br, HALF), BF16),
        "gos": ((D // 2 // br if nz > 1 else 1, br if nz > 1 else HALF, HALF), BF16),
        "dxs": ((OWN, D), BF16),
        "dxr": ((OWN, D), BF16),
        "dxb": ((TP * TOKENS, D), BF16),
        "sg": ((48, D), F32),
        "e3": ((TP, 2 * sh.pc, ACOLS), BF16),
        "r3": ((TP - 1, 2 * sh.pc, ACOLS), BF16),
        "s4": ((2, sh.pc, ACOLS), F32),
        "sf": ((2, sh.wrows, D), F32),
    }
    if nz > 1:
        s["gos"] = ((nz // 2, ny, br, HALF), BF16)
    else:
        s["gos"] = ((1, 1, HALF, HALF), BF16)
    sizes = {"x": TP, "z": nz, "y": ny}
    for name, order, cols, axes in scatter_jobs():
        left = [a for a in axes]
        for step, axis in enumerate(order):
            left = [a for a in left if a != axis]
            dims = tuple(sizes[a] for a in left)
            s[f"r{step}_{name}"] = ((max(1, sizes[axis] - 1),) + dims + (br, cols.stop - cols.start), BF16)
            if step < len(order) - 1:
                s[f"s{step}_{name}"] = (dims + (br, cols.stop - cols.start), BF16)
    return s


def scatter_jobs():
    orders = [("z", "y", "x"), ("x", "z", "y"), ("y", "x", "z")]
    jobs = []
    for kind in ("t", "i"):
        for j in range(3):
            jobs.append((f"{kind}{j}", orders[j], slice(128 * j, 128 * j + 128), ("x", "z", "y")))
    zy, yz = ("z", "y"), ("y", "z")
    jobs.append(("aw", yz, slice(WO, WO + HALF), zy))
    jobs.append(("a0", zy, slice(0, HALF), zy))
    jobs.append(("a1", yz, slice(HALF, 2 * HALF), zy))
    jobs.append(("a2", zy, slice(2 * HALF, 2 * HALF + 256), zy))
    jobs.append(("a3", yz, slice(2 * HALF + 256, 3 * HALF), zy))
    jobs.append(("as", yz, slice(4 * HALF, ACOLS), zy))
    return jobs


def gather_jobs():
    orders = [("x", "y", "z"), ("y", "z", "x"), ("z", "x", "y")]
    jobs = [(f"f{j}", orders[j], slice(256 * j, 256 * j + 256), ("x", "z", "y")) for j in range(3)]
    jobs.append(("a0", ("y", "z"), slice(0, CUT), ("z", "y")))
    jobs.append(("a1", ("z", "y"), slice(CUT, ACOLS), ("z", "y")))
    return jobs


WEIGHTS = {"f": "wf", "a": "wa"}
GRADS = {"t": "gt", "i": "gi", "a": "ga"}


def kernel(sh, names, *refs):
    xin, gin, gmem, pk, ff, packsel, smallsel = refs[:7]
    hout, mout, dxo, gao, gfo = refs[7:12]
    b = dict(zip(names, refs[12 : 12 + len(names)]))
    ssem, rsem, xsem, lsem = refs[12 + len(names) :]
    nz, ny, br, wr, pr = sh.nz, sh.ny, sh.brows, sh.wrows, sh.pr

    dp = lax.axis_index("dp")
    x = lax.axis_index("tp")
    core = dp % 2
    y = (dp // 2) % ny
    z = dp // (2 * ny)
    other = 1 - core
    chain = x // 2
    seg = jnp.where((x == 1) | (x == 2), 1, 0)
    at = {"x": x, "y": y, "z": z}
    size = {"x": TP, "y": ny, "z": nz}

    def device(x_=x, y_=y, z_=z, c_=core):
        return ((z_ * ny + y_) * 2 + c_, x_)

    def moved(axis, offset, core_=core):
        there = dict(at)
        there[axis] = (at[axis] + offset) % size[axis]
        return device(there["x"], there["y"], there["z"], core_)

    sibling = device(c_=other)
    counts = {"s": 0, "r": 0}
    sent = []

    def remote(src, dst, to):
        copy = pltpu.make_async_remote_copy(
            src_ref=src,
            dst_ref=dst,
            send_sem=ssem.at[counts["s"]],
            recv_sem=rsem.at[counts["r"]],
            device_id=to,
            device_id_type=MESH,
        )
        counts["s"] += 1
        counts["r"] += 1
        copy.start()
        sent.append(copy)
        return copy

    def arrived(copies):
        for copy in copies:
            copy.wait_recv()

    locals_ = [0]

    def local(src, dst):
        copy = pltpu.make_async_copy(src, dst, lsem.at[locals_[0]])
        locals_[0] += 1
        copy.start()
        return copy

    barrier = pltpu.get_barrier_semaphore()
    peers = [sibling]
    for o in range(1, TP):
        peers += [moved("x", o), moved("x", o, other)]
    for axis in ("y", "z"):
        for o in range(1, size[axis]):
            peers.append(moved(axis, o))
    for peer in peers:
        pl.semaphore_signal(barrier, inc=1, device_id=peer, device_id_type=MESH)
    pl.semaphore_wait(barrier, len(peers))

    pk_local = local(pk.at[core], b["p1"].at[core])
    ff_local = local(ff.at[core], b["f1"].at[core])
    pk_swap = remote(pk.at[other], b["p1"].at[core], sibling)
    ff_swap = remote(ff.at[other], b["f1"].at[core], sibling)

    conditional = []

    def to_device(src, dst, place, here, kind, send_slot):
        copy = pltpu.make_async_remote_copy(
            src_ref=src,
            dst_ref=dst,
            send_sem=xsem.at[kind, 8 + send_slot],
            recv_sem=here,
            device_id=device(x_=place[0], c_=place[1]),
            device_id_type=MESH,
        )
        same = (place[0] == x) & (place[1] == core)

        @pl.when(same)
        def _():
            pltpu.make_async_copy(src, dst, here).start()

        @pl.when(jnp.logical_not(same))
        def _():
            copy.start()

        conditional.append((same, copy))

    def from_device(dst, kind, slot):
        pltpu.make_async_copy(dst, dst, xsem.at[kind, slot]).wait()

    def chip_of(k, s):
        return s + k * (3 - 2 * s)

    def send_rows():
        for s in range(2):
            for j in range(2):
                to_device(
                    xin.at[s, pl.ds(TOKENS * j, TOKENS)],
                    b["x"].at[pl.ds(pl.multiple_of(OWN * j + TOKENS * x, 16), TOKENS)],
                    (chip_of(core, s), j),
                    xsem.at[0, x],
                    0,
                    2 * s + j,
                )

    def send_upstream():
        for s in range(2):
            for j in range(2):
                to_device(
                    gin.at[s, pl.ds(TOKENS * j, TOKENS)],
                    b["gyt"].at[pl.ds(pl.multiple_of(TOKENS * x, 16), TOKENS)],
                    (chip_of(core, s), j),
                    xsem.at[1, x],
                    1,
                    2 * s + j,
                )
            to_device(
                gmem.at[s], b["gm"].at[x % 2], (chip_of(core, s), x // 2), xsem.at[2, x % 2], 2, s
            )

    def part_of(job, step, place, half=None):
        name, order, cols, axes = job
        fixed = {a: at[a] for a in order[step:]}
        fixed[order[step]] = place
        where = []
        for a in axes:
            if a in fixed:
                where.append(fixed[a])
            elif half is not None:
                where.append(pl.ds(half * (size[a] // 2), size[a] // 2))
                half = None
            else:
                where.append(slice(None))
        return b[WEIGHTS[name[0]]].at[tuple(where) + (slice(None), cols)]

    def gather_start(name, step):
        job = gathers[name]
        axis = job[1][step]
        n = size[axis]
        own = part_of(job, step, at[axis])
        free = [a for a in job[3] if a not in job[1][step:]]
        relay = n == 4 and len(free) > 0 and size[free[0]] % 2 == 0
        state = {"step": step, "relay": relay}
        if relay:
            state["right"] = remote(own, own, moved(axis, 1))
            state["left"] = remote(own, own, moved(axis, n - 1))
        else:
            state["all"] = [remote(own, own, moved(axis, o)) for o in range(1, n)]
        flying[name] = state

    def gather_pass(name):
        job, state = gathers[name], flying[name]
        if not state["relay"]:
            return
        axis = job[1][state["step"]]
        n = size[axis]
        state["all"] = []
        for kind, back, onward, half in (("right", n - 1, 1, 0), ("left", 1, n - 1, 1)):
            arrived([state[kind]])
            piece = part_of(job, state["step"], (at[axis] + back) % n, half)
            state["all"].append(remote(piece, piece, moved(axis, onward)))

    def gather_done(name):
        arrived(flying[name]["all"])

    gathers = {j[0]: j for j in gather_jobs()}
    flying = {}

    pk_local.wait()
    arrived([pk_swap])
    two = [b["p1"][c].astype(F32)[: sh.pc] for c in range(2)]
    b["p2"][x] = jnp.concatenate(two, 0).astype(BF16)
    mine = b["p2"].at[x]
    steps = [remote(mine, mine, moved("x", o)) for o in range(1, TP)]
    ff_local.wait()
    arrived([ff_swap])
    two = [b["f1"][c].astype(F32)[:wr] for c in range(2)]
    b["wf"][x, z, y] = jnp.concatenate(two, 0).astype(BF16)
    for n in ("f1", "f2", "f0"):
        gather_start(n, 0)
    send_rows()
    arrived(steps)
    b["wa"][z, y] = dot(packsel[...], b["p2"][...].reshape(TP * 2 * sh.pc, ACOLS)).astype(BF16)
    for n in ("a0", "a1"):
        gather_start(n, 0)
    for n in ("f1", "f2", "f0"):
        gather_done(n)
        gather_start(n, 1)
    for n in ("a0", "a1"):
        gather_done(n)
        gather_start(n, 1)
    for n in ("f1", "f2", "f0"):
        gather_pass(n)
    gather_done("f1")
    gather_start("f1", 2)
    for n in ("a0", "a1"):
        gather_pass(n)
    for n in ("f2", "f0"):
        gather_done(n)
        gather_start(n, 2)

    for i in range(TP):
        from_device(b["x"].at[pl.ds(pl.multiple_of(OWN * core + TOKENS * i, 16), TOKENS)], 0, i)
    half = b["x"].at[pl.ds(pl.multiple_of(OWN * core, 16), TP * TOKENS)]
    x_swap = remote(half, half, sibling)
    gather_pass("f1")
    for n in ("a0", "a1"):
        gather_done(n)
    wo_cols = slice(WO, WO + HALF)
    wo_local = local(b["wa"].at[:, :, :, wo_cols], b["wo"].at[core])
    wo_swap = remote(b["wa"].at[:, :, :, wo_cols], b["wo"].at[core], sibling)
    send_upstream()

    def attention_weight():
        return b["wa"][:, :, :, :WO].reshape(D, WO)

    small = b["wa"][:, :, :, 4 * HALF :].reshape(D, SMALL)
    chosen = dot(smallsel[...], small, NT)
    b["par"][...] = chosen[0:8]
    b["x"][OWN + 256 : OWN + 272] = chosen[32:48].astype(BF16)

    @pl.when(seg == 0)
    def _():
        b["x"][256:272] = chosen[16:32].astype(BF16)

    @pl.when(seg == 1)
    def _():
        b["x"][256:272] = jnp.zeros((16, D), BF16)

    gains = [b["par"][i : i + 1] for i in range(2)]
    biases = [b["par"][2 + i : 3 + i] for i in range(2)]
    arrived([x_swap])

    hop_to = jnp.where(x == 0, 1, 2)
    hops = []
    for j in range(2):
        hops.append(
            pltpu.make_async_remote_copy(
                src_ref=b["hop"],
                dst_ref=b["hopin"],
                send_sem=xsem.at[6, j],
                recv_sem=xsem.at[6, 2],
                device_id=device(x_=hop_to, c_=j),
                device_id_type=MESH,
            )
        )

    own_rows = pl.ds(pl.multiple_of(OWN * core, 16), OWN)
    other_rows = pl.ds(pl.multiple_of(OWN * other, 16), OWN)

    out = dot(b["x"][...], attention_weight()).astype(BF16)
    for i in range(9):
        b["qkv"][i] = out[:, 128 * i : 128 * i + 128]

    def head_masks(hh):
        lane = lax.broadcasted_iota(jnp.int32, (ROWS, 128), 1)
        row = lax.broadcasted_iota(jnp.int32, (ROWS, 128), 0)
        inside = (lane // 64) == hh
        spare = lane == 64 * (1 - hh)
        memory = ((row >= 256) & (row < 272)) | (row >= OWN + 256)
        invalid = memory & (row % 8 >= 5)
        return inside, spare, invalid

    def forward_pair(p):
        qp, kp, vp = (b["qkv"][3 * p + i] for i in range(3))
        vt = vp.T
        for hh in range(2):
            inside, spare, invalid = head_masks(hh)
            zero = jnp.zeros_like(kp)
            kmask = jnp.where(spare & invalid, jnp.full_like(kp, MASKED), zero)
            km = jnp.where(inside, kp, kmask)
            qm = jnp.where(inside, qp, jnp.where(spare, jnp.ones_like(qp), zero))
            scores = dot(km, qm, NT)
            peak = jnp.max(scores, 0, keepdims=True)
            raised = jnp.exp2((scores - peak) * EXP_SCALE)
            total = jnp.sum(raised, 0, keepdims=True)
            probs = (raised * (1.0 / total)).astype(BF16)
            b["pt"][2 * p + hh] = probs
            b["ot"][p, 64 * hh : 64 * hh + 64] = dot(vt[64 * hh : 64 * hh + 64], probs).astype(BF16)
        b["oc"][:, 128 * p : 128 * p + 128] = b["ot"][p].T

    @pl.when(seg == 0)
    def _():
        forward_pair(0)
        forward_pair(1)

    for n in ("f2", "f0"):
        gather_pass(n)

    @pl.when(seg == 0)
    def _():
        forward_pair(2)

    @pl.when(seg == 1)
    def _():
        hops[0].wait_recv()
        b["x"][256:272] = b["hopin"][...]
        rows = dot(b["hopin"][...], attention_weight()).astype(BF16)
        for i in range(9):
            b["qkv"][i, 256:272] = rows[:, 128 * i : 128 * i + 128]
        for p in range(3):
            forward_pair(p)

    o_local = local(b["oc"].at[own_rows], b["oown"].at[core])
    o_swap = remote(b["oc"].at[other_rows], b["oown"].at[core], sibling)
    wo_local.wait()
    arrived([wo_swap])
    o_local.wait()
    arrived([o_swap])
    halves = []
    for h in range(2):
        w = b["wo"][h].reshape(D, HALF)
        halves.append(dot(b["oown"][0], w[:HALF]) + dot(b["oown"][1], w[HALF:]))
    attended = jnp.concatenate(halves, 1)
    h1, n1, inv1 = norm_forward(b["x"][own_rows].astype(F32) + attended, gains[0], biases[0])
    b["h1"][...] = h1
    b["n1"][...] = n1
    b["inv1"][...] = inv1
    b["h1b"][own_rows] = h1.astype(BF16)
    h_swap = remote(b["h1b"].at[own_rows], b["h1b"].at[own_rows], sibling)
    for n in ("f1", "f2", "f0"):
        gather_done(n)
    arrived([h_swap])

    def feed_weight(t, kind):
        cols = [256 * j + 128 * kind for j in range(3)]
        blocks = [b["wf"][2 * t + i, :, :, :, c : c + 128].reshape(D, 128) for i in range(2) for c in cols]
        return jnp.concatenate(blocks, 1)

    def up_weight(t):
        return feed_weight(t, 0)

    def down_weight(t):
        return feed_weight(t, 1)

    def activate(units):
        erf = 0.5 * (1.0 + lax.erf(units * INV_ROOT_TWO))
        return (units * erf).astype(BF16), erf

    early = pltpu.make_async_remote_copy(
        src_ref=b["es"],
        dst_ref=b["er"],
        send_sem=xsem.at[6, 3],
        recv_sem=xsem.at[6, 4],
        device_id=sibling,
        device_id_type=MESH,
    )
    row16 = lax.broadcasted_iota(jnp.int32, (16, D), 0)

    @pl.when(seg == 0)
    def _():
        rows = b["h1b"][OWN + 256 : OWN + 272]
        part = sum(dot(activate(dot(rows, up_weight(t)))[0], down_weight(t), NT) for t in range(2))

        @pl.when(core == 0)
        def _():
            b["es"][...] = part
            early.start()

        @pl.when(core == 1)
        def _():
            early.wait_recv()
            whole = b["h1"][256:272] + part + b["er"][...]
            written = norm_forward(whole, gains[1], biases[1])[0]
            b["hop"][...] = jnp.where(row16 % 8 < 5, written, 0.0).astype(BF16)
            hops[0].start()
            hops[1].start()

    for t in range(2):
        units = dot(b["h1b"][...], up_weight(t))
        active, erf = activate(units)
        b["gl"][t] = active
        b["sl"][t] = (erf + units * jnp.exp(-0.5 * units * units) * INV_ROOT_TWOPI).astype(BF16)

    def partial_down(rows):
        return sum(dot(b["gl"][t, rows], down_weight(t), NT) for t in range(2))

    b["fs"][...] = partial_down(other_rows).astype(BF16)
    f_swap = remote(b["fs"], b["fr"], sibling)
    branch = partial_down(own_rows)
    arrived([f_swap])
    out, n2, inv2 = norm_forward(b["h1"][...] + branch + b["fr"][...].astype(F32), gains[1], biases[1])
    low = out.astype(BF16)
    b["yb"][...] = low
    b["mo"][...] = low[256:272].astype(F32).reshape(2, 8, D)
    for i in range(TP):
        to_device(
            b["yb"].at[pl.ds(TOKENS * i, TOKENS)],
            hout.at[seg, pl.ds(pl.multiple_of(TOKENS * core, 16), TOKENS)],
            (i, chain),
            xsem.at[3, 2 * seg + core],
            3,
            i,
        )
    for i in range(2):
        to_device(b["mo"].at[i], mout.at[seg], (2 * core + i, chain), xsem.at[4, seg], 4, i)

    for i in range(TP):
        from_device(b["gyt"].at[pl.ds(TOKENS * i, TOKENS)], 1, i)
    for i in range(2):
        from_device(b["gm"].at[i], 2, i)
    upstream = jnp.concatenate([b["gyt"][...].astype(F32), b["gm"][...].reshape(16, D)], 0)
    b["sg"][...] = jnp.zeros((48, D), F32)
    b["sg"][1:2] = column_sum(upstream * n2)
    b["sg"][3:4] = column_sum(upstream)
    dz = norm_backward(upstream, n2, inv2, gains[1])
    b["dz"][...] = dz
    b["dfb"][own_rows] = dz.astype(BF16)
    df_swap = remote(b["dfb"].at[own_rows], b["dfb"].at[own_rows], sibling)
    arrived([df_swap])

    for t in range(2):
        b["du"][t] = (dot(b["dfb"][...], down_weight(t)) * b["sl"][t].astype(F32)).astype(BF16)

    def partial_up(rows):
        return sum(dot(b["du"][t, rows], up_weight(t), NT) for t in range(2))

    def weight_grad(name, left, right):
        for t in range(2):
            part = dot(left, b[right][t], TN).astype(BF16)
            for i in range(2):
                b[name][2 * t + i] = part[:, HALF * i : HALF * (i + 1)].reshape(nz, ny, br, HALF)

    b["dhs"][...] = partial_up(other_rows).astype(BF16)
    dh_swap = remote(b["dhs"], b["dhr"], sibling)
    b["dz"][...] = b["dz"][...] + partial_up(own_rows)
    weight_grad("gt", b["dfb"][...], "gl")

    def pick(axes, axis, place):
        return tuple(place if a == axis else slice(None) for a in axes)

    scatters = {j[0]: j for j in scatter_jobs()}
    rs = {}

    def scatter_send(name, step):
        _, order, cols, axes = scatters[name]
        axis = order[step]
        left = [a for a in axes if a not in order[:step]]
        if step == 0:
            source = b[GRADS[name[0]]]
            tail = (slice(None), cols)
        else:
            source = b[f"s{step - 1}_{name}"]
            tail = ()
        copies = []
        for o in range(1, size[axis]):
            there = (at[axis] + o) % size[axis]
            copies.append(
                remote(source.at[pick(left, axis, there) + tail], b[f"r{step}_{name}"].at[o - 1], moved(axis, o))
            )
        rs[name] = copies

    def scatter_sum(name, step):
        _, order, cols, axes = scatters[name]
        axis = order[step]
        left = [a for a in axes if a not in order[:step]]
        arrived(rs[name])
        if step == 0:
            mine = b[GRADS[name[0]]][pick(left, axis, at[axis]) + (slice(None), cols)]
        else:
            mine = b[f"s{step - 1}_{name}"][pick(left, axis, at[axis])]
        total = mine.astype(F32)
        for o in range(1, size[axis]):
            total = total + b[f"r{step}_{name}"][o - 1].astype(F32)
        if step < len(order) - 1:
            b[f"s{step}_{name}"][...] = total.astype(BF16)
        return total

    def scatter_on(names, step):
        for n in names:
            scatter_sum(n, step)
            scatter_send(n, step + 1)

    down_names, up_names = ("t0", "t1", "t2"), ("i0", "i1", "i2")
    for n in down_names:
        scatter_send(n, 0)
    weight_grad("gi", b["h1b"][...], "du")
    for n in up_names:
        scatter_send(n, 0)
    arrived([dh_swap])
    into_first = b["dz"][...] + b["dhr"][...].astype(F32)
    b["sg"][0:1] = column_sum(into_first * b["n1"][...])
    b["sg"][2:3] = column_sum(into_first)
    dr = norm_backward(into_first, b["n1"][...], b["inv1"][...], gains[0])
    b["dr"][...] = dr
    b["dab"][own_rows] = dr.astype(BF16)
    da_swap = remote(b["dab"].at[own_rows], b["dab"].at[own_rows], sibling)
    arrived([da_swap])

    def head_rows(ref, c):
        if nz > 1:
            return ref.at[pl.ds(c * (nz // 2), nz // 2)]
        return ref.at[:, :, pl.ds(pl.multiple_of(c * HALF, 16), HALF)]

    grad_mixed = 0.0
    for h in range(2):
        w = head_rows(b["wo"].at[h], core)[...].reshape(HALF, HALF)
        grad_mixed = grad_mixed + dot(b["dab"][:, HALF * h : HALF * (h + 1)], w, NT)
    for p in range(3):
        b["doc"][p] = grad_mixed[:, 128 * p : 128 * p + 128].astype(BF16)

    mixed_t = b["ot"][...].reshape(HALF, ROWS)

    def proj_grad(h):
        cols = pl.ds(pl.multiple_of(HALF * h, 128), HALF)
        return dot(mixed_t, b["dab"][:, cols]).astype(BF16).reshape(b["gos"].shape)

    def wo_part(c):
        return head_rows(b["ga"].at[:, :, :, wo_cols], c)

    b["gos"][...] = proj_grad(other)
    go_swap = remote(b["gos"], wo_part(core), sibling)
    wo_part(core)[...] = proj_grad(core)
    scatter_on(down_names, 0)
    arrived([go_swap])
    scatter_send("aw", 0)

    def backward_pair(p):
        qp, kp, vp = (b["qkv"][3 * p + i] for i in range(3))
        dop = b["doc"][p]
        kt = kp.T
        dv = dk = 0.0
        dq = []
        for hh in range(2):
            inside, _, _ = head_masks(hh)
            zero = jnp.zeros_like(kp)
            grad_probs = dot(jnp.where(inside, vp, zero), dop, NT)
            low_probs = b["pt"][2 * p + hh]
            probs = low_probs.astype(F32)
            row_term = jnp.sum(probs * grad_probs, 0, keepdims=True)
            ds = (probs * (grad_probs - row_term)).astype(BF16)
            dv = dv + dot(low_probs, jnp.where(inside, dop, zero))
            dk = dk + dot(ds, jnp.where(inside, qp, zero))
            dq.append(dot(kt[64 * hh : 64 * hh + 64], ds))
        b["dqkv"][3 * p] = (jnp.concatenate(dq, 0) * 0.125).T.astype(BF16)
        b["dqkv"][3 * p + 1] = (dk * 0.125).astype(BF16)
        b["dqkv"][3 * p + 2] = dv.astype(BF16)

    def joined(rows, wanted):
        return jnp.concatenate([b["dqkv"][i, rows] for i in wanted], 1)

    def attention_grad(p):
        part = dot(b["x"][...], joined(slice(None), range(3 * p, 3 * p + 3)), TN).astype(BF16)
        b["ga"][:, :, :, HALF * p : HALF * (p + 1)] = part.reshape(nz, ny, br, HALF)

    backward_pair(0)
    attention_grad(0)
    scatter_send("a0", 0)
    scatter_on(up_names, 0)
    backward_pair(1)
    attention_grad(1)
    scatter_send("a1", 0)
    scatter_on(down_names, 1)
    backward_pair(2)
    attention_grad(2)
    scatter_send("a2", 0)
    scatter_send("a3", 0)

    def partial_input(rows):
        return dot(joined(rows, range(9)), attention_weight(), NT)

    b["dxs"][...] = partial_input(other_rows).astype(BF16)
    dx_swap = remote(b["dxs"], b["dxr"], sibling)
    dx = partial_input(own_rows) + b["dr"][...]
    arrived([dx_swap])
    dx = dx + b["dxr"][...].astype(F32)
    b["dxb"][...] = dx[:256].astype(BF16)
    for i in range(TP):
        to_device(
            b["dxb"].at[pl.ds(TOKENS * i, TOKENS)],
            dxo.at[seg, pl.ds(pl.multiple_of(TOKENS * core, 16), TOKENS)],
            (i, chain),
            xsem.at[5, 2 * seg + core],
            5,
            i,
        )

    @pl.when((core == 0) & (seg == 0))
    def _():
        b["sg"][16:32] = dx[256:272]

    @pl.when(core == 1)
    def _():
        b["sg"][32:48] = dx[256:272]

    small_grads = dot(b["sg"][...].astype(BF16), smallsel[...], TN).astype(BF16)
    b["ga"][:, :, :, 4 * HALF :] = small_grads.reshape(nz, ny, br, SMALL)
    scatter_send("as", 0)
    attention_names = ("aw", "a0", "a1", "a2", "a3", "as")
    scatter_on(up_names, 1)
    scatter_on(attention_names, 0)

    def last_rows(names, first_col):
        for j, n in enumerate(names):
            total = scatter_sum(n, 2)
            cols = slice(first_col + 128 * j, first_col + 128 * j + 128)
            b["sf"][0, :, cols] = total[:wr]
            b["sf"][1, :, cols] = total[wr:]

    last_rows(down_names, HALF)
    for n in attention_names:
        cols = scatters[n][2]
        spread = dot(packsel[...], scatter_sum(n, 1).astype(BF16), TN).astype(BF16)
        b["e3"][:, :, cols] = spread.reshape(TP, 2 * sh.pc, cols.stop - cols.start)
    steps = [remote(b["e3"].at[(x + o) % TP], b["r3"].at[o - 1], moved("x", o)) for o in range(1, TP)]
    last_rows(up_names, 0)
    sf_local = local(b["sf"].at[core], gfo.at[core])
    sf_swap = remote(b["sf"].at[other], gfo.at[core], sibling)

    arrived(steps)
    total = b["e3"][x].astype(F32)
    for o in range(1, TP):
        total = total + b["r3"][o - 1].astype(F32)
    b["s4"][...] = total.reshape(2, sh.pc, ACOLS)
    s4_local = local(b["s4"].at[core], gao.at[core])
    s4_swap = remote(b["s4"].at[other], gao.at[core], sibling)

    for kind, out_ref in ((3, hout), (5, dxo)):
        for s in range(2):
            for j in range(2):
                from_device(out_ref.at[s, pl.ds(TOKENS * j, TOKENS)], kind, 2 * s + j)
    for s in range(2):
        from_device(mout.at[s], 4, s)
    sf_local.wait()
    s4_local.wait()
    arrived([sf_swap, s4_swap])

    for copy in sent:
        copy.wait_send()
    for same, copy in conditional:

        @pl.when(jnp.logical_not(same))
        def _():
            copy.wait_send()

    @pl.when((seg == 0) & (core == 1))
    def _():
        hops[0].wait_send()
        hops[1].wait_send()

    @pl.when((seg == 0) & (core == 0))
    def _():
        early.wait_send()


def layer(sh, arrays):
    pack, small = selections(sh)
    table = scratch_of(sh)
    names = list(table)
    vmem = pl.BlockSpec(memory_space=pltpu.VMEM)
    outs = [
        jax.ShapeDtypeStruct((2, 128, D), BF16),
        jax.ShapeDtypeStruct((2, 8, D), F32),
        jax.ShapeDtypeStruct((2, 128, D), BF16),
        jax.ShapeDtypeStruct((2, sh.pc, ACOLS), F32),
        jax.ShapeDtypeStruct((2, sh.wrows, D), F32),
    ]
    return pl.pallas_call(
        functools.partial(kernel, sh, names),
        name="layer",
        out_shape=outs,
        in_specs=[vmem] * 7,
        out_specs=[vmem] * len(outs),
        scratch_shapes=[pltpu.VMEM(*table[n]) for n in names]
        + [
            pltpu.SemaphoreType.DMA((200,)),
            pltpu.SemaphoreType.DMA((200,)),
            pltpu.SemaphoreType.DMA((7, 12)),
            pltpu.SemaphoreType.DMA((8,)),
        ],
        compiler_params=pltpu.CompilerParams(
            collective_id=0, has_side_effects=True, vmem_limit_bytes=64 * 2**20 - 2**17
        ),
    )(*arrays, jnp.asarray(pack, BF16), jnp.asarray(small, BF16))


def unpack_kernel(sh, hout, mout, dxo, gao, gfo, *outs):
    hidden, memory, grad_in, gq, gp, gains, biases, tokens, gi, gt = outs
    ar = sh.arows
    hidden[...] = hout[...]
    memory[...] = mout[...][:, :5].astype(BF16)
    grad_in[...] = dxo[...].astype(F32)
    for h in range(2):
        for p in range(3):
            for i in range(3):
                to = D * i + HALF * h + 128 * p
                first = HALF * p + 128 * i
                gq[:, to : to + 128] = gao[h, :ar, first : first + 128]
        gp[:, HALF * h : HALF * (h + 1)] = gao[h, :ar, WO : WO + HALF]
        gi[:, HALF * h : HALF * (h + 1)] = gfo[h, :, :HALF]
        gt[HALF * h : HALF * (h + 1), :] = gfo[h, :, HALF:].T
    small = (gao[0, :, 4 * HALF :] + gao[1, :, 4 * HALF :]).T[:, :ar]
    gains[...] = small[0:2]
    biases[...] = small[2:4]
    for kind in range(2):
        tokens[kind] = small[4 + MEM * kind : 4 + MEM * (kind + 1)]


def unpack(sh, *arrays):
    ar, wr = sh.arows, sh.wrows
    shapes = [
        ((2, 128, D), BF16),
        ((2, 5, D), BF16),
        ((2, 128, D), F32),
        ((ar, 3 * D), F32),
        ((ar, D), F32),
        ((2, ar), F32),
        ((2, ar), F32),
        ((2, MEM, ar), F32),
        ((wr, D), F32),
        ((D, wr), F32),
    ]
    vmem = pl.BlockSpec(memory_space=pltpu.VMEM)
    return pl.pallas_call(
        functools.partial(unpack_kernel, sh),
        name="unpack",
        out_shape=[jax.ShapeDtypeStruct(*one) for one in shapes],
        in_specs=[vmem] * 5,
        out_specs=[vmem] * len(shapes),
        compiler_params=pltpu.CompilerParams(vmem_limit_bytes=32 * 2**20),
    )(*arrays)


def body(
    sh,
    hidden_in,
    reset,
    w_qkv,
    w_attn_out,
    norm_gains,
    norm_biases,
    memory_tokens,
    w_in,
    w_out,
    grad_hidden,
    grad_memory,
):
    ar, wr = sh.arows, sh.wrows
    small = jnp.concatenate([norm_gains, norm_biases, memory_tokens.reshape(2 * MEM, ar)], 0).T
    small = jnp.pad(small, ((0, 0), (0, SMALL - small.shape[1])))
    by_half = w_qkv.reshape(ar, 3, 2, 3, 128).transpose(2, 0, 3, 1, 4).reshape(2, ar, 3 * HALF)
    proj = w_attn_out.reshape(ar, 2, HALF).transpose(1, 0, 2)
    pk = jnp.concatenate([by_half, proj, jnp.broadcast_to(small, (2, ar, SMALL))], 2)
    pk = jnp.pad(pk, ((0, 0), (0, sh.pr - ar), (0, 0)))
    both = jnp.stack([w_in.reshape(wr, 2, 3, 128), w_out.T.reshape(wr, 2, 3, 128)], 3)
    ff = both.transpose(1, 0, 2, 3, 4).reshape(2, wr, D)
    ff = jnp.pad(ff, ((0, 0), (0, sh.fr - wr), (0, 0)))
    gmem = jnp.pad(grad_memory.astype(F32), ((0, 0), (0, 3), (0, 0)))
    hout, mout, dxo, gao, gfo = layer(sh, (hidden_in, grad_hidden, gmem, pk, ff))

    return unpack(sh, hout, mout, dxo, gao, gfo)


def solution(mesh):
    sh = Shape(mesh.shape["dp"])
    return jax.shard_map(
        functools.partial(body, sh),
        mesh=mesh,
        in_specs=(
            P("dp", "tp", None),
            P("dp"),
            P(("dp", "tp"), None),
            P(("dp", "tp"), None),
            P(None, ("dp", "tp")),
            P(None, ("dp", "tp")),
            P(None, None, ("dp", "tp")),
            P("dp", "tp"),
            P("tp", "dp"),
            P("dp", "tp", None),
            P("dp", "tp", None),
        ),
        out_specs=(
            P("dp", "tp", None),
            P("dp", "tp", None),
            P("dp", "tp", None),
            P(("dp", "tp"), None),
            P(("dp", "tp"), None),
            P(None, ("dp", "tp")),
            P(None, ("dp", "tp")),
            P(None, None, ("dp", "tp")),
            P("dp", "tp"),
            P("tp", "dp"),
        ),
        check_vma=False,
    )
```

```python
import functools

import jax
import jax.numpy as jnp
import numpy as np
from jax import lax
from jax.experimental import pallas as pl
from jax.experimental.pallas import tpu as pltpu
from jax.sharding import PartitionSpec as P

D = 768
HALF = 384
MEM = 10
TOKENS = 64
OWN = 272
ROWS = 2 * OWN
TP = 4
SMALL = 128
ACOLS = 4 * HALF + SMALL
CUT = 768
WO = 3 * HALF
EPSILON = 1e-05
INV_ROOT_TWO = 0.7071067811865476
INV_ROOT_TWOPI = 0.3989422804014327
EXP_SCALE = 0.125 * 1.4426950408889634
MASKED = -1e30
F32 = jnp.float32
BF16 = jnp.bfloat16
MESH = pl.DeviceIdType.MESH
NN = (((1,), (0,)), ((), ()))
NT = (((1,), (1,)), ((), ()))
TN = (((0,), (0,)), ((), ()))


def dot(a, b, dims=NN):
    return lax.dot_general(a, b, dims, preferred_element_type=F32)


def up16(n):
    return -(-n // 16) * 16


class Shape:
    def __init__(self, dp):
        self.dp = dp
        planes = dp // 2
        self.ny = int(round(planes**0.5))
        self.nz = planes // self.ny
        self.wrows = D // dp
        self.arows = D // (dp * TP)
        self.brows = 2 * self.wrows
        self.pr = up16(self.arows)
        self.pc = -(-self.arows // 8) * 8
        self.fr = up16(self.wrows)


def selections(sh):
    pack = np.zeros((sh.brows, TP * 2 * sh.pc), np.float32)
    for c in range(2):
        for x in range(TP):
            for i in range(sh.arows):
                pack[c * sh.wrows + x * sh.arows + i, (x * 2 + c) * sh.pc + i] = 1
    small = np.zeros((48, SMALL), np.float32)
    for i in range(4):
        small[i, i] = 1
    for kind in range(2):
        for i in range(MEM):
            small[16 + 16 * kind + (i // 5) * 8 + i % 5, 4 + MEM * kind + i] = 1
    places = np.zeros((4, MEM, SMALL), np.float32)
    for kind, (rows, first) in enumerate(((2, 0), (2, 2), (MEM, 4), (MEM, 4 + MEM))):
        for i in range(rows):
            places[kind, i, first + i] = 1
    return pack, small, places


def norm_forward(inputs, gain, offset):
    centred = inputs - jnp.mean(inputs, -1, keepdims=True)
    spread = jnp.mean(centred * centred, -1, keepdims=True)
    inverse = lax.rsqrt(spread + EPSILON)
    normed = centred * inverse
    return normed * gain + offset, normed, inverse


def norm_backward(upstream, normed, inverse, gain):
    scaled = upstream * gain
    first_mean = jnp.mean(scaled, -1, keepdims=True)
    second_mean = jnp.mean(scaled * normed, -1, keepdims=True)
    return inverse * (scaled - first_mean - normed * second_mean)


def column_sum(a):
    return jnp.sum(a, 0, keepdims=True)


SCRATCH = {}


def scratch_of(sh):
    nz, ny, br = sh.nz, sh.ny, sh.brows
    s = {
        "pk": ((2, sh.pr, ACOLS), BF16),
        "ff": ((2, sh.fr, D), BF16),
        "gms": ((2, 8, D), F32),
        "p1": ((2, sh.pr, ACOLS), BF16),
        "p2": ((TP, 2 * sh.pc, ACOLS), BF16),
        "f1": ((2, sh.fr, D), BF16),
        "wa": ((nz, ny, br, ACOLS), BF16),
        "wf": ((TP, nz, ny, br, D), BF16),
        "wo": ((2, nz, ny, br, HALF), BF16),
        "par": ((8, D), F32),
        "x": ((ROWS, D), BF16),
        "gyt": ((TP * TOKENS, D), BF16),
        "gm": ((2, 8, D), F32),
        "qkv": ((9, ROWS, 128), BF16),
        "pt": ((6, ROWS, ROWS), BF16),
        "ot": ((3, 128, ROWS), BF16),
        "oc": ((ROWS, HALF), BF16),
        "oown": ((2, OWN, HALF), BF16),
        "h1": ((OWN, D), F32),
        "n1": ((OWN, D), F32),
        "inv1": ((OWN, 1), F32),
        "h1b": ((ROWS, D), BF16),
        "gl": ((2, ROWS, D), BF16),
        "sl": ((2, ROWS, D), BF16),
        "fs": ((OWN, D), BF16),
        "fr": ((OWN, D), BF16),
        "n2": ((OWN, D), F32),
        "yb": ((OWN, D), BF16),
        "mo": ((2, 8, D), F32),
        "hop": ((16, D), BF16),
        "hopin": ((16, D), BF16),
        "es": ((16, D), F32),
        "er": ((16, D), F32),
        "dz": ((OWN, D), F32),
        "dfb": ((ROWS, D), BF16),
        "du": ((2, ROWS, D), BF16),
        "dhs": ((OWN, D), BF16),
        "dhr": ((OWN, D), BF16),
        "dr": ((OWN, D), F32),
        "dab": ((ROWS, D), BF16),
        "doc": ((3, ROWS, 128), BF16),
        "dqkv": ((9, ROWS, 128), BF16),
        "ga": ((nz, ny, br, ACOLS), BF16),
        "gi": ((TP, nz, ny, br, HALF), BF16),
        "gt": ((TP, nz, ny, br, HALF), BF16),
        "gos": ((D // 2 // br if nz > 1 else 1, br if nz > 1 else HALF, HALF), BF16),
        "dxs": ((OWN, D), BF16),
        "dxr": ((OWN, D), BF16),
        "dxb": ((TP * TOKENS, D), BF16),
        "sg": ((48, D), F32),
        "e3": ((TP, 2 * sh.pc, ACOLS), BF16),
        "r3": ((TP - 1, 2 * sh.pc, ACOLS), BF16),
        "s4": ((2, sh.pc, ACOLS), F32),
        "sf": ((2, sh.wrows, D), F32),
    }
    if nz > 1:
        s["gos"] = ((nz // 2, ny, br, HALF), BF16)
    else:
        s["gos"] = ((1, 1, HALF, HALF), BF16)
    sizes = {"x": TP, "z": nz, "y": ny}
    for name, order, cols, axes in scatter_jobs():
        left = [a for a in axes]
        for step, axis in enumerate(order):
            left = [a for a in left if a != axis]
            dims = tuple(sizes[a] for a in left)
            s[f"r{step}_{name}"] = ((max(1, sizes[axis] - 1),) + dims + (br, cols.stop - cols.start), BF16)
            if step < len(order) - 1:
                s[f"s{step}_{name}"] = (dims + (br, cols.stop - cols.start), BF16)
    return s


def scatter_jobs():
    orders = [("z", "y", "x"), ("x", "z", "y"), ("y", "x", "z")]
    jobs = []
    for kind in ("t", "i"):
        for j in range(3):
            jobs.append((f"{kind}{j}", orders[j], slice(128 * j, 128 * j + 128), ("x", "z", "y")))
    zy, yz = ("z", "y"), ("y", "z")
    jobs.append(("aw", yz, slice(WO, WO + HALF), zy))
    jobs.append(("a0", zy, slice(0, HALF), zy))
    jobs.append(("a1", yz, slice(HALF, 2 * HALF), zy))
    jobs.append(("a2", zy, slice(2 * HALF, 2 * HALF + 256), zy))
    jobs.append(("a3", zy, slice(2 * HALF + 256, 3 * HALF), zy))
    jobs.append(("as", yz, slice(4 * HALF, ACOLS), zy))
    return jobs


def gather_jobs():
    orders = [("x", "y", "z"), ("y", "z", "x"), ("z", "x", "y")]
    jobs = [(f"f{j}", orders[j], slice(256 * j, 256 * j + 256), ("x", "z", "y")) for j in range(3)]
    jobs.append(("a0", ("y", "z"), slice(0, CUT), ("z", "y")))
    jobs.append(("a1", ("z", "y"), slice(CUT, ACOLS), ("z", "y")))
    return jobs


WEIGHTS = {"f": "wf", "a": "wa"}
GRADS = {"t": "gt", "i": "gi", "a": "ga"}


def kernel(sh, names, *refs):
    xin, gin, gmem, wq, wp, gain_in, bias_in, token_in, up_in, down_in, packsel, smallsel, places = refs[:13]
    hout, mout, dxo, gao, gfo = refs[13:18]
    b = dict(zip(names, refs[18 : 18 + len(names)]))
    ssem, rsem, xsem, lsem = refs[18 + len(names) :]
    nz, ny, br, wr, ar = sh.nz, sh.ny, sh.brows, sh.wrows, sh.arows
    pk, ff, gms = b["pk"], b["ff"], b["gms"]

    dp = lax.axis_index("dp")
    x = lax.axis_index("tp")
    core = dp % 2
    y = (dp // 2) % ny
    z = dp // (2 * ny)
    other = 1 - core
    chain = x // 2
    seg = jnp.where((x == 1) | (x == 2), 1, 0)
    at = {"x": x, "y": y, "z": z}
    size = {"x": TP, "y": ny, "z": nz}

    def device(x_=x, y_=y, z_=z, c_=core):
        return ((z_ * ny + y_) * 2 + c_, x_)

    def moved(axis, offset, core_=core):
        there = dict(at)
        there[axis] = (at[axis] + offset) % size[axis]
        return device(there["x"], there["y"], there["z"], core_)

    sibling = device(c_=other)
    counts = {"s": 0, "r": 0}
    sent = []

    def remote(src, dst, to):
        copy = pltpu.make_async_remote_copy(
            src_ref=src,
            dst_ref=dst,
            send_sem=ssem.at[counts["s"]],
            recv_sem=rsem.at[counts["r"]],
            device_id=to,
            device_id_type=MESH,
        )
        counts["s"] += 1
        counts["r"] += 1
        copy.start()
        sent.append(copy)
        return copy

    def arrived(copies):
        for copy in copies:
            copy.wait_recv()

    locals_ = [0]

    def local(src, dst):
        copy = pltpu.make_async_copy(src, dst, lsem.at[locals_[0]])
        locals_[0] += 1
        copy.start()
        return copy

    barrier = pltpu.get_barrier_semaphore()
    peers = [sibling]
    for o in range(1, TP):
        peers += [moved("x", o), moved("x", o, other)]
    for axis in ("y", "z"):
        for o in range(1, size[axis]):
            peers.append(moved(axis, o))
    for peer in peers:
        pl.semaphore_signal(barrier, inc=1, device_id=peer, device_id_type=MESH)

    small = dot(gain_in[...], places[0, :2], TN) + dot(bias_in[...], places[1, :2], TN)
    small = small + dot(token_in[:, 0], places[2]) + dot(token_in[:, 1], places[3])
    small = small.astype(BF16)
    pk[...] = jnp.zeros(pk.shape, BF16)
    ff[...] = jnp.zeros(ff.shape, BF16)
    gms[...] = jnp.zeros(gms.shape, F32)
    for h in range(2):
        for p in range(3):
            for i in range(3):
                first = D * i + HALF * h + 128 * p
                pk[h, :ar, HALF * p + 128 * i : HALF * p + 128 * (i + 1)] = wq[:, first : first + 128]
        pk[h, :ar, WO : WO + HALF] = wp[:, HALF * h : HALF * (h + 1)]
        pk[h, :ar, 4 * HALF :] = small
        for j in range(3):
            cols = slice(HALF * h + 128 * j, HALF * h + 128 * (j + 1))
            ff[h, :wr, 256 * j : 256 * j + 128] = up_in[:, cols]
            ff[h, :wr, 256 * j + 128 : 256 * j + 256] = down_in[:, cols]
        gms[h, 0:5] = gmem[:, h].astype(F32)
    pl.semaphore_wait(barrier, len(peers))

    pk_local = local(pk.at[core], b["p1"].at[core])
    ff_local = local(ff.at[core], b["f1"].at[core])
    pk_swap = remote(pk.at[other], b["p1"].at[core], sibling)
    ff_swap = remote(ff.at[other], b["f1"].at[core], sibling)

    conditional = []

    def to_device(src, dst, place, here, kind, send_slot):
        copy = pltpu.make_async_remote_copy(
            src_ref=src,
            dst_ref=dst,
            send_sem=xsem.at[kind, 8 + send_slot],
            recv_sem=here,
            device_id=device(x_=place[0], c_=place[1]),
            device_id_type=MESH,
        )
        same = (place[0] == x) & (place[1] == core)

        @pl.when(same)
        def _():
            pltpu.make_async_copy(src, dst, here).start()

        @pl.when(jnp.logical_not(same))
        def _():
            copy.start()

        conditional.append((same, copy))

    def from_device(dst, kind, slot):
        pltpu.make_async_copy(dst, dst, xsem.at[kind, slot]).wait()

    def chip_of(k, s):
        return s + k * (3 - 2 * s)

    def send_rows():
        for s in range(2):
            for j in range(2):
                to_device(
                    xin.at[s, pl.ds(TOKENS * j, TOKENS)],
                    b["x"].at[pl.ds(pl.multiple_of(OWN * j + TOKENS * x, 16), TOKENS)],
                    (chip_of(core, s), j),
                    xsem.at[0, x],
                    0,
                    2 * s + j,
                )

    def send_upstream():
        for s in range(2):
            for j in range(2):
                to_device(
                    gin.at[s, pl.ds(TOKENS * j, TOKENS)],
                    b["gyt"].at[pl.ds(pl.multiple_of(TOKENS * x, 16), TOKENS)],
                    (chip_of(core, s), j),
                    xsem.at[1, x],
                    1,
                    2 * s + j,
                )
            to_device(
                gms.at[s], b["gm"].at[x % 2], (chip_of(core, s), x // 2), xsem.at[2, x % 2], 2, s
            )

    def part_of(job, step, place, half=None):
        name, order, cols, axes = job
        fixed = {a: at[a] for a in order[step:]}
        fixed[order[step]] = place
        where = []
        for a in axes:
            if a in fixed:
                where.append(fixed[a])
            elif half is not None:
                where.append(pl.ds(half * (size[a] // 2), size[a] // 2))
                half = None
            else:
                where.append(slice(None))
        return b[WEIGHTS[name[0]]].at[tuple(where) + (slice(None), cols)]

    def gather_start(name, step):
        job = gathers[name]
        axis = job[1][step]
        n = size[axis]
        own = part_of(job, step, at[axis])
        free = [a for a in job[3] if a not in job[1][step:]]
        relay = n == 4 and len(free) > 0 and size[free[0]] % 2 == 0
        state = {"step": step, "relay": relay}
        if relay:
            state["right"] = remote(own, own, moved(axis, 1))
            state["left"] = remote(own, own, moved(axis, n - 1))
        else:
            state["all"] = [remote(own, own, moved(axis, o)) for o in range(1, n)]
        flying[name] = state

    def gather_pass(name):
        job, state = gathers[name], flying[name]
        if not state["relay"]:
            return
        axis = job[1][state["step"]]
        n = size[axis]
        state["all"] = []
        for kind, back, onward, half in (("right", n - 1, 1, 0), ("left", 1, n - 1, 1)):
            arrived([state[kind]])
            piece = part_of(job, state["step"], (at[axis] + back) % n, half)
            state["all"].append(remote(piece, piece, moved(axis, onward)))

    def gather_done(name):
        arrived(flying[name]["all"])

    gathers = {j[0]: j for j in gather_jobs()}
    flying = {}

    pk_local.wait()
    arrived([pk_swap])
    two = [b["p1"][c].astype(F32)[: sh.pc] for c in range(2)]
    b["p2"][x] = jnp.concatenate(two, 0).astype(BF16)
    mine = b["p2"].at[x]
    steps = [remote(mine, mine, moved("x", o)) for o in range(1, TP)]
    ff_local.wait()
    arrived([ff_swap])
    two = [b["f1"][c].astype(F32)[:wr] for c in range(2)]
    b["wf"][x, z, y] = jnp.concatenate(two, 0).astype(BF16)
    for n in ("f1", "f2", "f0"):
        gather_start(n, 0)
    send_rows()
    arrived(steps)
    b["wa"][z, y] = dot(packsel[...], b["p2"][...].reshape(TP * 2 * sh.pc, ACOLS)).astype(BF16)
    for n in ("a0", "a1"):
        gather_start(n, 0)
    for n in ("f1", "f2", "f0"):
        gather_done(n)
        gather_start(n, 1)
    for n in ("a0", "a1"):
        gather_done(n)
        gather_start(n, 1)
    for n in ("f1", "f2", "f0"):
        gather_pass(n)
    gather_done("f1")
    gather_start("f1", 2)
    for n in ("a0", "a1"):
        gather_pass(n)
    for n in ("f2", "f0"):
        gather_done(n)
        gather_start(n, 2)

    for i in range(TP):
        from_device(b["x"].at[pl.ds(pl.multiple_of(OWN * core + TOKENS * i, 16), TOKENS)], 0, i)
    half = b["x"].at[pl.ds(pl.multiple_of(OWN * core, 16), TP * TOKENS)]
    x_swap = remote(half, half, sibling)
    gather_pass("f1")
    for n in ("a0", "a1"):
        gather_done(n)
    wo_cols = slice(WO, WO + HALF)
    wo_local = local(b["wa"].at[:, :, :, wo_cols], b["wo"].at[core])
    wo_swap = remote(b["wa"].at[:, :, :, wo_cols], b["wo"].at[core], sibling)
    send_upstream()

    def attention_weight():
        return b["wa"][:, :, :, :WO].reshape(D, WO)

    small = b["wa"][:, :, :, 4 * HALF :].reshape(D, SMALL)
    chosen = dot(smallsel[...], small, NT)
    b["par"][...] = chosen[0:8]
    b["x"][OWN + 256 : OWN + 272] = chosen[32:48].astype(BF16)

    @pl.when(seg == 0)
    def _():
        b["x"][256:272] = chosen[16:32].astype(BF16)

    @pl.when(seg == 1)
    def _():
        b["x"][256:272] = jnp.zeros((16, D), BF16)

    gains = [b["par"][i : i + 1] for i in range(2)]
    biases = [b["par"][2 + i : 3 + i] for i in range(2)]
    arrived([x_swap])

    hop_to = jnp.where(x == 0, 1, 2)
    hops = []
    for j in range(2):
        hops.append(
            pltpu.make_async_remote_copy(
                src_ref=b["hop"],
                dst_ref=b["hopin"],
                send_sem=xsem.at[6, j],
                recv_sem=xsem.at[6, 2],
                device_id=device(x_=hop_to, c_=j),
                device_id_type=MESH,
            )
        )

    own_rows = pl.ds(pl.multiple_of(OWN * core, 16), OWN)
    other_rows = pl.ds(pl.multiple_of(OWN * other, 16), OWN)

    out = dot(b["x"][...], attention_weight()).astype(BF16)
    for i in range(9):
        b["qkv"][i] = out[:, 128 * i : 128 * i + 128]

    def head_masks(hh):
        lane = lax.broadcasted_iota(jnp.int32, (ROWS, 128), 1)
        row = lax.broadcasted_iota(jnp.int32, (ROWS, 128), 0)
        inside = (lane // 64) == hh
        spare = lane == 64 * (1 - hh)
        memory = ((row >= 256) & (row < 272)) | (row >= OWN + 256)
        invalid = memory & (row % 8 >= 5)
        return inside, spare, invalid

    def forward_pair(p):
        qp, kp, vp = (b["qkv"][3 * p + i] for i in range(3))
        vt = vp.T
        for hh in range(2):
            inside, spare, invalid = head_masks(hh)
            zero = jnp.zeros_like(kp)
            kmask = jnp.where(spare & invalid, jnp.full_like(kp, MASKED), zero)
            km = jnp.where(inside, kp, kmask)
            qm = jnp.where(inside, qp, jnp.where(spare, jnp.ones_like(qp), zero))
            scores = dot(km, qm, NT)
            peak = jnp.max(scores, 0, keepdims=True)
            raised = jnp.exp2((scores - peak) * EXP_SCALE)
            total = jnp.sum(raised, 0, keepdims=True)
            probs = (raised * (1.0 / total)).astype(BF16)
            b["pt"][2 * p + hh] = probs
            b["ot"][p, 64 * hh : 64 * hh + 64] = dot(vt[64 * hh : 64 * hh + 64], probs).astype(BF16)
        b["oc"][:, 128 * p : 128 * p + 128] = b["ot"][p].T

    @pl.when(seg == 0)
    def _():
        forward_pair(0)
        forward_pair(1)

    for n in ("f2", "f0"):
        gather_pass(n)

    @pl.when(seg == 0)
    def _():
        forward_pair(2)

    @pl.when(seg == 1)
    def _():
        hops[0].wait_recv()
        b["x"][256:272] = b["hopin"][...]
        rows = dot(b["hopin"][...], attention_weight()).astype(BF16)
        for i in range(9):
            b["qkv"][i, 256:272] = rows[:, 128 * i : 128 * i + 128]
        for p in range(3):
            forward_pair(p)

    o_local = local(b["oc"].at[own_rows], b["oown"].at[core])
    o_swap = remote(b["oc"].at[other_rows], b["oown"].at[core], sibling)
    wo_local.wait()
    arrived([wo_swap])
    o_local.wait()
    arrived([o_swap])
    halves = []
    for h in range(2):
        w = b["wo"][h].reshape(D, HALF)
        halves.append(dot(b["oown"][0], w[:HALF]) + dot(b["oown"][1], w[HALF:]))
    attended = jnp.concatenate(halves, 1)
    h1, n1, inv1 = norm_forward(b["x"][own_rows].astype(F32) + attended, gains[0], biases[0])
    b["h1"][...] = h1
    b["n1"][...] = n1
    b["inv1"][...] = inv1
    b["h1b"][own_rows] = h1.astype(BF16)
    h_swap = remote(b["h1b"].at[own_rows], b["h1b"].at[own_rows], sibling)
    for n in ("f1", "f2", "f0"):
        gather_done(n)
    arrived([h_swap])

    def feed_weight(t, kind):
        cols = [256 * j + 128 * kind for j in range(3)]
        blocks = [b["wf"][2 * t + i, :, :, :, c : c + 128].reshape(D, 128) for i in range(2) for c in cols]
        return jnp.concatenate(blocks, 1)

    def up_weight(t):
        return feed_weight(t, 0)

    def down_weight(t):
        return feed_weight(t, 1)

    def activate(units):
        erf = 0.5 * (1.0 + lax.erf(units * INV_ROOT_TWO))
        return (units * erf).astype(BF16), erf

    early = pltpu.make_async_remote_copy(
        src_ref=b["es"],
        dst_ref=b["er"],
        send_sem=xsem.at[6, 3],
        recv_sem=xsem.at[6, 4],
        device_id=sibling,
        device_id_type=MESH,
    )
    row16 = lax.broadcasted_iota(jnp.int32, (16, D), 0)

    @pl.when(seg == 0)
    def _():
        rows = b["h1b"][OWN + 256 : OWN + 272]
        part = sum(dot(activate(dot(rows, up_weight(t)))[0], down_weight(t), NT) for t in range(2))

        @pl.when(core == 0)
        def _():
            b["es"][...] = part
            early.start()

        @pl.when(core == 1)
        def _():
            early.wait_recv()
            whole = b["h1"][256:272] + part + b["er"][...]
            written = norm_forward(whole, gains[1], biases[1])[0]
            b["hop"][...] = jnp.where(row16 % 8 < 5, written, 0.0).astype(BF16)
            hops[0].start()
            hops[1].start()

    for t in range(2):
        units = dot(b["h1b"][...], up_weight(t))
        active, erf = activate(units)
        b["gl"][t] = active
        b["sl"][t] = (erf + units * jnp.exp(-0.5 * units * units) * INV_ROOT_TWOPI).astype(BF16)

    def partial_down(rows):
        return sum(dot(b["gl"][t, rows], down_weight(t), NT) for t in range(2))

    b["fs"][...] = partial_down(other_rows).astype(BF16)
    f_swap = remote(b["fs"], b["fr"], sibling)
    branch = partial_down(own_rows)
    arrived([f_swap])
    out, n2, inv2 = norm_forward(b["h1"][...] + branch + b["fr"][...].astype(F32), gains[1], biases[1])
    low = out.astype(BF16)
    b["yb"][...] = low
    b["mo"][...] = low[256:272].astype(F32).reshape(2, 8, D)
    for i in range(TP):
        to_device(
            b["yb"].at[pl.ds(TOKENS * i, TOKENS)],
            hout.at[seg, pl.ds(pl.multiple_of(TOKENS * core, 16), TOKENS)],
            (i, chain),
            xsem.at[3, 2 * seg + core],
            3,
            i,
        )
    for i in range(2):
        to_device(b["mo"].at[i], mout.at[seg], (2 * core + i, chain), xsem.at[4, seg], 4, i)

    for i in range(TP):
        from_device(b["gyt"].at[pl.ds(TOKENS * i, TOKENS)], 1, i)
    for i in range(2):
        from_device(b["gm"].at[i], 2, i)
    upstream = jnp.concatenate([b["gyt"][...].astype(F32), b["gm"][...].reshape(16, D)], 0)
    b["sg"][...] = jnp.zeros((48, D), F32)
    b["sg"][1:2] = column_sum(upstream * n2)
    b["sg"][3:4] = column_sum(upstream)
    dz = norm_backward(upstream, n2, inv2, gains[1])
    b["dz"][...] = dz
    b["dfb"][own_rows] = dz.astype(BF16)
    df_swap = remote(b["dfb"].at[own_rows], b["dfb"].at[own_rows], sibling)
    arrived([df_swap])

    def weight_grad(name, left, right):
        for t in range(2):
            part = dot(left, b[right][t], TN).astype(BF16)
            for i in range(2):
                b[name][2 * t + i] = part[:, HALF * i : HALF * (i + 1)].reshape(nz, ny, br, HALF)

    def pick(axes, axis, place):
        return tuple(place if a == axis else slice(None) for a in axes)

    scatters = {j[0]: j for j in scatter_jobs()}
    rs = {}

    def scatter_send(name, step):
        _, order, cols, axes = scatters[name]
        axis = order[step]
        left = [a for a in axes if a not in order[:step]]
        if step == 0:
            source = b[GRADS[name[0]]]
            tail = (slice(None), cols)
        else:
            source = b[f"s{step - 1}_{name}"]
            tail = ()
        copies = []
        for o in range(1, size[axis]):
            there = (at[axis] + o) % size[axis]
            copies.append(
                remote(source.at[pick(left, axis, there) + tail], b[f"r{step}_{name}"].at[o - 1], moved(axis, o))
            )
        rs[name] = copies

    def scatter_sum(name, step):
        _, order, cols, axes = scatters[name]
        axis = order[step]
        left = [a for a in axes if a not in order[:step]]
        arrived(rs[name])
        if step == 0:
            mine = b[GRADS[name[0]]][pick(left, axis, at[axis]) + (slice(None), cols)]
        else:
            mine = b[f"s{step - 1}_{name}"][pick(left, axis, at[axis])]
        total = mine.astype(F32)
        for o in range(1, size[axis]):
            total = total + b[f"r{step}_{name}"][o - 1].astype(F32)
        if step < len(order) - 1:
            b[f"s{step}_{name}"][...] = total.astype(BF16)
        return total

    def scatter_on(names, step):
        for n in names:
            scatter_sum(n, step)
            scatter_send(n, step + 1)

    down_names, up_names = ("t0", "t1", "t2"), ("i0", "i1", "i2")
    weight_grad("gt", b["dfb"][...], "gl")
    for n in down_names:
        scatter_send(n, 0)
    for t in range(2):
        b["du"][t] = (dot(b["dfb"][...], down_weight(t)) * b["sl"][t].astype(F32)).astype(BF16)

    def partial_up(rows):
        return sum(dot(b["du"][t, rows], up_weight(t), NT) for t in range(2))

    b["dhs"][...] = partial_up(other_rows).astype(BF16)
    dh_swap = remote(b["dhs"], b["dhr"], sibling)
    b["dz"][...] = b["dz"][...] + partial_up(own_rows)
    weight_grad("gi", b["h1b"][...], "du")
    for n in up_names:
        scatter_send(n, 0)
    arrived([dh_swap])
    into_first = b["dz"][...] + b["dhr"][...].astype(F32)
    b["sg"][0:1] = column_sum(into_first * b["n1"][...])
    b["sg"][2:3] = column_sum(into_first)
    dr = norm_backward(into_first, b["n1"][...], b["inv1"][...], gains[0])
    b["dr"][...] = dr
    b["dab"][own_rows] = dr.astype(BF16)
    da_swap = remote(b["dab"].at[own_rows], b["dab"].at[own_rows], sibling)
    arrived([da_swap])

    def head_rows(ref, c):
        if nz > 1:
            return ref.at[pl.ds(c * (nz // 2), nz // 2)]
        return ref.at[:, :, pl.ds(pl.multiple_of(c * HALF, 16), HALF)]

    grad_mixed = 0.0
    for h in range(2):
        w = head_rows(b["wo"].at[h], core)[...].reshape(HALF, HALF)
        grad_mixed = grad_mixed + dot(b["dab"][:, HALF * h : HALF * (h + 1)], w, NT)
    for p in range(3):
        b["doc"][p] = grad_mixed[:, 128 * p : 128 * p + 128].astype(BF16)

    mixed_t = b["ot"][...].reshape(HALF, ROWS)

    def proj_grad(h):
        cols = pl.ds(pl.multiple_of(HALF * h, 128), HALF)
        return dot(mixed_t, b["dab"][:, cols]).astype(BF16).reshape(b["gos"].shape)

    def wo_part(c):
        return head_rows(b["ga"].at[:, :, :, wo_cols], c)

    b["gos"][...] = proj_grad(other)
    go_swap = remote(b["gos"], wo_part(core), sibling)
    wo_part(core)[...] = proj_grad(core)

    def backward_pair(p):
        qp, kp, vp = (b["qkv"][3 * p + i] for i in range(3))
        dop = b["doc"][p]
        kt = kp.T
        dv = dk = 0.0
        dq = []
        for hh in range(2):
            inside, _, _ = head_masks(hh)
            zero = jnp.zeros_like(kp)
            grad_probs = dot(jnp.where(inside, vp, zero), dop, NT)
            low_probs = b["pt"][2 * p + hh]
            probs = low_probs.astype(F32)
            row_term = jnp.sum(probs * grad_probs, 0, keepdims=True)
            ds = (probs * (grad_probs - row_term)).astype(BF16)
            dv = dv + dot(low_probs, jnp.where(inside, dop, zero))
            dk = dk + dot(ds, jnp.where(inside, qp, zero))
            dq.append(dot(kt[64 * hh : 64 * hh + 64], ds))
        b["dqkv"][3 * p] = (jnp.concatenate(dq, 0) * 0.125).T.astype(BF16)
        b["dqkv"][3 * p + 1] = (dk * 0.125).astype(BF16)
        b["dqkv"][3 * p + 2] = dv.astype(BF16)

    def joined(rows, wanted):
        return jnp.concatenate([b["dqkv"][i, rows] for i in wanted], 1)

    def attention_grad(p):
        part = dot(b["x"][...], joined(slice(None), range(3 * p, 3 * p + 3)), TN).astype(BF16)
        b["ga"][:, :, :, HALF * p : HALF * (p + 1)] = part.reshape(nz, ny, br, HALF)

    backward_pair(0)
    attention_grad(0)
    arrived([go_swap])
    scatter_send("aw", 0)
    scatter_send("a0", 0)
    scatter_on(down_names, 0)
    backward_pair(1)
    attention_grad(1)
    scatter_send("a1", 0)
    scatter_on(up_names, 0)
    backward_pair(2)
    attention_grad(2)
    scatter_send("a2", 0)
    scatter_send("a3", 0)

    def partial_input(rows):
        return dot(joined(rows, range(9)), attention_weight(), NT)

    b["dxs"][...] = partial_input(other_rows).astype(BF16)
    dx_swap = remote(b["dxs"], b["dxr"], sibling)
    dx = partial_input(own_rows) + b["dr"][...]
    arrived([dx_swap])
    dx = dx + b["dxr"][...].astype(F32)
    b["dxb"][...] = dx[:256].astype(BF16)
    for i in range(TP):
        to_device(
            b["dxb"].at[pl.ds(TOKENS * i, TOKENS)],
            dxo.at[seg, pl.ds(pl.multiple_of(TOKENS * core, 16), TOKENS)],
            (i, chain),
            xsem.at[5, 2 * seg + core],
            5,
            i,
        )

    @pl.when((core == 0) & (seg == 0))
    def _():
        b["sg"][16:32] = dx[256:272]

    @pl.when(core == 1)
    def _():
        b["sg"][32:48] = dx[256:272]

    small_grads = dot(b["sg"][...].astype(BF16), smallsel[...], TN).astype(BF16)
    b["ga"][:, :, :, 4 * HALF :] = small_grads.reshape(nz, ny, br, SMALL)
    scatter_send("as", 0)
    attention_names = ("aw", "a0", "a1", "a2", "a3", "as")
    scatter_on(down_names, 1)
    scatter_on(attention_names, 0)
    scatter_on(up_names, 1)

    def last_rows(names, first_col):
        for j, n in enumerate(names):
            total = scatter_sum(n, 2)
            cols = slice(first_col + 128 * j, first_col + 128 * j + 128)
            b["sf"][0, :, cols] = total[:wr]
            b["sf"][1, :, cols] = total[wr:]

    for n in attention_names:
        cols = scatters[n][2]
        spread = dot(packsel[...], scatter_sum(n, 1).astype(BF16), TN).astype(BF16)
        b["e3"][:, :, cols] = spread.reshape(TP, 2 * sh.pc, cols.stop - cols.start)
    steps = [remote(b["e3"].at[(x + o) % TP], b["r3"].at[o - 1], moved("x", o)) for o in range(1, TP)]
    last_rows(down_names, HALF)
    last_rows(up_names, 0)
    sf_local = local(b["sf"].at[core], gfo.at[core])
    sf_swap = remote(b["sf"].at[other], gfo.at[core], sibling)

    arrived(steps)
    total = b["e3"][x].astype(F32)
    for o in range(1, TP):
        total = total + b["r3"][o - 1].astype(F32)
    b["s4"][...] = total.reshape(2, sh.pc, ACOLS)
    s4_local = local(b["s4"].at[core], gao.at[core])
    s4_swap = remote(b["s4"].at[other], gao.at[core], sibling)

    for kind, out_ref in ((3, hout), (5, dxo)):
        for s in range(2):
            for j in range(2):
                from_device(out_ref.at[s, pl.ds(TOKENS * j, TOKENS)], kind, 2 * s + j)
    for s in range(2):
        from_device(mout.at[s], 4, s)
    sf_local.wait()
    s4_local.wait()
    arrived([sf_swap, s4_swap])

    for copy in sent:
        copy.wait_send()
    for same, copy in conditional:

        @pl.when(jnp.logical_not(same))
        def _():
            copy.wait_send()

    @pl.when((seg == 0) & (core == 1))
    def _():
        hops[0].wait_send()
        hops[1].wait_send()

    @pl.when((seg == 0) & (core == 0))
    def _():
        early.wait_send()


def layer(sh, arrays):
    constants = [jnp.asarray(a, BF16) for a in selections(sh)]
    table = scratch_of(sh)
    names = list(table)
    vmem = pl.BlockSpec(memory_space=pltpu.VMEM)
    outs = [
        jax.ShapeDtypeStruct((2, 128, D), BF16),
        jax.ShapeDtypeStruct((2, 8, D), F32),
        jax.ShapeDtypeStruct((2, 128, D), BF16),
        jax.ShapeDtypeStruct((2, sh.pc, ACOLS), F32),
        jax.ShapeDtypeStruct((2, sh.wrows, D), F32),
    ]
    return pl.pallas_call(
        functools.partial(kernel, sh, names),
        name="layer",
        out_shape=outs,
        in_specs=[pl.BlockSpec(memory_space=pl.ANY)] * 2 + [vmem] * 11,
        out_specs=[pl.BlockSpec(memory_space=pl.ANY), vmem] * 2 + [vmem],
        scratch_shapes=[pltpu.VMEM(*table[n]) for n in names]
        + [
            pltpu.SemaphoreType.DMA((200,)),
            pltpu.SemaphoreType.DMA((200,)),
            pltpu.SemaphoreType.DMA((7, 12)),
            pltpu.SemaphoreType.DMA((8,)),
        ],
        compiler_params=pltpu.CompilerParams(
            collective_id=0, has_side_effects=True, vmem_limit_bytes=64 * 2**20 - 2**17
        ),
    )(*arrays, *constants)


def unpack_kernel(sh, hout, mout, dxo, gao, gfo, *outs):
    hidden, memory, grad_in, gq, gp, gains, biases, tokens, gi, gt = outs
    ar = sh.arows
    hidden[...] = hout[...]
    for i in range(2):
        memory[:, i] = mout[i, :5].astype(BF16)
    grad_in[...] = dxo[...].astype(F32)
    for h in range(2):
        for p in range(3):
            for i in range(3):
                to = D * i + HALF * h + 128 * p
                first = HALF * p + 128 * i
                gq[:, to : to + 128] = gao[h, :ar, first : first + 128]
        gp[:, HALF * h : HALF * (h + 1)] = gao[h, :ar, WO : WO + HALF]
        gi[:, HALF * h : HALF * (h + 1)] = gfo[h, :, :HALF]
        gt[:, HALF * h : HALF * (h + 1)] = gfo[h, :, HALF:]
    small = gao[0, :, 4 * HALF :] + gao[1, :, 4 * HALF :]
    turned = small.T[:, :ar]
    gains[...] = turned[0:2]
    biases[...] = turned[2:4]
    for kind in range(2):
        tokens[:, kind] = small[:ar, 4 + MEM * kind : 4 + MEM * (kind + 1)]


def unpack(sh, *arrays):
    ar, wr = sh.arows, sh.wrows
    shapes = [
        ((2, 128, D), BF16),
        ((5, 2, D), BF16),
        ((2, 128, D), F32),
        ((ar, 3 * D), F32),
        ((ar, D), F32),
        ((2, ar), F32),
        ((2, ar), F32),
        ((ar, 2, MEM), F32),
        ((wr, D), F32),
        ((wr, D), F32),
    ]
    vmem = pl.BlockSpec(memory_space=pltpu.VMEM)
    return pl.pallas_call(
        functools.partial(unpack_kernel, sh),
        name="unpack",
        out_shape=[jax.ShapeDtypeStruct(*one) for one in shapes],
        in_specs=[vmem] * 5,
        out_specs=[vmem] * len(shapes),
        compiler_params=pltpu.CompilerParams(vmem_limit_bytes=64 * 2**20 - 2**17),
    )(*arrays)


def body(
    sh,
    hidden_in,
    reset,
    w_qkv,
    w_attn_out,
    norm_gains,
    norm_biases,
    memory_tokens,
    w_in,
    w_out,
    grad_hidden,
    grad_memory,
):
    arrays = (
        hidden_in,
        grad_hidden,
        grad_memory.transpose(1, 0, 2),
        w_qkv,
        w_attn_out,
        norm_gains,
        norm_biases,
        memory_tokens.transpose(2, 0, 1),
        w_in,
        w_out.T,
    )
    hidden, memory, *middle, tokens, gi, gt = unpack(sh, *layer(sh, arrays))
    return hidden, memory.transpose(1, 0, 2), *middle, tokens.transpose(1, 2, 0), gi, gt.T


def solution(mesh):
    sh = Shape(mesh.shape["dp"])
    return jax.shard_map(
        functools.partial(body, sh),
        mesh=mesh,
        in_specs=(
            P("dp", "tp", None),
            P("dp"),
            P(("dp", "tp"), None),
            P(("dp", "tp"), None),
            P(None, ("dp", "tp")),
            P(None, ("dp", "tp")),
            P(None, None, ("dp", "tp")),
            P("dp", "tp"),
            P("tp", "dp"),
            P("dp", "tp", None),
            P("dp", "tp", None),
        ),
        out_specs=(
            P("dp", "tp", None),
            P("dp", "tp", None),
            P("dp", "tp", None),
            P(("dp", "tp"), None),
            P(("dp", "tp"), None),
            P(None, ("dp", "tp")),
            P(None, ("dp", "tp")),
            P(None, None, ("dp", "tp")),
            P("dp", "tp"),
            P("tp", "dp"),
        ),
        check_vma=False,
    )
```

```python
import functools

import jax
import jax.numpy as jnp
import numpy as np
from jax import lax
from jax.experimental import pallas as pl
from jax.experimental.pallas import tpu as pltpu
from jax.sharding import PartitionSpec as P

D = 768
HALF = 384
MEM = 10
TOKENS = 64
OWN = 272
ROWS = 2 * OWN
TP = 4
SMALL = 128
ACOLS = 4 * HALF + SMALL
REST = ACOLS - HALF
CUT = HALF + 640
WO = 3 * HALF
EPSILON = 1e-05
INV_ROOT_TWO = 0.7071067811865476
INV_ROOT_TWOPI = 0.3989422804014327
EXP_SCALE = 0.125 * 1.4426950408889634
MASKED = -1e30
F32 = jnp.float32
BF16 = jnp.bfloat16
MESH = pl.DeviceIdType.MESH
NN = (((1,), (0,)), ((), ()))
NT = (((1,), (1,)), ((), ()))
TN = (((0,), (0,)), ((), ()))


def dot(a, b, dims=NN):
    return lax.dot_general(a, b, dims, preferred_element_type=F32)


def up16(n):
    return -(-n // 16) * 16


class Shape:
    def __init__(self, dp):
        self.dp = dp
        planes = dp // 2
        self.ny = int(round(planes**0.5))
        self.nz = planes // self.ny
        self.wrows = D // dp
        self.arows = D // (dp * TP)
        self.brows = 2 * self.wrows
        self.pr = up16(self.arows)
        self.xrows = 2 * self.arows * self.ny
        self.pc = -(-self.arows // 8) * 8
        self.fr = up16(self.wrows)


def selections(sh):
    pack = np.zeros((sh.brows, TP * 2 * sh.pc), np.float32)
    for c in range(2):
        for x in range(TP):
            for i in range(sh.arows):
                pack[c * sh.wrows + x * sh.arows + i, (x * 2 + c) * sh.pc + i] = 1
    packy = np.zeros((sh.xrows, sh.ny * 2 * sh.pc), np.float32)
    turn = np.zeros((D, D), np.float32)
    ar = sh.arows
    for c in range(2):
        for y in range(sh.ny):
            for i in range(ar):
                row = (y * 2 + c) * ar + i
                packy[row, (y * 2 + c) * sh.pc + i] = 1
                for x in range(TP):
                    for z in range(sh.nz):
                        place = (z * sh.ny + y) * sh.brows + (c * TP + x) * ar + i
                        turn[(x * sh.nz + z) * sh.xrows + row, place] = 1
    small = np.zeros((48, SMALL), np.float32)
    for i in range(4):
        small[i, i] = 1
    for kind in range(2):
        for i in range(MEM):
            small[16 + 16 * kind + (i // 5) * 8 + i % 5, 4 + MEM * kind + i] = 1
    places = np.zeros((4, MEM, SMALL), np.float32)
    for kind, (rows, first) in enumerate(((2, 0), (2, 2), (MEM, 4), (MEM, 4 + MEM))):
        for i in range(rows):
            places[kind, i, first + i] = 1
    return pack, small, places, packy, turn


def norm_forward(inputs, gain, offset):
    centred = inputs - jnp.mean(inputs, -1, keepdims=True)
    spread = jnp.mean(centred * centred, -1, keepdims=True)
    inverse = lax.rsqrt(spread + EPSILON)
    normed = centred * inverse
    return normed * gain + offset, normed, inverse


def norm_backward(upstream, normed, inverse, gain):
    scaled = upstream * gain
    first_mean = jnp.mean(scaled, -1, keepdims=True)
    second_mean = jnp.mean(scaled * normed, -1, keepdims=True)
    return inverse * (scaled - first_mean - normed * second_mean)


def column_sum(a):
    return jnp.sum(a, 0, keepdims=True)


SCRATCH = {}


def scratch_of(sh):
    nz, ny, br = sh.nz, sh.ny, sh.brows
    s = {
        "pk": ((2, sh.pr, ACOLS), BF16),
        "ff": ((2, sh.fr, D), BF16),
        "gms": ((2, 8, D), F32),
        "p1": ((2, sh.pr, ACOLS), BF16),
        "p2": ((TP, 2 * sh.pc, REST), BF16),
        "p2y": ((ny, 2 * sh.pc, HALF), BF16),
        "turn": ((D, D), BF16),
        "xp": ((ROWS, D), BF16),
        "wx": ((TP, nz, sh.xrows, HALF), BF16),
        "gx": ((TP, nz, sh.xrows, HALF), BF16),
        "f1": ((2, sh.fr, D), BF16),
        "wa": ((nz, ny, br, ACOLS), BF16),
        "wf": ((TP, nz, ny, br, D), BF16),
        "wo": ((2, nz, ny, br, HALF), BF16),
        "par": ((8, D), F32),
        "x": ((ROWS, D), BF16),
        "gyt": ((TP * TOKENS, D), BF16),
        "gm": ((2, 8, D), F32),
        "qkv": ((9, ROWS, 128), BF16),
        "pt": ((6, ROWS, ROWS), BF16),
        "ot": ((3, 128, ROWS), BF16),
        "oc": ((ROWS, HALF), BF16),
        "oown": ((2, OWN, HALF), BF16),
        "h1": ((OWN, D), F32),
        "n1": ((OWN, D), F32),
        "inv1": ((OWN, 1), F32),
        "h1b": ((ROWS, D), BF16),
        "gl": ((2, ROWS, D), BF16),
        "sl": ((2, ROWS, D), BF16),
        "fs": ((OWN, D), BF16),
        "fr": ((OWN, D), BF16),
        "n2": ((OWN, D), F32),
        "yb": ((OWN, D), BF16),
        "mo": ((2, 8, D), F32),
        "hop": ((16, D), BF16),
        "hopin": ((16, D), BF16),
        "es": ((16, D), F32),
        "er": ((16, D), F32),
        "dz": ((OWN, D), F32),
        "dfb": ((ROWS, D), BF16),
        "du": ((2, ROWS, D), BF16),
        "dhs": ((OWN, D), BF16),
        "dhr": ((OWN, D), BF16),
        "dr": ((OWN, D), F32),
        "dab": ((ROWS, D), BF16),
        "doc": ((3, ROWS, 128), BF16),
        "dqkv": ((9, ROWS, 128), BF16),
        "ga": ((nz, ny, br, ACOLS), BF16),
        "gi": ((TP, nz, ny, br, HALF), BF16),
        "gt": ((TP, nz, ny, br, HALF), BF16),
        "gos": ((D // 2 // br if nz > 1 else 1, br if nz > 1 else HALF, HALF), BF16),
        "dxs": ((OWN, D), BF16),
        "dxr": ((OWN, D), BF16),
        "dxb": ((TP * TOKENS, D), BF16),
        "sg": ((48, D), F32),
        "e3": ((TP, 2 * sh.pc, REST), BF16),
        "r3": ((TP - 1, 2 * sh.pc, REST), BF16),
        "e3y": ((ny, 2 * sh.pc, HALF), BF16),
        "r3y": ((max(1, ny - 1), 2 * sh.pc, HALF), BF16),
        "s4": ((2, sh.pc, ACOLS), F32),
        "sf": ((2, sh.wrows, D), F32),
    }
    if nz > 1:
        s["gos"] = ((nz // 2, ny, br, HALF), BF16)
    else:
        s["gos"] = ((1, 1, HALF, HALF), BF16)
    sizes = {"x": TP, "z": nz, "y": ny}
    for name, order, cols, axes in scatter_jobs():
        left = [a for a in axes]
        block = (sh.xrows if name[0] == "x" else br, cols.stop - cols.start)
        for step, axis in enumerate(order):
            left = [a for a in left if a != axis]
            dims = tuple(sizes[a] for a in left)
            s[f"r{step}_{name}"] = ((max(1, sizes[axis] - 1),) + dims + block, BF16)
            if step < len(order) - 1:
                s[f"s{step}_{name}"] = (dims + block, BF16)
    return s


def scatter_jobs():
    orders = [("z", "y", "x"), ("x", "z", "y"), ("y", "x", "z")]
    jobs = []
    for kind in ("t", "i"):
        for j in range(3):
            jobs.append((f"{kind}{j}", orders[j], slice(128 * j, 128 * j + 128), ("x", "z", "y")))
    zy, yz = ("z", "y"), ("y", "z")
    jobs.append(("aw", yz, slice(WO, WO + HALF), zy))
    jobs.append(("x0", ("x", "z"), slice(0, HALF), ("x", "z")))
    jobs.append(("a1", zy, slice(HALF, 2 * HALF), zy))
    jobs.append(("a2", yz, slice(2 * HALF, 2 * HALF + 256), zy))
    jobs.append(("a3", zy, slice(2 * HALF + 256, 3 * HALF), zy))
    jobs.append(("as", zy, slice(4 * HALF, ACOLS), zy))
    return jobs


def gather_jobs():
    orders = [("x", "y", "z"), ("y", "z", "x"), ("z", "x", "y")]
    jobs = [(f"f{j}", orders[j], slice(256 * j, 256 * j + 256), ("x", "z", "y")) for j in range(3)]
    jobs.append(("x0", ("z", "x"), slice(0, HALF), ("x", "z")))
    jobs.append(("a0", ("y", "z"), slice(HALF, CUT), ("z", "y")))
    jobs.append(("a1", ("z", "y"), slice(CUT, ACOLS), ("z", "y")))
    return jobs


WEIGHTS = {"f": "wf", "a": "wa", "x": "wx"}
GRADS = {"t": "gt", "i": "gi", "a": "ga", "x": "gx"}


def kernel(sh, names, *refs):
    xin, gin, gmem, wq, wp, gain_in, bias_in, token_in, up_in, down_in = refs[:10]
    packsel, smallsel, places, packy, turn = refs[10:15]
    hout, mout, dxo, gao, gfo = refs[15:20]
    b = dict(zip(names, refs[20 : 20 + len(names)]))
    ssem, rsem, xsem, lsem = refs[20 + len(names) :]
    nz, ny, br, wr, ar = sh.nz, sh.ny, sh.brows, sh.wrows, sh.arows
    pk, ff, gms = b["pk"], b["ff"], b["gms"]

    dp = lax.axis_index("dp")
    x = lax.axis_index("tp")
    core = dp % 2
    y = (dp // 2) % ny
    z = dp // (2 * ny)
    other = 1 - core
    chain = x // 2
    seg = jnp.where((x == 1) | (x == 2), 1, 0)
    at = {"x": x, "y": y, "z": z}
    size = {"x": TP, "y": ny, "z": nz}

    def device(x_=x, y_=y, z_=z, c_=core):
        return ((z_ * ny + y_) * 2 + c_, x_)

    def moved(axis, offset, core_=core):
        there = dict(at)
        there[axis] = (at[axis] + offset) % size[axis]
        return device(there["x"], there["y"], there["z"], core_)

    sibling = device(c_=other)
    counts = {"s": 0, "r": 0}
    sent = []

    def remote(src, dst, to):
        copy = pltpu.make_async_remote_copy(
            src_ref=src,
            dst_ref=dst,
            send_sem=ssem.at[counts["s"]],
            recv_sem=rsem.at[counts["r"]],
            device_id=to,
            device_id_type=MESH,
        )
        counts["s"] += 1
        counts["r"] += 1
        copy.start()
        sent.append(copy)
        return copy

    def arrived(copies):
        for copy in copies:
            copy.wait_recv()

    locals_ = [0]

    def local(src, dst):
        copy = pltpu.make_async_copy(src, dst, lsem.at[locals_[0]])
        locals_[0] += 1
        copy.start()
        return copy

    barrier = pltpu.get_barrier_semaphore()
    peers = [sibling]
    for o in range(1, TP):
        peers += [moved("x", o), moved("x", o, other)]
    for axis in ("y", "z"):
        for o in range(1, size[axis]):
            peers.append(moved(axis, o))
    for peer in peers:
        pl.semaphore_signal(barrier, inc=1, device_id=peer, device_id_type=MESH)

    turn_local = local(turn, b["turn"])

    small = dot(gain_in[...], places[0, :2], TN) + dot(bias_in[...], places[1, :2], TN)
    small = small + dot(token_in[:, 0], places[2]) + dot(token_in[:, 1], places[3])
    small = small.astype(BF16)
    pk[...] = jnp.zeros(pk.shape, BF16)
    ff[...] = jnp.zeros(ff.shape, BF16)
    gms[...] = jnp.zeros(gms.shape, F32)
    for h in range(2):
        for p in range(3):
            for i in range(3):
                first = D * i + HALF * h + 128 * p
                pk[h, :ar, HALF * p + 128 * i : HALF * p + 128 * (i + 1)] = wq[:, first : first + 128]
        pk[h, :ar, WO : WO + HALF] = wp[:, HALF * h : HALF * (h + 1)]
        pk[h, :ar, 4 * HALF :] = small
        for j in range(3):
            cols = slice(HALF * h + 128 * j, HALF * h + 128 * (j + 1))
            ff[h, :wr, 256 * j : 256 * j + 128] = up_in[:, cols]
            ff[h, :wr, 256 * j + 128 : 256 * j + 256] = down_in[:, cols]
        gms[h, 0:5] = gmem[:, h].astype(F32)
    pl.semaphore_wait(barrier, len(peers))

    pk_local = local(pk.at[core], b["p1"].at[core])
    ff_local = local(ff.at[core], b["f1"].at[core])
    pk_swap = remote(pk.at[other], b["p1"].at[core], sibling)
    ff_swap = remote(ff.at[other], b["f1"].at[core], sibling)

    conditional = []

    def to_device(src, dst, place, here, kind, send_slot):
        copy = pltpu.make_async_remote_copy(
            src_ref=src,
            dst_ref=dst,
            send_sem=xsem.at[kind, 8 + send_slot],
            recv_sem=here,
            device_id=device(x_=place[0], c_=place[1]),
            device_id_type=MESH,
        )
        same = (place[0] == x) & (place[1] == core)

        @pl.when(same)
        def _():
            pltpu.make_async_copy(src, dst, here).start()

        @pl.when(jnp.logical_not(same))
        def _():
            copy.start()

        conditional.append((same, copy))

    def from_device(dst, kind, slot):
        pltpu.make_async_copy(dst, dst, xsem.at[kind, slot]).wait()

    def chip_of(k, s):
        return s + k * (3 - 2 * s)

    def send_rows():
        for s in range(2):
            for j in range(2):
                to_device(
                    xin.at[s, pl.ds(TOKENS * j, TOKENS)],
                    b["x"].at[pl.ds(pl.multiple_of(OWN * j + TOKENS * x, 16), TOKENS)],
                    (chip_of(core, s), j),
                    xsem.at[0, x],
                    0,
                    2 * s + j,
                )

    def send_upstream():
        for s in range(2):
            for j in range(2):
                to_device(
                    gin.at[s, pl.ds(TOKENS * j, TOKENS)],
                    b["gyt"].at[pl.ds(pl.multiple_of(TOKENS * x, 16), TOKENS)],
                    (chip_of(core, s), j),
                    xsem.at[1, x],
                    1,
                    2 * s + j,
                )
            to_device(
                gms.at[s], b["gm"].at[x % 2], (chip_of(core, s), x // 2), xsem.at[2, x % 2], 2, s
            )

    def part_of(job, step, place, half=None):
        name, order, cols, axes = job
        fixed = {a: at[a] for a in order[step:]}
        fixed[order[step]] = place
        where = []
        for a in axes:
            if a in fixed:
                where.append(fixed[a])
            elif half is not None:
                where.append(pl.ds(half * (size[a] // 2), size[a] // 2))
                half = None
            else:
                where.append(slice(None))
        return b[WEIGHTS[name[0]]].at[tuple(where) + (slice(None), cols)]

    def gather_start(name, step):
        job = gathers[name]
        axis = job[1][step]
        n = size[axis]
        own = part_of(job, step, at[axis])
        free = [a for a in job[3] if a not in job[1][step:]]
        relay = n == 4 and step == len(job[1]) - 1 and size[free[0]] % 2 == 0
        state = {"step": step, "relay": relay}
        if relay:
            state["right"] = remote(own, own, moved(axis, 1))
            state["left"] = remote(own, own, moved(axis, n - 1))
        else:
            state["all"] = [remote(own, own, moved(axis, o)) for o in range(1, n)]
        flying[name] = state

    def gather_pass(name):
        job, state = gathers[name], flying[name]
        if not state["relay"]:
            return
        axis = job[1][state["step"]]
        n = size[axis]
        state["all"] = []
        for kind, back, onward, half in (("right", n - 1, 1, 0), ("left", 1, n - 1, 1)):
            arrived([state[kind]])
            piece = part_of(job, state["step"], (at[axis] + back) % n, half)
            state["all"].append(remote(piece, piece, moved(axis, onward)))

    def gather_done(name):
        arrived(flying[name]["all"])

    gathers = {j[0]: j for j in gather_jobs()}
    flying = {}

    pk_local.wait()
    arrived([pk_swap])
    packed = jnp.concatenate([b["p1"][c].astype(F32)[: sh.pc] for c in range(2)], 0).astype(BF16)
    b["p2y"][y] = packed[:, :HALF]
    b["p2"][x] = packed[:, HALF:]
    mine = b["p2y"].at[y]
    ysteps = [remote(mine, mine, moved("y", o)) for o in range(1, ny)]
    mine = b["p2"].at[x]
    xsteps = [remote(mine, mine, moved("x", o)) for o in range(1, TP)]
    ff_local.wait()
    arrived([ff_swap])
    two = [b["f1"][c].astype(F32)[:wr] for c in range(2)]
    b["wf"][x, z, y] = jnp.concatenate(two, 0).astype(BF16)
    feed_names, first_names = ("f1", "f2", "f0"), ("x0", "a0", "a1")
    for n in feed_names:
        gather_start(n, 0)
    send_rows()
    arrived(ysteps)
    b["wx"][x, z] = dot(packy[...], b["p2y"][...].reshape(ny * 2 * sh.pc, HALF)).astype(BF16)
    gather_start("x0", 0)
    arrived(xsteps)
    b["wa"][z, y, :, HALF:] = dot(packsel[...], b["p2"][...].reshape(TP * 2 * sh.pc, REST)).astype(BF16)
    for n in ("a0", "a1"):
        gather_start(n, 0)
    for n in feed_names:
        gather_done(n)
        gather_start(n, 1)
    for n in first_names:
        gather_done(n)
        gather_start(n, 1)
    for n in feed_names:
        gather_done(n)
        if n == "f1":
            gather_start(n, 2)
    for n in first_names:
        gather_pass(n)
    for n in ("f2", "f0"):
        gather_start(n, 2)

    for i in range(TP):
        from_device(b["x"].at[pl.ds(pl.multiple_of(OWN * core + TOKENS * i, 16), TOKENS)], 0, i)
    half = b["x"].at[pl.ds(pl.multiple_of(OWN * core, 16), TP * TOKENS)]
    x_swap = remote(half, half, sibling)
    for first in (256, OWN + 256):
        b["x"][first : first + 16] = jnp.zeros((16, D), BF16)
    turn_local.wait()
    arrived([x_swap])
    b["xp"][...] = dot(b["x"][...], b["turn"][...], NT).astype(BF16)
    for n in first_names:
        gather_done(n)
    wo_cols = slice(WO, WO + HALF)
    wo_local = local(b["wa"].at[:, :, :, wo_cols], b["wo"].at[core])
    wo_swap = remote(b["wa"].at[:, :, :, wo_cols], b["wo"].at[core], sibling)
    gather_pass("f1")
    send_upstream()

    def attention_weight():
        return b["wa"][:, :, :, :WO].reshape(D, WO)

    small = b["wa"][:, :, :, 4 * HALF :].reshape(D, SMALL)
    chosen = dot(smallsel[...], small, NT)
    b["par"][...] = chosen[0:8]
    memory = chosen[16:48].astype(BF16)
    b["x"][OWN + 256 : OWN + 272] = memory[16:]
    turned = dot(memory, b["turn"][...], NT).astype(BF16)
    b["xp"][OWN + 256 : OWN + 272] = turned[16:]

    @pl.when(seg == 0)
    def _():
        b["x"][256:272] = memory[:16]
        b["xp"][256:272] = turned[:16]

    gains = [b["par"][i : i + 1] for i in range(2)]
    biases = [b["par"][2 + i : 3 + i] for i in range(2)]

    hop_to = jnp.where(x == 0, 1, 2)
    hops = []
    for j in range(2):
        hops.append(
            pltpu.make_async_remote_copy(
                src_ref=b["hop"],
                dst_ref=b["hopin"],
                send_sem=xsem.at[6, j],
                recv_sem=xsem.at[6, 2],
                device_id=device(x_=hop_to, c_=j),
                device_id_type=MESH,
            )
        )

    own_rows = pl.ds(pl.multiple_of(OWN * core, 16), OWN)
    other_rows = pl.ds(pl.multiple_of(OWN * other, 16), OWN)

    out = dot(b["xp"][...], b["wx"][...].reshape(D, HALF)).astype(BF16)
    for i in range(3):
        b["qkv"][i] = out[:, 128 * i : 128 * i + 128]
    out = dot(b["x"][...], b["wa"][:, :, :, HALF:WO].reshape(D, 2 * HALF)).astype(BF16)
    for i in range(3, 9):
        b["qkv"][i] = out[:, 128 * (i - 3) : 128 * (i - 2)]

    def head_masks(hh):
        lane = lax.broadcasted_iota(jnp.int32, (ROWS, 128), 1)
        row = lax.broadcasted_iota(jnp.int32, (ROWS, 128), 0)
        inside = (lane // 64) == hh
        spare = lane == 64 * (1 - hh)
        memory = ((row >= 256) & (row < 272)) | (row >= OWN + 256)
        invalid = memory & (row % 8 >= 5)
        return inside, spare, invalid

    def forward_pair(p):
        qp, kp, vp = (b["qkv"][3 * p + i] for i in range(3))
        vt = vp.T
        for hh in range(2):
            inside, spare, invalid = head_masks(hh)
            zero = jnp.zeros_like(kp)
            kmask = jnp.where(spare & invalid, jnp.full_like(kp, MASKED), zero)
            km = jnp.where(inside, kp, kmask)
            qm = jnp.where(inside, qp, jnp.where(spare, jnp.ones_like(qp), zero))
            scores = dot(km, qm, NT)
            peak = jnp.max(scores, 0, keepdims=True)
            raised = jnp.exp2((scores - peak) * EXP_SCALE)
            total = jnp.sum(raised, 0, keepdims=True)
            probs = (raised * (1.0 / total)).astype(BF16)
            b["pt"][2 * p + hh] = probs
            b["ot"][p, 64 * hh : 64 * hh + 64] = dot(vt[64 * hh : 64 * hh + 64], probs).astype(BF16)
        b["oc"][:, 128 * p : 128 * p + 128] = b["ot"][p].T

    @pl.when(seg == 0)
    def _():
        forward_pair(0)
        forward_pair(1)

    ordered = dot(b["turn"][...], b["wx"][...].reshape(D, HALF), TN).astype(BF16)
    b["wa"][:, :, :, :HALF] = ordered.reshape(nz, ny, br, HALF)
    for n in ("f2", "f0"):
        gather_pass(n)

    @pl.when(seg == 0)
    def _():
        forward_pair(2)

    @pl.when(seg == 1)
    def _():
        hops[0].wait_recv()
        b["x"][256:272] = b["hopin"][...]
        b["xp"][256:272] = dot(b["hopin"][...], b["turn"][...], NT).astype(BF16)
        rows = dot(b["hopin"][...], attention_weight()).astype(BF16)
        for i in range(9):
            b["qkv"][i, 256:272] = rows[:, 128 * i : 128 * i + 128]
        for p in range(3):
            forward_pair(p)

    o_local = local(b["oc"].at[own_rows], b["oown"].at[core])
    o_swap = remote(b["oc"].at[other_rows], b["oown"].at[core], sibling)
    wo_local.wait()
    arrived([wo_swap])
    o_local.wait()
    arrived([o_swap])
    halves = []
    for h in range(2):
        w = b["wo"][h].reshape(D, HALF)
        halves.append(dot(b["oown"][0], w[:HALF]) + dot(b["oown"][1], w[HALF:]))
    attended = jnp.concatenate(halves, 1)
    h1, n1, inv1 = norm_forward(b["x"][own_rows].astype(F32) + attended, gains[0], biases[0])
    b["h1"][...] = h1
    b["n1"][...] = n1
    b["inv1"][...] = inv1
    b["h1b"][own_rows] = h1.astype(BF16)
    h_swap = remote(b["h1b"].at[own_rows], b["h1b"].at[own_rows], sibling)
    for n in ("f1", "f2", "f0"):
        gather_done(n)
    arrived([h_swap])

    def feed_weight(t, kind):
        cols = [256 * j + 128 * kind for j in range(3)]
        blocks = [b["wf"][2 * t + i, :, :, :, c : c + 128].reshape(D, 128) for i in range(2) for c in cols]
        return jnp.concatenate(blocks, 1)

    def up_weight(t):
        return feed_weight(t, 0)

    def down_weight(t):
        return feed_weight(t, 1)

    def activate(units):
        erf = 0.5 * (1.0 + lax.erf(units * INV_ROOT_TWO))
        return (units * erf).astype(BF16), erf

    early = pltpu.make_async_remote_copy(
        src_ref=b["es"],
        dst_ref=b["er"],
        send_sem=xsem.at[6, 3],
        recv_sem=xsem.at[6, 4],
        device_id=sibling,
        device_id_type=MESH,
    )
    row16 = lax.broadcasted_iota(jnp.int32, (16, D), 0)

    @pl.when(seg == 0)
    def _():
        rows = b["h1b"][OWN + 256 : OWN + 272]
        part = sum(dot(activate(dot(rows, up_weight(t)))[0], down_weight(t), NT) for t in range(2))

        @pl.when(core == 0)
        def _():
            b["es"][...] = part
            early.start()

        @pl.when(core == 1)
        def _():
            early.wait_recv()
            whole = b["h1"][256:272] + part + b["er"][...]
            written = norm_forward(whole, gains[1], biases[1])[0]
            b["hop"][...] = jnp.where(row16 % 8 < 5, written, 0.0).astype(BF16)
            hops[0].start()
            hops[1].start()

    for t in range(2):
        units = dot(b["h1b"][...], up_weight(t))
        active, erf = activate(units)
        b["gl"][t] = active
        b["sl"][t] = (erf + units * jnp.exp(-0.5 * units * units) * INV_ROOT_TWOPI).astype(BF16)

    def partial_down(rows):
        return sum(dot(b["gl"][t, rows], down_weight(t), NT) for t in range(2))

    b["fs"][...] = partial_down(other_rows).astype(BF16)
    f_swap = remote(b["fs"], b["fr"], sibling)
    branch = partial_down(own_rows)
    arrived([f_swap])
    out, n2, inv2 = norm_forward(b["h1"][...] + branch + b["fr"][...].astype(F32), gains[1], biases[1])
    low = out.astype(BF16)
    b["yb"][...] = low
    b["mo"][...] = low[256:272].astype(F32).reshape(2, 8, D)
    for i in range(TP):
        to_device(
            b["yb"].at[pl.ds(TOKENS * i, TOKENS)],
            hout.at[seg, pl.ds(pl.multiple_of(TOKENS * core, 16), TOKENS)],
            (i, chain),
            xsem.at[3, 2 * seg + core],
            3,
            i,
        )
    for i in range(2):
        to_device(b["mo"].at[i], mout.at[seg], (2 * core + i, chain), xsem.at[4, seg], 4, i)

    for i in range(TP):
        from_device(b["gyt"].at[pl.ds(TOKENS * i, TOKENS)], 1, i)
    for i in range(2):
        from_device(b["gm"].at[i], 2, i)
    upstream = jnp.concatenate([b["gyt"][...].astype(F32), b["gm"][...].reshape(16, D)], 0)
    b["sg"][...] = jnp.zeros((48, D), F32)
    b["sg"][1:2] = column_sum(upstream * n2)
    b["sg"][3:4] = column_sum(upstream)
    dz = norm_backward(upstream, n2, inv2, gains[1])
    b["dz"][...] = dz
    b["dfb"][own_rows] = dz.astype(BF16)
    df_swap = remote(b["dfb"].at[own_rows], b["dfb"].at[own_rows], sibling)
    arrived([df_swap])

    def weight_grad(name, left, right):
        for t in range(2):
            part = dot(left, b[right][t], TN).astype(BF16)
            for i in range(2):
                b[name][2 * t + i] = part[:, HALF * i : HALF * (i + 1)].reshape(nz, ny, br, HALF)

    def pick(axes, axis, place):
        return tuple(place if a == axis else slice(None) for a in axes)

    scatters = {j[0]: j for j in scatter_jobs()}
    rs = {}

    def scatter_send(name, step):
        _, order, cols, axes = scatters[name]
        axis = order[step]
        left = [a for a in axes if a not in order[:step]]
        if step == 0:
            source = b[GRADS[name[0]]]
            tail = (slice(None), cols)
        else:
            source = b[f"s{step - 1}_{name}"]
            tail = ()
        copies = []
        for o in range(1, size[axis]):
            there = (at[axis] + o) % size[axis]
            copies.append(
                remote(source.at[pick(left, axis, there) + tail], b[f"r{step}_{name}"].at[o - 1], moved(axis, o))
            )
        rs[name] = copies

    def scatter_sum(name, step):
        _, order, cols, axes = scatters[name]
        axis = order[step]
        left = [a for a in axes if a not in order[:step]]
        arrived(rs[name])
        if step == 0:
            mine = b[GRADS[name[0]]][pick(left, axis, at[axis]) + (slice(None), cols)]
        else:
            mine = b[f"s{step - 1}_{name}"][pick(left, axis, at[axis])]
        total = mine.astype(F32)
        for o in range(1, size[axis]):
            total = total + b[f"r{step}_{name}"][o - 1].astype(F32)
        if step < len(order) - 1:
            b[f"s{step}_{name}"][...] = total.astype(BF16)
        return total

    def scatter_on(names, step):
        for n in names:
            scatter_sum(n, step)
            scatter_send(n, step + 1)

    down_names, up_names = ("t0", "t1", "t2"), ("i0", "i1", "i2")
    weight_grad("gt", b["dfb"][...], "gl")
    for n in down_names:
        scatter_send(n, 0)
    for t in range(2):
        b["du"][t] = (dot(b["dfb"][...], down_weight(t)) * b["sl"][t].astype(F32)).astype(BF16)

    def partial_up(rows):
        return sum(dot(b["du"][t, rows], up_weight(t), NT) for t in range(2))

    b["dhs"][...] = partial_up(other_rows).astype(BF16)
    dh_swap = remote(b["dhs"], b["dhr"], sibling)
    b["dz"][...] = b["dz"][...] + partial_up(own_rows)
    weight_grad("gi", b["h1b"][...], "du")
    for n in up_names:
        scatter_send(n, 0)
    arrived([dh_swap])
    into_first = b["dz"][...] + b["dhr"][...].astype(F32)
    b["sg"][0:1] = column_sum(into_first * b["n1"][...])
    b["sg"][2:3] = column_sum(into_first)
    dr = norm_backward(into_first, b["n1"][...], b["inv1"][...], gains[0])
    b["dr"][...] = dr
    b["dab"][own_rows] = dr.astype(BF16)
    da_swap = remote(b["dab"].at[own_rows], b["dab"].at[own_rows], sibling)
    arrived([da_swap])

    def head_rows(ref, c):
        if nz > 1:
            return ref.at[pl.ds(c * (nz // 2), nz // 2)]
        return ref.at[:, :, pl.ds(pl.multiple_of(c * HALF, 16), HALF)]

    grad_mixed = 0.0
    for h in range(2):
        w = head_rows(b["wo"].at[h], core)[...].reshape(HALF, HALF)
        grad_mixed = grad_mixed + dot(b["dab"][:, HALF * h : HALF * (h + 1)], w, NT)
    for p in range(3):
        b["doc"][p] = grad_mixed[:, 128 * p : 128 * p + 128].astype(BF16)

    mixed_t = b["ot"][...].reshape(HALF, ROWS)

    def proj_grad(h):
        cols = pl.ds(pl.multiple_of(HALF * h, 128), HALF)
        return dot(mixed_t, b["dab"][:, cols]).astype(BF16).reshape(b["gos"].shape)

    def wo_part(c):
        return head_rows(b["ga"].at[:, :, :, wo_cols], c)

    b["gos"][...] = proj_grad(other)
    go_swap = remote(b["gos"], wo_part(core), sibling)
    wo_part(core)[...] = proj_grad(core)

    def backward_pair(p):
        qp, kp, vp = (b["qkv"][3 * p + i] for i in range(3))
        dop = b["doc"][p]
        kt = kp.T
        dv = dk = 0.0
        dq = []
        for hh in range(2):
            inside, _, _ = head_masks(hh)
            zero = jnp.zeros_like(kp)
            grad_probs = dot(jnp.where(inside, vp, zero), dop, NT)
            low_probs = b["pt"][2 * p + hh]
            probs = low_probs.astype(F32)
            row_term = jnp.sum(probs * grad_probs, 0, keepdims=True)
            ds = (probs * (grad_probs - row_term)).astype(BF16)
            dv = dv + dot(low_probs, jnp.where(inside, dop, zero))
            dk = dk + dot(ds, jnp.where(inside, qp, zero))
            dq.append(dot(kt[64 * hh : 64 * hh + 64], ds))
        b["dqkv"][3 * p] = (jnp.concatenate(dq, 0) * 0.125).T.astype(BF16)
        b["dqkv"][3 * p + 1] = (dk * 0.125).astype(BF16)
        b["dqkv"][3 * p + 2] = dv.astype(BF16)

    def joined(rows, wanted):
        return jnp.concatenate([b["dqkv"][i, rows] for i in wanted], 1)

    def attention_grad(p):
        rows = b["xp" if p == 0 else "x"][...]
        part = dot(rows, joined(slice(None), range(3 * p, 3 * p + 3)), TN).astype(BF16)
        if p == 0:
            b["gx"][...] = part.reshape(TP, nz, sh.xrows, HALF)
        else:
            b["ga"][:, :, :, HALF * p : HALF * (p + 1)] = part.reshape(nz, ny, br, HALF)

    backward_pair(0)
    attention_grad(0)
    arrived([go_swap])
    scatter_send("aw", 0)
    scatter_send("x0", 0)
    scatter_on(down_names, 0)
    backward_pair(1)
    attention_grad(1)
    scatter_send("a1", 0)
    scatter_on(up_names, 0)
    backward_pair(2)
    attention_grad(2)
    scatter_send("a2", 0)
    scatter_send("a3", 0)

    def partial_input(rows):
        return dot(joined(rows, range(9)), attention_weight(), NT)

    b["dxs"][...] = partial_input(other_rows).astype(BF16)
    dx_swap = remote(b["dxs"], b["dxr"], sibling)
    dx = partial_input(own_rows) + b["dr"][...]
    arrived([dx_swap])
    dx = dx + b["dxr"][...].astype(F32)
    b["dxb"][...] = dx[:256].astype(BF16)
    for i in range(TP):
        to_device(
            b["dxb"].at[pl.ds(TOKENS * i, TOKENS)],
            dxo.at[seg, pl.ds(pl.multiple_of(TOKENS * core, 16), TOKENS)],
            (i, chain),
            xsem.at[5, 2 * seg + core],
            5,
            i,
        )

    @pl.when((core == 0) & (seg == 0))
    def _():
        b["sg"][16:32] = dx[256:272]

    @pl.when(core == 1)
    def _():
        b["sg"][32:48] = dx[256:272]

    small_grads = dot(b["sg"][...].astype(BF16), smallsel[...], TN).astype(BF16)
    b["ga"][:, :, :, 4 * HALF :] = small_grads.reshape(nz, ny, br, SMALL)
    scatter_send("as", 0)
    attention_names = ("aw", "x0", "a1", "a2", "a3", "as")
    scatter_on(down_names, 1)
    scatter_on(attention_names, 0)
    scatter_on(up_names, 1)

    def last_rows(names, first_col):
        for j, n in enumerate(names):
            total = scatter_sum(n, 2)
            cols = slice(first_col + 128 * j, first_col + 128 * j + 128)
            b["sf"][0, :, cols] = total[:wr]
            b["sf"][1, :, cols] = total[wr:]

    for n in attention_names:
        cols = scatters[n][2]
        total = scatter_sum(n, 1).astype(BF16)
        if n == "x0":
            spread = dot(packy[...], total, TN).astype(BF16)
            b["e3y"][...] = spread.reshape(ny, 2 * sh.pc, HALF)
            ysteps = [remote(b["e3y"].at[(y + o) % ny], b["r3y"].at[o - 1], moved("y", o)) for o in range(1, ny)]
        else:
            spread = dot(packsel[...], total, TN).astype(BF16)
            b["e3"][:, :, cols.start - HALF : cols.stop - HALF] = spread.reshape(TP, 2 * sh.pc, cols.stop - cols.start)
    steps = [remote(b["e3"].at[(x + o) % TP], b["r3"].at[o - 1], moved("x", o)) for o in range(1, TP)]
    last_rows(down_names, HALF)
    last_rows(up_names, 0)
    sf_local = local(b["sf"].at[core], gfo.at[core])
    sf_swap = remote(b["sf"].at[other], gfo.at[core], sibling)

    arrived(steps)
    total = b["e3"][x].astype(F32)
    for o in range(1, TP):
        total = total + b["r3"][o - 1].astype(F32)
    b["s4"][:, :, HALF:] = total.reshape(2, sh.pc, REST)
    arrived(ysteps)
    total = b["e3y"][y].astype(F32)
    for o in range(1, ny):
        total = total + b["r3y"][o - 1].astype(F32)
    b["s4"][:, :, :HALF] = total.reshape(2, sh.pc, HALF)
    s4_local = local(b["s4"].at[core], gao.at[core])
    s4_swap = remote(b["s4"].at[other], gao.at[core], sibling)

    for kind, out_ref in ((3, hout), (5, dxo)):
        for s in range(2):
            for j in range(2):
                from_device(out_ref.at[s, pl.ds(TOKENS * j, TOKENS)], kind, 2 * s + j)
    for s in range(2):
        from_device(mout.at[s], 4, s)
    sf_local.wait()
    s4_local.wait()
    arrived([sf_swap, s4_swap])

    for copy in sent:
        copy.wait_send()
    for same, copy in conditional:

        @pl.when(jnp.logical_not(same))
        def _():
            copy.wait_send()

    @pl.when((seg == 0) & (core == 1))
    def _():
        hops[0].wait_send()
        hops[1].wait_send()

    @pl.when((seg == 0) & (core == 0))
    def _():
        early.wait_send()


def layer(sh, arrays):
    constants = [jnp.asarray(a, BF16) for a in selections(sh)]
    table = scratch_of(sh)
    names = list(table)
    vmem = pl.BlockSpec(memory_space=pltpu.VMEM)
    outs = [
        jax.ShapeDtypeStruct((2, 128, D), BF16),
        jax.ShapeDtypeStruct((2, 8, D), F32),
        jax.ShapeDtypeStruct((2, 128, D), BF16),
        jax.ShapeDtypeStruct((2, sh.pc, ACOLS), F32),
        jax.ShapeDtypeStruct((2, sh.wrows, D), F32),
    ]
    return pl.pallas_call(
        functools.partial(kernel, sh, names),
        name="layer",
        out_shape=outs,
        in_specs=[pl.BlockSpec(memory_space=pl.ANY)] * 2 + [vmem] * 12 + [pl.BlockSpec(memory_space=pl.ANY)],
        out_specs=[pl.BlockSpec(memory_space=pl.ANY), vmem] * 2 + [vmem],
        scratch_shapes=[pltpu.VMEM(*table[n]) for n in names]
        + [
            pltpu.SemaphoreType.DMA((200,)),
            pltpu.SemaphoreType.DMA((200,)),
            pltpu.SemaphoreType.DMA((7, 12)),
            pltpu.SemaphoreType.DMA((8,)),
        ],
        compiler_params=pltpu.CompilerParams(
            collective_id=0, has_side_effects=True, vmem_limit_bytes=64 * 2**20 - 2**17
        ),
    )(*arrays, *constants)


def unpack_kernel(sh, hout, mout, dxo, gao, gfo, *outs):
    hidden, memory, grad_in, gq, gp, gains, biases, tokens, gi, gt = outs
    ar = sh.arows
    hidden[...] = hout[...]
    for i in range(2):
        memory[:, i] = mout[i, :5].astype(BF16)
    grad_in[...] = dxo[...].astype(F32)
    for h in range(2):
        for p in range(3):
            for i in range(3):
                to = D * i + HALF * h + 128 * p
                first = HALF * p + 128 * i
                gq[:, to : to + 128] = gao[h, :ar, first : first + 128]
        gp[:, HALF * h : HALF * (h + 1)] = gao[h, :ar, WO : WO + HALF]
        gi[:, HALF * h : HALF * (h + 1)] = gfo[h, :, :HALF]
        gt[:, HALF * h : HALF * (h + 1)] = gfo[h, :, HALF:]
    small = gao[0, :, 4 * HALF :] + gao[1, :, 4 * HALF :]
    turned = small.T[:, :ar]
    gains[...] = turned[0:2]
    biases[...] = turned[2:4]
    for kind in range(2):
        tokens[:, kind] = small[:ar, 4 + MEM * kind : 4 + MEM * (kind + 1)]


def unpack(sh, *arrays):
    ar, wr = sh.arows, sh.wrows
    shapes = [
        ((2, 128, D), BF16),
        ((5, 2, D), BF16),
        ((2, 128, D), F32),
        ((ar, 3 * D), F32),
        ((ar, D), F32),
        ((2, ar), F32),
        ((2, ar), F32),
        ((ar, 2, MEM), F32),
        ((wr, D), F32),
        ((wr, D), F32),
    ]
    vmem = pl.BlockSpec(memory_space=pltpu.VMEM)
    return pl.pallas_call(
        functools.partial(unpack_kernel, sh),
        name="unpack",
        out_shape=[jax.ShapeDtypeStruct(*one) for one in shapes],
        in_specs=[vmem] * 5,
        out_specs=[vmem] * len(shapes),
        compiler_params=pltpu.CompilerParams(vmem_limit_bytes=64 * 2**20 - 2**17),
    )(*arrays)


def body(
    sh,
    hidden_in,
    reset,
    w_qkv,
    w_attn_out,
    norm_gains,
    norm_biases,
    memory_tokens,
    w_in,
    w_out,
    grad_hidden,
    grad_memory,
):
    arrays = (
        hidden_in,
        grad_hidden,
        grad_memory.transpose(1, 0, 2),
        w_qkv,
        w_attn_out,
        norm_gains,
        norm_biases,
        memory_tokens.transpose(2, 0, 1),
        w_in,
        w_out.T,
    )
    hidden, memory, *middle, tokens, gi, gt = unpack(sh, *layer(sh, arrays))
    return hidden, memory.transpose(1, 0, 2), *middle, tokens.transpose(1, 2, 0), gi, gt.T


def solution(mesh):
    sh = Shape(mesh.shape["dp"])
    return jax.shard_map(
        functools.partial(body, sh),
        mesh=mesh,
        in_specs=(
            P("dp", "tp", None),
            P("dp"),
            P(("dp", "tp"), None),
            P(("dp", "tp"), None),
            P(None, ("dp", "tp")),
            P(None, ("dp", "tp")),
            P(None, None, ("dp", "tp")),
            P("dp", "tp"),
            P("tp", "dp"),
            P("dp", "tp", None),
            P("dp", "tp", None),
        ),
        out_specs=(
            P("dp", "tp", None),
            P("dp", "tp", None),
            P("dp", "tp", None),
            P(("dp", "tp"), None),
            P(("dp", "tp"), None),
            P(None, ("dp", "tp")),
            P(None, ("dp", "tp")),
            P(None, None, ("dp", "tp")),
            P("dp", "tp"),
            P("tp", "dp"),
        ),
        check_vma=False,
    )
```

```python
import functools

import jax
import jax.numpy as jnp
import numpy as np
from jax import lax
from jax.experimental import pallas as pl
from jax.experimental.pallas import tpu as pltpu
from jax.sharding import PartitionSpec as P

D = 768
HALF = 384
MEM = 10
TOKENS = 64
OWN = 272
ROWS = 2 * OWN
TP = 4
SMALL = 128
ACOLS = 4 * HALF + SMALL
REST = ACOLS - HALF
CUT = HALF + 640
WO = 3 * HALF
EPSILON = 1e-05
INV_ROOT_TWO = 0.7071067811865476
INV_ROOT_TWOPI = 0.3989422804014327
EXP_SCALE = 0.125 * 1.4426950408889634
MASKED = -1e30
F32 = jnp.float32
BF16 = jnp.bfloat16
MESH = pl.DeviceIdType.MESH
NN = (((1,), (0,)), ((), ()))
NT = (((1,), (1,)), ((), ()))
TN = (((0,), (0,)), ((), ()))


def dot(a, b, dims=NN):
    return lax.dot_general(a, b, dims, preferred_element_type=F32)


def up16(n):
    return -(-n // 16) * 16


class Shape:
    def __init__(self, dp):
        self.dp = dp
        planes = dp // 2
        self.ny = int(round(planes**0.5))
        self.nz = planes // self.ny
        self.wrows = D // dp
        self.arows = D // (dp * TP)
        self.brows = 2 * self.wrows
        self.pr = up16(self.arows)
        self.xrows = 2 * self.arows * self.ny
        self.pc = -(-self.arows // 8) * 8
        self.fr = up16(self.wrows)


def selections(sh):
    pack = np.zeros((sh.brows, TP * 2 * sh.pc), np.float32)
    for c in range(2):
        for x in range(TP):
            for i in range(sh.arows):
                pack[c * sh.wrows + x * sh.arows + i, (x * 2 + c) * sh.pc + i] = 1
    packy = np.zeros((sh.xrows, sh.ny * 2 * sh.pc), np.float32)
    turn = np.zeros((D, D), np.float32)
    ar = sh.arows
    for c in range(2):
        for y in range(sh.ny):
            for i in range(ar):
                row = (y * 2 + c) * ar + i
                packy[row, (y * 2 + c) * sh.pc + i] = 1
                for x in range(TP):
                    for z in range(sh.nz):
                        place = (z * sh.ny + y) * sh.brows + (c * TP + x) * ar + i
                        turn[(x * sh.nz + z) * sh.xrows + row, place] = 1
    small = np.zeros((48, SMALL), np.float32)
    for i in range(4):
        small[i, i] = 1
    for kind in range(2):
        for i in range(MEM):
            small[16 + 16 * kind + (i // 5) * 8 + i % 5, 4 + MEM * kind + i] = 1
    places = np.zeros((4, MEM, SMALL), np.float32)
    for kind, (rows, first) in enumerate(((2, 0), (2, 2), (MEM, 4), (MEM, 4 + MEM))):
        for i in range(rows):
            places[kind, i, first + i] = 1
    return pack, small, places, packy, turn


def norm_forward(inputs, gain, offset):
    centred = inputs - jnp.mean(inputs, -1, keepdims=True)
    spread = jnp.mean(centred * centred, -1, keepdims=True)
    inverse = lax.rsqrt(spread + EPSILON)
    normed = centred * inverse
    return normed * gain + offset, normed, inverse


def norm_backward(upstream, normed, inverse, gain):
    scaled = upstream * gain
    first_mean = jnp.mean(scaled, -1, keepdims=True)
    second_mean = jnp.mean(scaled * normed, -1, keepdims=True)
    return inverse * (scaled - first_mean - normed * second_mean)


def column_sum(a):
    return jnp.sum(a, 0, keepdims=True)


SCRATCH = {}


def scratch_of(sh):
    nz, ny, br = sh.nz, sh.ny, sh.brows
    ar, wr = sh.arows, sh.wrows
    operands = [
        (5, 2, D),
        (ar, 3 * D),
        (ar, D),
        (2, ar),
        (2, ar),
        (ar, 2, MEM),
        (wr, D),
        (wr, D),
        (br, TP * 2 * sh.pc),
        (48, SMALL),
        (4, MEM, SMALL),
        (sh.xrows, ny * 2 * sh.pc),
    ]
    s = {f"in{i}": (dims, BF16) for i, dims in enumerate(operands)}
    s |= {
        "pk": ((2, sh.pr, ACOLS), BF16),
        "ff": ((2, sh.fr, D), BF16),
        "gms": ((2, 8, D), F32),
        "p1": ((2, sh.pr, ACOLS), BF16),
        "p2": ((TP, 2 * sh.pc, REST), BF16),
        "p2y": ((ny, 2 * sh.pc, HALF), BF16),
        "turn": ((D, D), BF16),
        "xp": ((ROWS, D), BF16),
        "wx": ((TP, nz, sh.xrows, HALF), BF16),
        "gx": ((TP, nz, sh.xrows, HALF), BF16),
        "f1": ((2, sh.fr, D), BF16),
        "wa": ((nz, ny, br, ACOLS), BF16),
        "wf": ((TP, nz, ny, br, D), BF16),
        "wo": ((2, nz, ny, br, HALF), BF16),
        "par": ((8, D), F32),
        "x": ((ROWS, D), BF16),
        "gyt": ((TP * TOKENS, D), BF16),
        "gm": ((2, 8, D), F32),
        "qkv": ((9, ROWS, 128), BF16),
        "pt": ((6, ROWS, ROWS), BF16),
        "ot": ((3, 128, ROWS), BF16),
        "oc": ((ROWS, HALF), BF16),
        "oown": ((2, OWN, HALF), BF16),
        "h1": ((OWN, D), F32),
        "n1": ((OWN, D), F32),
        "inv1": ((OWN, 1), F32),
        "h1b": ((ROWS, D), BF16),
        "gl": ((2, ROWS, D), BF16),
        "sl": ((2, ROWS, D), BF16),
        "fs": ((OWN, D), BF16),
        "fr": ((OWN, D), BF16),
        "n2": ((OWN, D), F32),
        "yb": ((OWN, D), BF16),
        "mo": ((2, 8, D), F32),
        "hop": ((16, D), BF16),
        "hopin": ((16, D), BF16),
        "es": ((16, D), F32),
        "er": ((16, D), F32),
        "dz": ((OWN, D), F32),
        "dfb": ((ROWS, D), BF16),
        "du": ((2, ROWS, D), BF16),
        "dhs": ((OWN, D), BF16),
        "dhr": ((OWN, D), BF16),
        "dr": ((OWN, D), F32),
        "dab": ((ROWS, D), BF16),
        "doc": ((3, ROWS, 128), BF16),
        "dqkv": ((9, ROWS, 128), BF16),
        "ga": ((nz, ny, br, ACOLS), BF16),
        "gi": ((TP, nz, ny, br, HALF), BF16),
        "gt": ((TP, nz, ny, br, HALF), BF16),
        "gos": ((D // 2 // br if nz > 1 else 1, br if nz > 1 else HALF, HALF), BF16),
        "dxs": ((OWN, D), BF16),
        "dxr": ((OWN, D), BF16),
        "dxb": ((TP * TOKENS, D), BF16),
        "sg": ((48, D), F32),
        "e3": ((TP, 2 * sh.pc, REST), BF16),
        "r3": ((TP - 1, 2 * sh.pc, REST), BF16),
        "e3y": ((ny, 2 * sh.pc, HALF), BF16),
        "r3y": ((max(1, ny - 1), 2 * sh.pc, HALF), BF16),
        "s4": ((2, sh.pc, ACOLS), F32),
        "sf": ((2, sh.wrows, D), F32),
    }
    if nz > 1:
        s["gos"] = ((nz // 2, ny, br, HALF), BF16)
    else:
        s["gos"] = ((1, 1, HALF, HALF), BF16)
    sizes = {"x": TP, "z": nz, "y": ny}
    for name, order, cols, axes in scatter_jobs():
        left = [a for a in axes]
        block = (sh.xrows if name[0] == "x" else br, cols.stop - cols.start)
        for step, axis in enumerate(order):
            left = [a for a in left if a != axis]
            dims = tuple(sizes[a] for a in left)
            s[f"r{step}_{name}"] = ((max(1, sizes[axis] - 1),) + dims + block, BF16)
            if step < len(order) - 1:
                s[f"s{step}_{name}"] = (dims + block, BF16)
            if step == 0 and name in RINGS and sizes[axis] == 4:
                s[f"q_{name}"] = ((2, dims[0] // 2) + dims[1:] + block, BF16)
                s[f"u_{name}"] = s[f"q_{name}"]
    return s


def scatter_jobs():
    orders = [("z", "y", "x"), ("x", "z", "y"), ("y", "x", "z")]
    jobs = []
    for kind in ("t", "i"):
        for j in range(3):
            jobs.append((f"{kind}{j}", orders[j], slice(128 * j, 128 * j + 128), ("x", "z", "y")))
    zy, yz = ("z", "y"), ("y", "z")
    jobs.append(("aw", yz, slice(WO, WO + HALF), zy))
    jobs.append(("x0", ("x", "z"), slice(0, HALF), ("x", "z")))
    jobs.append(("a1", zy, slice(HALF, 2 * HALF), zy))
    jobs.append(("a2", yz, slice(2 * HALF, 2 * HALF + 256), zy))
    jobs.append(("a3", zy, slice(2 * HALF + 256, 3 * HALF), zy))
    jobs.append(("as", zy, slice(4 * HALF, ACOLS), zy))
    return jobs


def gather_jobs():
    orders = [("x", "y", "z"), ("y", "z", "x"), ("z", "x", "y")]
    jobs = [(f"f{j}", orders[j], slice(256 * j, 256 * j + 256), ("x", "z", "y")) for j in range(3)]
    jobs.append(("x0", ("z", "x"), slice(0, HALF), ("x", "z")))
    jobs.append(("a0", ("y", "z"), slice(HALF, CUT), ("z", "y")))
    jobs.append(("a1", ("z", "y"), slice(CUT, ACOLS), ("z", "y")))
    return jobs


RINGS = ("t0", "t1", "t2", "i0", "i1", "i2", "aw", "x0", "a1")
WEIGHTS = {"f": "wf", "a": "wa", "x": "wx"}
GRADS = {"t": "gt", "i": "gi", "a": "ga", "x": "gx"}


def kernel(sh, names, *refs):
    xin, gin = refs[:2]
    hout, mout, dxo, gao, gfo = refs[15:20]
    b = dict(zip(names, refs[20 : 20 + len(names)]))
    ssem, rsem, xsem, lsem = refs[20 + len(names) :]
    staged = [b[f"in{i}"] for i in range(12)]
    gmem, wq, wp, gain_in, bias_in, token_in, up_in, down_in = staged[:8]
    packsel, smallsel, places, packy = staged[8:]
    turn = refs[14]
    nz, ny, br, wr, ar = sh.nz, sh.ny, sh.brows, sh.wrows, sh.arows
    pk, ff, gms = b["pk"], b["ff"], b["gms"]

    dp = lax.axis_index("dp")
    x = lax.axis_index("tp")
    core = dp % 2
    y = (dp // 2) % ny
    z = dp // (2 * ny)
    other = 1 - core
    chain = x // 2
    seg = jnp.where((x == 1) | (x == 2), 1, 0)
    at = {"x": x, "y": y, "z": z}
    size = {"x": TP, "y": ny, "z": nz}

    def device(x_=x, y_=y, z_=z, c_=core):
        return ((z_ * ny + y_) * 2 + c_, x_)

    def moved(axis, offset, core_=core):
        there = dict(at)
        there[axis] = (at[axis] + offset) % size[axis]
        return device(there["x"], there["y"], there["z"], core_)

    sibling = device(c_=other)
    counts = {"s": 0, "r": 0}
    sent = []

    def remote(src, dst, to):
        copy = pltpu.make_async_remote_copy(
            src_ref=src,
            dst_ref=dst,
            send_sem=ssem.at[counts["s"]],
            recv_sem=rsem.at[counts["r"]],
            device_id=to,
            device_id_type=MESH,
        )
        counts["s"] += 1
        counts["r"] += 1
        copy.start()
        sent.append(copy)
        return copy

    def arrived(copies):
        for copy in copies:
            copy.wait_recv()

    locals_ = [0]

    def local(src, dst):
        copy = pltpu.make_async_copy(src, dst, lsem.at[locals_[0]])
        locals_[0] += 1
        copy.start()
        return copy

    staging = [local(refs[2 + i], staged[i]) for i in range(12)]
    turn_local = local(turn, b["turn"])

    barrier = pltpu.get_barrier_semaphore()
    peers = [sibling]
    for o in range(1, TP):
        peers += [moved("x", o), moved("x", o, other)]
    for axis in ("y", "z"):
        for o in range(1, size[axis]):
            peers.append(moved(axis, o))
    for peer in peers:
        pl.semaphore_signal(barrier, inc=1, device_id=peer, device_id_type=MESH)

    pk[...] = jnp.zeros(pk.shape, BF16)
    ff[...] = jnp.zeros(ff.shape, BF16)
    gms[...] = jnp.zeros(gms.shape, F32)
    for copy in staging:
        copy.wait()
    small = dot(gain_in[...], places[0, :2], TN) + dot(bias_in[...], places[1, :2], TN)
    small = small + dot(token_in[:, 0], places[2]) + dot(token_in[:, 1], places[3])
    small = small.astype(BF16)
    for h in range(2):
        for p in range(3):
            for i in range(3):
                first = D * i + HALF * h + 128 * p
                pk[h, :ar, HALF * p + 128 * i : HALF * p + 128 * (i + 1)] = wq[:, first : first + 128]
        pk[h, :ar, WO : WO + HALF] = wp[:, HALF * h : HALF * (h + 1)]
        pk[h, :ar, 4 * HALF :] = small
        for j in range(3):
            cols = slice(HALF * h + 128 * j, HALF * h + 128 * (j + 1))
            ff[h, :wr, 256 * j : 256 * j + 128] = up_in[:, cols]
            ff[h, :wr, 256 * j + 128 : 256 * j + 256] = down_in[:, cols]
        gms[h, 0:5] = gmem[:, h].astype(F32)
    pl.semaphore_wait(barrier, len(peers))

    pk_local = local(pk.at[core], b["p1"].at[core])
    ff_local = local(ff.at[core], b["f1"].at[core])
    pk_swap = remote(pk.at[other], b["p1"].at[core], sibling)
    ff_swap = remote(ff.at[other], b["f1"].at[core], sibling)

    conditional = []

    def to_device(src, dst, place, here, kind, send_slot):
        copy = pltpu.make_async_remote_copy(
            src_ref=src,
            dst_ref=dst,
            send_sem=xsem.at[kind, 8 + send_slot],
            recv_sem=here,
            device_id=device(x_=place[0], c_=place[1]),
            device_id_type=MESH,
        )
        same = (place[0] == x) & (place[1] == core)

        @pl.when(same)
        def _():
            pltpu.make_async_copy(src, dst, here).start()

        @pl.when(jnp.logical_not(same))
        def _():
            copy.start()

        conditional.append((same, copy))

    def from_device(dst, kind, slot):
        pltpu.make_async_copy(dst, dst, xsem.at[kind, slot]).wait()

    def chip_of(k, s):
        return s + k * (3 - 2 * s)

    def send_rows():
        for s in range(2):
            for j in range(2):
                to_device(
                    xin.at[s, pl.ds(TOKENS * j, TOKENS)],
                    b["x"].at[pl.ds(pl.multiple_of(OWN * j + TOKENS * x, 16), TOKENS)],
                    (chip_of(core, s), j),
                    xsem.at[0, x],
                    0,
                    2 * s + j,
                )

    def send_upstream():
        for s in range(2):
            for j in range(2):
                to_device(
                    gin.at[s, pl.ds(TOKENS * j, TOKENS)],
                    b["gyt"].at[pl.ds(pl.multiple_of(TOKENS * x, 16), TOKENS)],
                    (chip_of(core, s), j),
                    xsem.at[1, x],
                    1,
                    2 * s + j,
                )
            to_device(
                gms.at[s], b["gm"].at[x % 2], (chip_of(core, s), x // 2), xsem.at[2, x % 2], 2, s
            )

    def part_of(job, step, place, half=None):
        name, order, cols, axes = job
        fixed = {a: at[a] for a in order[step:]}
        fixed[order[step]] = place
        where = []
        for a in axes:
            if a in fixed:
                where.append(fixed[a])
            elif half is not None:
                where.append(pl.ds(half * (size[a] // 2), size[a] // 2))
                half = None
            else:
                where.append(slice(None))
        return b[WEIGHTS[name[0]]].at[tuple(where) + (slice(None), cols)]

    def gather_start(name, step):
        job = gathers[name]
        axis = job[1][step]
        n = size[axis]
        own = part_of(job, step, at[axis])
        free = [a for a in job[3] if a not in job[1][step:]]
        relay = n == 4 and step == len(job[1]) - 1 and size[free[0]] % 2 == 0
        state = {"step": step, "relay": relay}
        if relay:
            first = [part_of(job, step, at[axis], h) for h in range(2)]
            right, left = moved(axis, 1), moved(axis, n - 1)
            state["right"] = remote(first[0], first[0], right)
            state["left"] = remote(first[1], first[1], left)
            state["all"] = [remote(first[1], first[1], right), remote(first[0], first[0], left)]
        else:
            state["all"] = [remote(own, own, moved(axis, o)) for o in range(1, n)]
        flying[name] = state

    def gather_pass(name):
        job, state = gathers[name], flying[name]
        if not state["relay"]:
            return
        axis = job[1][state["step"]]
        n = size[axis]
        for kind, back, onward, half in (("right", n - 1, 1, 0), ("left", 1, n - 1, 1)):
            arrived([state[kind]])
            piece = part_of(job, state["step"], (at[axis] + back) % n, half)
            state["all"].append(remote(piece, piece, moved(axis, onward)))

    def gather_done(name):
        arrived(flying[name]["all"])

    gathers = {j[0]: j for j in gather_jobs()}
    flying = {}

    pk_local.wait()
    arrived([pk_swap])
    packed = jnp.concatenate([b["p1"][c].astype(F32)[: sh.pc] for c in range(2)], 0).astype(BF16)
    b["p2y"][y] = packed[:, :HALF]
    b["p2"][x] = packed[:, HALF:]
    mine = b["p2y"].at[y]
    ysteps = [remote(mine, mine, moved("y", o)) for o in range(1, ny)]
    mine = b["p2"].at[x]
    xsteps = [remote(mine, mine, moved("x", o)) for o in range(1, TP)]
    ff_local.wait()
    arrived([ff_swap])
    two = [b["f1"][c].astype(F32)[:wr] for c in range(2)]
    b["wf"][x, z, y] = jnp.concatenate(two, 0).astype(BF16)
    feed_names, first_names = ("f1", "f2", "f0"), ("x0", "a0", "a1")
    for n in feed_names:
        gather_start(n, 0)
    send_rows()
    arrived(ysteps)
    b["wx"][x, z] = dot(packy[...], b["p2y"][...].reshape(ny * 2 * sh.pc, HALF)).astype(BF16)
    gather_start("x0", 0)
    arrived(xsteps)
    b["wa"][z, y, :, HALF:] = dot(packsel[...], b["p2"][...].reshape(TP * 2 * sh.pc, REST)).astype(BF16)
    for n in ("a0", "a1"):
        gather_start(n, 0)
    for n in feed_names:
        gather_done(n)
        gather_start(n, 1)
    for n in first_names:
        gather_done(n)
        gather_start(n, 1)
    for n in first_names:
        gather_pass(n)
    for n in feed_names:
        gather_done(n)
        gather_start(n, 2)

    for i in range(TP):
        from_device(b["x"].at[pl.ds(pl.multiple_of(OWN * core + TOKENS * i, 16), TOKENS)], 0, i)
    half = b["x"].at[pl.ds(pl.multiple_of(OWN * core, 16), TP * TOKENS)]
    x_swap = remote(half, half, sibling)
    for first in (256, OWN + 256):
        b["x"][first : first + 16] = jnp.zeros((16, D), BF16)
    turn_local.wait()
    arrived([x_swap])
    b["xp"][...] = dot(b["x"][...], b["turn"][...], NT).astype(BF16)
    for n in first_names:
        gather_done(n)
    wo_cols = slice(WO, WO + HALF)
    wo_local = local(b["wa"].at[:, :, :, wo_cols], b["wo"].at[core])
    wo_swap = remote(b["wa"].at[:, :, :, wo_cols], b["wo"].at[core], sibling)
    gather_pass("f1")
    send_upstream()

    def attention_weight():
        return b["wa"][:, :, :, :WO].reshape(D, WO)

    small = b["wa"][:, :, :, 4 * HALF :].reshape(D, SMALL)
    chosen = dot(smallsel[...], small, NT)
    b["par"][...] = chosen[0:8]
    memory = chosen[16:48].astype(BF16)
    b["x"][OWN + 256 : OWN + 272] = memory[16:]
    turned = dot(memory, b["turn"][...], NT).astype(BF16)
    b["xp"][OWN + 256 : OWN + 272] = turned[16:]

    @pl.when(seg == 0)
    def _():
        b["x"][256:272] = memory[:16]
        b["xp"][256:272] = turned[:16]

    gains = [b["par"][i : i + 1] for i in range(2)]
    biases = [b["par"][2 + i : 3 + i] for i in range(2)]

    hop_to = jnp.where(x == 0, 1, 2)
    hops = []
    for j in range(2):
        hops.append(
            pltpu.make_async_remote_copy(
                src_ref=b["hop"],
                dst_ref=b["hopin"],
                send_sem=xsem.at[6, j],
                recv_sem=xsem.at[6, 2],
                device_id=device(x_=hop_to, c_=j),
                device_id_type=MESH,
            )
        )

    own_rows = pl.ds(pl.multiple_of(OWN * core, 16), OWN)
    other_rows = pl.ds(pl.multiple_of(OWN * other, 16), OWN)

    out = dot(b["xp"][...], b["wx"][...].reshape(D, HALF)).astype(BF16)
    for i in range(3):
        b["qkv"][i] = out[:, 128 * i : 128 * i + 128]
    out = dot(b["x"][...], b["wa"][:, :, :, HALF:WO].reshape(D, 2 * HALF)).astype(BF16)
    for i in range(3, 9):
        b["qkv"][i] = out[:, 128 * (i - 3) : 128 * (i - 2)]

    def head_masks(hh):
        lane = lax.broadcasted_iota(jnp.int32, (ROWS, 128), 1)
        row = lax.broadcasted_iota(jnp.int32, (ROWS, 128), 0)
        inside = (lane // 64) == hh
        spare = lane == 64 * (1 - hh)
        memory = ((row >= 256) & (row < 272)) | (row >= OWN + 256)
        invalid = memory & (row % 8 >= 5)
        return inside, spare, invalid

    def forward_pair(p):
        qp, kp, vp = (b["qkv"][3 * p + i] for i in range(3))
        vt = vp.T
        for hh in range(2):
            inside, spare, invalid = head_masks(hh)
            zero = jnp.zeros_like(kp)
            kmask = jnp.where(spare & invalid, jnp.full_like(kp, MASKED), zero)
            km = jnp.where(inside, kp, kmask)
            qm = jnp.where(inside, qp, jnp.where(spare, jnp.ones_like(qp), zero))
            scores = dot(km, qm, NT)
            peak = jnp.max(scores, 0, keepdims=True)
            raised = jnp.exp2((scores - peak) * EXP_SCALE)
            total = jnp.sum(raised, 0, keepdims=True)
            probs = (raised * (1.0 / total)).astype(BF16)
            b["pt"][2 * p + hh] = probs
            b["ot"][p, 64 * hh : 64 * hh + 64] = dot(vt[64 * hh : 64 * hh + 64], probs).astype(BF16)
        b["oc"][:, 128 * p : 128 * p + 128] = b["ot"][p].T

    @pl.when(seg == 0)
    def _():
        forward_pair(0)
        forward_pair(1)

    ordered = dot(b["turn"][...], b["wx"][...].reshape(D, HALF), TN).astype(BF16)
    b["wa"][:, :, :, :HALF] = ordered.reshape(nz, ny, br, HALF)
    for n in ("f2", "f0"):
        gather_pass(n)

    @pl.when(seg == 0)
    def _():
        forward_pair(2)

    @pl.when(seg == 1)
    def _():
        hops[0].wait_recv()
        b["x"][256:272] = b["hopin"][...]
        b["xp"][256:272] = dot(b["hopin"][...], b["turn"][...], NT).astype(BF16)
        rows = dot(b["hopin"][...], attention_weight()).astype(BF16)
        for i in range(9):
            b["qkv"][i, 256:272] = rows[:, 128 * i : 128 * i + 128]
        for p in range(3):
            forward_pair(p)

    o_local = local(b["oc"].at[own_rows], b["oown"].at[core])
    o_swap = remote(b["oc"].at[other_rows], b["oown"].at[core], sibling)
    wo_local.wait()
    arrived([wo_swap])
    o_local.wait()
    arrived([o_swap])
    halves = []
    for h in range(2):
        w = b["wo"][h].reshape(D, HALF)
        halves.append(dot(b["oown"][0], w[:HALF]) + dot(b["oown"][1], w[HALF:]))
    attended = jnp.concatenate(halves, 1)
    h1, n1, inv1 = norm_forward(b["x"][own_rows].astype(F32) + attended, gains[0], biases[0])
    b["h1"][...] = h1
    b["n1"][...] = n1
    b["inv1"][...] = inv1
    b["h1b"][own_rows] = h1.astype(BF16)
    h_swap = remote(b["h1b"].at[own_rows], b["h1b"].at[own_rows], sibling)
    for n in ("f1", "f2", "f0"):
        gather_done(n)
    arrived([h_swap])

    def feed_weight(t, kind):
        cols = [256 * j + 128 * kind for j in range(3)]
        blocks = [b["wf"][2 * t + i, :, :, :, c : c + 128].reshape(D, 128) for i in range(2) for c in cols]
        return jnp.concatenate(blocks, 1)

    def up_weight(t):
        return feed_weight(t, 0)

    def down_weight(t):
        return feed_weight(t, 1)

    def activate(units):
        erf = 0.5 * (1.0 + lax.erf(units * INV_ROOT_TWO))
        return (units * erf).astype(BF16), erf

    early = pltpu.make_async_remote_copy(
        src_ref=b["es"],
        dst_ref=b["er"],
        send_sem=xsem.at[6, 3],
        recv_sem=xsem.at[6, 4],
        device_id=sibling,
        device_id_type=MESH,
    )
    row16 = lax.broadcasted_iota(jnp.int32, (16, D), 0)

    @pl.when(seg == 0)
    def _():
        rows = b["h1b"][OWN + 256 : OWN + 272]
        part = sum(dot(activate(dot(rows, up_weight(t)))[0], down_weight(t), NT) for t in range(2))

        @pl.when(core == 0)
        def _():
            b["es"][...] = part
            early.start()

        @pl.when(core == 1)
        def _():
            early.wait_recv()
            whole = b["h1"][256:272] + part + b["er"][...]
            written = norm_forward(whole, gains[1], biases[1])[0]
            b["hop"][...] = jnp.where(row16 % 8 < 5, written, 0.0).astype(BF16)
            hops[0].start()
            hops[1].start()

    for t in range(2):
        units = dot(b["h1b"][...], up_weight(t))
        active, erf = activate(units)
        b["gl"][t] = active
        b["sl"][t] = (erf + units * jnp.exp(-0.5 * units * units) * INV_ROOT_TWOPI).astype(BF16)

    def partial_down(rows):
        return sum(dot(b["gl"][t, rows], down_weight(t), NT) for t in range(2))

    b["fs"][...] = partial_down(other_rows).astype(BF16)
    f_swap = remote(b["fs"], b["fr"], sibling)
    branch = partial_down(own_rows)
    arrived([f_swap])
    out, n2, inv2 = norm_forward(b["h1"][...] + branch + b["fr"][...].astype(F32), gains[1], biases[1])
    low = out.astype(BF16)
    b["yb"][...] = low
    b["mo"][...] = low[256:272].astype(F32).reshape(2, 8, D)
    for i in range(TP):
        to_device(
            b["yb"].at[pl.ds(TOKENS * i, TOKENS)],
            hout.at[seg, pl.ds(pl.multiple_of(TOKENS * core, 16), TOKENS)],
            (i, chain),
            xsem.at[3, 2 * seg + core],
            3,
            i,
        )
    for i in range(2):
        to_device(b["mo"].at[i], mout.at[seg], (2 * core + i, chain), xsem.at[4, seg], 4, i)

    for i in range(TP):
        from_device(b["gyt"].at[pl.ds(TOKENS * i, TOKENS)], 1, i)
    for i in range(2):
        from_device(b["gm"].at[i], 2, i)
    upstream = jnp.concatenate([b["gyt"][...].astype(F32), b["gm"][...].reshape(16, D)], 0)
    b["sg"][...] = jnp.zeros((48, D), F32)
    b["sg"][1:2] = column_sum(upstream * n2)
    b["sg"][3:4] = column_sum(upstream)
    dz = norm_backward(upstream, n2, inv2, gains[1])
    b["dz"][...] = dz
    b["dfb"][own_rows] = dz.astype(BF16)
    df_swap = remote(b["dfb"].at[own_rows], b["dfb"].at[own_rows], sibling)
    arrived([df_swap])

    def weight_grad(name, left, right):
        for t in range(2):
            part = dot(left, b[right][t], TN).astype(BF16)
            for i in range(2):
                b[name][2 * t + i] = part[:, HALF * i : HALF * (i + 1)].reshape(nz, ny, br, HALF)

    scatters = {j[0]: j for j in scatter_jobs()}
    rs = {}

    def is_ring(name, step):
        _, order, cols, axes = scatters[name]
        return step == 0 and name in RINGS and size[order[0]] == 4

    def source_of(name, step):
        _, order, cols, axes = scatters[name]
        axis = order[step]
        left = [a for a in axes if a not in order[:step]]
        array = b[GRADS[name[0]]] if step == 0 else b[f"s{step - 1}_{name}"]
        tail = (slice(None), cols) if step == 0 else ()

        def part(place, half=None):
            where = []
            for a in left:
                if a == axis:
                    where.append(place)
                elif half is not None:
                    where.append(pl.ds(half * (size[a] // 2), size[a] // 2))
                    half = None
                else:
                    where.append(slice(None))
            return array.at[tuple(where) + tail]

        return part

    def scatter_send(name, step):
        axis = scatters[name][1][step]
        n = size[axis]
        part = source_of(name, step)
        landing = b[f"r{step}_{name}"]
        if is_ring(name, step):
            right, left, far = ((at[axis] + o) % n for o in (1, n - 1, 2))
            to_right, to_left = moved(axis, 1), moved(axis, n - 1)
            half = size[[a for a in scatters[name][3] if a != axis][0]] // 2
            over = b[f"q_{name}"]
            passing = [
                remote(part(far, 0), over.at[0], to_right),
                remote(part(far, 1), over.at[1], to_left),
            ]
            coming = [
                remote(part(right, 1), landing.at[0, half:], to_right),
                remote(part(left, 0), landing.at[1, :half], to_left),
            ]
            rs[name] = (passing, coming, half, (right, left), (to_right, to_left))
            return
        rs[name] = [
            remote(part((at[axis] + o) % n), landing.at[o - 1], moved(axis, o)) for o in range(1, n)
        ]

    def scatter_pass(name):
        if not is_ring(name, 0):
            return
        passing, coming, half, places_, devices = rs[name]
        part = source_of(name, 0)
        landing, over, updated = b[f"r0_{name}"], b[f"q_{name}"], b[f"u_{name}"]
        for i in range(2):
            arrived([passing[i]])
            updated[i] = (part(places_[i], i)[...].astype(F32) + over[i].astype(F32)).astype(BF16)
            where = landing.at[0, :half] if i == 0 else landing.at[1, half:]
            coming.append(remote(updated.at[i], where, devices[i]))

    def scatter_sum(name, step):
        _, order, cols, axes = scatters[name]
        axis = order[step]
        total = source_of(name, step)(at[axis])[...].astype(F32)
        ring = is_ring(name, step)
        arrived(rs[name][1] if ring else rs[name])
        for o in range(2 if ring else size[axis] - 1):
            total = total + b[f"r{step}_{name}"][o].astype(F32)
        if step < len(order) - 1:
            b[f"s{step}_{name}"][...] = total.astype(BF16)
        return total

    def scatter_on(names, step):
        for n in names:
            scatter_sum(n, step)
            scatter_send(n, step + 1)

    down_names, up_names = ("t0", "t1", "t2"), ("i0", "i1", "i2")
    weight_grad("gt", b["dfb"][...], "gl")
    for n in down_names:
        scatter_send(n, 0)
    for t in range(2):
        b["du"][t] = (dot(b["dfb"][...], down_weight(t)) * b["sl"][t].astype(F32)).astype(BF16)

    def partial_up(rows):
        return sum(dot(b["du"][t, rows], up_weight(t), NT) for t in range(2))

    b["dhs"][...] = partial_up(other_rows).astype(BF16)
    dh_swap = remote(b["dhs"], b["dhr"], sibling)
    b["dz"][...] = b["dz"][...] + partial_up(own_rows)
    weight_grad("gi", b["h1b"][...], "du")
    for n in up_names:
        scatter_send(n, 0)
    for n in down_names:
        scatter_pass(n)
    arrived([dh_swap])
    into_first = b["dz"][...] + b["dhr"][...].astype(F32)
    b["sg"][0:1] = column_sum(into_first * b["n1"][...])
    b["sg"][2:3] = column_sum(into_first)
    dr = norm_backward(into_first, b["n1"][...], b["inv1"][...], gains[0])
    b["dr"][...] = dr
    b["dab"][own_rows] = dr.astype(BF16)
    da_swap = remote(b["dab"].at[own_rows], b["dab"].at[own_rows], sibling)
    arrived([da_swap])

    def head_rows(ref, c):
        if nz > 1:
            return ref.at[pl.ds(c * (nz // 2), nz // 2)]
        return ref.at[:, :, pl.ds(pl.multiple_of(c * HALF, 16), HALF)]

    grad_mixed = 0.0
    for h in range(2):
        w = head_rows(b["wo"].at[h], core)[...].reshape(HALF, HALF)
        grad_mixed = grad_mixed + dot(b["dab"][:, HALF * h : HALF * (h + 1)], w, NT)
    for p in range(3):
        b["doc"][p] = grad_mixed[:, 128 * p : 128 * p + 128].astype(BF16)

    mixed_t = b["ot"][...].reshape(HALF, ROWS)

    def proj_grad(h):
        cols = pl.ds(pl.multiple_of(HALF * h, 128), HALF)
        return dot(mixed_t, b["dab"][:, cols]).astype(BF16).reshape(b["gos"].shape)

    def wo_part(c):
        return head_rows(b["ga"].at[:, :, :, wo_cols], c)

    b["gos"][...] = proj_grad(other)
    go_swap = remote(b["gos"], wo_part(core), sibling)
    wo_part(core)[...] = proj_grad(core)

    def backward_pair(p):
        qp, kp, vp = (b["qkv"][3 * p + i] for i in range(3))
        dop = b["doc"][p]
        kt = kp.T
        dv = dk = 0.0
        dq = []
        for hh in range(2):
            inside, _, _ = head_masks(hh)
            zero = jnp.zeros_like(kp)
            grad_probs = dot(jnp.where(inside, vp, zero), dop, NT)
            low_probs = b["pt"][2 * p + hh]
            probs = low_probs.astype(F32)
            row_term = jnp.sum(probs * grad_probs, 0, keepdims=True)
            ds = (probs * (grad_probs - row_term)).astype(BF16)
            dv = dv + dot(low_probs, jnp.where(inside, dop, zero))
            dk = dk + dot(ds, jnp.where(inside, qp, zero))
            dq.append(dot(kt[64 * hh : 64 * hh + 64], ds))
        b["dqkv"][3 * p] = (jnp.concatenate(dq, 0) * 0.125).T.astype(BF16)
        b["dqkv"][3 * p + 1] = (dk * 0.125).astype(BF16)
        b["dqkv"][3 * p + 2] = dv.astype(BF16)

    def joined(rows, wanted):
        return jnp.concatenate([b["dqkv"][i, rows] for i in wanted], 1)

    def attention_grad(p):
        rows = b["xp" if p == 0 else "x"][...]
        part = dot(rows, joined(slice(None), range(3 * p, 3 * p + 3)), TN).astype(BF16)
        if p == 0:
            b["gx"][...] = part.reshape(TP, nz, sh.xrows, HALF)
        else:
            b["ga"][:, :, :, HALF * p : HALF * (p + 1)] = part.reshape(nz, ny, br, HALF)

    backward_pair(0)
    attention_grad(0)
    arrived([go_swap])
    scatter_send("aw", 0)
    scatter_send("x0", 0)
    backward_pair(1)
    attention_grad(1)
    for n in up_names:
        scatter_pass(n)
    scatter_send("a1", 0)
    scatter_on(down_names, 0)
    for n in ("aw", "x0"):
        scatter_pass(n)
    backward_pair(2)
    attention_grad(2)
    scatter_send("a2", 0)
    scatter_send("a3", 0)
    scatter_pass("a1")

    def partial_input(rows):
        return dot(joined(rows, range(9)), attention_weight(), NT)

    b["dxs"][...] = partial_input(other_rows).astype(BF16)
    dx_swap = remote(b["dxs"], b["dxr"], sibling)
    dx = partial_input(own_rows) + b["dr"][...]
    arrived([dx_swap])
    dx = dx + b["dxr"][...].astype(F32)
    b["dxb"][...] = dx[:256].astype(BF16)
    for i in range(TP):
        to_device(
            b["dxb"].at[pl.ds(TOKENS * i, TOKENS)],
            dxo.at[seg, pl.ds(pl.multiple_of(TOKENS * core, 16), TOKENS)],
            (i, chain),
            xsem.at[5, 2 * seg + core],
            5,
            i,
        )

    @pl.when((core == 0) & (seg == 0))
    def _():
        b["sg"][16:32] = dx[256:272]

    @pl.when(core == 1)
    def _():
        b["sg"][32:48] = dx[256:272]

    small_grads = dot(b["sg"][...].astype(BF16), smallsel[...], TN).astype(BF16)
    b["ga"][:, :, :, 4 * HALF :] = small_grads.reshape(nz, ny, br, SMALL)
    scatter_send("as", 0)
    attention_names = ("aw", "x0", "a1", "a2", "a3", "as")
    scatter_on(up_names, 0)
    scatter_on(down_names, 1)
    scatter_on(attention_names, 0)
    scatter_on(up_names, 1)

    def last_rows(names, first_col):
        for j, n in enumerate(names):
            total = scatter_sum(n, 2)
            cols = slice(first_col + 128 * j, first_col + 128 * j + 128)
            b["sf"][0, :, cols] = total[:wr]
            b["sf"][1, :, cols] = total[wr:]

    for n in attention_names:
        cols = scatters[n][2]
        total = scatter_sum(n, 1).astype(BF16)
        if n == "x0":
            spread = dot(packy[...], total, TN).astype(BF16)
            b["e3y"][...] = spread.reshape(ny, 2 * sh.pc, HALF)
            ysteps = [remote(b["e3y"].at[(y + o) % ny], b["r3y"].at[o - 1], moved("y", o)) for o in range(1, ny)]
        else:
            spread = dot(packsel[...], total, TN).astype(BF16)
            b["e3"][:, :, cols.start - HALF : cols.stop - HALF] = spread.reshape(TP, 2 * sh.pc, cols.stop - cols.start)
    steps = [remote(b["e3"].at[(x + o) % TP], b["r3"].at[o - 1], moved("x", o)) for o in range(1, TP)]
    last_rows(down_names, HALF)
    last_rows(up_names, 0)
    sf_local = local(b["sf"].at[core], gfo.at[core])
    sf_swap = remote(b["sf"].at[other], gfo.at[core], sibling)

    arrived(steps)
    total = b["e3"][x].astype(F32)
    for o in range(1, TP):
        total = total + b["r3"][o - 1].astype(F32)
    b["s4"][:, :, HALF:] = total.reshape(2, sh.pc, REST)
    arrived(ysteps)
    total = b["e3y"][y].astype(F32)
    for o in range(1, ny):
        total = total + b["r3y"][o - 1].astype(F32)
    b["s4"][:, :, :HALF] = total.reshape(2, sh.pc, HALF)
    s4_local = local(b["s4"].at[core], gao.at[core])
    s4_swap = remote(b["s4"].at[other], gao.at[core], sibling)

    for kind, out_ref in ((3, hout), (5, dxo)):
        for s in range(2):
            for j in range(2):
                from_device(out_ref.at[s, pl.ds(TOKENS * j, TOKENS)], kind, 2 * s + j)
    for s in range(2):
        from_device(mout.at[s], 4, s)
    sf_local.wait()
    s4_local.wait()
    arrived([sf_swap, s4_swap])

    for copy in sent:
        copy.wait_send()
    for same, copy in conditional:

        @pl.when(jnp.logical_not(same))
        def _():
            copy.wait_send()

    @pl.when((seg == 0) & (core == 1))
    def _():
        hops[0].wait_send()
        hops[1].wait_send()

    @pl.when((seg == 0) & (core == 0))
    def _():
        early.wait_send()


def layer(sh, arrays):
    constants = [jnp.asarray(a, BF16) for a in selections(sh)]
    table = scratch_of(sh)
    names = list(table)
    anywhere = pl.BlockSpec(memory_space=pl.ANY)
    outs = [
        jax.ShapeDtypeStruct((2, 128, D), BF16),
        jax.ShapeDtypeStruct((2, 8, D), F32),
        jax.ShapeDtypeStruct((2, 128, D), BF16),
        jax.ShapeDtypeStruct((2, sh.pc, ACOLS), F32),
        jax.ShapeDtypeStruct((2, sh.wrows, D), F32),
    ]
    return pl.pallas_call(
        functools.partial(kernel, sh, names),
        name="layer",
        out_shape=outs,
        in_specs=[anywhere] * 15,
        out_specs=[anywhere] * len(outs),
        scratch_shapes=[pltpu.VMEM(*table[n]) for n in names]
        + [
            pltpu.SemaphoreType.DMA((250,)),
            pltpu.SemaphoreType.DMA((250,)),
            pltpu.SemaphoreType.DMA((7, 12)),
            pltpu.SemaphoreType.DMA((24,)),
        ],
        compiler_params=pltpu.CompilerParams(
            collective_id=0, has_side_effects=True, vmem_limit_bytes=64 * 2**20 - 2**17
        ),
    )(*arrays, *constants)


def unpack_kernel(sh, hout, mout, dxo, gao, gfo, *outs):
    hidden, memory, grad_in, gq, gp, gains, biases, tokens, gi, gt = outs
    ar = sh.arows
    hidden[...] = hout[...]
    for i in range(2):
        memory[:, i] = mout[i, :5].astype(BF16)
    grad_in[...] = dxo[...].astype(F32)
    for h in range(2):
        for p in range(3):
            for i in range(3):
                to = D * i + HALF * h + 128 * p
                first = HALF * p + 128 * i
                gq[:, to : to + 128] = gao[h, :ar, first : first + 128]
        gp[:, HALF * h : HALF * (h + 1)] = gao[h, :ar, WO : WO + HALF]
        gi[:, HALF * h : HALF * (h + 1)] = gfo[h, :, :HALF]
        gt[:, HALF * h : HALF * (h + 1)] = gfo[h, :, HALF:]
    small = gao[0, :, 4 * HALF :] + gao[1, :, 4 * HALF :]
    turned = small.T[:, :ar]
    gains[...] = turned[0:2]
    biases[...] = turned[2:4]
    for kind in range(2):
        tokens[:, kind] = small[:ar, 4 + MEM * kind : 4 + MEM * (kind + 1)]


def unpack(sh, *arrays):
    ar, wr = sh.arows, sh.wrows
    shapes = [
        ((2, 128, D), BF16),
        ((5, 2, D), BF16),
        ((2, 128, D), F32),
        ((ar, 3 * D), F32),
        ((ar, D), F32),
        ((2, ar), F32),
        ((2, ar), F32),
        ((ar, 2, MEM), F32),
        ((wr, D), F32),
        ((wr, D), F32),
    ]
    vmem = pl.BlockSpec(memory_space=pltpu.VMEM)
    return pl.pallas_call(
        functools.partial(unpack_kernel, sh),
        name="unpack",
        out_shape=[jax.ShapeDtypeStruct(*one) for one in shapes],
        in_specs=[vmem] * 5,
        out_specs=[vmem] * len(shapes),
        compiler_params=pltpu.CompilerParams(vmem_limit_bytes=64 * 2**20 - 2**17),
    )(*arrays)


def body(
    sh,
    hidden_in,
    reset,
    w_qkv,
    w_attn_out,
    norm_gains,
    norm_biases,
    memory_tokens,
    w_in,
    w_out,
    grad_hidden,
    grad_memory,
):
    arrays = (
        hidden_in,
        grad_hidden,
        grad_memory.transpose(1, 0, 2),
        w_qkv,
        w_attn_out,
        norm_gains,
        norm_biases,
        memory_tokens.transpose(2, 0, 1),
        w_in,
        w_out.T,
    )
    hidden, memory, *middle, tokens, gi, gt = unpack(sh, *layer(sh, arrays))
    return hidden, memory.transpose(1, 0, 2), *middle, tokens.transpose(1, 2, 0), gi, gt.T


def solution(mesh):
    sh = Shape(mesh.shape["dp"])
    return jax.shard_map(
        functools.partial(body, sh),
        mesh=mesh,
        in_specs=(
            P("dp", "tp", None),
            P("dp"),
            P(("dp", "tp"), None),
            P(("dp", "tp"), None),
            P(None, ("dp", "tp")),
            P(None, ("dp", "tp")),
            P(None, None, ("dp", "tp")),
            P("dp", "tp"),
            P("tp", "dp"),
            P("dp", "tp", None),
            P("dp", "tp", None),
        ),
        out_specs=(
            P("dp", "tp", None),
            P("dp", "tp", None),
            P("dp", "tp", None),
            P(("dp", "tp"), None),
            P(("dp", "tp"), None),
            P(None, ("dp", "tp")),
            P(None, ("dp", "tp")),
            P(None, None, ("dp", "tp")),
            P("dp", "tp"),
            P("tp", "dp"),
        ),
        check_vma=False,
    )
```

```python
import functools
import types

import jax
import jax.numpy as jnp
import numpy as np
from jax import lax
from jax.experimental import pallas as pl
from jax.experimental.pallas import tpu as pltpu
from jax.sharding import PartitionSpec as P

D = 768
HALF = 384
MEM = 10
TOKENS = 64
OWN = 272
ROWS = 2 * OWN
TP = 4
SMALL = 128
ACOLS = 4 * HALF + SMALL
REST = ACOLS - HALF
CUT = HALF + 640
WO = 3 * HALF
EPSILON = 1e-05
INV_ROOT_TWO = 0.7071067811865476
INV_ROOT_TWOPI = 0.3989422804014327
EXP_SCALE = 0.125 * 1.4426950408889634
MASKED = -1e30
F32 = jnp.float32
BF16 = jnp.bfloat16
MESH = pl.DeviceIdType.MESH
NN = (((1,), (0,)), ((), ()))
NT = (((1,), (1,)), ((), ()))
TN = (((0,), (0,)), ((), ()))


def dot(a, b, dims=NN):
    return lax.dot_general(a, b, dims, preferred_element_type=F32)


def up16(n):
    return -(-n // 16) * 16


class Shape:
    def __init__(self, dp):
        self.dp = dp
        planes = dp // 2
        self.ny = int(round(planes**0.5))
        self.nz = planes // self.ny
        self.wrows = D // dp
        self.arows = D // (dp * TP)
        self.brows = 2 * self.wrows
        self.pr = up16(self.arows)
        self.xrows = 2 * self.arows * self.ny
        self.pc = -(-self.arows // 8) * 8
        self.fr = up16(self.wrows)


def selections(sh):
    pack = np.zeros((sh.brows, TP * 2 * sh.pc), np.float32)
    for c in range(2):
        for x in range(TP):
            for i in range(sh.arows):
                pack[c * sh.wrows + x * sh.arows + i, (x * 2 + c) * sh.pc + i] = 1
    packy = np.zeros((sh.xrows, sh.ny * 2 * sh.pc), np.float32)
    turn = np.zeros((D, D), np.float32)
    ar = sh.arows
    for c in range(2):
        for y in range(sh.ny):
            for i in range(ar):
                row = (y * 2 + c) * ar + i
                packy[row, (y * 2 + c) * sh.pc + i] = 1
                for x in range(TP):
                    for z in range(sh.nz):
                        place = (z * sh.ny + y) * sh.brows + (c * TP + x) * ar + i
                        turn[(x * sh.nz + z) * sh.xrows + row, place] = 1
    small = np.zeros((48, SMALL), np.float32)
    for i in range(4):
        small[i, i] = 1
    for kind in range(2):
        for i in range(MEM):
            small[16 + 16 * kind + (i // 5) * 8 + i % 5, 4 + MEM * kind + i] = 1
    places = np.zeros((4, MEM, SMALL), np.float32)
    for kind, (rows, first) in enumerate(((2, 0), (2, 2), (MEM, 4), (MEM, 4 + MEM))):
        for i in range(rows):
            places[kind, i, first + i] = 1
    return pack, small, places, packy, turn


def norm_forward(inputs, gain, offset):
    centred = inputs - jnp.mean(inputs, -1, keepdims=True)
    spread = jnp.mean(centred * centred, -1, keepdims=True)
    inverse = lax.rsqrt(spread + EPSILON)
    normed = centred * inverse
    return normed * gain + offset, normed, inverse


def norm_backward(upstream, normed, inverse, gain):
    scaled = upstream * gain
    first_mean = jnp.mean(scaled, -1, keepdims=True)
    second_mean = jnp.mean(scaled * normed, -1, keepdims=True)
    return inverse * (scaled - first_mean - normed * second_mean)


def column_sum(a):
    return jnp.sum(a, 0, keepdims=True)


XBASE = (0, 4, 8, 10, 14, 16, 20)
SENDS = 40
STAGED, LANDED, SUMMED, PASSED, UPDATED = range(5)


def scratch_of(sh):
    nz, ny, br = sh.nz, sh.ny, sh.brows
    ar, wr = sh.arows, sh.wrows
    operands = [
        (5, 2, D),
        (ar, 3 * D),
        (ar, D),
        (2, ar),
        (2, ar),
        (ar, 2, MEM),
        (wr, D),
        (wr, D),
        (br, TP * 2 * sh.pc),
        (48, SMALL),
        (4, MEM, SMALL),
        (sh.xrows, ny * 2 * sh.pc),
    ]
    jobs = {(STAGED, i, 0): (dims, BF16) for i, dims in enumerate(operands)}
    s = dict(
        pk=((2, sh.pr, ACOLS), BF16),
        ff=((2, sh.fr, D), BF16),
        gms=((2, 8, D), F32),
        p1=((2, sh.pr, ACOLS), BF16),
        p2=((TP, 2 * sh.pc, REST), BF16),
        p2y=((ny, 2 * sh.pc, HALF), BF16),
        turn=((D, D), BF16),
        xp=((ROWS, D), BF16),
        wx=((TP, nz, sh.xrows, HALF), BF16),
        gx=((TP, nz, sh.xrows, HALF), BF16),
        f1=((2, sh.fr, D), BF16),
        wa=((nz, ny, br, ACOLS), BF16),
        wf=((TP, nz, ny, br, D), BF16),
        wo=((2, nz, ny, br, HALF), BF16),
        par=((8, D), F32),
        x=((ROWS, D), BF16),
        gyt=((TP * TOKENS, D), BF16),
        gm=((2, 8, D), F32),
        qkv=((9, ROWS, 128), BF16),
        pt=((6, ROWS, ROWS), BF16),
        ot=((3, 128, ROWS), BF16),
        oc=((ROWS, HALF), BF16),
        oin=((OWN, HALF), BF16),
        h1=((OWN, D), F32),
        n1=((OWN, D), F32),
        inv1=((OWN, 1), F32),
        h1b=((ROWS, D), BF16),
        gl=((2, ROWS, D), BF16),
        sl=((2, ROWS, D), BF16),
        fs=((OWN, D), BF16),
        fr=((OWN, D), BF16),
        n2=((OWN, D), F32),
        yb=((OWN, D), BF16),
        mo=((2, 8, D), F32),
        hop=((16, D), BF16),
        hopin=((16, D), BF16),
        es=((16, D), F32),
        er=((16, D), F32),
        dz=((OWN, D), F32),
        dfb=((ROWS, D), BF16),
        du=((2, ROWS, D), BF16),
        dhs=((OWN, D), BF16),
        dhr=((OWN, D), BF16),
        dr=((OWN, D), F32),
        dab=((ROWS, D), BF16),
        doc=((3, ROWS, 128), BF16),
        dqkv=((9, ROWS, 128), BF16),
        ga=((nz, ny, br, ACOLS), BF16),
        gi=((TP, nz, ny, br, HALF), BF16),
        gt=((TP, nz, ny, br, HALF), BF16),
        dxs=((OWN, D), BF16),
        dxr=((OWN, D), BF16),
        dxb=((TP * TOKENS, D), BF16),
        sg=((48, D), F32),
        e3=((TP, 2 * sh.pc, REST), BF16),
        r3=((TP - 1, 2 * sh.pc, REST), BF16),
        e3y=((ny, 2 * sh.pc, HALF), BF16),
        r3y=((max(1, ny - 1), 2 * sh.pc, HALF), BF16),
        s4=((2, sh.pc, ACOLS), F32),
        sf=((2, sh.wrows, D), F32),
    )
    s.update(gos=((nz // 2, ny, br, HALF) if nz > 1 else (1, 1, HALF, HALF), BF16))
    sizes = {"x": TP, "z": nz, "y": ny}
    for name, order, cols, axes in scatter_jobs():
        left = [a for a in axes]
        block = (sh.xrows if name[0] == "x" else br, cols.stop - cols.start)
        for step, axis in enumerate(order):
            left = [a for a in left if a != axis]
            dims = tuple(sizes[a] for a in left)
            ring = step == 0 and name in RINGS and sizes[axis] == 4
            jobs[LANDED, step, name] = ((2 if ring else max(1, sizes[axis] - 1),) + dims + block, BF16)
            if step < len(order) - 1:
                jobs[SUMMED, step, name] = (dims + block, BF16)
            if ring:
                jobs[PASSED, 0, name] = ((2, dims[0] // 2) + dims[1:] + block, BF16)
                jobs[UPDATED, 0, name] = jobs[PASSED, 0, name]
    return s, jobs


def scatter_jobs():
    orders = [("z", "y", "x"), ("x", "z", "y"), ("y", "x", "z")]
    jobs = []
    for kind in ("t", "i"):
        for j in range(3):
            jobs.append((f"{kind}{j}", orders[j], slice(128 * j, 128 * j + 128), ("x", "z", "y")))
    zy, yz = ("z", "y"), ("y", "z")
    jobs.append(("aw", yz, slice(WO, WO + HALF), zy))
    jobs.append(("x0", ("x", "z"), slice(0, HALF), ("x", "z")))
    jobs.append(("a1", zy, slice(HALF, 2 * HALF), zy))
    jobs.append(("a2", yz, slice(2 * HALF, 2 * HALF + 256), zy))
    jobs.append(("a3", zy, slice(2 * HALF + 256, 3 * HALF), zy))
    jobs.append(("as", zy, slice(4 * HALF, ACOLS), zy))
    return jobs


def gather_jobs():
    orders = [("x", "y", "z"), ("y", "z", "x"), ("z", "x", "y")]
    jobs = [(f"f{j}", orders[j], slice(256 * j, 256 * j + 256), ("x", "z", "y")) for j in range(3)]
    jobs.append(("x0", ("z", "x"), slice(0, HALF), ("x", "z")))
    jobs.append(("a0", ("y", "z"), slice(HALF, CUT), ("z", "y")))
    jobs.append(("a1", ("z", "y"), slice(CUT, ACOLS), ("z", "y")))
    return jobs


RINGS = ("t0", "t1", "t2", "i0", "i1", "i2", "aw", "x0", "a1")
WEIGHTS = {"f": "wf", "a": "wa", "x": "wx"}
GRADS = {"t": "gt", "i": "gi", "a": "ga", "x": "gx"}


def kernel(sh, names, *refs):
    xin, gin = refs[:2]
    hout, mout, dxo, gao, gfo = refs[15:20]
    ssem, rsem, xsem, lsem = refs[-4:]
    count = len(names[0])
    b = types.SimpleNamespace(**dict(zip(names[0], refs[20 : 20 + count])))
    k = dict(zip(names[1], refs[20 + count : -4]))
    staged = [k[STAGED, i, 0] for i in range(12)]
    gmem, wq, wp, gain_in, bias_in, token_in, up_in, down_in = staged[:8]
    packsel, smallsel, places, packy = staged[8:]
    turn = refs[14]
    nz, ny, br, wr, ar = sh.nz, sh.ny, sh.brows, sh.wrows, sh.arows
    pk, ff, gms = b.pk, b.ff, b.gms

    dp = lax.axis_index("dp")
    x = lax.axis_index("tp")
    core = dp % 2
    y = (dp // 2) % ny
    z = dp // (2 * ny)
    other = 1 - core
    chain = x // 2
    seg = jnp.where((x == 1) | (x == 2), 1, 0)
    at = {"x": x, "y": y, "z": z}
    size = {"x": TP, "y": ny, "z": nz}

    def device(x_=x, y_=y, z_=z, c_=core):
        return ((z_ * ny + y_) * 2 + c_, x_)

    def moved(axis, offset, core_=core):
        there = dict(at)
        there[axis] = (at[axis] + offset) % size[axis]
        return device(there["x"], there["y"], there["z"], core_)

    sibling = device(c_=other)
    sent = []

    class Group:
        def __init__(self, like):
            if len(sent) >= SENDS:
                sent[-SENDS].wait_send()
            self.like = like
            self.send_sem = ssem.at[len(sent) % SENDS]
            self.recv_sem = rsem.at[len(sent)]
            sent.append(self)

        def add(self, src, dst, to):
            pltpu.make_async_remote_copy(
                src_ref=src,
                dst_ref=dst,
                send_sem=self.send_sem,
                recv_sem=self.recv_sem,
                device_id=to,
                device_id_type=MESH,
            ).start()

        def wait_send(self):
            pltpu.make_async_copy(self.like, self.like, self.send_sem).wait()

        def wait_recv(self):
            pltpu.make_async_copy(self.like, self.like, self.recv_sem).wait()

    def remote(src, dst, to):
        group = Group(dst)
        group.add(src, dst, to)
        return group

    def arrived(groups):
        for group in groups:
            group.wait_recv()

    locals_ = [0]

    def local(src, dst):
        copy = pltpu.make_async_copy(src, dst, lsem.at[locals_[0]])
        locals_[0] += 1
        copy.start()
        return copy

    staging = [local(refs[2 + i], staged[i]) for i in range(12)]
    turn_local = local(turn, b.turn)

    barrier = pltpu.get_barrier_semaphore()
    peers = [sibling]
    for o in range(1, TP):
        peers += [moved("x", o), moved("x", o, other)]
    for axis in ("y", "z"):
        for o in range(1, size[axis]):
            peers.append(moved(axis, o))
    for peer in peers:
        pl.semaphore_signal(barrier, inc=1, device_id=peer, device_id_type=MESH)

    pk[...] = jnp.zeros(pk.shape, BF16)
    ff[...] = jnp.zeros(ff.shape, BF16)
    gms[...] = jnp.zeros(gms.shape, F32)
    for copy in staging:
        copy.wait()
    small = dot(gain_in[...], places[0, :2], TN) + dot(bias_in[...], places[1, :2], TN)
    small = small + dot(token_in[:, 0], places[2]) + dot(token_in[:, 1], places[3])
    small = small.astype(BF16)
    for h in range(2):
        for p in range(3):
            for i in range(3):
                first = D * i + HALF * h + 128 * p
                pk[h, :ar, HALF * p + 128 * i : HALF * p + 128 * (i + 1)] = wq[:, first : first + 128]
        pk[h, :ar, WO : WO + HALF] = wp[:, HALF * h : HALF * (h + 1)]
        pk[h, :ar, 4 * HALF :] = small
        for j in range(3):
            cols = slice(HALF * h + 128 * j, HALF * h + 128 * (j + 1))
            ff[h, :wr, 256 * j : 256 * j + 128] = up_in[:, cols]
            ff[h, :wr, 256 * j + 128 : 256 * j + 256] = down_in[:, cols]
        gms[h, 0:5] = gmem[:, h].astype(F32)
    pl.semaphore_wait(barrier, len(peers))

    pk_local = local(pk.at[core], b.p1.at[core])
    ff_local = local(ff.at[core], b.f1.at[core])
    pk_swap = remote(pk.at[other], b.p1.at[core], sibling)
    ff_swap = remote(ff.at[other], b.f1.at[core], sibling)

    conditional = []

    def to_device(src, dst, place, here, kind, send_slot):
        copy = pltpu.make_async_remote_copy(
            src_ref=src,
            dst_ref=dst,
            send_sem=xsem.at[25 + XBASE[kind] + send_slot],
            recv_sem=here,
            device_id=device(x_=place[0], c_=place[1]),
            device_id_type=MESH,
        )
        same = (place[0] == x) & (place[1] == core)

        @pl.when(same)
        def _():
            pltpu.make_async_copy(src, dst, here).start()

        @pl.when(jnp.logical_not(same))
        def _():
            copy.start()

        conditional.append((same, copy))

    def from_device(dst, kind, slot):
        pltpu.make_async_copy(dst, dst, xsem.at[XBASE[kind] + slot]).wait()

    def chip_of(k, s):
        return s + k * (3 - 2 * s)

    def send_rows():
        for s in range(2):
            for j in range(2):
                to_device(
                    xin.at[s, pl.ds(TOKENS * j, TOKENS)],
                    b.x.at[pl.ds(pl.multiple_of(OWN * j + TOKENS * x, 16), TOKENS)],
                    (chip_of(core, s), j),
                    xsem.at[XBASE[0] + x],
                    0,
                    2 * s + j,
                )

    def send_upstream():
        for s in range(2):
            for j in range(2):
                to_device(
                    gin.at[s, pl.ds(TOKENS * j, TOKENS)],
                    b.gyt.at[pl.ds(pl.multiple_of(TOKENS * x, 16), TOKENS)],
                    (chip_of(core, s), j),
                    xsem.at[XBASE[1] + x],
                    1,
                    2 * s + j,
                )
            to_device(
                gms.at[s], b.gm.at[x % 2], (chip_of(core, s), x // 2), xsem.at[XBASE[2] + x % 2], 2, s
            )

    def part_of(job, step, place, half=None):
        name, order, cols, axes = job
        fixed = {a: at[a] for a in order[step:]}
        fixed[order[step]] = place
        where = []
        for a in axes:
            if a in fixed:
                where.append(fixed[a])
            elif half is not None:
                where.append(pl.ds(half * (size[a] // 2), size[a] // 2))
                half = None
            else:
                where.append(slice(None))
        return getattr(b, WEIGHTS[name[0]]).at[tuple(where) + (slice(None), cols)]

    def gather_start(name, step):
        job = gathers[name]
        axis = job[1][step]
        n = size[axis]
        own = part_of(job, step, at[axis])
        free = [a for a in job[3] if a not in job[1][step:]]
        relay = n == 4 and step == len(job[1]) - 1 and size[free[0]] % 2 == 0
        state = types.SimpleNamespace(step=step, relay=relay)
        if relay:
            first = [part_of(job, step, at[axis], h) for h in range(2)]
            right, left = moved(axis, 1), moved(axis, n - 1)
            state.right = remote(first[0], first[0], right)
            state.left = remote(first[1], first[1], left)
            state.every = [Group(part_of(job, step, pl.ds(0, 2)))]
            state.every[0].add(first[1], first[1], right)
            state.every[0].add(first[0], first[0], left)
        else:
            state.every = [Group(part_of(job, step, pl.ds(0, n - 1)))] if n > 1 else []
            for o in range(1, n):
                state.every[0].add(own, own, moved(axis, o))
        flying[name] = state

    def gather_pass(name):
        job, state = gathers[name], flying[name]
        if not state.relay:
            return
        axis = job[1][state.step]
        n = size[axis]
        for copy, back, onward, half in ((state.right, n - 1, 1, 0), (state.left, 1, n - 1, 1)):
            arrived([copy])
            piece = part_of(job, state.step, (at[axis] + back) % n, half)
            state.every[0].add(piece, piece, moved(axis, onward))

    def gather_done(name):
        arrived(flying[name].every)

    gathers = {j[0]: j for j in gather_jobs()}
    flying = {}

    pk_local.wait()
    arrived([pk_swap])
    packed = jnp.concatenate([b.p1[c].astype(F32)[: sh.pc] for c in range(2)], 0).astype(BF16)
    b.p2y[y] = packed[:, :HALF]
    b.p2[x] = packed[:, HALF:]
    mine = b.p2y.at[y]
    ysteps, xsteps = [], [Group(b.p2.at[: TP - 1])]
    if ny > 1:
        ysteps.append(Group(b.p2y.at[: ny - 1]))
    for o in range(1, ny):
        ysteps[0].add(mine, mine, moved("y", o))
    mine = b.p2.at[x]
    for o in range(1, TP):
        xsteps[0].add(mine, mine, moved("x", o))
    ff_local.wait()
    arrived([ff_swap])
    two = [b.f1[c].astype(F32)[:wr] for c in range(2)]
    b.wf[x, z, y] = jnp.concatenate(two, 0).astype(BF16)
    feed_names, first_names = ("f1", "f2", "f0"), ("x0", "a0", "a1")
    for n in feed_names:
        gather_start(n, 0)
    send_rows()
    arrived(ysteps)
    b.wx[x, z] = dot(packy[...], b.p2y[...].reshape(ny * 2 * sh.pc, HALF)).astype(BF16)
    gather_start("x0", 0)
    arrived(xsteps)
    b.wa[z, y, :, HALF:] = dot(packsel[...], b.p2[...].reshape(TP * 2 * sh.pc, REST)).astype(BF16)
    for n in ("a0", "a1"):
        gather_start(n, 0)
    for n in feed_names:
        gather_done(n)
        gather_start(n, 1)
    for n in first_names:
        gather_done(n)
        gather_start(n, 1)
    for n in first_names:
        gather_pass(n)
    for n in feed_names:
        gather_done(n)
        gather_start(n, 2)

    for i in range(TP):
        from_device(b.x.at[pl.ds(pl.multiple_of(OWN * core + TOKENS * i, 16), TOKENS)], 0, i)
    half = b.x.at[pl.ds(pl.multiple_of(OWN * core, 16), TP * TOKENS)]
    x_swap = remote(half, half, sibling)
    for first in (256, OWN + 256):
        b.x[first : first + 16] = jnp.zeros((16, D), BF16)
    turn_local.wait()
    arrived([x_swap])
    b.xp[...] = dot(b.x[...], b.turn[...], NT).astype(BF16)
    for n in first_names:
        gather_done(n)
    wo_cols = slice(WO, WO + HALF)
    wo_local = local(b.wa.at[:, :, :, wo_cols], b.wo.at[core])
    wo_swap = remote(b.wa.at[:, :, :, wo_cols], b.wo.at[core], sibling)
    gather_pass("f1")
    send_upstream()

    def attention_weight():
        return b.wa[:, :, :, :WO].reshape(D, WO)

    small = b.wa[:, :, :, 4 * HALF :].reshape(D, SMALL)
    chosen = dot(smallsel[...], small, NT)
    b.par[...] = chosen[0:8]
    memory = chosen[16:48].astype(BF16)
    b.x[OWN + 256 : OWN + 272] = memory[16:]
    turned = dot(memory, b.turn[...], NT).astype(BF16)
    b.xp[OWN + 256 : OWN + 272] = turned[16:]

    @pl.when(seg == 0)
    def _():
        b.x[256:272] = memory[:16]
        b.xp[256:272] = turned[:16]

    gains = [b.par[i : i + 1] for i in range(2)]
    biases = [b.par[2 + i : 3 + i] for i in range(2)]

    hop_to = jnp.where(x == 0, 1, 2)
    hops = []
    for j in range(2):
        hops.append(
            pltpu.make_async_remote_copy(
                src_ref=b.hop,
                dst_ref=b.hopin,
                send_sem=xsem.at[XBASE[6] + j],
                recv_sem=xsem.at[XBASE[6] + 2],
                device_id=device(x_=hop_to, c_=j),
                device_id_type=MESH,
            )
        )

    own_rows = pl.ds(pl.multiple_of(OWN * core, 16), OWN)
    other_rows = pl.ds(pl.multiple_of(OWN * other, 16), OWN)

    out = dot(b.xp[...], b.wx[...].reshape(D, HALF)).astype(BF16)
    for i in range(3):
        b.qkv[i] = out[:, 128 * i : 128 * i + 128]
    out = dot(b.x[...], b.wa[:, :, :, HALF:WO].reshape(D, 2 * HALF)).astype(BF16)
    for i in range(3, 9):
        b.qkv[i] = out[:, 128 * (i - 3) : 128 * (i - 2)]

    def head_masks(hh):
        lane = lax.broadcasted_iota(jnp.int32, (ROWS, 128), 1)
        row = lax.broadcasted_iota(jnp.int32, (ROWS, 128), 0)
        inside = (lane // 64) == hh
        spare = lane == 64 * (1 - hh)
        memory = ((row >= 256) & (row < 272)) | (row >= OWN + 256)
        invalid = memory & (row % 8 >= 5)
        return inside, spare, invalid

    def forward_pair(p):
        qp, kp, vp = (b.qkv[3 * p + i] for i in range(3))
        vt = vp.T
        for hh in range(2):
            inside, spare, invalid = head_masks(hh)
            zero = jnp.zeros_like(kp)
            kmask = jnp.where(spare & invalid, jnp.full_like(kp, MASKED), zero)
            km = jnp.where(inside, kp, kmask)
            qm = jnp.where(inside, qp, jnp.where(spare, jnp.ones_like(qp), zero))
            scores = dot(km, qm, NT)
            peak = jnp.max(scores, 0, keepdims=True)
            raised = jnp.exp2((scores - peak) * EXP_SCALE)
            total = jnp.sum(raised, 0, keepdims=True)
            probs = (raised * (1.0 / total)).astype(BF16)
            b.pt[2 * p + hh] = probs
            b.ot[p, 64 * hh : 64 * hh + 64] = dot(vt[64 * hh : 64 * hh + 64], probs).astype(BF16)
        b.oc[:, 128 * p : 128 * p + 128] = b.ot[p].T

    @pl.when(seg == 0)
    def _():
        forward_pair(0)
        forward_pair(1)

    ordered = dot(b.turn[...], b.wx[...].reshape(D, HALF), TN).astype(BF16)
    b.wa[:, :, :, :HALF] = ordered.reshape(nz, ny, br, HALF)
    for n in ("f2", "f0"):
        gather_pass(n)

    @pl.when(seg == 0)
    def _():
        forward_pair(2)

    @pl.when(seg == 1)
    def _():
        hops[0].wait_recv()
        b.x[256:272] = b.hopin[...]
        b.xp[256:272] = dot(b.hopin[...], b.turn[...], NT).astype(BF16)
        rows = dot(b.hopin[...], attention_weight()).astype(BF16)
        for i in range(9):
            b.qkv[i, 256:272] = rows[:, 128 * i : 128 * i + 128]
        for p in range(3):
            forward_pair(p)

    def head_rows(ref, c):
        if nz > 1:
            return ref.at[pl.ds(c * (nz // 2), nz // 2)]
        return ref.at[:, :, pl.ds(pl.multiple_of(c * HALF, 16), HALF)]

    def wo_rows(h, c):
        return head_rows(b.wo.at[h], c)[...].reshape(HALF, HALF)

    o_swap = remote(b.oc.at[other_rows], b.oin, sibling)
    wo_local.wait()
    arrived([wo_swap])
    halves = [dot(b.oc[own_rows], wo_rows(h, core)) for h in range(2)]
    arrived([o_swap])
    attended = jnp.concatenate([halves[h] + dot(b.oin[...], wo_rows(h, other)) for h in range(2)], 1)
    h1, n1, inv1 = norm_forward(b.x[own_rows].astype(F32) + attended, gains[0], biases[0])
    b.h1[...] = h1
    b.n1[...] = n1
    b.inv1[...] = inv1
    b.h1b[own_rows] = h1.astype(BF16)
    h_swap = remote(b.h1b.at[own_rows], b.h1b.at[own_rows], sibling)
    for n in ("f1", "f2", "f0"):
        gather_done(n)

    def feed_weight(t, kind):
        cols = [256 * j + 128 * kind for j in range(3)]
        blocks = [b.wf[2 * t + i, :, :, :, c : c + 128].reshape(D, 128) for i in range(2) for c in cols]
        return jnp.concatenate(blocks, 1)

    def up_weight(t):
        return feed_weight(t, 0)

    def down_weight(t):
        return feed_weight(t, 1)

    def activate(units):
        erf = 0.5 * (1.0 + lax.erf(units * INV_ROOT_TWO))
        return (units * erf).astype(BF16), erf

    early = pltpu.make_async_remote_copy(
        src_ref=b.es,
        dst_ref=b.er,
        send_sem=xsem.at[XBASE[6] + 3],
        recv_sem=xsem.at[XBASE[6] + 4],
        device_id=sibling,
        device_id_type=MESH,
    )
    row16 = lax.broadcasted_iota(jnp.int32, (16, D), 0)

    @pl.when(seg == 0)
    def _():
        arrived([h_swap])
        rows = b.h1b[OWN + 256 : OWN + 272]
        part = sum(dot(activate(dot(rows, up_weight(t)))[0], down_weight(t), NT) for t in range(2))

        @pl.when(core == 0)
        def _():
            b.es[...] = part
            early.start()

        @pl.when(core == 1)
        def _():
            early.wait_recv()
            whole = b.h1[256:272] + part + b.er[...]
            written = norm_forward(whole, gains[1], biases[1])[0]
            b.hop[...] = jnp.where(row16 % 8 < 5, written, 0.0).astype(BF16)
            hops[0].start()
            hops[1].start()

    def project_up(rows):
        for t in range(2):
            units = dot(b.h1b[rows], up_weight(t))
            active, erf = activate(units)
            b.gl[t, rows] = active
            b.sl[t, rows] = (erf + units * jnp.exp(-0.5 * units * units) * INV_ROOT_TWOPI).astype(BF16)

    project_up(own_rows)

    @pl.when(seg == 1)
    def _():
        arrived([h_swap])

    project_up(other_rows)

    def partial_down(rows):
        return sum(dot(b.gl[t, rows], down_weight(t), NT) for t in range(2))

    b.fs[...] = partial_down(other_rows).astype(BF16)
    f_swap = remote(b.fs, b.fr, sibling)
    branch = partial_down(own_rows)
    arrived([f_swap])
    out, n2, inv2 = norm_forward(b.h1[...] + branch + b.fr[...].astype(F32), gains[1], biases[1])
    low = out.astype(BF16)
    b.yb[...] = low
    b.mo[...] = low[256:272].astype(F32).reshape(2, 8, D)
    for i in range(TP):
        to_device(
            b.yb.at[pl.ds(TOKENS * i, TOKENS)],
            hout.at[seg, pl.ds(pl.multiple_of(TOKENS * core, 16), TOKENS)],
            (i, chain),
            xsem.at[XBASE[3] + 2 * seg + core],
            3,
            i,
        )
    for i in range(2):
        to_device(b.mo.at[i], mout.at[seg], (2 * core + i, chain), xsem.at[XBASE[4] + seg], 4, i)

    for i in range(TP):
        from_device(b.gyt.at[pl.ds(TOKENS * i, TOKENS)], 1, i)
    for i in range(2):
        from_device(b.gm.at[i], 2, i)
    upstream = jnp.concatenate([b.gyt[...].astype(F32), b.gm[...].reshape(16, D)], 0)
    b.sg[...] = jnp.zeros((48, D), F32)
    b.sg[1:2] = column_sum(upstream * n2)
    b.sg[3:4] = column_sum(upstream)
    dz = norm_backward(upstream, n2, inv2, gains[1])
    b.dz[...] = dz
    b.dfb[own_rows] = dz.astype(BF16)
    df_swap = remote(b.dfb.at[own_rows], b.dfb.at[own_rows], sibling)

    def weight_grad(name, left, right):
        for t in range(2):
            part = dot(left, getattr(b, right)[t], TN).astype(BF16)
            for i in range(2):
                getattr(b, name)[2 * t + i] = part[:, HALF * i : HALF * (i + 1)].reshape(nz, ny, br, HALF)

    scatters = {j[0]: j for j in scatter_jobs()}
    rs = {}

    def is_ring(name, step):
        _, order, cols, axes = scatters[name]
        return step == 0 and name in RINGS and size[order[0]] == 4

    def source_of(name, step):
        _, order, cols, axes = scatters[name]
        axis = order[step]
        left = [a for a in axes if a not in order[:step]]
        array = getattr(b, GRADS[name[0]]) if step == 0 else k[SUMMED, step - 1, name]
        tail = (slice(None), cols) if step == 0 else ()

        def part(place, half=None):
            where = []
            for a in left:
                if a == axis:
                    where.append(place)
                elif half is not None:
                    where.append(pl.ds(half * (size[a] // 2), size[a] // 2))
                    half = None
                else:
                    where.append(slice(None))
            return array.at[tuple(where) + tail]

        return part

    def scatter_send(name, step):
        axis = scatters[name][1][step]
        n = size[axis]
        part = source_of(name, step)
        landing = k[LANDED, step, name]
        if is_ring(name, step):
            right, left, far = ((at[axis] + o) % n for o in (1, n - 1, 2))
            to_right, to_left = moved(axis, 1), moved(axis, n - 1)
            half = size[[a for a in scatters[name][3] if a != axis][0]] // 2
            over = k[PASSED, 0, name]
            passing = [
                remote(part(far, 0), over.at[0], to_right),
                remote(part(far, 1), over.at[1], to_left),
            ]
            coming = Group(landing)
            coming.add(part(right, 1), landing.at[0, half:], to_right)
            coming.add(part(left, 0), landing.at[1, :half], to_left)
            rs[name] = (passing, coming, half, (right, left), (to_right, to_left))
            return
        rs[name] = [Group(landing)] if n > 1 else []
        for o in range(1, n):
            rs[name][0].add(part((at[axis] + o) % n), landing.at[o - 1], moved(axis, o))

    def scatter_pass(name):
        if not is_ring(name, 0):
            return
        passing, coming, half, places_, devices = rs[name]
        part = source_of(name, 0)
        landing, over, updated = k[LANDED, 0, name], k[PASSED, 0, name], k[UPDATED, 0, name]
        for i in range(2):
            arrived([passing[i]])
            updated[i] = (part(places_[i], i)[...].astype(F32) + over[i].astype(F32)).astype(BF16)
            where = landing.at[0, :half] if i == 0 else landing.at[1, half:]
            coming.add(updated.at[i], where, devices[i])

    def scatter_sum(name, step):
        _, order, cols, axes = scatters[name]
        axis = order[step]
        total = source_of(name, step)(at[axis])[...].astype(F32)
        ring = is_ring(name, step)
        arrived([rs[name][1]] if ring else rs[name])
        for o in range(2 if ring else size[axis] - 1):
            total = total + k[LANDED, step, name][o].astype(F32)
        if step < len(order) - 1:
            k[SUMMED, step, name][...] = total.astype(BF16)
        return total

    def scatter_on(names, step):
        for n in names:
            scatter_sum(n, step)
            scatter_send(n, step + 1)

    down_names, up_names = ("t0", "t1", "t2"), ("i0", "i1", "i2")
    def units_back(rows):
        for t in range(2):
            b.du[t, rows] = (dot(b.dfb[rows], down_weight(t)) * b.sl[t, rows].astype(F32)).astype(BF16)

    units_back(own_rows)
    arrived([df_swap])
    weight_grad("gt", b.dfb[...], "gl")
    for n in down_names:
        scatter_send(n, 0)
    units_back(other_rows)

    def partial_up(rows):
        return sum(dot(b.du[t, rows], up_weight(t), NT) for t in range(2))

    b.dhs[...] = partial_up(other_rows).astype(BF16)
    dh_swap = remote(b.dhs, b.dhr, sibling)
    b.dz[...] = b.dz[...] + partial_up(own_rows)
    weight_grad("gi", b.h1b[...], "du")
    for n in up_names:
        scatter_send(n, 0)
    for n in down_names:
        scatter_pass(n)
    arrived([dh_swap])
    into_first = b.dz[...] + b.dhr[...].astype(F32)
    b.sg[0:1] = column_sum(into_first * b.n1[...])
    b.sg[2:3] = column_sum(into_first)
    dr = norm_backward(into_first, b.n1[...], b.inv1[...], gains[0])
    b.dr[...] = dr
    b.dab[own_rows] = dr.astype(BF16)
    da_swap = remote(b.dab.at[own_rows], b.dab.at[own_rows], sibling)

    def grad_mixed(rows):
        parts = [dot(b.dab[rows, HALF * h : HALF * (h + 1)], wo_rows(h, core), NT) for h in range(2)]
        for p in range(3):
            b.doc[p, rows] = (parts[0] + parts[1])[:, 128 * p : 128 * p + 128].astype(BF16)

    grad_mixed(own_rows)
    arrived([da_swap])
    grad_mixed(other_rows)

    mixed_t = b.ot[...].reshape(HALF, ROWS)

    def proj_grad(h):
        cols = pl.ds(pl.multiple_of(HALF * h, 128), HALF)
        return dot(mixed_t, b.dab[:, cols]).astype(BF16).reshape(b.gos.shape)

    def wo_part(c):
        return head_rows(b.ga.at[:, :, :, wo_cols], c)

    b.gos[...] = proj_grad(other)
    go_swap = remote(b.gos, wo_part(core), sibling)
    wo_part(core)[...] = proj_grad(core)

    def backward_pair(p):
        qp, kp, vp = (b.qkv[3 * p + i] for i in range(3))
        dop = b.doc[p]
        kt = kp.T
        dv = dk = 0.0
        dq = []
        for hh in range(2):
            inside, _, _ = head_masks(hh)
            zero = jnp.zeros_like(kp)
            grad_probs = dot(jnp.where(inside, vp, zero), dop, NT)
            low_probs = b.pt[2 * p + hh]
            probs = low_probs.astype(F32)
            row_term = jnp.sum(probs * grad_probs, 0, keepdims=True)
            ds = (probs * (grad_probs - row_term)).astype(BF16)
            dv = dv + dot(low_probs, jnp.where(inside, dop, zero))
            dk = dk + dot(ds, jnp.where(inside, qp, zero))
            dq.append(dot(kt[64 * hh : 64 * hh + 64], ds))
        b.dqkv[3 * p] = (jnp.concatenate(dq, 0) * 0.125).T.astype(BF16)
        b.dqkv[3 * p + 1] = (dk * 0.125).astype(BF16)
        b.dqkv[3 * p + 2] = dv.astype(BF16)

    def joined(rows, wanted):
        return jnp.concatenate([b.dqkv[i, rows] for i in wanted], 1)

    def attention_grad(p):
        rows = (b.xp if p == 0 else b.x)[...]
        part = dot(rows, joined(slice(None), range(3 * p, 3 * p + 3)), TN).astype(BF16)
        if p == 0:
            b.gx[...] = part.reshape(TP, nz, sh.xrows, HALF)
        else:
            b.ga[:, :, :, HALF * p : HALF * (p + 1)] = part.reshape(nz, ny, br, HALF)

    backward_pair(0)
    attention_grad(0)
    arrived([go_swap])
    scatter_send("aw", 0)
    scatter_send("x0", 0)
    backward_pair(1)
    attention_grad(1)
    for n in up_names:
        scatter_pass(n)
    scatter_send("a1", 0)
    scatter_on(down_names, 0)
    for n in ("aw", "x0"):
        scatter_pass(n)
    backward_pair(2)
    attention_grad(2)
    scatter_send("a2", 0)
    scatter_send("a3", 0)
    scatter_pass("a1")

    def partial_input(rows):
        return dot(joined(rows, range(9)), attention_weight(), NT)

    b.dxs[...] = partial_input(other_rows).astype(BF16)
    dx_swap = remote(b.dxs, b.dxr, sibling)
    dx = partial_input(own_rows) + b.dr[...]
    arrived([dx_swap])
    dx = dx + b.dxr[...].astype(F32)
    b.dxb[...] = dx[:256].astype(BF16)
    for i in range(TP):
        to_device(
            b.dxb.at[pl.ds(TOKENS * i, TOKENS)],
            dxo.at[seg, pl.ds(pl.multiple_of(TOKENS * core, 16), TOKENS)],
            (i, chain),
            xsem.at[XBASE[5] + 2 * seg + core],
            5,
            i,
        )

    @pl.when((core == 0) & (seg == 0))
    def _():
        b.sg[16:32] = dx[256:272]

    @pl.when(core == 1)
    def _():
        b.sg[32:48] = dx[256:272]

    small_grads = dot(b.sg[...].astype(BF16), smallsel[...], TN).astype(BF16)
    b.ga[:, :, :, 4 * HALF :] = small_grads.reshape(nz, ny, br, SMALL)
    scatter_send("as", 0)
    attention_names = ("aw", "x0", "a1", "a2", "a3", "as")
    scatter_on(up_names, 0)
    scatter_on(down_names, 1)
    scatter_on(attention_names, 0)
    scatter_on(up_names, 1)

    def last_rows(names, first_col):
        for j, n in enumerate(names):
            total = scatter_sum(n, 2)
            cols = slice(first_col + 128 * j, first_col + 128 * j + 128)
            b.sf[0, :, cols] = total[:wr]
            b.sf[1, :, cols] = total[wr:]

    for n in attention_names:
        cols = scatters[n][2]
        total = scatter_sum(n, 1).astype(BF16)
        if n == "x0":
            spread = dot(packy[...], total, TN).astype(BF16)
            b.e3y[...] = spread.reshape(ny, 2 * sh.pc, HALF)
            ysteps = [Group(b.r3y)] if ny > 1 else []
            for o in range(1, ny):
                ysteps[0].add(b.e3y.at[(y + o) % ny], b.r3y.at[o - 1], moved("y", o))
        else:
            spread = dot(packsel[...], total, TN).astype(BF16)
            b.e3[:, :, cols.start - HALF : cols.stop - HALF] = spread.reshape(TP, 2 * sh.pc, cols.stop - cols.start)
    steps = [Group(b.r3)]
    for o in range(1, TP):
        steps[0].add(b.e3.at[(x + o) % TP], b.r3.at[o - 1], moved("x", o))
    last_rows(down_names, HALF)
    last_rows(up_names, 0)
    sf_local = local(b.sf.at[core], gfo.at[core])
    sf_swap = remote(b.sf.at[other], gfo.at[core], sibling)

    arrived(steps)
    total = b.e3[x].astype(F32)
    for o in range(1, TP):
        total = total + b.r3[o - 1].astype(F32)
    b.s4[:, :, HALF:] = total.reshape(2, sh.pc, REST)
    arrived(ysteps)
    total = b.e3y[y].astype(F32)
    for o in range(1, ny):
        total = total + b.r3y[o - 1].astype(F32)
    b.s4[:, :, :HALF] = total.reshape(2, sh.pc, HALF)
    s4_local = local(b.s4.at[core], gao.at[core])
    s4_swap = remote(b.s4.at[other], gao.at[core], sibling)

    for kind, out_ref in ((3, hout), (5, dxo)):
        for s in range(2):
            for j in range(2):
                from_device(out_ref.at[s, pl.ds(TOKENS * j, TOKENS)], kind, 2 * s + j)
    for s in range(2):
        from_device(mout.at[s], 4, s)
    sf_local.wait()
    s4_local.wait()
    arrived([sf_swap, s4_swap])

    for group in sent[-SENDS:]:
        group.wait_send()
    for same, copy in conditional:

        @pl.when(jnp.logical_not(same))
        def _():
            copy.wait_send()

    @pl.when((seg == 0) & (core == 1))
    def _():
        hops[0].wait_send()
        hops[1].wait_send()

    @pl.when((seg == 0) & (core == 0))
    def _():
        early.wait_send()


def layer(sh, arrays):
    constants = [jnp.asarray(a, BF16) for a in selections(sh)]
    tables = scratch_of(sh)
    names = [list(table) for table in tables]
    anywhere = pl.BlockSpec(memory_space=pl.ANY)
    outs = [
        jax.ShapeDtypeStruct((2, 128, D), BF16),
        jax.ShapeDtypeStruct((2, 8, D), F32),
        jax.ShapeDtypeStruct((2, 128, D), BF16),
        jax.ShapeDtypeStruct((2, sh.pc, ACOLS), F32),
        jax.ShapeDtypeStruct((2, sh.wrows, D), F32),
    ]
    return pl.pallas_call(
        functools.partial(kernel, sh, names),
        name="layer",
        out_shape=outs,
        in_specs=[anywhere] * 15,
        out_specs=[anywhere] * len(outs),
        scratch_shapes=[pltpu.VMEM(*one) for table in tables for one in table.values()]
        + [
            pltpu.SemaphoreType.DMA((SENDS,)),
            pltpu.SemaphoreType.DMA((96,)),
            pltpu.SemaphoreType.DMA((45,)),
            pltpu.SemaphoreType.DMA((20,)),
        ],
        compiler_params=pltpu.CompilerParams(
            collective_id=0, has_side_effects=True, vmem_limit_bytes=64 * 2**20 - 2**17
        ),
    )(*arrays, *constants)


def unpack_kernel(sh, *refs):
    arrays, results, held, outs, sems = refs[:5], refs[5:15], refs[15:20], refs[20:30], refs[30]
    loads = [pltpu.make_async_copy(arrays[i], held[i], sems.at[i]) for i in range(5)]
    stores = [pltpu.make_async_copy(outs[i], results[i], sems.at[5 + i]) for i in range(10)]
    for copy in loads:
        copy.start()
    hout, mout, dxo, gao, gfo = held
    hidden, memory, grad_in, gq, gp, gains, biases, tokens, gi, gt = outs
    ar = sh.arows
    loads[0].wait()
    hidden[...] = hout[...]
    stores[0].start()
    loads[2].wait()
    grad_in[...] = dxo[...].astype(F32)
    stores[2].start()
    loads[1].wait()
    for i in range(2):
        memory[:, i] = mout[i, :5].astype(BF16)
    stores[1].start()
    loads[3].wait()
    for h in range(2):
        for p in range(3):
            for i in range(3):
                to = D * i + HALF * h + 128 * p
                first = HALF * p + 128 * i
                gq[:, to : to + 128] = gao[h, :ar, first : first + 128]
        gp[:, HALF * h : HALF * (h + 1)] = gao[h, :ar, WO : WO + HALF]
    small = gao[0, :, 4 * HALF :] + gao[1, :, 4 * HALF :]
    turned = small.T[:, :ar]
    gains[...] = turned[0:2]
    biases[...] = turned[2:4]
    for kind in range(2):
        tokens[:, kind] = small[:ar, 4 + MEM * kind : 4 + MEM * (kind + 1)]
    for i in range(3, 8):
        stores[i].start()
    loads[4].wait()
    for h in range(2):
        gi[:, HALF * h : HALF * (h + 1)] = gfo[h, :, :HALF]
        gt[:, HALF * h : HALF * (h + 1)] = gfo[h, :, HALF:]
    for i in range(8, 10):
        stores[i].start()
    for copy in stores:
        copy.wait()


def unpack(sh, *arrays):
    ar, wr = sh.arows, sh.wrows
    shapes = [
        ((2, 128, D), BF16),
        ((5, 2, D), BF16),
        ((2, 128, D), F32),
        ((ar, 3 * D), F32),
        ((ar, D), F32),
        ((2, ar), F32),
        ((2, ar), F32),
        ((ar, 2, MEM), F32),
        ((wr, D), F32),
        ((wr, D), F32),
    ]
    anywhere = pl.BlockSpec(memory_space=pl.ANY)
    return pl.pallas_call(
        functools.partial(unpack_kernel, sh),
        name="unpack",
        out_shape=[jax.ShapeDtypeStruct(*one) for one in shapes],
        in_specs=[anywhere] * 5,
        out_specs=[anywhere] * len(shapes),
        scratch_shapes=[pltpu.VMEM(a.shape, a.dtype) for a in arrays]
        + [pltpu.VMEM(*one) for one in shapes]
        + [pltpu.SemaphoreType.DMA((15,))],
        compiler_params=pltpu.CompilerParams(vmem_limit_bytes=64 * 2**20 - 2**17),
    )(*arrays)


def body(
    sh,
    hidden_in,
    reset,
    w_qkv,
    w_attn_out,
    norm_gains,
    norm_biases,
    memory_tokens,
    w_in,
    w_out,
    grad_hidden,
    grad_memory,
):
    arrays = (
        hidden_in,
        grad_hidden,
        grad_memory.transpose(1, 0, 2),
        w_qkv,
        w_attn_out,
        norm_gains,
        norm_biases,
        memory_tokens.transpose(2, 0, 1),
        w_in,
        w_out.T,
    )
    hidden, memory, *middle, tokens, gi, gt = unpack(sh, *layer(sh, arrays))
    return hidden, memory.transpose(1, 0, 2), *middle, tokens.transpose(1, 2, 0), gi, gt.T


def solution(mesh):
    sh = Shape(mesh.shape["dp"])
    return jax.shard_map(
        functools.partial(body, sh),
        mesh=mesh,
        in_specs=(
            P("dp", "tp", None),
            P("dp"),
            P(("dp", "tp"), None),
            P(("dp", "tp"), None),
            P(None, ("dp", "tp")),
            P(None, ("dp", "tp")),
            P(None, None, ("dp", "tp")),
            P("dp", "tp"),
            P("tp", "dp"),
            P("dp", "tp", None),
            P("dp", "tp", None),
        ),
        out_specs=(
            P("dp", "tp", None),
            P("dp", "tp", None),
            P("dp", "tp", None),
            P(("dp", "tp"), None),
            P(("dp", "tp"), None),
            P(None, ("dp", "tp")),
            P(None, ("dp", "tp")),
            P(None, None, ("dp", "tp")),
            P("dp", "tp"),
            P("tp", "dp"),
        ),
        check_vma=False,
    )
```

```python
import functools
import types

import jax
import jax.numpy as jnp
import numpy as np
from jax import lax
from jax.experimental import pallas as pl
from jax.experimental.pallas import tpu as pltpu
from jax.sharding import PartitionSpec as P

D = 768
HALF = 384
MEM = 10
TOKENS = 64
OWN = 272
ROWS = 2 * OWN
TP = 4
SMALL = 128
ACOLS = 4 * HALF + SMALL
REST = ACOLS - HALF
CUT = HALF + 640
WO = 3 * HALF
EPSILON = 1e-05
INV_ROOT_TWO = 0.7071067811865476
INV_ROOT_TWOPI = 0.3989422804014327
EXP_SCALE = 0.125 * 1.4426950408889634
MASKED = -1e30
F32 = jnp.float32
BF16 = jnp.bfloat16
MESH = pl.DeviceIdType.MESH
NN = (((1,), (0,)), ((), ()))
NT = (((1,), (1,)), ((), ()))
TN = (((0,), (0,)), ((), ()))


def dot(a, b, dims=NN):
    return lax.dot_general(a, b, dims, preferred_element_type=F32)


def up16(n):
    return -(-n // 16) * 16


class Shape:
    def __init__(self, dp):
        self.dp = dp
        planes = dp // 2
        self.ny = int(round(planes**0.5))
        self.nz = planes // self.ny
        self.wrows = D // dp
        self.arows = D // (dp * TP)
        self.brows = 2 * self.wrows
        self.pr = up16(self.arows)
        self.xrows = 2 * self.arows * self.ny
        self.pc = -(-self.arows // 8) * 8
        self.fr = up16(self.wrows)


def selections(sh):
    pack = np.zeros((sh.brows, TP * 2 * sh.pc), np.float32)
    for c in range(2):
        for x in range(TP):
            for i in range(sh.arows):
                pack[c * sh.wrows + x * sh.arows + i, (x * 2 + c) * sh.pc + i] = 1
    packy = np.zeros((sh.xrows, sh.ny * 2 * sh.pc), np.float32)
    turn = np.zeros((D, D), np.float32)
    ar = sh.arows
    for c in range(2):
        for y in range(sh.ny):
            for i in range(ar):
                row = (y * 2 + c) * ar + i
                packy[row, (y * 2 + c) * sh.pc + i] = 1
                for x in range(TP):
                    for z in range(sh.nz):
                        place = (z * sh.ny + y) * sh.brows + (c * TP + x) * ar + i
                        turn[(x * sh.nz + z) * sh.xrows + row, place] = 1
    small = np.zeros((48, SMALL), np.float32)
    for i in range(4):
        small[i, i] = 1
    for kind in range(2):
        for i in range(MEM):
            small[16 + 16 * kind + (i // 5) * 8 + i % 5, 4 + MEM * kind + i] = 1
    places = np.zeros((4, MEM, SMALL), np.float32)
    for kind, (rows, first) in enumerate(((2, 0), (2, 2), (MEM, 4), (MEM, 4 + MEM))):
        for i in range(rows):
            places[kind, i, first + i] = 1
    return pack, small, places, packy, turn


def norm_forward(inputs, gain, offset):
    centred = inputs - jnp.mean(inputs, -1, keepdims=True)
    spread = jnp.mean(centred * centred, -1, keepdims=True)
    inverse = lax.rsqrt(spread + EPSILON)
    normed = centred * inverse
    return normed * gain + offset, normed, inverse


def norm_backward(upstream, normed, inverse, gain):
    scaled = upstream * gain
    first_mean = jnp.mean(scaled, -1, keepdims=True)
    second_mean = jnp.mean(scaled * normed, -1, keepdims=True)
    return inverse * (scaled - first_mean - normed * second_mean)


def column_sum(a):
    return jnp.sum(a, 0, keepdims=True)


XBASE = (0, 4, 8, 10, 14, 16, 20)
SENDS = 40
STAGED, LANDED, SUMMED, PASSED, UPDATED = range(5)


def scratch_of(sh):
    nz, ny, br = sh.nz, sh.ny, sh.brows
    ar, wr = sh.arows, sh.wrows
    operands = [
        (5, 2, D),
        (ar, 3 * D),
        (ar, D),
        (2, ar),
        (2, ar),
        (ar, 2, MEM),
        (wr, D),
        (wr, D),
        (br, TP * 2 * sh.pc),
        (48, SMALL),
        (4, MEM, SMALL),
        (sh.xrows, ny * 2 * sh.pc),
    ]
    jobs = {(STAGED, i, 0): (dims, BF16) for i, dims in enumerate(operands)}
    s = dict(
        pk=((2, sh.pr, ACOLS), BF16),
        ff=((2, sh.fr, D), BF16),
        gms=((2, 8, D), F32),
        p1=((2, sh.pr, ACOLS), BF16),
        p2=((TP, 2 * sh.pc, REST), BF16),
        p2y=((ny, 2 * sh.pc, HALF), BF16),
        turn=((D, D), BF16),
        xp=((ROWS, D), BF16),
        wx=((TP, nz, sh.xrows, HALF), BF16),
        gx=((TP, nz, sh.xrows, HALF), BF16),
        f1=((2, sh.fr, D), BF16),
        wa=((nz, ny, br, ACOLS), BF16),
        wf=((TP, nz, ny, br, D), BF16),
        wo=((2, nz, ny, br, HALF), BF16),
        par=((8, D), F32),
        x=((ROWS, D), BF16),
        gyt=((TP * TOKENS, D), BF16),
        gm=((2, 8, D), F32),
        qkv=((9, ROWS, 128), BF16),
        pt=((6, ROWS, ROWS), BF16),
        ot=((3, 128, ROWS), BF16),
        oc=((ROWS, HALF), BF16),
        oin=((OWN, HALF), BF16),
        h1=((OWN, D), F32),
        n1=((OWN, D), F32),
        inv1=((OWN, 1), F32),
        h1b=((ROWS, D), BF16),
        gl=((2, ROWS, D), BF16),
        sl=((2, ROWS, D), BF16),
        fs=((OWN, D), BF16),
        fr=((OWN, D), BF16),
        n2=((OWN, D), F32),
        yb=((OWN, D), BF16),
        mo=((2, 8, D), F32),
        hop=((16, D), BF16),
        hopin=((16, D), BF16),
        es=((16, D), F32),
        er=((16, D), F32),
        dz=((OWN, D), F32),
        dfb=((ROWS, D), BF16),
        du=((2, ROWS, D), BF16),
        dhs=((OWN, D), BF16),
        dhr=((OWN, D), BF16),
        dr=((OWN, D), F32),
        dab=((ROWS, D), BF16),
        doc=((3, ROWS, 128), BF16),
        dqkv=((9, ROWS, 128), BF16),
        ga=((nz, ny, br, ACOLS), BF16),
        gi=((TP, nz, ny, br, HALF), BF16),
        gt=((TP, nz, ny, br, HALF), BF16),
        dxs=((OWN, D), BF16),
        dxr=((OWN, D), BF16),
        dxb=((TP * TOKENS, D), BF16),
        sg=((48, D), F32),
        e3=((TP, 2 * sh.pc, REST), BF16),
        r3=((TP - 1, 2 * sh.pc, REST), BF16),
        e3y=((ny, 2 * sh.pc, HALF), BF16),
        r3y=((max(1, ny - 1), 2 * sh.pc, HALF), BF16),
        s4=((2, sh.pc, ACOLS), F32),
        sf=((2, sh.wrows, D), F32),
    )
    s.update(gos=((nz // 2, ny, br, HALF) if nz > 1 else (1, 1, HALF, HALF), BF16))
    sizes = {"x": TP, "z": nz, "y": ny}
    for name, order, cols, axes in scatter_jobs():
        left = [a for a in axes]
        block = (sh.xrows if name[0] == "x" else br, cols.stop - cols.start)
        for step, axis in enumerate(order):
            left = [a for a in left if a != axis]
            dims = tuple(sizes[a] for a in left)
            ring = step == 0 and name in RINGS and sizes[axis] == 4
            jobs[LANDED, step, name] = ((2 if ring else max(1, sizes[axis] - 1),) + dims + block, BF16)
            if step < len(order) - 1:
                jobs[SUMMED, step, name] = (dims + block, BF16)
            if ring:
                jobs[PASSED, 0, name] = ((2, dims[0] // 2) + dims[1:] + block, BF16)
                jobs[UPDATED, 0, name] = jobs[PASSED, 0, name]
    return s, jobs


def scatter_jobs():
    orders = [("z", "y", "x"), ("x", "z", "y"), ("y", "x", "z")]
    jobs = []
    for kind in ("t", "i"):
        for j in range(3):
            jobs.append((f"{kind}{j}", orders[j], slice(128 * j, 128 * j + 128), ("x", "z", "y")))
    zy, yz = ("z", "y"), ("y", "z")
    jobs.append(("aw", yz, slice(WO, WO + HALF), zy))
    jobs.append(("x0", ("x", "z"), slice(0, HALF), ("x", "z")))
    jobs.append(("a1", zy, slice(HALF, 2 * HALF), zy))
    jobs.append(("a2", yz, slice(2 * HALF, 2 * HALF + 256), zy))
    jobs.append(("a3", zy, slice(2 * HALF + 256, 3 * HALF), zy))
    jobs.append(("as", zy, slice(4 * HALF, ACOLS), zy))
    return jobs


def gather_jobs():
    orders = [("x", "y", "z"), ("y", "z", "x"), ("z", "x", "y")]
    jobs = [(f"f{j}", orders[j], slice(256 * j, 256 * j + 256), ("x", "z", "y")) for j in range(3)]
    jobs.append(("x0", ("z", "x"), slice(0, HALF), ("x", "z")))
    jobs.append(("a0", ("y", "z"), slice(HALF, CUT), ("z", "y")))
    jobs.append(("a1", ("z", "y"), slice(CUT, ACOLS), ("z", "y")))
    return jobs


RINGS = ("t0", "t1", "t2", "i0", "i1", "i2", "aw", "x0", "a1")
WEIGHTS = {"f": "wf", "a": "wa", "x": "wx"}
GRADS = {"t": "gt", "i": "gi", "a": "ga", "x": "gx"}


def kernel(sh, names, *refs):
    xin, gin = refs[:2]
    hout, mout, dxo, gao, gfo = refs[15:20]
    ssem, rsem, xsem, lsem = refs[-4:]
    count = len(names[0])
    b = types.SimpleNamespace(**dict(zip(names[0], refs[20 : 20 + count])))
    k = dict(zip(names[1], refs[20 + count : -4]))
    staged = [k[STAGED, i, 0] for i in range(12)]
    gmem, wq, wp, gain_in, bias_in, token_in, up_in, down_in = staged[:8]
    packsel, smallsel, places, packy = staged[8:]
    turn = refs[14]
    nz, ny, br, wr, ar = sh.nz, sh.ny, sh.brows, sh.wrows, sh.arows
    pk, ff, gms = b.pk, b.ff, b.gms

    dp = lax.axis_index("dp")
    x = lax.axis_index("tp")
    core = dp % 2
    y = (dp // 2) % ny
    z = dp // (2 * ny)
    other = 1 - core
    chain = x // 2
    seg = jnp.where((x == 1) | (x == 2), 1, 0)
    at = {"x": x, "y": y, "z": z}
    size = {"x": TP, "y": ny, "z": nz}

    def device(x_=x, y_=y, z_=z, c_=core):
        return ((z_ * ny + y_) * 2 + c_, x_)

    near = {a: [(at[a] + o) % size[a] for o in range(size[a])] for a in at}

    def moved_to(axis, offset, core_=core):
        there = dict(at)
        there[axis] = near[axis][offset]
        return device(there["x"], there["y"], there["z"], core_)

    neighbours = {a: [moved_to(a, o) for o in range(size[a])] for a in at}

    def moved(axis, offset):
        return neighbours[axis][offset]

    sibling = device(c_=other)
    sent = []

    class Group:
        def __init__(self, like):
            if len(sent) >= SENDS:
                sent[-SENDS].wait_send()
            self.like = like
            self.number = len(sent)
            sent.append(self)

        def add(self, src, dst, to):
            pltpu.make_async_remote_copy(
                src_ref=src,
                dst_ref=dst,
                send_sem=ssem.at[self.number % SENDS],
                recv_sem=rsem.at[self.number],
                device_id=to,
                device_id_type=MESH,
            ).start()

        def wait_send(self):
            like = self.like()
            pltpu.make_async_copy(like, like, ssem.at[self.number % SENDS]).wait()

        def wait_recv(self):
            like = self.like()
            pltpu.make_async_copy(like, like, rsem.at[self.number]).wait()

    def remote(src, dst, to):
        where = dst if callable(dst) else lambda: dst
        group = Group(where)
        group.add(src, where(), to)
        return group

    def arrived(groups):
        for group in groups:
            group.wait_recv()

    locals_ = [0]

    def local(src, dst):
        copy = pltpu.make_async_copy(src, dst, lsem.at[locals_[0]])
        locals_[0] += 1
        copy.start()
        return copy

    staging = [local(refs[2 + i], staged[i]) for i in range(12)]
    turn_local = local(turn, b.turn)

    barrier = pltpu.get_barrier_semaphore()
    peers = [sibling]
    for o in range(1, TP):
        peers += [moved("x", o), moved_to("x", o, other)]
    for axis in ("y", "z"):
        for o in range(1, size[axis]):
            peers.append(moved(axis, o))
    for peer in peers:
        pl.semaphore_signal(barrier, inc=1, device_id=peer, device_id_type=MESH)

    pk[...] = jnp.zeros(pk.shape, BF16)
    ff[...] = jnp.zeros(ff.shape, BF16)
    gms[...] = jnp.zeros(gms.shape, F32)
    for copy in staging:
        copy.wait()
    small = dot(gain_in[...], places[0, :2], TN) + dot(bias_in[...], places[1, :2], TN)
    small = small + dot(token_in[:, 0], places[2]) + dot(token_in[:, 1], places[3])
    small = small.astype(BF16)
    for h in range(2):
        for p in range(3):
            for i in range(3):
                first = D * i + HALF * h + 128 * p
                pk[h, :ar, HALF * p + 128 * i : HALF * p + 128 * (i + 1)] = wq[:, first : first + 128]
        pk[h, :ar, WO : WO + HALF] = wp[:, HALF * h : HALF * (h + 1)]
        pk[h, :ar, 4 * HALF :] = small
        for j in range(3):
            cols = slice(HALF * h + 128 * j, HALF * h + 128 * (j + 1))
            ff[h, :wr, 256 * j : 256 * j + 128] = up_in[:, cols]
            ff[h, :wr, 256 * j + 128 : 256 * j + 256] = down_in[:, cols]
        gms[h, 0:5] = gmem[:, h].astype(F32)
    pl.semaphore_wait(barrier, len(peers))

    pk_local = local(pk.at[core], b.p1.at[core])
    ff_local = local(ff.at[core], b.f1.at[core])
    pk_swap = remote(pk.at[other], b.p1.at[core], sibling)
    ff_swap = remote(ff.at[other], b.f1.at[core], sibling)

    conditional = []

    def to_device(src, dst, place, here, kind, send_slot):
        copy = pltpu.make_async_remote_copy(
            src_ref=src,
            dst_ref=dst,
            send_sem=xsem.at[25 + XBASE[kind] + send_slot],
            recv_sem=here,
            device_id=device(x_=place[0], c_=place[1]),
            device_id_type=MESH,
        )
        same = (place[0] == x) & (place[1] == core)

        @pl.when(same)
        def _():
            pltpu.make_async_copy(src, dst, here).start()

        @pl.when(jnp.logical_not(same))
        def _():
            copy.start()

        conditional.append((same, copy))

    def from_device(dst, kind, slot):
        pltpu.make_async_copy(dst, dst, xsem.at[XBASE[kind] + slot]).wait()

    def chip_of(k, s):
        return s + k * (3 - 2 * s)

    def send_rows():
        for s in range(2):
            for j in range(2):
                to_device(
                    xin.at[s, pl.ds(TOKENS * j, TOKENS)],
                    b.x.at[pl.ds(pl.multiple_of(OWN * j + TOKENS * x, 16), TOKENS)],
                    (chip_of(core, s), j),
                    xsem.at[XBASE[0] + x],
                    0,
                    2 * s + j,
                )

    def send_upstream():
        for s in range(2):
            for j in range(2):
                to_device(
                    gin.at[s, pl.ds(TOKENS * j, TOKENS)],
                    b.gyt.at[pl.ds(pl.multiple_of(TOKENS * x, 16), TOKENS)],
                    (chip_of(core, s), j),
                    xsem.at[XBASE[1] + x],
                    1,
                    2 * s + j,
                )
            to_device(
                gms.at[s], b.gm.at[x % 2], (chip_of(core, s), x // 2), xsem.at[XBASE[2] + x % 2], 2, s
            )

    def part_of(job, step, place, half=None):
        name, order, cols, axes = job
        fixed = {a: at[a] for a in order[step:]}
        fixed[order[step]] = place
        where = []
        for a in axes:
            if a in fixed:
                where.append(fixed[a])
            elif half is not None:
                where.append(pl.ds(half * (size[a] // 2), size[a] // 2))
                half = None
            else:
                where.append(slice(None))
        return getattr(b, WEIGHTS[name[0]]).at[tuple(where) + (slice(None), cols)]

    def gather_start(name, step):
        job = gathers[name]
        axis = job[1][step]
        n = size[axis]
        own = part_of(job, step, at[axis])
        free = [a for a in job[3] if a not in job[1][step:]]
        relay = n == 4 and step == len(job[1]) - 1 and size[free[0]] % 2 == 0
        state = types.SimpleNamespace(step=step, relay=relay)
        if relay:
            first = [part_of(job, step, at[axis], h) for h in range(2)]
            right, left = moved(axis, 1), moved(axis, n - 1)
            state.right, state.left = (
                remote(first[h], lambda h=h: part_of(job, step, at[axis], h), to) for h, to in ((0, right), (1, left))
            )
            state.every = [Group(lambda: part_of(job, step, pl.ds(0, 2)))]
            state.every[0].add(first[1], first[1], right)
            state.every[0].add(first[0], first[0], left)
        else:
            state.every = [Group(lambda: part_of(job, step, pl.ds(0, n - 1)))] if n > 1 else []
            for o in range(1, n):
                state.every[0].add(own, own, moved(axis, o))
        flying[name] = state

    def gather_pass(name):
        job, state = gathers[name], flying[name]
        if not state.relay:
            return
        axis = job[1][state.step]
        n = size[axis]
        for copy, back, onward, half in ((state.right, n - 1, 1, 0), (state.left, 1, n - 1, 1)):
            arrived([copy])
            piece = part_of(job, state.step, near[axis][back], half)
            state.every[0].add(piece, piece, moved(axis, onward))

    def gather_done(name):
        arrived(flying[name].every)

    gathers = {j[0]: j for j in gather_jobs()}
    flying = {}

    pk_local.wait()
    arrived([pk_swap])
    packed = jnp.concatenate([b.p1[c].astype(F32)[: sh.pc] for c in range(2)], 0).astype(BF16)
    b.p2y[y] = packed[:, :HALF]
    b.p2[x] = packed[:, HALF:]
    mine = b.p2y.at[y]
    ysteps, xsteps = [], [Group(lambda: b.p2.at[: TP - 1])]
    if ny > 1:
        ysteps.append(Group(lambda: b.p2y.at[: ny - 1]))
    for o in range(1, ny):
        ysteps[0].add(mine, mine, moved("y", o))
    mine = b.p2.at[x]
    for o in range(1, TP):
        xsteps[0].add(mine, mine, moved("x", o))
    ff_local.wait()
    arrived([ff_swap])
    two = [b.f1[c].astype(F32)[:wr] for c in range(2)]
    b.wf[x, z, y] = jnp.concatenate(two, 0).astype(BF16)
    feed_names, first_names = ("f1", "f2", "f0"), ("x0", "a0", "a1")
    for n in feed_names:
        gather_start(n, 0)
    send_rows()
    arrived(ysteps)
    b.wx[x, z] = dot(packy[...], b.p2y[...].reshape(ny * 2 * sh.pc, HALF)).astype(BF16)
    gather_start("x0", 0)
    arrived(xsteps)
    b.wa[z, y, :, HALF:] = dot(packsel[...], b.p2[...].reshape(TP * 2 * sh.pc, REST)).astype(BF16)
    for n in ("a0", "a1"):
        gather_start(n, 0)
    for n in feed_names:
        gather_done(n)
        gather_start(n, 1)
    for n in first_names:
        gather_done(n)
        gather_start(n, 1)
    for n in first_names:
        gather_pass(n)
    for n in feed_names:
        gather_done(n)
        gather_start(n, 2)

    for i in range(TP):
        from_device(b.x.at[pl.ds(pl.multiple_of(OWN * core + TOKENS * i, 16), TOKENS)], 0, i)
    half = b.x.at[pl.ds(pl.multiple_of(OWN * core, 16), TP * TOKENS)]
    x_swap = remote(half, half, sibling)
    for first in (256, OWN + 256):
        b.x[first : first + 16] = jnp.zeros((16, D), BF16)
    turn_local.wait()
    arrived([x_swap])

    @pl.loop(0, 2)
    def _(i):
        rows = pl.ds(pl.multiple_of(OWN * i, 16), OWN)
        b.xp[rows] = dot(b.x[rows], b.turn[...], NT).astype(BF16)

    for n in first_names:
        gather_done(n)
    wo_cols = slice(WO, WO + HALF)
    wo_local = local(b.wa.at[:, :, :, wo_cols], b.wo.at[core])
    wo_swap = remote(b.wa.at[:, :, :, wo_cols], b.wo.at[core], sibling)
    gather_pass("f1")
    send_upstream()

    def attention_weight():
        return b.wa[:, :, :, :WO].reshape(D, WO)

    small = b.wa[:, :, :, 4 * HALF :].reshape(D, SMALL)
    chosen = dot(smallsel[...], small, NT)
    b.par[...] = chosen[0:8]
    memory = chosen[16:48].astype(BF16)
    b.x[OWN + 256 : OWN + 272] = memory[16:]
    turned = dot(memory, b.turn[...], NT).astype(BF16)
    b.xp[OWN + 256 : OWN + 272] = turned[16:]

    @pl.when(seg == 0)
    def _():
        b.x[256:272] = memory[:16]
        b.xp[256:272] = turned[:16]

    gains = [b.par[i : i + 1] for i in range(2)]
    biases = [b.par[2 + i : 3 + i] for i in range(2)]

    hop_to = jnp.where(x == 0, 1, 2)
    hops = []
    for j in range(2):
        hops.append(
            pltpu.make_async_remote_copy(
                src_ref=b.hop,
                dst_ref=b.hopin,
                send_sem=xsem.at[XBASE[6] + j],
                recv_sem=xsem.at[XBASE[6] + 2],
                device_id=device(x_=hop_to, c_=j),
                device_id_type=MESH,
            )
        )

    own_rows = pl.ds(pl.multiple_of(OWN * core, 16), OWN)
    other_rows = pl.ds(pl.multiple_of(OWN * other, 16), OWN)

    out = dot(b.xp[...], b.wx[...].reshape(D, HALF)).astype(BF16)
    for i in range(3):
        b.qkv[i] = out[:, 128 * i : 128 * i + 128]
    out = dot(b.x[...], b.wa[:, :, :, HALF:WO].reshape(D, 2 * HALF)).astype(BF16)
    for i in range(3, 9):
        b.qkv[i] = out[:, 128 * (i - 3) : 128 * (i - 2)]

    def head_masks(hh):
        lane = lax.broadcasted_iota(jnp.int32, (ROWS, 128), 1)
        row = lax.broadcasted_iota(jnp.int32, (ROWS, 128), 0)
        inside = (lane // 64) == hh
        spare = lane == 64 * (1 - hh)
        memory = ((row >= 256) & (row < 272)) | (row >= OWN + 256)
        invalid = memory & (row % 8 >= 5)
        return inside, spare, invalid

    def forward_pair(p):
        qp, kp, vp = (b.qkv[3 * p + i] for i in range(3))
        vt = vp.T
        for hh in range(2):
            inside, spare, invalid = head_masks(hh)
            zero = jnp.zeros_like(kp)
            kmask = jnp.where(spare & invalid, jnp.full_like(kp, MASKED), zero)
            km = jnp.where(inside, kp, kmask)
            qm = jnp.where(inside, qp, jnp.where(spare, jnp.ones_like(qp), zero))
            scores = dot(km, qm, NT)
            peak = jnp.max(scores, 0, keepdims=True)
            raised = jnp.exp2((scores - peak) * EXP_SCALE)
            total = jnp.sum(raised, 0, keepdims=True)
            probs = (raised * (1.0 / total)).astype(BF16)
            b.pt[2 * p + hh] = probs
            b.ot[p, 64 * hh : 64 * hh + 64] = dot(vt[64 * hh : 64 * hh + 64], probs).astype(BF16)
        b.oc[:, pl.ds(pl.multiple_of(128 * p, 128), 128)] = b.ot[p].T

    @pl.loop(0, 3)
    def _(j):
        cols = pl.ds(pl.multiple_of(128 * j, 128), 128)
        block = dot(b.turn[...], b.wx[:, :, :, cols].reshape(D, 128), TN).astype(BF16)
        b.wa[:, :, :, cols] = block.reshape(nz, ny, br, 128)

    @pl.loop(0, 6)
    def _(i):
        @pl.when((i // 3) == seg)
        def _():
            forward_pair(i % 3)

        @pl.when(i == 1)
        def _():
            for n in ("f2", "f0"):
                gather_pass(n)

        @pl.when((i == 2) & (seg == 1))
        def _():
            hops[0].wait_recv()
            b.x[256:272] = b.hopin[...]
            b.xp[256:272] = dot(b.hopin[...], b.turn[...], NT).astype(BF16)
            rows = dot(b.hopin[...], attention_weight()).astype(BF16)
            for j in range(9):
                b.qkv[j, 256:272] = rows[:, 128 * j : 128 * j + 128]

    def head_rows(ref, c):
        if nz > 1:
            return ref.at[pl.ds(c * (nz // 2), nz // 2)]
        return ref.at[:, :, pl.ds(pl.multiple_of(c * HALF, 16), HALF)]

    def wo_rows(h, c):
        return head_rows(b.wo.at[h], c)[...].reshape(HALF, HALF)

    o_swap = remote(b.oc.at[other_rows], b.oin, sibling)
    wo_local.wait()
    arrived([wo_swap])
    halves = [dot(b.oc[own_rows], wo_rows(h, core)) for h in range(2)]
    arrived([o_swap])
    attended = jnp.concatenate([halves[h] + dot(b.oin[...], wo_rows(h, other)) for h in range(2)], 1)
    h1, n1, inv1 = norm_forward(b.x[own_rows].astype(F32) + attended, gains[0], biases[0])
    b.h1[...] = h1
    b.n1[...] = n1
    b.inv1[...] = inv1
    b.h1b[own_rows] = h1.astype(BF16)
    h_swap = remote(b.h1b.at[own_rows], b.h1b.at[own_rows], sibling)
    for n in ("f1", "f2", "f0"):
        gather_done(n)

    def feed_weight(t, kind):
        cols = [256 * j + 128 * kind for j in range(3)]
        blocks = [b.wf[2 * t + i, :, :, :, c : c + 128].reshape(D, 128) for i in range(2) for c in cols]
        return jnp.concatenate(blocks, 1)

    def up_weight(t):
        return feed_weight(t, 0)

    def down_weight(t):
        return feed_weight(t, 1)

    def activate(units):
        erf = 0.5 * (1.0 + lax.erf(units * INV_ROOT_TWO))
        return (units * erf).astype(BF16), erf

    early = pltpu.make_async_remote_copy(
        src_ref=b.es,
        dst_ref=b.er,
        send_sem=xsem.at[XBASE[6] + 3],
        recv_sem=xsem.at[XBASE[6] + 4],
        device_id=sibling,
        device_id_type=MESH,
    )
    row16 = lax.broadcasted_iota(jnp.int32, (16, D), 0)

    @pl.when(seg == 0)
    def _():
        arrived([h_swap])
        rows = b.h1b[OWN + 256 : OWN + 272]
        part = sum(dot(activate(dot(rows, up_weight(t)))[0], down_weight(t), NT) for t in range(2))

        @pl.when(core == 0)
        def _():
            b.es[...] = part
            early.start()

        @pl.when(core == 1)
        def _():
            early.wait_recv()
            whole = b.h1[256:272] + part + b.er[...]
            written = norm_forward(whole, gains[1], biases[1])[0]
            b.hop[...] = jnp.where(row16 % 8 < 5, written, 0.0).astype(BF16)
            hops[0].start()
            hops[1].start()

    def project_up(rows):
        for t in range(2):
            units = dot(b.h1b[rows], up_weight(t))
            active, erf = activate(units)
            b.gl[t, rows] = active
            b.sl[t, rows] = (erf + units * jnp.exp(-0.5 * units * units) * INV_ROOT_TWOPI).astype(BF16)

    @pl.loop(0, 2)
    def _(i):
        @pl.when((i == 1) & (seg == 1))
        def _():
            arrived([h_swap])

        project_up(pl.ds(pl.multiple_of(OWN * jnp.where(i == 0, core, other), 16), OWN))


    def partial_down(rows):
        return sum(dot(b.gl[t, rows], down_weight(t), NT) for t in range(2))

    b.fs[...] = partial_down(other_rows).astype(BF16)
    f_swap = remote(b.fs, b.fr, sibling)
    branch = partial_down(own_rows)
    arrived([f_swap])
    out, n2, inv2 = norm_forward(b.h1[...] + branch + b.fr[...].astype(F32), gains[1], biases[1])
    low = out.astype(BF16)
    b.yb[...] = low
    b.mo[...] = low[256:272].astype(F32).reshape(2, 8, D)
    for i in range(TP):
        to_device(
            b.yb.at[pl.ds(TOKENS * i, TOKENS)],
            hout.at[seg, pl.ds(pl.multiple_of(TOKENS * core, 16), TOKENS)],
            (i, chain),
            xsem.at[XBASE[3] + 2 * seg + core],
            3,
            i,
        )
    for i in range(2):
        to_device(b.mo.at[i], mout.at[seg], (2 * core + i, chain), xsem.at[XBASE[4] + seg], 4, i)

    for i in range(TP):
        from_device(b.gyt.at[pl.ds(TOKENS * i, TOKENS)], 1, i)
    for i in range(2):
        from_device(b.gm.at[i], 2, i)
    upstream = jnp.concatenate([b.gyt[...].astype(F32), b.gm[...].reshape(16, D)], 0)
    b.sg[...] = jnp.zeros((48, D), F32)
    b.sg[1:2] = column_sum(upstream * n2)
    b.sg[3:4] = column_sum(upstream)
    dz = norm_backward(upstream, n2, inv2, gains[1])
    b.dz[...] = dz
    b.dfb[own_rows] = dz.astype(BF16)
    df_swap = remote(b.dfb.at[own_rows], b.dfb.at[own_rows], sibling)

    def weight_grad(into, left, right):
        @pl.loop(0, 2)
        def _(t):
            part = dot(left[...], right[t], TN).astype(BF16)
            for i in range(2):
                into[2 * t + i] = part[:, HALF * i : HALF * (i + 1)].reshape(nz, ny, br, HALF)

    scatters = {j[0]: j for j in scatter_jobs()}
    rs = {}

    def is_ring(name, step):
        _, order, cols, axes = scatters[name]
        return step == 0 and name in RINGS and size[order[0]] == 4

    def source_of(name, step):
        _, order, cols, axes = scatters[name]
        axis = order[step]
        left = [a for a in axes if a not in order[:step]]
        array = getattr(b, GRADS[name[0]]) if step == 0 else k[SUMMED, step - 1, name]
        tail = (slice(None), cols) if step == 0 else ()

        def part(place, half=None):
            where = []
            for a in left:
                if a == axis:
                    where.append(place)
                elif half is not None:
                    where.append(pl.ds(half * (size[a] // 2), size[a] // 2))
                    half = None
                else:
                    where.append(slice(None))
            return array.at[tuple(where) + tail]

        return part

    def scatter_send(name, step):
        axis = scatters[name][1][step]
        n = size[axis]
        part = source_of(name, step)
        landing = k[LANDED, step, name]
        if is_ring(name, step):
            right, left, far = (near[axis][o] for o in (1, n - 1, 2))
            to_right, to_left = moved(axis, 1), moved(axis, n - 1)
            half = size[[a for a in scatters[name][3] if a != axis][0]] // 2
            over = k[PASSED, 0, name]
            passing = [
                remote(part(far, 0), lambda: over.at[0], to_right),
                remote(part(far, 1), lambda: over.at[1], to_left),
            ]
            coming = Group(lambda: landing)
            coming.add(part(right, 1), landing.at[0, half:], to_right)
            coming.add(part(left, 0), landing.at[1, :half], to_left)
            rs[name] = (passing, coming, half, (right, left), (to_right, to_left))
            return
        rs[name] = [Group(lambda: landing)] if n > 1 else []
        for o in range(1, n):
            rs[name][0].add(part(near[axis][o]), landing.at[o - 1], moved(axis, o))

    def scatter_pass(name):
        if not is_ring(name, 0):
            return
        passing, coming, half, places_, devices = rs[name]
        part = source_of(name, 0)
        landing, over, updated = k[LANDED, 0, name], k[PASSED, 0, name], k[UPDATED, 0, name]
        for i in range(2):
            arrived([passing[i]])
            updated[i] = (part(places_[i], i)[...].astype(F32) + over[i].astype(F32)).astype(BF16)
            where = landing.at[0, :half] if i == 0 else landing.at[1, half:]
            coming.add(updated.at[i], where, devices[i])

    def scatter_sum(name, step):
        _, order, cols, axes = scatters[name]
        axis = order[step]
        total = source_of(name, step)(at[axis])[...].astype(F32)
        ring = is_ring(name, step)
        arrived([rs[name][1]] if ring else rs[name])
        for o in range(2 if ring else size[axis] - 1):
            total = total + k[LANDED, step, name][o].astype(F32)
        if step < len(order) - 1:
            k[SUMMED, step, name][...] = total.astype(BF16)
        return total

    def scatter_on(names, step):
        for n in names:
            scatter_sum(n, step)
            scatter_send(n, step + 1)

    down_names, up_names = ("t0", "t1", "t2"), ("i0", "i1", "i2")
    def units_back(rows):
        for t in range(2):
            b.du[t, rows] = (dot(b.dfb[rows], down_weight(t)) * b.sl[t, rows].astype(F32)).astype(BF16)

    units_back(own_rows)
    arrived([df_swap])
    weight_grad(b.gt, b.dfb, b.gl)
    for n in down_names:
        scatter_send(n, 0)
    units_back(other_rows)

    def partial_up(rows):
        return sum(dot(b.du[t, rows], up_weight(t), NT) for t in range(2))

    b.dhs[...] = partial_up(other_rows).astype(BF16)
    dh_swap = remote(b.dhs, b.dhr, sibling)
    b.dz[...] = b.dz[...] + partial_up(own_rows)
    weight_grad(b.gi, b.h1b, b.du)
    for n in up_names:
        scatter_send(n, 0)
    for n in down_names:
        scatter_pass(n)
    arrived([dh_swap])
    into_first = b.dz[...] + b.dhr[...].astype(F32)
    b.sg[0:1] = column_sum(into_first * b.n1[...])
    b.sg[2:3] = column_sum(into_first)
    dr = norm_backward(into_first, b.n1[...], b.inv1[...], gains[0])
    b.dr[...] = dr
    b.dab[own_rows] = dr.astype(BF16)
    da_swap = remote(b.dab.at[own_rows], b.dab.at[own_rows], sibling)

    def grad_mixed(rows):
        parts = [dot(b.dab[rows, HALF * h : HALF * (h + 1)], wo_rows(h, core), NT) for h in range(2)]
        for p in range(3):
            b.doc[p, rows] = (parts[0] + parts[1])[:, 128 * p : 128 * p + 128].astype(BF16)

    grad_mixed(own_rows)
    arrived([da_swap])
    grad_mixed(other_rows)

    mixed_t = b.ot[...].reshape(HALF, ROWS)

    def proj_grad(h):
        cols = pl.ds(pl.multiple_of(HALF * h, 128), HALF)
        return dot(mixed_t, b.dab[:, cols]).astype(BF16).reshape(b.gos.shape)

    def wo_part(c):
        return head_rows(b.ga.at[:, :, :, wo_cols], c)

    b.gos[...] = proj_grad(other)
    go_swap = remote(b.gos, wo_part(core), sibling)
    wo_part(core)[...] = proj_grad(core)

    def backward_pair(p):
        qp, kp, vp = (b.qkv[3 * p + i] for i in range(3))
        dop = b.doc[p]
        kt = kp.T
        dv = dk = 0.0
        dq = []
        for hh in range(2):
            inside, _, _ = head_masks(hh)
            zero = jnp.zeros_like(kp)
            grad_probs = dot(jnp.where(inside, vp, zero), dop, NT)
            low_probs = b.pt[2 * p + hh]
            probs = low_probs.astype(F32)
            row_term = jnp.sum(probs * grad_probs, 0, keepdims=True)
            ds = (probs * (grad_probs - row_term)).astype(BF16)
            dv = dv + dot(low_probs, jnp.where(inside, dop, zero))
            dk = dk + dot(ds, jnp.where(inside, qp, zero))
            dq.append(dot(kt[64 * hh : 64 * hh + 64], ds))
        b.dqkv[3 * p] = (jnp.concatenate(dq, 0) * 0.125).T.astype(BF16)
        b.dqkv[3 * p + 1] = (dk * 0.125).astype(BF16)
        b.dqkv[3 * p + 2] = dv.astype(BF16)

    def joined(rows, wanted):
        return jnp.concatenate([b.dqkv[i, rows] for i in wanted], 1)

    def attention_grad(p):
        grads = jnp.concatenate([b.dqkv[3 * p + i] for i in range(3)], 1)

        @pl.when(p == 0)
        def _():
            b.gx[...] = dot(b.xp[...], grads, TN).astype(BF16).reshape(TP, nz, sh.xrows, HALF)

        @pl.when(p > 0)
        def _():
            cols = pl.ds(pl.multiple_of(HALF * p, 128), HALF)
            b.ga[:, :, :, cols] = dot(b.x[...], grads, TN).astype(BF16).reshape(nz, ny, br, HALF)

    @pl.loop(0, 3)
    def _(p):
        backward_pair(p)
        attention_grad(p)

        @pl.when(p == 0)
        def _():
            arrived([go_swap])
            scatter_send("aw", 0)
            scatter_send("x0", 0)

        @pl.when(p == 1)
        def _():
            for n in up_names:
                scatter_pass(n)
            scatter_send("a1", 0)
            scatter_on(down_names, 0)
            for n in ("aw", "x0"):
                scatter_pass(n)

        @pl.when(p == 2)
        def _():
            scatter_send("a2", 0)
            scatter_send("a3", 0)
            scatter_pass("a1")


    def partial_input(rows):
        return dot(joined(rows, range(9)), attention_weight(), NT)

    b.dxs[...] = partial_input(other_rows).astype(BF16)
    dx_swap = remote(b.dxs, b.dxr, sibling)
    dx = partial_input(own_rows) + b.dr[...]
    arrived([dx_swap])
    dx = dx + b.dxr[...].astype(F32)
    b.dxb[...] = dx[:256].astype(BF16)
    for i in range(TP):
        to_device(
            b.dxb.at[pl.ds(TOKENS * i, TOKENS)],
            dxo.at[seg, pl.ds(pl.multiple_of(TOKENS * core, 16), TOKENS)],
            (i, chain),
            xsem.at[XBASE[5] + 2 * seg + core],
            5,
            i,
        )

    @pl.when((core == 0) & (seg == 0))
    def _():
        b.sg[16:32] = dx[256:272]

    @pl.when(core == 1)
    def _():
        b.sg[32:48] = dx[256:272]

    small_grads = dot(b.sg[...].astype(BF16), smallsel[...], TN).astype(BF16)
    b.ga[:, :, :, 4 * HALF :] = small_grads.reshape(nz, ny, br, SMALL)
    scatter_send("as", 0)
    attention_names = ("aw", "x0", "a1", "a2", "a3", "as")
    scatter_on(up_names, 0)
    scatter_on(down_names, 1)
    scatter_on(attention_names, 0)
    scatter_on(up_names, 1)

    def last_rows(names, first_col):
        for j, n in enumerate(names):
            total = scatter_sum(n, 2)
            cols = slice(first_col + 128 * j, first_col + 128 * j + 128)
            b.sf[0, :, cols] = total[:wr]
            b.sf[1, :, cols] = total[wr:]

    for n in attention_names:
        cols = scatters[n][2]
        total = scatter_sum(n, 1).astype(BF16)
        if n == "x0":
            spread = dot(packy[...], total, TN).astype(BF16)
            b.e3y[...] = spread.reshape(ny, 2 * sh.pc, HALF)
            ysteps = [Group(lambda: b.r3y)] if ny > 1 else []
            for o in range(1, ny):
                ysteps[0].add(b.e3y.at[(y + o) % ny], b.r3y.at[o - 1], moved("y", o))
        else:
            spread = dot(packsel[...], total, TN).astype(BF16)
            b.e3[:, :, cols.start - HALF : cols.stop - HALF] = spread.reshape(TP, 2 * sh.pc, cols.stop - cols.start)
    steps = [Group(lambda: b.r3)]
    for o in range(1, TP):
        steps[0].add(b.e3.at[(x + o) % TP], b.r3.at[o - 1], moved("x", o))
    last_rows(down_names, HALF)
    last_rows(up_names, 0)
    sf_local = local(b.sf.at[core], gfo.at[core])
    sf_swap = remote(b.sf.at[other], gfo.at[core], sibling)

    arrived(steps)
    total = b.e3[x].astype(F32)
    for o in range(1, TP):
        total = total + b.r3[o - 1].astype(F32)
    b.s4[:, :, HALF:] = total.reshape(2, sh.pc, REST)
    arrived(ysteps)
    total = b.e3y[y].astype(F32)
    for o in range(1, ny):
        total = total + b.r3y[o - 1].astype(F32)
    b.s4[:, :, :HALF] = total.reshape(2, sh.pc, HALF)
    s4_local = local(b.s4.at[core], gao.at[core])
    s4_swap = remote(b.s4.at[other], gao.at[core], sibling)

    for kind, out_ref in ((3, hout), (5, dxo)):
        for s in range(2):
            for j in range(2):
                from_device(out_ref.at[s, pl.ds(TOKENS * j, TOKENS)], kind, 2 * s + j)
    for s in range(2):
        from_device(mout.at[s], 4, s)
    sf_local.wait()
    s4_local.wait()
    arrived([sf_swap, s4_swap])

    for group in sent[-SENDS:]:
        group.wait_send()
    for same, copy in conditional:

        @pl.when(jnp.logical_not(same))
        def _():
            copy.wait_send()

    @pl.when((seg == 0) & (core == 1))
    def _():
        hops[0].wait_send()
        hops[1].wait_send()

    @pl.when((seg == 0) & (core == 0))
    def _():
        early.wait_send()


def layer(sh, arrays):
    constants = [jnp.asarray(a, BF16) for a in selections(sh)]
    tables = scratch_of(sh)
    names = [list(table) for table in tables]
    anywhere = pl.BlockSpec(memory_space=pl.ANY)
    outs = [
        jax.ShapeDtypeStruct((2, 128, D), BF16),
        jax.ShapeDtypeStruct((2, 8, D), F32),
        jax.ShapeDtypeStruct((2, 128, D), BF16),
        jax.ShapeDtypeStruct((2, sh.pc, ACOLS), F32),
        jax.ShapeDtypeStruct((2, sh.wrows, D), F32),
    ]
    return pl.pallas_call(
        functools.partial(kernel, sh, names),
        name="layer",
        out_shape=outs,
        in_specs=[anywhere] * 15,
        out_specs=[anywhere] * len(outs),
        scratch_shapes=[pltpu.VMEM(*one) for table in tables for one in table.values()]
        + [
            pltpu.SemaphoreType.DMA((SENDS,)),
            pltpu.SemaphoreType.DMA((96,)),
            pltpu.SemaphoreType.DMA((45,)),
            pltpu.SemaphoreType.DMA((20,)),
        ],
        compiler_params=pltpu.CompilerParams(
            collective_id=0, has_side_effects=True, vmem_limit_bytes=64 * 2**20 - 2**17
        ),
    )(*arrays, *constants)


def unpack_kernel(sh, *refs):
    arrays, results, held, outs, sems = refs[:5], refs[5:15], refs[15:20], refs[20:30], refs[30]
    loads = [pltpu.make_async_copy(arrays[i], held[i], sems.at[i]) for i in range(5)]
    stores = [pltpu.make_async_copy(outs[i], results[i], sems.at[5 + i]) for i in range(10)]
    for copy in loads:
        copy.start()
    hout, mout, dxo, gao, gfo = held
    hidden, memory, grad_in, gq, gp, gains, biases, tokens, gi, gt = outs
    ar = sh.arows
    loads[0].wait()
    hidden[...] = hout[...]
    stores[0].start()
    loads[2].wait()
    grad_in[...] = dxo[...].astype(F32)
    stores[2].start()
    loads[1].wait()
    for i in range(2):
        memory[:, i] = mout[i, :5].astype(BF16)
    stores[1].start()
    loads[3].wait()
    for h in range(2):
        for p in range(3):
            for i in range(3):
                to = D * i + HALF * h + 128 * p
                first = HALF * p + 128 * i
                gq[:, to : to + 128] = gao[h, :ar, first : first + 128]
        gp[:, HALF * h : HALF * (h + 1)] = gao[h, :ar, WO : WO + HALF]
    small = gao[0, :, 4 * HALF :] + gao[1, :, 4 * HALF :]
    turned = small.T[:, :ar]
    gains[...] = turned[0:2]
    biases[...] = turned[2:4]
    for kind in range(2):
        tokens[:, kind] = small[:ar, 4 + MEM * kind : 4 + MEM * (kind + 1)]
    for i in range(3, 8):
        stores[i].start()
    loads[4].wait()
    for h in range(2):
        gi[:, HALF * h : HALF * (h + 1)] = gfo[h, :, :HALF]
        gt[:, HALF * h : HALF * (h + 1)] = gfo[h, :, HALF:]
    for i in range(8, 10):
        stores[i].start()
    for copy in stores:
        copy.wait()


def unpack(sh, *arrays):
    ar, wr = sh.arows, sh.wrows
    shapes = [
        ((2, 128, D), BF16),
        ((5, 2, D), BF16),
        ((2, 128, D), F32),
        ((ar, 3 * D), F32),
        ((ar, D), F32),
        ((2, ar), F32),
        ((2, ar), F32),
        ((ar, 2, MEM), F32),
        ((wr, D), F32),
        ((wr, D), F32),
    ]
    anywhere = pl.BlockSpec(memory_space=pl.ANY)
    return pl.pallas_call(
        functools.partial(unpack_kernel, sh),
        name="unpack",
        out_shape=[jax.ShapeDtypeStruct(*one) for one in shapes],
        in_specs=[anywhere] * 5,
        out_specs=[anywhere] * len(shapes),
        scratch_shapes=[pltpu.VMEM(a.shape, a.dtype) for a in arrays]
        + [pltpu.VMEM(*one) for one in shapes]
        + [pltpu.SemaphoreType.DMA((15,))],
        compiler_params=pltpu.CompilerParams(vmem_limit_bytes=64 * 2**20 - 2**17),
    )(*arrays)


def body(
    sh,
    hidden_in,
    reset,
    w_qkv,
    w_attn_out,
    norm_gains,
    norm_biases,
    memory_tokens,
    w_in,
    w_out,
    grad_hidden,
    grad_memory,
):
    arrays = (
        hidden_in,
        grad_hidden,
        grad_memory.transpose(1, 0, 2),
        w_qkv,
        w_attn_out,
        norm_gains,
        norm_biases,
        memory_tokens.transpose(2, 0, 1),
        w_in,
        w_out.T,
    )
    hidden, memory, *middle, tokens, gi, gt = unpack(sh, *layer(sh, arrays))
    return hidden, memory.transpose(1, 0, 2), *middle, tokens.transpose(1, 2, 0), gi, gt.T


def solution(mesh):
    sh = Shape(mesh.shape["dp"])
    return jax.shard_map(
        functools.partial(body, sh),
        mesh=mesh,
        in_specs=(
            P("dp", "tp", None),
            P("dp"),
            P(("dp", "tp"), None),
            P(("dp", "tp"), None),
            P(None, ("dp", "tp")),
            P(None, ("dp", "tp")),
            P(None, None, ("dp", "tp")),
            P("dp", "tp"),
            P("tp", "dp"),
            P("dp", "tp", None),
            P("dp", "tp", None),
        ),
        out_specs=(
            P("dp", "tp", None),
            P("dp", "tp", None),
            P("dp", "tp", None),
            P(("dp", "tp"), None),
            P(("dp", "tp"), None),
            P(None, ("dp", "tp")),
            P(None, ("dp", "tp")),
            P(None, None, ("dp", "tp")),
            P("dp", "tp"),
            P("tp", "dp"),
        ),
        check_vma=False,
    )
```

```python
import functools
import types

import jax
import jax.numpy as jnp
import numpy as np
from jax import lax
from jax.experimental import pallas as pl
from jax.experimental.pallas import tpu as pltpu
from jax.sharding import PartitionSpec as P

D = 768
HALF = 384
MEM = 10
TOKENS = 64
OWN = 272
ROWS = 2 * OWN
TP = 4
SMALL = 128
ACOLS = 4 * HALF + SMALL
REST = ACOLS - HALF
CUT = HALF + 640
WO = 3 * HALF
EPSILON = 1e-05
INV_ROOT_TWO = 0.7071067811865476
INV_ROOT_TWOPI = 0.3989422804014327
EXP_SCALE = 0.125 * 1.4426950408889634
MASKED = -1e30
F32 = jnp.float32
BF16 = jnp.bfloat16
MESH = pl.DeviceIdType.MESH
NN = (((1,), (0,)), ((), ()))
NT = (((1,), (1,)), ((), ()))
TN = (((0,), (0,)), ((), ()))


def dot(a, b, dims=NN):
    return lax.dot_general(a, b, dims, preferred_element_type=F32)


def up16(n):
    return -(-n // 16) * 16


class Shape:
    def __init__(self, dp):
        self.dp = dp
        planes = dp // 2
        self.ny = int(round(planes**0.5))
        self.nz = planes // self.ny
        self.wrows = D // dp
        self.arows = D // (dp * TP)
        self.brows = 2 * self.wrows
        self.pr = up16(self.arows)
        self.xrows = 2 * self.arows * self.ny
        self.pc = -(-self.arows // 8) * 8
        self.fr = up16(self.wrows)


def selections(sh):
    pack = np.zeros((sh.brows, TP * 2 * sh.pc), np.float32)
    for c in range(2):
        for x in range(TP):
            for i in range(sh.arows):
                pack[c * sh.wrows + x * sh.arows + i, (x * 2 + c) * sh.pc + i] = 1
    packy = np.zeros((sh.xrows, sh.ny * 2 * sh.pc), np.float32)
    turn = np.zeros((D, D), np.float32)
    ar = sh.arows
    for c in range(2):
        for y in range(sh.ny):
            for i in range(ar):
                row = (y * 2 + c) * ar + i
                packy[row, (y * 2 + c) * sh.pc + i] = 1
                for x in range(TP):
                    for z in range(sh.nz):
                        place = (z * sh.ny + y) * sh.brows + (c * TP + x) * ar + i
                        turn[(x * sh.nz + z) * sh.xrows + row, place] = 1
    small = np.zeros((48, SMALL), np.float32)
    for i in range(4):
        small[i, i] = 1
    for kind in range(2):
        for i in range(MEM):
            small[16 + 16 * kind + (i // 5) * 8 + i % 5, 4 + MEM * kind + i] = 1
    places = np.zeros((4, MEM, SMALL), np.float32)
    for kind, (rows, first) in enumerate(((2, 0), (2, 2), (MEM, 4), (MEM, 4 + MEM))):
        for i in range(rows):
            places[kind, i, first + i] = 1
    return pack, small, places, packy, turn


def norm_forward(inputs, gain, offset):
    centred = inputs - jnp.mean(inputs, -1, keepdims=True)
    spread = jnp.mean(centred * centred, -1, keepdims=True)
    inverse = lax.rsqrt(spread + EPSILON)
    normed = centred * inverse
    return normed * gain + offset, normed, inverse


def norm_backward(upstream, normed, inverse, gain):
    scaled = upstream * gain
    first_mean = jnp.mean(scaled, -1, keepdims=True)
    second_mean = jnp.mean(scaled * normed, -1, keepdims=True)
    return inverse * (scaled - first_mean - normed * second_mean)


def column_sum(a):
    return jnp.sum(a, 0, keepdims=True)


XBASE = (0, 4, 8, 10, 14, 16, 20)
SENDS = 40
STAGED, LANDED, SUMMED, PASSED, UPDATED = range(5)


def scratch_of(sh):
    nz, ny, br = sh.nz, sh.ny, sh.brows
    ar, wr = sh.arows, sh.wrows
    operands = [
        (5, 2, D),
        (ar, 3 * D),
        (ar, D),
        (2, ar),
        (2, ar),
        (ar, 2, MEM),
        (wr, D),
        (wr, D),
        (br, TP * 2 * sh.pc),
        (48, SMALL),
        (4, MEM, SMALL),
        (sh.xrows, ny * 2 * sh.pc),
    ]
    jobs = {(STAGED, i, 0): (dims, BF16) for i, dims in enumerate(operands)}
    s = dict(
        pk=((2, sh.pr, ACOLS), BF16),
        ff=((2, sh.fr, D), BF16),
        gms=((2, 8, D), F32),
        p1=((2, sh.pr, ACOLS), BF16),
        p2=((TP, 2 * sh.pc, REST), BF16),
        p2y=((ny, 2 * sh.pc, HALF), BF16),
        turn=((D, D), BF16),
        wx=((TP, nz, sh.xrows, HALF), BF16),
        gx=((TP, nz, sh.xrows, HALF), BF16),
        f1=((2, sh.fr, D), BF16),
        wa=((nz, ny, br, ACOLS), BF16),
        wf=((TP, nz, ny, br, D), BF16),
        wo=((2, nz, ny, br, HALF), BF16),
        par=((8, D), F32),
        both=((2, ROWS, D), BF16),
        gyt=((TP * TOKENS, D), BF16),
        gm=((2, 8, D), F32),
        qkv=((9, ROWS, 128), BF16),
        pt=((6, ROWS, ROWS), BF16),
        ot=((3, 128, ROWS), BF16),
        oc=((ROWS, HALF), BF16),
        oin=((OWN, HALF), BF16),
        h1=((OWN, D), F32),
        n1=((OWN, D), F32),
        inv1=((OWN, 1), F32),
        h1b=((ROWS, D), BF16),
        gl=((2, ROWS, D), BF16),
        ul=((2, ROWS, D), F32),
        fs=((OWN, D), BF16),
        fr=((OWN, D), BF16),
        n2=((OWN, D), F32),
        yb=((OWN, D), BF16),
        mo=((2, 8, D), F32),
        hop=((16, D), BF16),
        hopin=((16, D), BF16),
        es=((16, D), F32),
        er=((16, D), F32),
        dz=((OWN, D), F32),
        dfb=((ROWS, D), BF16),
        du=((2, ROWS, D), BF16),
        dhs=((OWN, D), BF16),
        dhr=((OWN, D), BF16),
        dr=((OWN, D), F32),
        dab=((ROWS, D), BF16),
        doc=((3, ROWS, 128), BF16),
        dqkv=((9, ROWS, 128), BF16),
        ga=((nz, ny, br, ACOLS), BF16),
        gi=((TP, nz, ny, br, HALF), BF16),
        gt=((TP, nz, ny, br, HALF), BF16),
        dxs=((OWN, D), BF16),
        dxr=((OWN, D), BF16),
        dxb=((TP * TOKENS, D), BF16),
        sg=((48, D), F32),
        e3=((TP, 2 * sh.pc, REST), BF16),
        r3=((TP - 1, 2 * sh.pc, REST), BF16),
        e3y=((ny, 2 * sh.pc, HALF), BF16),
        r3y=((max(1, ny - 1), 2 * sh.pc, HALF), BF16),
        s4=((2, sh.pc, ACOLS), F32),
        sf=((2, sh.wrows, D), F32),
    )
    s.update(gos=((nz // 2, ny, br, HALF) if nz > 1 else (1, 1, HALF, HALF), BF16))
    sizes = {"x": TP, "z": nz, "y": ny}
    for name, order, cols, axes in scatter_jobs():
        left = [a for a in axes]
        block = (sh.xrows if name[0] == "x" else br, cols.stop - cols.start)
        for step, axis in enumerate(order):
            left = [a for a in left if a != axis]
            dims = tuple(sizes[a] for a in left)
            ring = step == 0 and name in RINGS and sizes[axis] == 4
            jobs[LANDED, step, name] = ((2 if ring else max(1, sizes[axis] - 1),) + dims + block, BF16)
            if step < len(order) - 1:
                jobs[SUMMED, step, name] = (dims + block, BF16)
            if ring:
                jobs[PASSED, 0, name] = ((2, dims[0] // 2) + dims[1:] + block, BF16)
                jobs[UPDATED, 0, name] = jobs[PASSED, 0, name]
    return s, jobs


def scatter_jobs():
    orders = [("z", "y", "x"), ("x", "z", "y"), ("y", "x", "z")]
    jobs = []
    for kind in ("t", "i"):
        for j in range(3):
            jobs.append((f"{kind}{j}", orders[j], slice(128 * j, 128 * j + 128), ("x", "z", "y")))
    zy, yz = ("z", "y"), ("y", "z")
    jobs.append(("aw", yz, slice(WO, WO + HALF), zy))
    jobs.append(("x0", ("x", "z"), slice(0, HALF), ("x", "z")))
    jobs.append(("a1", zy, slice(HALF, 2 * HALF), zy))
    jobs.append(("a2", yz, slice(2 * HALF, 2 * HALF + 256), zy))
    jobs.append(("a3", zy, slice(2 * HALF + 256, 3 * HALF), zy))
    jobs.append(("as", zy, slice(4 * HALF, ACOLS), zy))
    return jobs


def gather_jobs():
    orders = [("x", "y", "z"), ("y", "z", "x"), ("z", "x", "y")]
    jobs = [(f"f{j}", orders[j], slice(256 * j, 256 * j + 256), ("x", "z", "y")) for j in range(3)]
    jobs.append(("x0", ("z", "x"), slice(0, HALF), ("x", "z")))
    jobs.append(("a0", ("y", "z"), slice(HALF, CUT), ("z", "y")))
    jobs.append(("a1", ("z", "y"), slice(CUT, ACOLS), ("z", "y")))
    return jobs


RINGS = ("t0", "t1", "t2", "i0", "i1", "i2", "aw", "x0", "a1")
WEIGHTS = {"f": "wf", "a": "wa", "x": "wx"}
GRADS = {"t": "gt", "i": "gi", "a": "ga", "x": "gx"}


def kernel(sh, names, *refs):
    xin, gin = refs[:2]
    hout, mout, dxo, gao, gfo = refs[15:20]
    ssem, rsem, xsem, lsem = refs[-4:]
    count = len(names[0])
    b = types.SimpleNamespace(**dict(zip(names[0], refs[20 : 20 + count])))
    b.xp, b.x = b.both.at[0], b.both.at[1]
    k = dict(zip(names[1], refs[20 + count : -4]))
    staged = [k[STAGED, i, 0] for i in range(12)]
    gmem, wq, wp, gain_in, bias_in, token_in, up_in, down_in = staged[:8]
    packsel, smallsel, places, packy = staged[8:]
    turn = refs[14]
    nz, ny, br, wr, ar = sh.nz, sh.ny, sh.brows, sh.wrows, sh.arows
    pk, ff, gms = b.pk, b.ff, b.gms

    dp = lax.axis_index("dp")
    x = lax.axis_index("tp")
    core = dp % 2
    y = (dp // 2) % ny
    z = dp // (2 * ny)
    other = 1 - core
    chain = x // 2
    seg = jnp.where((x == 1) | (x == 2), 1, 0)
    at = {"x": x, "y": y, "z": z}
    size = {"x": TP, "y": ny, "z": nz}

    def device(x_=x, y_=y, z_=z, c_=core):
        return ((z_ * ny + y_) * 2 + c_, x_)

    near = {a: [(at[a] + o) % size[a] for o in range(size[a])] for a in at}

    def moved_to(axis, offset, core_=core):
        there = dict(at)
        there[axis] = near[axis][offset]
        return device(there["x"], there["y"], there["z"], core_)

    neighbours = {a: [moved_to(a, o) for o in range(size[a])] for a in at}

    def moved(axis, offset):
        return neighbours[axis][offset]

    sibling = device(c_=other)
    sent = []

    class Group:
        def __init__(self, like):
            if len(sent) >= SENDS:
                sent[-SENDS].wait_send()
            self.like = like
            self.number = len(sent)
            sent.append(self)

        def add(self, src, dst, to):
            pltpu.make_async_remote_copy(
                src_ref=src,
                dst_ref=dst,
                send_sem=ssem.at[self.number % SENDS],
                recv_sem=rsem.at[self.number],
                device_id=to,
                device_id_type=MESH,
            ).start()

        def wait_send(self):
            like = self.like()
            pltpu.make_async_copy(like, like, ssem.at[self.number % SENDS]).wait()

        def wait_recv(self):
            like = self.like()
            pltpu.make_async_copy(like, like, rsem.at[self.number]).wait()

    def remote(src, dst, to):
        where = dst if callable(dst) else lambda: dst
        group = Group(where)
        group.add(src, where(), to)
        return group

    def arrived(groups):
        for group in groups:
            group.wait_recv()

    locals_ = [0]

    def local(src, dst):
        copy = pltpu.make_async_copy(src, dst, lsem.at[locals_[0]])
        locals_[0] += 1
        copy.start()
        return copy

    staging = [local(refs[2 + i], staged[i]) for i in range(12)]
    turn_local = local(turn, b.turn)

    barrier = pltpu.get_barrier_semaphore()
    peers = [sibling]
    for o in range(1, TP):
        peers += [moved("x", o), moved_to("x", o, other)]
    for axis in ("y", "z"):
        for o in range(1, size[axis]):
            peers.append(moved(axis, o))
    for peer in peers:
        pl.semaphore_signal(barrier, inc=1, device_id=peer, device_id_type=MESH)

    pk[...] = jnp.zeros(pk.shape, BF16)
    ff[...] = jnp.zeros(ff.shape, BF16)
    gms[...] = jnp.zeros(gms.shape, F32)
    for copy in staging:
        copy.wait()
    small = dot(gain_in[...], places[0, :2], TN) + dot(bias_in[...], places[1, :2], TN)
    small = small + dot(token_in[:, 0], places[2]) + dot(token_in[:, 1], places[3])
    small = small.astype(BF16)
    for h in range(2):
        for p in range(3):
            for i in range(3):
                first = D * i + HALF * h + 128 * p
                pk[h, :ar, HALF * p + 128 * i : HALF * p + 128 * (i + 1)] = wq[:, first : first + 128]
        pk[h, :ar, WO : WO + HALF] = wp[:, HALF * h : HALF * (h + 1)]
        pk[h, :ar, 4 * HALF :] = small
        for j in range(3):
            cols = slice(HALF * h + 128 * j, HALF * h + 128 * (j + 1))
            ff[h, :wr, 256 * j : 256 * j + 128] = up_in[:, cols]
            ff[h, :wr, 256 * j + 128 : 256 * j + 256] = down_in[:, cols]
        gms[h, 0:5] = gmem[:, h].astype(F32)
    pl.semaphore_wait(barrier, len(peers))

    pk_local = local(pk.at[core], b.p1.at[core])
    ff_local = local(ff.at[core], b.f1.at[core])
    pk_swap = remote(pk.at[other], b.p1.at[core], sibling)
    ff_swap = remote(ff.at[other], b.f1.at[core], sibling)

    conditional = []

    def to_device(src, dst, place, here, kind, send_slot):
        copy = pltpu.make_async_remote_copy(
            src_ref=src,
            dst_ref=dst,
            send_sem=xsem.at[25 + XBASE[kind] + send_slot],
            recv_sem=here,
            device_id=device(x_=place[0], c_=place[1]),
            device_id_type=MESH,
        )
        same = (place[0] == x) & (place[1] == core)

        @pl.when(same)
        def _():
            pltpu.make_async_copy(src, dst, here).start()

        @pl.when(jnp.logical_not(same))
        def _():
            copy.start()

        conditional.append((same, copy))

    def from_device(dst, kind, slot):
        pltpu.make_async_copy(dst, dst, xsem.at[XBASE[kind] + slot]).wait()

    def chip_of(k, s):
        return s + k * (3 - 2 * s)

    def send_rows():
        for s in range(2):
            for j in range(2):
                to_device(
                    xin.at[s, pl.ds(TOKENS * j, TOKENS)],
                    b.x.at[pl.ds(pl.multiple_of(OWN * j + TOKENS * x, 16), TOKENS)],
                    (chip_of(core, s), j),
                    xsem.at[XBASE[0] + x],
                    0,
                    2 * s + j,
                )

    def send_upstream():
        for s in range(2):
            for j in range(2):
                to_device(
                    gin.at[s, pl.ds(TOKENS * j, TOKENS)],
                    b.gyt.at[pl.ds(pl.multiple_of(TOKENS * x, 16), TOKENS)],
                    (chip_of(core, s), j),
                    xsem.at[XBASE[1] + x],
                    1,
                    2 * s + j,
                )
            to_device(
                gms.at[s], b.gm.at[x % 2], (chip_of(core, s), x // 2), xsem.at[XBASE[2] + x % 2], 2, s
            )

    def part_of(job, step, place, half=None):
        name, order, cols, axes = job
        fixed = {a: at[a] for a in order[step:]}
        fixed[order[step]] = place
        where = []
        for a in axes:
            if a in fixed:
                where.append(fixed[a])
            elif half is not None:
                where.append(pl.ds(half * (size[a] // 2), size[a] // 2))
                half = None
            else:
                where.append(slice(None))
        return getattr(b, WEIGHTS[name[0]]).at[tuple(where) + (slice(None), cols)]

    def gather_start(name, step):
        job = gathers[name]
        axis = job[1][step]
        n = size[axis]
        own = part_of(job, step, at[axis])
        free = [a for a in job[3] if a not in job[1][step:]]
        relay = n == 4 and step == len(job[1]) - 1 and size[free[0]] % 2 == 0
        state = types.SimpleNamespace(step=step, relay=relay)
        if relay:
            first = [part_of(job, step, at[axis], h) for h in range(2)]
            right, left = moved(axis, 1), moved(axis, n - 1)
            state.right, state.left = (
                remote(first[h], lambda h=h: part_of(job, step, at[axis], h), to) for h, to in ((0, right), (1, left))
            )
            state.every = [Group(lambda: part_of(job, step, pl.ds(0, 2)))]
            state.every[0].add(first[1], first[1], right)
            state.every[0].add(first[0], first[0], left)
        else:
            state.every = [Group(lambda: part_of(job, step, pl.ds(0, n - 1)))] if n > 1 else []
            for o in range(1, n):
                state.every[0].add(own, own, moved(axis, o))
        flying[name] = state

    def gather_pass(name):
        job, state = gathers[name], flying[name]
        if not state.relay:
            return
        axis = job[1][state.step]
        n = size[axis]
        for copy, back, onward, half in ((state.right, n - 1, 1, 0), (state.left, 1, n - 1, 1)):
            arrived([copy])
            piece = part_of(job, state.step, near[axis][back], half)
            state.every[0].add(piece, piece, moved(axis, onward))

    def gather_done(name):
        arrived(flying[name].every)

    gathers = {j[0]: j for j in gather_jobs()}
    flying = {}

    pk_local.wait()
    arrived([pk_swap])
    packed = jnp.concatenate([b.p1[c].astype(F32)[: sh.pc] for c in range(2)], 0).astype(BF16)
    b.p2y[y] = packed[:, :HALF]
    b.p2[x] = packed[:, HALF:]
    mine = b.p2y.at[y]
    ysteps, xsteps = [], [Group(lambda: b.p2.at[: TP - 1])]
    if ny > 1:
        ysteps.append(Group(lambda: b.p2y.at[: ny - 1]))
    for o in range(1, ny):
        ysteps[0].add(mine, mine, moved("y", o))
    mine = b.p2.at[x]
    for o in range(1, TP):
        xsteps[0].add(mine, mine, moved("x", o))
    ff_local.wait()
    arrived([ff_swap])
    two = [b.f1[c].astype(F32)[:wr] for c in range(2)]
    b.wf[x, z, y] = jnp.concatenate(two, 0).astype(BF16)
    feed_names, first_names = ("f1", "f2", "f0"), ("x0", "a0", "a1")
    for n in feed_names:
        gather_start(n, 0)
    send_rows()
    arrived(ysteps)
    b.wx[x, z] = dot(packy[...], b.p2y[...].reshape(ny * 2 * sh.pc, HALF)).astype(BF16)
    gather_start("x0", 0)
    arrived(xsteps)
    b.wa[z, y, :, HALF:] = dot(packsel[...], b.p2[...].reshape(TP * 2 * sh.pc, REST)).astype(BF16)
    for n in ("a0", "a1"):
        gather_start(n, 0)
    for n in feed_names:
        gather_done(n)
        gather_start(n, 1)
    for n in first_names:
        gather_done(n)
        gather_start(n, 1)
    for n in first_names:
        gather_pass(n)
    for n in feed_names:
        gather_done(n)
        gather_start(n, 2)

    for i in range(TP):
        from_device(b.x.at[pl.ds(pl.multiple_of(OWN * core + TOKENS * i, 16), TOKENS)], 0, i)
    half = b.x.at[pl.ds(pl.multiple_of(OWN * core, 16), TP * TOKENS)]
    x_swap = remote(half, half, sibling)
    for first in (256, OWN + 256):
        b.x[first : first + 16] = jnp.zeros((16, D), BF16)
    turn_local.wait()
    arrived([x_swap])

    @pl.loop(0, 2)
    def _(i):
        rows = pl.ds(pl.multiple_of(OWN * i, 16), OWN)
        b.xp[rows] = dot(b.x[rows], b.turn[...], NT).astype(BF16)

    for n in first_names:
        gather_done(n)
    wo_cols = slice(WO, WO + HALF)
    wo_local = local(b.wa.at[:, :, :, wo_cols], b.wo.at[core])
    wo_swap = remote(b.wa.at[:, :, :, wo_cols], b.wo.at[core], sibling)
    gather_pass("f1")
    send_upstream()

    def attention_weight():
        return b.wa[:, :, :, :WO].reshape(D, WO)

    small = b.wa[:, :, :, 4 * HALF :].reshape(D, SMALL)
    chosen = dot(smallsel[...], small, NT)
    b.par[...] = chosen[0:8]
    memory = chosen[16:48].astype(BF16)
    b.x[OWN + 256 : OWN + 272] = memory[16:]
    turned = dot(memory, b.turn[...], NT).astype(BF16)
    b.xp[OWN + 256 : OWN + 272] = turned[16:]

    @pl.when(seg == 0)
    def _():
        b.x[256:272] = memory[:16]
        b.xp[256:272] = turned[:16]

    gains = [b.par[i : i + 1] for i in range(2)]
    biases = [b.par[2 + i : 3 + i] for i in range(2)]

    hop_to = jnp.where(x == 0, 1, 2)
    hops = []
    for j in range(2):
        hops.append(
            pltpu.make_async_remote_copy(
                src_ref=b.hop,
                dst_ref=b.hopin,
                send_sem=xsem.at[XBASE[6] + j],
                recv_sem=xsem.at[XBASE[6] + 2],
                device_id=device(x_=hop_to, c_=j),
                device_id_type=MESH,
            )
        )

    own_rows = pl.ds(pl.multiple_of(OWN * core, 16), OWN)
    other_rows = pl.ds(pl.multiple_of(OWN * other, 16), OWN)

    out = dot(b.xp[...], b.wx[...].reshape(D, HALF)).astype(BF16)
    for i in range(3):
        b.qkv[i] = out[:, 128 * i : 128 * i + 128]
    out = dot(b.x[...], b.wa[:, :, :, HALF:WO].reshape(D, 2 * HALF)).astype(BF16)
    for i in range(3, 9):
        b.qkv[i] = out[:, 128 * (i - 3) : 128 * (i - 2)]

    def head_masks(hh):
        lane = lax.broadcasted_iota(jnp.int32, (ROWS, 128), 1)
        row = lax.broadcasted_iota(jnp.int32, (ROWS, 128), 0)
        inside = (lane // 64) == hh
        spare = lane == 64 * (1 - hh)
        memory = ((row >= 256) & (row < 272)) | (row >= OWN + 256)
        invalid = memory & (row % 8 >= 5)
        return inside, spare, invalid

    def forward_pair(p):
        qp, kp, vp = (b.qkv[3 * p + i] for i in range(3))
        vt = vp.T
        for hh in range(2):
            inside, spare, invalid = head_masks(hh)
            zero = jnp.zeros_like(kp)
            kmask = jnp.where(spare & invalid, jnp.full_like(kp, MASKED), zero)
            km = jnp.where(inside, kp, kmask)
            qm = jnp.where(inside, qp, jnp.where(spare, jnp.ones_like(qp), zero))
            scores = dot(km, qm, NT)
            peak = jnp.max(scores, 0, keepdims=True)
            raised = jnp.exp2((scores - peak) * EXP_SCALE)
            total = jnp.sum(raised, 0, keepdims=True)
            probs = (raised * (1.0 / total)).astype(BF16)
            b.pt[2 * p + hh] = probs
            b.ot[p, 64 * hh : 64 * hh + 64] = dot(vt[64 * hh : 64 * hh + 64], probs).astype(BF16)
        b.oc[:, pl.ds(pl.multiple_of(128 * p, 128), 128)] = b.ot[p].T

    @pl.loop(0, 3)
    def _(j):
        cols = pl.ds(pl.multiple_of(128 * j, 128), 128)
        block = dot(b.turn[...], b.wx[:, :, :, cols].reshape(D, 128), TN).astype(BF16)
        b.wa[:, :, :, cols] = block.reshape(nz, ny, br, 128)

    @pl.loop(0, 2)
    def _(i):
        @pl.when((i == 1) & (seg == 1))
        def _():
            hops[0].wait_recv()
            b.x[256:272] = b.hopin[...]
            rows = dot(b.hopin[...], attention_weight()).astype(BF16)
            for j in range(9):
                b.qkv[j, 256:272] = rows[:, 128 * j : 128 * j + 128]

        @pl.when(i == seg)
        def _():
            for p in range(3):
                forward_pair(p)

        @pl.when(i == 0)
        def _():
            for n in ("f2", "f0"):
                gather_pass(n)

    def head_rows(ref, c):
        if nz > 1:
            return ref.at[pl.ds(c * (nz // 2), nz // 2)]
        return ref.at[:, :, pl.ds(pl.multiple_of(c * HALF, 16), HALF)]

    def wo_rows(h, c):
        return head_rows(b.wo.at[h], c)[...].reshape(HALF, HALF)

    o_swap = remote(b.oc.at[other_rows], b.oin, sibling)
    wo_local.wait()
    arrived([wo_swap])
    halves = [dot(b.oc[own_rows], wo_rows(h, core)) for h in range(2)]
    arrived([o_swap])
    attended = jnp.concatenate([halves[h] + dot(b.oin[...], wo_rows(h, other)) for h in range(2)], 1)
    h1, n1, inv1 = norm_forward(b.x[own_rows].astype(F32) + attended, gains[0], biases[0])
    b.h1[...] = h1
    b.n1[...] = n1
    b.inv1[...] = inv1
    b.h1b[own_rows] = h1.astype(BF16)
    h_swap = remote(b.h1b.at[own_rows], b.h1b.at[own_rows], sibling)

    @pl.when(seg == 1)
    def _():
        b.xp[256:272] = dot(b.hopin[...], b.turn[...], NT).astype(BF16)

    for n in ("f1", "f2", "f0"):
        gather_done(n)

    def feed_weight(t, kind):
        cols = [256 * j + 128 * kind for j in range(3)]
        blocks = [b.wf[2 * t + i, :, :, :, c : c + 128].reshape(D, 128) for i in range(2) for c in cols]
        return jnp.concatenate(blocks, 1)

    def up_weight(t):
        return feed_weight(t, 0)

    def down_weight(t):
        return feed_weight(t, 1)

    def gelu_share(units):
        return 0.5 * (1.0 + lax.erf(units * INV_ROOT_TWO))

    early = pltpu.make_async_remote_copy(
        src_ref=b.es,
        dst_ref=b.er,
        send_sem=xsem.at[XBASE[6] + 3],
        recv_sem=xsem.at[XBASE[6] + 4],
        device_id=sibling,
        device_id_type=MESH,
    )
    row16 = lax.broadcasted_iota(jnp.int32, (16, D), 0)

    @pl.when(seg == 0)
    def _():
        arrived([h_swap])
        rows = b.h1b[OWN + 256 : OWN + 272]
        units = [dot(rows, up_weight(t)) for t in range(2)]
        part = sum(dot((units[t] * gelu_share(units[t])).astype(BF16), down_weight(t), NT) for t in range(2))

        @pl.when(core == 0)
        def _():
            b.es[...] = part
            early.start()

        @pl.when(core == 1)
        def _():
            early.wait_recv()
            whole = b.h1[256:272] + part + b.er[...]
            written = norm_forward(whole, gains[1], biases[1])[0]
            b.hop[...] = jnp.where(row16 % 8 < 5, written, 0.0).astype(BF16)
            hops[0].start()
            hops[1].start()

    def project_up(rows):
        for t in range(2):
            units = dot(b.h1b[rows], up_weight(t))
            b.ul[t, rows] = units
            b.gl[t, rows] = (units * gelu_share(units)).astype(BF16)

    @pl.loop(0, 2)
    def _(i):
        @pl.when((i == 1) & (seg == 1))
        def _():
            arrived([h_swap])

        project_up(pl.ds(pl.multiple_of(OWN * jnp.where(i == 0, core, other), 16), OWN))


    def partial_down(rows):
        return sum(dot(b.gl[t, rows], down_weight(t), NT) for t in range(2))

    b.fs[...] = partial_down(other_rows).astype(BF16)
    f_swap = remote(b.fs, b.fr, sibling)
    branch = partial_down(own_rows)
    arrived([f_swap])
    out, n2, inv2 = norm_forward(b.h1[...] + branch + b.fr[...].astype(F32), gains[1], biases[1])
    low = out.astype(BF16)
    b.yb[...] = low
    b.mo[...] = low[256:272].astype(F32).reshape(2, 8, D)
    for i in range(TP):
        to_device(
            b.yb.at[pl.ds(TOKENS * i, TOKENS)],
            hout.at[seg, pl.ds(pl.multiple_of(TOKENS * core, 16), TOKENS)],
            (i, chain),
            xsem.at[XBASE[3] + 2 * seg + core],
            3,
            i,
        )
    for i in range(2):
        to_device(b.mo.at[i], mout.at[seg], (2 * core + i, chain), xsem.at[XBASE[4] + seg], 4, i)

    for i in range(TP):
        from_device(b.gyt.at[pl.ds(TOKENS * i, TOKENS)], 1, i)
    for i in range(2):
        from_device(b.gm.at[i], 2, i)
    upstream = jnp.concatenate([b.gyt[...].astype(F32), b.gm[...].reshape(16, D)], 0)
    b.sg[...] = jnp.zeros((48, D), F32)
    b.sg[1:2] = column_sum(upstream * n2)
    b.sg[3:4] = column_sum(upstream)
    dz = norm_backward(upstream, n2, inv2, gains[1])
    b.dz[...] = dz
    b.dfb[own_rows] = dz.astype(BF16)
    df_swap = remote(b.dfb.at[own_rows], b.dfb.at[own_rows], sibling)

    def weight_grad(into, left, right):
        @pl.loop(0, 2)
        def _(t):
            part = dot(left[...], right[t], TN).astype(BF16)
            for i in range(2):
                into[2 * t + i] = part[:, HALF * i : HALF * (i + 1)].reshape(nz, ny, br, HALF)

    scatters = {j[0]: j for j in scatter_jobs()}
    rs = {}

    def is_ring(name, step):
        _, order, cols, axes = scatters[name]
        return step == 0 and name in RINGS and size[order[0]] == 4

    def source_of(name, step):
        _, order, cols, axes = scatters[name]
        axis = order[step]
        left = [a for a in axes if a not in order[:step]]
        array = getattr(b, GRADS[name[0]]) if step == 0 else k[SUMMED, step - 1, name]
        tail = (slice(None), cols) if step == 0 else ()

        def part(place, half=None):
            where = []
            for a in left:
                if a == axis:
                    where.append(place)
                elif half is not None:
                    where.append(pl.ds(half * (size[a] // 2), size[a] // 2))
                    half = None
                else:
                    where.append(slice(None))
            return array.at[tuple(where) + tail]

        return part

    def scatter_send(name, step):
        axis = scatters[name][1][step]
        n = size[axis]
        part = source_of(name, step)
        landing = k[LANDED, step, name]
        if is_ring(name, step):
            right, left, far = (near[axis][o] for o in (1, n - 1, 2))
            to_right, to_left = moved(axis, 1), moved(axis, n - 1)
            half = size[[a for a in scatters[name][3] if a != axis][0]] // 2
            over = k[PASSED, 0, name]
            passing = [
                remote(part(far, 0), lambda: over.at[0], to_right),
                remote(part(far, 1), lambda: over.at[1], to_left),
            ]
            coming = Group(lambda: landing)
            coming.add(part(right, 1), landing.at[0, half:], to_right)
            coming.add(part(left, 0), landing.at[1, :half], to_left)
            rs[name] = (passing, coming, half, (right, left), (to_right, to_left))
            return
        rs[name] = [Group(lambda: landing)] if n > 1 else []
        for o in range(1, n):
            rs[name][0].add(part(near[axis][o]), landing.at[o - 1], moved(axis, o))

    def scatter_pass(name):
        if not is_ring(name, 0):
            return
        passing, coming, half, places_, devices = rs[name]
        part = source_of(name, 0)
        landing, over, updated = k[LANDED, 0, name], k[PASSED, 0, name], k[UPDATED, 0, name]
        for i in range(2):
            arrived([passing[i]])
            updated[i] = (part(places_[i], i)[...].astype(F32) + over[i].astype(F32)).astype(BF16)
            where = landing.at[0, :half] if i == 0 else landing.at[1, half:]
            coming.add(updated.at[i], where, devices[i])

    def scatter_sum(name, step):
        _, order, cols, axes = scatters[name]
        axis = order[step]
        total = source_of(name, step)(at[axis])[...].astype(F32)
        ring = is_ring(name, step)
        arrived([rs[name][1]] if ring else rs[name])
        for o in range(2 if ring else size[axis] - 1):
            total = total + k[LANDED, step, name][o].astype(F32)
        if step < len(order) - 1:
            k[SUMMED, step, name][...] = total.astype(BF16)
        return total

    def scatter_on(names, step):
        for n in names:
            scatter_sum(n, step)
            scatter_send(n, step + 1)

    down_names, up_names = ("t0", "t1", "t2"), ("i0", "i1", "i2")
    arrived([df_swap])
    weight_grad(b.gt, b.dfb, b.gl)
    for n in down_names:
        scatter_send(n, 0)
    @pl.loop(0, 2)
    def _(i):
        rows = pl.ds(pl.multiple_of(OWN * i, 16), OWN)
        for t in range(2):
            units = b.ul[t, rows]
            slope = gelu_share(units) + units * jnp.exp(-0.5 * units * units) * INV_ROOT_TWOPI
            b.du[t, rows] = (dot(b.dfb[rows], down_weight(t)) * slope).astype(BF16)


    def partial_up(rows):
        return sum(dot(b.du[t, rows], up_weight(t), NT) for t in range(2))

    dh_swap = Group(lambda: b.dhr)

    @pl.loop(0, 2)
    def _(i):
        part = partial_up(pl.ds(pl.multiple_of(OWN * jnp.where(i == 0, other, core), 16), OWN))

        @pl.when(i == 0)
        def _():
            b.dhs[...] = part.astype(BF16)
            dh_swap.add(b.dhs, b.dhr, sibling)

        @pl.when(i == 1)
        def _():
            b.dz[...] = b.dz[...] + part

    weight_grad(b.gi, b.h1b, b.du)
    for n in up_names:
        scatter_send(n, 0)
    for n in down_names:
        scatter_pass(n)
    arrived([dh_swap])
    into_first = b.dz[...] + b.dhr[...].astype(F32)
    b.sg[0:1] = column_sum(into_first * b.n1[...])
    b.sg[2:3] = column_sum(into_first)
    dr = norm_backward(into_first, b.n1[...], b.inv1[...], gains[0])
    b.dr[...] = dr
    b.dab[own_rows] = dr.astype(BF16)
    da_swap = remote(b.dab.at[own_rows], b.dab.at[own_rows], sibling)

    def grad_mixed(rows):
        parts = [dot(b.dab[rows, HALF * h : HALF * (h + 1)], wo_rows(h, core), NT) for h in range(2)]
        for p in range(3):
            b.doc[p, rows] = (parts[0] + parts[1])[:, 128 * p : 128 * p + 128].astype(BF16)

    grad_mixed(own_rows)
    arrived([da_swap])
    grad_mixed(other_rows)

    mixed_t = b.ot[...].reshape(HALF, ROWS)

    def proj_grad(h):
        cols = pl.ds(pl.multiple_of(HALF * h, 128), HALF)
        return dot(mixed_t, b.dab[:, cols]).astype(BF16).reshape(b.gos.shape)

    def wo_part(c):
        return head_rows(b.ga.at[:, :, :, wo_cols], c)

    b.gos[...] = proj_grad(other)
    go_swap = remote(b.gos, wo_part(core), sibling)
    wo_part(core)[...] = proj_grad(core)

    def backward_pair(p):
        qp, kp, vp = (b.qkv[3 * p + i] for i in range(3))
        dop = b.doc[p]
        kt = kp.T
        dv = dk = 0.0
        dq = []
        for hh in range(2):
            inside, _, _ = head_masks(hh)
            zero = jnp.zeros_like(kp)
            grad_probs = dot(jnp.where(inside, vp, zero), dop, NT)
            low_probs = b.pt[2 * p + hh]
            probs = low_probs.astype(F32)
            row_term = jnp.sum(probs * grad_probs, 0, keepdims=True)
            ds = (probs * (grad_probs - row_term)).astype(BF16)
            dv = dv + dot(low_probs, jnp.where(inside, dop, zero))
            dk = dk + dot(ds, jnp.where(inside, qp, zero))
            dq.append(dot(kt[64 * hh : 64 * hh + 64], ds))
        b.dqkv[3 * p] = (jnp.concatenate(dq, 0) * 0.125).T.astype(BF16)
        b.dqkv[3 * p + 1] = (dk * 0.125).astype(BF16)
        b.dqkv[3 * p + 2] = dv.astype(BF16)

    def joined(rows, wanted):
        return jnp.concatenate([b.dqkv[i, rows] for i in wanted], 1)

    def attention_grad(p):
        grads = jnp.concatenate([b.dqkv[3 * p + i] for i in range(3)], 1)

        part = dot(b.both[jnp.minimum(p, 1)], grads, TN).astype(BF16)

        @pl.when(p == 0)
        def _():
            b.gx[...] = part.reshape(TP, nz, sh.xrows, HALF)

        @pl.when(p > 0)
        def _():
            cols = pl.ds(pl.multiple_of(HALF * p, 128), HALF)
            b.ga[:, :, :, cols] = part.reshape(nz, ny, br, HALF)

    @pl.loop(0, 3)
    def _(p):
        backward_pair(p)
        attention_grad(p)

        @pl.when(p == 0)
        def _():
            arrived([go_swap])
            scatter_send("aw", 0)
            scatter_send("x0", 0)

        @pl.when(p == 1)
        def _():
            for n in up_names:
                scatter_pass(n)
            scatter_send("a1", 0)
            scatter_on(down_names, 0)
            for n in ("aw", "x0"):
                scatter_pass(n)

        @pl.when(p == 2)
        def _():
            scatter_send("a2", 0)
            scatter_send("a3", 0)
            scatter_pass("a1")


    def partial_input(rows):
        return dot(joined(rows, range(9)), attention_weight(), NT)

    b.dxs[...] = partial_input(other_rows).astype(BF16)
    dx_swap = remote(b.dxs, b.dxr, sibling)
    dx = partial_input(own_rows) + b.dr[...]
    arrived([dx_swap])
    dx = dx + b.dxr[...].astype(F32)
    b.dxb[...] = dx[:256].astype(BF16)
    for i in range(TP):
        to_device(
            b.dxb.at[pl.ds(TOKENS * i, TOKENS)],
            dxo.at[seg, pl.ds(pl.multiple_of(TOKENS * core, 16), TOKENS)],
            (i, chain),
            xsem.at[XBASE[5] + 2 * seg + core],
            5,
            i,
        )

    @pl.when((core == 0) & (seg == 0))
    def _():
        b.sg[16:32] = dx[256:272]

    @pl.when(core == 1)
    def _():
        b.sg[32:48] = dx[256:272]

    small_grads = dot(b.sg[...].astype(BF16), smallsel[...], TN).astype(BF16)
    b.ga[:, :, :, 4 * HALF :] = small_grads.reshape(nz, ny, br, SMALL)
    scatter_send("as", 0)
    attention_names = ("aw", "x0", "a1", "a2", "a3", "as")
    scatter_on(up_names, 0)
    scatter_on(down_names, 1)
    scatter_on(attention_names, 0)
    scatter_on(up_names, 1)

    def last_rows(names, first_col):
        for j, n in enumerate(names):
            total = scatter_sum(n, 2)
            cols = slice(first_col + 128 * j, first_col + 128 * j + 128)
            b.sf[0, :, cols] = total[:wr]
            b.sf[1, :, cols] = total[wr:]

    for n in attention_names:
        cols = scatters[n][2]
        total = scatter_sum(n, 1).astype(BF16)
        if n == "x0":
            spread = dot(packy[...], total, TN).astype(BF16)
            b.e3y[...] = spread.reshape(ny, 2 * sh.pc, HALF)
            ysteps = [Group(lambda: b.r3y)] if ny > 1 else []
            for o in range(1, ny):
                ysteps[0].add(b.e3y.at[(y + o) % ny], b.r3y.at[o - 1], moved("y", o))
        else:
            spread = dot(packsel[...], total, TN).astype(BF16)
            b.e3[:, :, cols.start - HALF : cols.stop - HALF] = spread.reshape(TP, 2 * sh.pc, cols.stop - cols.start)
    steps = [Group(lambda: b.r3)]
    for o in range(1, TP):
        steps[0].add(b.e3.at[(x + o) % TP], b.r3.at[o - 1], moved("x", o))
    last_rows(down_names, HALF)
    last_rows(up_names, 0)
    sf_local = local(b.sf.at[core], gfo.at[core])
    sf_swap = remote(b.sf.at[other], gfo.at[core], sibling)

    arrived(steps)
    total = b.e3[x].astype(F32)
    for o in range(1, TP):
        total = total + b.r3[o - 1].astype(F32)
    b.s4[:, :, HALF:] = total.reshape(2, sh.pc, REST)
    arrived(ysteps)
    total = b.e3y[y].astype(F32)
    for o in range(1, ny):
        total = total + b.r3y[o - 1].astype(F32)
    b.s4[:, :, :HALF] = total.reshape(2, sh.pc, HALF)
    s4_local = local(b.s4.at[core], gao.at[core])
    s4_swap = remote(b.s4.at[other], gao.at[core], sibling)

    for kind, out_ref in ((3, hout), (5, dxo)):
        for s in range(2):
            for j in range(2):
                from_device(out_ref.at[s, pl.ds(TOKENS * j, TOKENS)], kind, 2 * s + j)
    for s in range(2):
        from_device(mout.at[s], 4, s)
    sf_local.wait()
    s4_local.wait()
    arrived([sf_swap, s4_swap])

    for group in sent[-SENDS:]:
        group.wait_send()
    for same, copy in conditional:

        @pl.when(jnp.logical_not(same))
        def _():
            copy.wait_send()

    @pl.when((seg == 0) & (core == 1))
    def _():
        hops[0].wait_send()
        hops[1].wait_send()

    @pl.when((seg == 0) & (core == 0))
    def _():
        early.wait_send()


def layer(sh, arrays):
    constants = [jnp.asarray(a, BF16) for a in selections(sh)]
    tables = scratch_of(sh)
    names = [list(table) for table in tables]
    anywhere = pl.BlockSpec(memory_space=pl.ANY)
    outs = [
        jax.ShapeDtypeStruct((2, 128, D), BF16),
        jax.ShapeDtypeStruct((2, 8, D), F32),
        jax.ShapeDtypeStruct((2, 128, D), BF16),
        jax.ShapeDtypeStruct((2, sh.pc, ACOLS), F32),
        jax.ShapeDtypeStruct((2, sh.wrows, D), F32),
    ]
    return pl.pallas_call(
        functools.partial(kernel, sh, names),
        name="layer",
        out_shape=outs,
        in_specs=[anywhere] * 15,
        out_specs=[anywhere] * len(outs),
        scratch_shapes=[pltpu.VMEM(*one) for table in tables for one in table.values()]
        + [
            pltpu.SemaphoreType.DMA((SENDS,)),
            pltpu.SemaphoreType.DMA((96,)),
            pltpu.SemaphoreType.DMA((45,)),
            pltpu.SemaphoreType.DMA((20,)),
        ],
        compiler_params=pltpu.CompilerParams(
            collective_id=0, has_side_effects=True, vmem_limit_bytes=64 * 2**20 - 2**17
        ),
    )(*arrays, *constants)


def unpack_kernel(sh, *refs):
    arrays, results, held, outs, sems = refs[:5], refs[5:15], refs[15:20], refs[20:30], refs[30]
    loads = [pltpu.make_async_copy(arrays[i], held[i], sems.at[i]) for i in range(5)]
    stores = [pltpu.make_async_copy(outs[i], results[i], sems.at[5 + i]) for i in range(10)]
    for copy in loads:
        copy.start()
    hout, mout, dxo, gao, gfo = held
    hidden, memory, grad_in, gq, gp, gains, biases, tokens, gi, gt = outs
    ar = sh.arows
    loads[0].wait()
    hidden[...] = hout[...]
    stores[0].start()
    loads[2].wait()
    grad_in[...] = dxo[...].astype(F32)
    stores[2].start()
    loads[1].wait()
    for i in range(2):
        memory[:, i] = mout[i, :5].astype(BF16)
    stores[1].start()
    loads[3].wait()
    for h in range(2):
        for p in range(3):
            for i in range(3):
                to = D * i + HALF * h + 128 * p
                first = HALF * p + 128 * i
                gq[:, to : to + 128] = gao[h, :ar, first : first + 128]
        gp[:, HALF * h : HALF * (h + 1)] = gao[h, :ar, WO : WO + HALF]
    small = gao[0, :, 4 * HALF :] + gao[1, :, 4 * HALF :]
    turned = small.T[:, :ar]
    gains[...] = turned[0:2]
    biases[...] = turned[2:4]
    for kind in range(2):
        tokens[:, kind] = small[:ar, 4 + MEM * kind : 4 + MEM * (kind + 1)]
    for i in range(3, 8):
        stores[i].start()
    loads[4].wait()
    for h in range(2):
        gi[:, HALF * h : HALF * (h + 1)] = gfo[h, :, :HALF]
        gt[:, HALF * h : HALF * (h + 1)] = gfo[h, :, HALF:]
    for i in range(8, 10):
        stores[i].start()
    for copy in stores:
        copy.wait()


def unpack(sh, *arrays):
    ar, wr = sh.arows, sh.wrows
    shapes = [
        ((2, 128, D), BF16),
        ((5, 2, D), BF16),
        ((2, 128, D), F32),
        ((ar, 3 * D), F32),
        ((ar, D), F32),
        ((2, ar), F32),
        ((2, ar), F32),
        ((ar, 2, MEM), F32),
        ((wr, D), F32),
        ((wr, D), F32),
    ]
    anywhere = pl.BlockSpec(memory_space=pl.ANY)
    return pl.pallas_call(
        functools.partial(unpack_kernel, sh),
        name="unpack",
        out_shape=[jax.ShapeDtypeStruct(*one) for one in shapes],
        in_specs=[anywhere] * 5,
        out_specs=[anywhere] * len(shapes),
        scratch_shapes=[pltpu.VMEM(a.shape, a.dtype) for a in arrays]
        + [pltpu.VMEM(*one) for one in shapes]
        + [pltpu.SemaphoreType.DMA((15,))],
        compiler_params=pltpu.CompilerParams(vmem_limit_bytes=64 * 2**20 - 2**17),
    )(*arrays)


def body(
    sh,
    hidden_in,
    reset,
    w_qkv,
    w_attn_out,
    norm_gains,
    norm_biases,
    memory_tokens,
    w_in,
    w_out,
    grad_hidden,
    grad_memory,
):
    arrays = (
        hidden_in,
        grad_hidden,
        grad_memory.transpose(1, 0, 2),
        w_qkv,
        w_attn_out,
        norm_gains,
        norm_biases,
        memory_tokens.transpose(2, 0, 1),
        w_in,
        w_out.T,
    )
    hidden, memory, *middle, tokens, gi, gt = unpack(sh, *layer(sh, arrays))
    return hidden, memory.transpose(1, 0, 2), *middle, tokens.transpose(1, 2, 0), gi, gt.T


def solution(mesh):
    sh = Shape(mesh.shape["dp"])
    return jax.shard_map(
        functools.partial(body, sh),
        mesh=mesh,
        in_specs=(
            P("dp", "tp", None),
            P("dp"),
            P(("dp", "tp"), None),
            P(("dp", "tp"), None),
            P(None, ("dp", "tp")),
            P(None, ("dp", "tp")),
            P(None, None, ("dp", "tp")),
            P("dp", "tp"),
            P("tp", "dp"),
            P("dp", "tp", None),
            P("dp", "tp", None),
        ),
        out_specs=(
            P("dp", "tp", None),
            P("dp", "tp", None),
            P("dp", "tp", None),
            P(("dp", "tp"), None),
            P(("dp", "tp"), None),
            P(None, ("dp", "tp")),
            P(None, ("dp", "tp")),
            P(None, None, ("dp", "tp")),
            P("dp", "tp"),
            P("tp", "dp"),
        ),
        check_vma=False,
    )
```

```python
import functools
import types

import jax
import jax.numpy as jnp
import numpy as np
from jax import lax
from jax.experimental import pallas as pl
from jax.experimental.pallas import tpu as pltpu
from jax.sharding import PartitionSpec as P

D = 768
HALF = 384
MEM = 10
TOKENS = 64
OWN = 272
ROWS = 2 * OWN
TP = 4
SMALL = 128
ACOLS = 4 * HALF + SMALL
REST = ACOLS - HALF
CUT = HALF + 640
WO = 3 * HALF
EPSILON = 1e-05
INV_ROOT_TWO = 0.7071067811865476
INV_ROOT_TWOPI = 0.3989422804014327
EXP_SCALE = 0.125 * 1.4426950408889634
MASKED = -1e30
F32 = jnp.float32
BF16 = jnp.bfloat16
MESH = pl.DeviceIdType.MESH
NN = (((1,), (0,)), ((), ()))
NT = (((1,), (1,)), ((), ()))
TN = (((0,), (0,)), ((), ()))


def dot(a, b, dims=NN):
    return lax.dot_general(a, b, dims, preferred_element_type=F32)


def up16(n):
    return -(-n // 16) * 16


class Shape:
    def __init__(self, dp):
        self.dp = dp
        planes = dp // 2
        self.ny = int(round(planes**0.5))
        self.nz = planes // self.ny
        self.wrows = D // dp
        self.arows = D // (dp * TP)
        self.brows = 2 * self.wrows
        self.pr = up16(self.arows)
        self.xrows = 2 * self.arows * self.ny
        self.pc = -(-self.arows // 8) * 8
        self.fr = up16(self.wrows)


def selections(sh):
    pack = np.zeros((sh.brows, TP * 2 * sh.pc), np.float32)
    for c in range(2):
        for x in range(TP):
            for i in range(sh.arows):
                pack[c * sh.wrows + x * sh.arows + i, (x * 2 + c) * sh.pc + i] = 1
    packy = np.zeros((sh.xrows, sh.ny * 2 * sh.pc), np.float32)
    turn = np.zeros((D, D), np.float32)
    ar = sh.arows
    for c in range(2):
        for y in range(sh.ny):
            for i in range(ar):
                row = (y * 2 + c) * ar + i
                packy[row, (y * 2 + c) * sh.pc + i] = 1
                for x in range(TP):
                    for z in range(sh.nz):
                        place = (z * sh.ny + y) * sh.brows + (c * TP + x) * ar + i
                        turn[(x * sh.nz + z) * sh.xrows + row, place] = 1
    small = np.zeros((48, SMALL), np.float32)
    for i in range(4):
        small[i, i] = 1
    for kind in range(2):
        for i in range(MEM):
            small[16 + 16 * kind + (i // 5) * 8 + i % 5, 4 + MEM * kind + i] = 1
    places = np.zeros((4, MEM, SMALL), np.float32)
    for kind, (rows, first) in enumerate(((2, 0), (2, 2), (MEM, 4), (MEM, 4 + MEM))):
        for i in range(rows):
            places[kind, i, first + i] = 1
    return pack, small, places, packy, turn


def norm_forward(inputs, gain, offset):
    centred = inputs - jnp.mean(inputs, -1, keepdims=True)
    spread = jnp.mean(centred * centred, -1, keepdims=True)
    inverse = lax.rsqrt(spread + EPSILON)
    normed = centred * inverse
    return normed * gain + offset, normed, inverse


def norm_backward(upstream, normed, inverse, gain):
    scaled = upstream * gain
    first_mean = jnp.mean(scaled, -1, keepdims=True)
    second_mean = jnp.mean(scaled * normed, -1, keepdims=True)
    return inverse * (scaled - first_mean - normed * second_mean)


def column_sum(a):
    return jnp.sum(a, 0, keepdims=True)


XBASE = (0, 4, 8, 10, 14, 16, 20)
SENDS = 40
STAGED, LANDED, SUMMED, PASSED, UPDATED = range(5)


def scratch_of(sh):
    nz, ny, br = sh.nz, sh.ny, sh.brows
    ar, wr = sh.arows, sh.wrows
    operands = [
        (5, 2, D),
        (ar, 3 * D),
        (ar, D),
        (2, ar),
        (2, ar),
        (ar, 2, MEM),
        (wr, D),
        (wr, D),
        (br, TP * 2 * sh.pc),
        (48, SMALL),
        (4, MEM, SMALL),
        (sh.xrows, ny * 2 * sh.pc),
    ]
    jobs = {(STAGED, i, 0): (dims, BF16) for i, dims in enumerate(operands)}
    s = dict(
        pk=((2, sh.pr, ACOLS), BF16),
        ff=((2, sh.fr, D), BF16),
        gms=((2, 8, D), F32),
        p1=((2, sh.pr, ACOLS), BF16),
        p2=((TP, 2 * sh.pc, REST), BF16),
        p2y=((ny, 2 * sh.pc, HALF), BF16),
        turn=((D, D), BF16),
        wx=((TP, nz, sh.xrows, HALF), BF16),
        gx=((TP, nz, sh.xrows, HALF), BF16),
        f1=((2, sh.fr, D), BF16),
        wa=((nz, ny, br, ACOLS), BF16),
        wf=((TP, nz, ny, br, D), BF16),
        wo=((2, nz, ny, br, HALF), BF16),
        par=((8, D), F32),
        both=((2, ROWS, D), BF16),
        gyt=((TP * TOKENS, D), BF16),
        gm=((2, 8, D), F32),
        qkv=((9, ROWS, 128), BF16),
        pt=((6, ROWS, ROWS), BF16),
        ot=((3, 128, ROWS), BF16),
        oc=((ROWS, HALF), BF16),
        oin=((OWN, HALF), BF16),
        h1=((OWN, D), F32),
        n1=((OWN, D), F32),
        inv1=((OWN, 1), F32),
        h1b=((ROWS, D), BF16),
        gl=((2, ROWS, D), BF16),
        ul=((2, ROWS, D), F32),
        fs=((OWN, D), BF16),
        fr=((OWN, D), BF16),
        n2=((OWN, D), F32),
        yb=((OWN, D), BF16),
        mo=((2, 8, D), F32),
        hop=((16, D), BF16),
        hopin=((16, D), BF16),
        es=((16, D), F32),
        er=((16, D), F32),
        dz=((OWN, D), F32),
        dfb=((ROWS, D), BF16),
        du=((2, ROWS, D), BF16),
        dhs=((OWN, D), BF16),
        dhr=((OWN, D), BF16),
        dr=((OWN, D), F32),
        dab=((ROWS, D), BF16),
        doc=((3, ROWS, 128), BF16),
        dqkv=((9, ROWS, 128), BF16),
        ga=((nz, ny, br, ACOLS), BF16),
        gi=((TP, nz, ny, br, HALF), BF16),
        gt=((TP, nz, ny, br, HALF), BF16),
        dxs=((OWN, D), BF16),
        dxr=((OWN, D), BF16),
        dxb=((TP * TOKENS, D), BF16),
        sg=((48, D), F32),
        e3=((TP, 2 * sh.pc, REST), BF16),
        r3=((TP - 1, 2 * sh.pc, REST), BF16),
        e3y=((ny, 2 * sh.pc, HALF), BF16),
        r3y=((max(1, ny - 1), 2 * sh.pc, HALF), BF16),
        s4=((2, sh.pc, ACOLS), F32),
        sf=((2, sh.wrows, D), F32),
    )
    s.update(gos=((nz // 2, ny, br, HALF) if nz > 1 else (1, 1, HALF, HALF), BF16))
    sizes = {"x": TP, "z": nz, "y": ny}
    for name, order, cols, axes in scatter_jobs():
        left = [a for a in axes]
        block = (sh.xrows if name[0] == "x" else br, cols.stop - cols.start)
        for step, axis in enumerate(order):
            left = [a for a in left if a != axis]
            dims = tuple(sizes[a] for a in left)
            ring = step == 0 and name in RINGS and sizes[axis] == 4
            jobs[LANDED, step, name] = ((2 if ring else max(1, sizes[axis] - 1),) + dims + block, BF16)
            if step < len(order) - 1:
                jobs[SUMMED, step, name] = (dims + block, BF16)
            if ring:
                jobs[PASSED, 0, name] = ((2, dims[0] // 2) + dims[1:] + block, BF16)
                jobs[UPDATED, 0, name] = jobs[PASSED, 0, name]
    return s, jobs


def scatter_jobs():
    orders = [("z", "y", "x"), ("x", "z", "y"), ("y", "x", "z")]
    jobs = []
    for kind in ("t", "i"):
        for j in range(3):
            jobs.append((f"{kind}{j}", orders[j], slice(128 * j, 128 * j + 128), ("x", "z", "y")))
    zy, yz = ("z", "y"), ("y", "z")
    jobs.append(("aw", yz, slice(WO, WO + HALF), zy))
    jobs.append(("x0", ("x", "z"), slice(0, HALF), ("x", "z")))
    jobs.append(("a1", zy, slice(HALF, 2 * HALF), zy))
    jobs.append(("a2", yz, slice(2 * HALF, 2 * HALF + 256), zy))
    jobs.append(("a3", zy, slice(2 * HALF + 256, 3 * HALF), zy))
    jobs.append(("as", yz, slice(4 * HALF, ACOLS), zy))
    return jobs


def gather_jobs():
    orders = [("x", "y", "z"), ("y", "z", "x"), ("z", "x", "y")]
    jobs = [(f"f{j}", orders[j], slice(256 * j, 256 * j + 256), ("x", "z", "y")) for j in range(3)]
    jobs.append(("x0", ("z", "x"), slice(0, HALF), ("x", "z")))
    jobs.append(("a0", ("y", "z"), slice(HALF, CUT), ("z", "y")))
    jobs.append(("a1", ("z", "y"), slice(CUT, ACOLS), ("z", "y")))
    return jobs


RINGS = ("t0", "t1", "t2", "i0", "i1", "i2", "aw", "x0", "a1")
WEIGHTS = {"f": "wf", "a": "wa", "x": "wx"}
GRADS = {"t": "gt", "i": "gi", "a": "ga", "x": "gx"}


def kernel(sh, names, *refs):
    xin, gin = refs[:2]
    hout, mout, dxo, gao, gfo = refs[15:20]
    ssem, rsem, xsem, lsem = refs[-4:]
    count = len(names[0])
    b = types.SimpleNamespace(**dict(zip(names[0], refs[20 : 20 + count])))
    b.xp, b.x = b.both.at[0], b.both.at[1]
    k = dict(zip(names[1], refs[20 + count : -4]))
    staged = [k[STAGED, i, 0] for i in range(12)]
    gmem, wq, wp, gain_in, bias_in, token_in, up_in, down_in = staged[:8]
    packsel, smallsel, places, packy = staged[8:]
    turn = refs[14]
    nz, ny, br, wr, ar = sh.nz, sh.ny, sh.brows, sh.wrows, sh.arows
    pk, ff, gms = b.pk, b.ff, b.gms

    dp = lax.axis_index("dp")
    x = lax.axis_index("tp")
    core = dp % 2
    y = (dp // 2) % ny
    z = dp // (2 * ny)
    other = 1 - core
    chain = x // 2
    seg = jnp.where((x == 1) | (x == 2), 1, 0)
    at = {"x": x, "y": y, "z": z}
    size = {"x": TP, "y": ny, "z": nz}

    def device(x_=x, y_=y, z_=z, c_=core):
        return ((z_ * ny + y_) * 2 + c_, x_)

    near = {a: [(at[a] + o) % size[a] for o in range(size[a])] for a in at}

    def moved_to(axis, offset, core_=core):
        there = dict(at)
        there[axis] = near[axis][offset]
        return device(there["x"], there["y"], there["z"], core_)

    neighbours = {a: [moved_to(a, o) for o in range(size[a])] for a in at}

    def moved(axis, offset):
        return neighbours[axis][offset]

    sibling = device(c_=other)
    sent = []

    class Group:
        def __init__(self, like):
            if len(sent) >= SENDS:
                sent[-SENDS].wait_send()
            self.like = like
            self.number = len(sent)
            sent.append(self)

        def add(self, src, dst, to):
            pltpu.make_async_remote_copy(
                src_ref=src,
                dst_ref=dst,
                send_sem=ssem.at[self.number % SENDS],
                recv_sem=rsem.at[self.number],
                device_id=to,
                device_id_type=MESH,
            ).start()

        def wait_send(self):
            like = self.like()
            pltpu.make_async_copy(like, like, ssem.at[self.number % SENDS]).wait()

        def wait_recv(self):
            like = self.like()
            pltpu.make_async_copy(like, like, rsem.at[self.number]).wait()

    def remote(src, dst, to):
        where = dst if callable(dst) else lambda: dst
        group = Group(where)
        group.add(src, where(), to)
        return group

    def arrived(groups):
        for group in groups:
            group.wait_recv()

    locals_ = [0]

    def local(src, dst):
        copy = pltpu.make_async_copy(src, dst, lsem.at[locals_[0]])
        locals_[0] += 1
        copy.start()
        return copy

    staging = [local(refs[2 + i], staged[i]) for i in range(12)]
    turn_local = local(turn, b.turn)

    barrier = pltpu.get_barrier_semaphore()
    peers = [sibling]
    for o in range(1, TP):
        peers += [moved("x", o), moved_to("x", o, other)]
    for axis in ("y", "z"):
        for o in range(1, size[axis]):
            peers.append(moved(axis, o))
    for peer in peers:
        pl.semaphore_signal(barrier, inc=1, device_id=peer, device_id_type=MESH)

    pk[...] = jnp.zeros(pk.shape, BF16)
    ff[...] = jnp.zeros(ff.shape, BF16)
    gms[...] = jnp.zeros(gms.shape, F32)
    for copy in staging:
        copy.wait()
    small = dot(gain_in[...], places[0, :2], TN) + dot(bias_in[...], places[1, :2], TN)
    small = small + dot(token_in[:, 0], places[2]) + dot(token_in[:, 1], places[3])
    small = small.astype(BF16)
    for h in range(2):
        for p in range(3):
            for i in range(3):
                first = D * i + HALF * h + 128 * p
                pk[h, :ar, HALF * p + 128 * i : HALF * p + 128 * (i + 1)] = wq[:, first : first + 128]
        pk[h, :ar, WO : WO + HALF] = wp[:, HALF * h : HALF * (h + 1)]
        pk[h, :ar, 4 * HALF :] = small
        for j in range(3):
            cols = slice(HALF * h + 128 * j, HALF * h + 128 * (j + 1))
            ff[h, :wr, 256 * j : 256 * j + 128] = up_in[:, cols]
            ff[h, :wr, 256 * j + 128 : 256 * j + 256] = down_in[:, cols]
        gms[h, 0:5] = gmem[:, h].astype(F32)
    pl.semaphore_wait(barrier, len(peers))

    pk_local = local(pk.at[core], b.p1.at[core])
    ff_local = local(ff.at[core], b.f1.at[core])
    pk_swap = remote(pk.at[other], b.p1.at[core], sibling)
    ff_swap = remote(ff.at[other], b.f1.at[core], sibling)

    conditional = []

    def to_device(src, dst, place, here, kind, send_slot):
        copy = pltpu.make_async_remote_copy(
            src_ref=src,
            dst_ref=dst,
            send_sem=xsem.at[25 + XBASE[kind] + send_slot],
            recv_sem=here,
            device_id=device(x_=place[0], c_=place[1]),
            device_id_type=MESH,
        )
        same = (place[0] == x) & (place[1] == core)

        @pl.when(same)
        def _():
            pltpu.make_async_copy(src, dst, here).start()

        @pl.when(jnp.logical_not(same))
        def _():
            copy.start()

        conditional.append((same, copy))

    def from_device(dst, kind, slot):
        pltpu.make_async_copy(dst, dst, xsem.at[XBASE[kind] + slot]).wait()

    def chip_of(k, s):
        return s + k * (3 - 2 * s)

    def send_rows():
        for s in range(2):
            for j in range(2):
                to_device(
                    xin.at[s, pl.ds(TOKENS * j, TOKENS)],
                    b.x.at[pl.ds(pl.multiple_of(OWN * j + TOKENS * x, 16), TOKENS)],
                    (chip_of(core, s), j),
                    xsem.at[XBASE[0] + x],
                    0,
                    2 * s + j,
                )

    def send_upstream():
        for s in range(2):
            for j in range(2):
                to_device(
                    gin.at[s, pl.ds(TOKENS * j, TOKENS)],
                    b.gyt.at[pl.ds(pl.multiple_of(TOKENS * x, 16), TOKENS)],
                    (chip_of(core, s), j),
                    xsem.at[XBASE[1] + x],
                    1,
                    2 * s + j,
                )
            to_device(
                gms.at[s], b.gm.at[x % 2], (chip_of(core, s), x // 2), xsem.at[XBASE[2] + x % 2], 2, s
            )

    def part_of(job, step, place, half=None):
        name, order, cols, axes = job
        fixed = {a: at[a] for a in order[step:]}
        fixed[order[step]] = place
        where = []
        for a in axes:
            if a in fixed:
                where.append(fixed[a])
            elif half is not None:
                where.append(pl.ds(half * (size[a] // 2), size[a] // 2))
                half = None
            else:
                where.append(slice(None))
        return getattr(b, WEIGHTS[name[0]]).at[tuple(where) + (slice(None), cols)]

    def gather_start(name, step):
        job = gathers[name]
        axis = job[1][step]
        n = size[axis]
        own = part_of(job, step, at[axis])
        free = [a for a in job[3] if a not in job[1][step:]]
        relay = n == 4 and step == len(job[1]) - 1 and size[free[0]] % 2 == 0
        state = types.SimpleNamespace(step=step, relay=relay)
        if relay:
            first = [part_of(job, step, at[axis], h) for h in range(2)]
            right, left = moved(axis, 1), moved(axis, n - 1)
            state.right, state.left = (
                remote(first[h], lambda h=h: part_of(job, step, at[axis], h), to) for h, to in ((0, right), (1, left))
            )
            state.every = [Group(lambda: part_of(job, step, pl.ds(0, 2)))]
            state.every[0].add(first[1], first[1], right)
            state.every[0].add(first[0], first[0], left)
        else:
            state.every = [Group(lambda: part_of(job, step, pl.ds(0, n - 1)))] if n > 1 else []
            for o in range(1, n):
                state.every[0].add(own, own, moved(axis, o))
        flying[name] = state

    def gather_pass(name):
        job, state = gathers[name], flying[name]
        if not state.relay:
            return
        axis = job[1][state.step]
        n = size[axis]
        for copy, back, onward, half in ((state.right, n - 1, 1, 0), (state.left, 1, n - 1, 1)):
            arrived([copy])
            piece = part_of(job, state.step, near[axis][back], half)
            state.every[0].add(piece, piece, moved(axis, onward))

    def gather_done(name):
        arrived(flying[name].every)

    gathers = {j[0]: j for j in gather_jobs()}
    flying = {}

    pk_local.wait()
    arrived([pk_swap])
    packed = jnp.concatenate([b.p1[c].astype(F32)[: sh.pc] for c in range(2)], 0).astype(BF16)
    b.p2y[y] = packed[:, :HALF]
    b.p2[x] = packed[:, HALF:]
    mine = b.p2y.at[y]
    ysteps, xsteps = [], [Group(lambda: b.p2.at[: TP - 1])]
    if ny > 1:
        ysteps.append(Group(lambda: b.p2y.at[: ny - 1]))
    for o in range(1, ny):
        ysteps[0].add(mine, mine, moved("y", o))
    mine = b.p2.at[x]
    for o in range(1, TP):
        xsteps[0].add(mine, mine, moved("x", o))
    ff_local.wait()
    arrived([ff_swap])
    two = [b.f1[c].astype(F32)[:wr] for c in range(2)]
    b.wf[x, z, y] = jnp.concatenate(two, 0).astype(BF16)
    feed_names, first_names = ("f1", "f2", "f0"), ("x0", "a0", "a1")
    for n in feed_names:
        gather_start(n, 0)
    send_rows()
    arrived(ysteps)
    b.wx[x, z] = dot(packy[...], b.p2y[...].reshape(ny * 2 * sh.pc, HALF)).astype(BF16)
    gather_start("x0", 0)
    arrived(xsteps)
    b.wa[z, y, :, HALF:] = dot(packsel[...], b.p2[...].reshape(TP * 2 * sh.pc, REST)).astype(BF16)
    for n in ("a0", "a1"):
        gather_start(n, 0)
    for n in feed_names:
        gather_done(n)
        gather_start(n, 1)
    for n in first_names:
        gather_done(n)
        gather_start(n, 1)
    for n in first_names:
        gather_pass(n)
    for n in feed_names:
        gather_done(n)
        gather_start(n, 2)

    for i in range(TP):
        from_device(b.x.at[pl.ds(pl.multiple_of(OWN * core + TOKENS * i, 16), TOKENS)], 0, i)
    half = b.x.at[pl.ds(pl.multiple_of(OWN * core, 16), TP * TOKENS)]
    x_swap = remote(half, half, sibling)
    for first in (256, OWN + 256):
        b.x[first : first + 16] = jnp.zeros((16, D), BF16)
    turn_local.wait()
    arrived([x_swap])

    @pl.loop(0, 2)
    def _(i):
        rows = pl.ds(pl.multiple_of(OWN * i, 16), OWN)
        b.xp[rows] = dot(b.x[rows], b.turn[...], NT).astype(BF16)

    for n in first_names:
        gather_done(n)
    wo_cols = slice(WO, WO + HALF)
    wo_local = local(b.wa.at[:, :, :, wo_cols], b.wo.at[core])
    wo_swap = remote(b.wa.at[:, :, :, wo_cols], b.wo.at[core], sibling)
    gather_pass("f1")
    send_upstream()

    def attention_weight():
        return b.wa[:, :, :, :WO].reshape(D, WO)

    small = b.wa[:, :, :, 4 * HALF :].reshape(D, SMALL)
    chosen = dot(smallsel[...], small, NT)
    b.par[...] = chosen[0:8]
    memory = chosen[16:48].astype(BF16)
    b.x[OWN + 256 : OWN + 272] = memory[16:]
    turned = dot(memory, b.turn[...], NT).astype(BF16)
    b.xp[OWN + 256 : OWN + 272] = turned[16:]

    @pl.when(seg == 0)
    def _():
        b.x[256:272] = memory[:16]
        b.xp[256:272] = turned[:16]

    gains = [b.par[i : i + 1] for i in range(2)]
    biases = [b.par[2 + i : 3 + i] for i in range(2)]

    hop_to = jnp.where(x == 0, 1, 2)
    hops = []
    for j in range(2):
        hops.append(
            pltpu.make_async_remote_copy(
                src_ref=b.hop,
                dst_ref=b.hopin,
                send_sem=xsem.at[XBASE[6] + j],
                recv_sem=xsem.at[XBASE[6] + 2],
                device_id=device(x_=hop_to, c_=j),
                device_id_type=MESH,
            )
        )

    own_rows = pl.ds(pl.multiple_of(OWN * core, 16), OWN)
    other_rows = pl.ds(pl.multiple_of(OWN * other, 16), OWN)

    out = dot(b.xp[...], b.wx[...].reshape(D, HALF)).astype(BF16)
    for i in range(3):
        b.qkv[i] = out[:, 128 * i : 128 * i + 128]
    out = dot(b.x[...], b.wa[:, :, :, HALF:WO].reshape(D, 2 * HALF)).astype(BF16)
    for i in range(3, 9):
        b.qkv[i] = out[:, 128 * (i - 3) : 128 * (i - 2)]

    def head_masks(hh):
        lane = lax.broadcasted_iota(jnp.int32, (ROWS, 128), 1)
        row = lax.broadcasted_iota(jnp.int32, (ROWS, 128), 0)
        inside = (lane // 64) == hh
        spare = lane == 64 * (1 - hh)
        memory = ((row >= 256) & (row < 272)) | (row >= OWN + 256)
        invalid = memory & (row % 8 >= 5)
        return inside, spare, invalid

    def forward_pair(p):
        qp, kp, vp = (b.qkv[3 * p + i] for i in range(3))
        vt = vp.T
        for hh in range(2):
            inside, spare, invalid = head_masks(hh)
            zero = jnp.zeros_like(kp)
            kmask = jnp.where(spare & invalid, jnp.full_like(kp, MASKED), zero)
            km = jnp.where(inside, kp, kmask)
            qm = jnp.where(inside, qp, jnp.where(spare, jnp.ones_like(qp), zero))
            scores = dot(km, qm, NT)
            peak = jnp.max(scores, 0, keepdims=True)
            raised = jnp.exp2((scores - peak) * EXP_SCALE)
            total = jnp.sum(raised, 0, keepdims=True)
            probs = (raised * (1.0 / total)).astype(BF16)
            b.pt[2 * p + hh] = probs
            b.ot[p, 64 * hh : 64 * hh + 64] = dot(vt[64 * hh : 64 * hh + 64], probs).astype(BF16)
        b.oc[:, pl.ds(pl.multiple_of(128 * p, 128), 128)] = b.ot[p].T

    @pl.loop(0, 3)
    def _(j):
        cols = pl.ds(pl.multiple_of(128 * j, 128), 128)
        block = dot(b.turn[...], b.wx[:, :, :, cols].reshape(D, 128), TN).astype(BF16)
        b.wa[:, :, :, cols] = block.reshape(nz, ny, br, 128)

    @pl.loop(0, 2)
    def _(i):
        @pl.when((i == 1) & (seg == 1))
        def _():
            hops[0].wait_recv()
            b.x[256:272] = b.hopin[...]
            rows = dot(b.hopin[...], attention_weight()).astype(BF16)
            for j in range(9):
                b.qkv[j, 256:272] = rows[:, 128 * j : 128 * j + 128]

        @pl.when(i == seg)
        def _():
            for p in range(3):
                forward_pair(p)

        @pl.when(i == 0)
        def _():
            for n in ("f2", "f0"):
                gather_pass(n)

    def head_rows(ref, c):
        if nz > 1:
            return ref.at[pl.ds(c * (nz // 2), nz // 2)]
        return ref.at[:, :, pl.ds(pl.multiple_of(c * HALF, 16), HALF)]

    def wo_rows(h, c):
        return head_rows(b.wo.at[h], c)[...].reshape(HALF, HALF)

    o_swap = remote(b.oc.at[other_rows], b.oin, sibling)
    wo_local.wait()
    arrived([wo_swap])
    halves = [dot(b.oc[own_rows], wo_rows(h, core)) for h in range(2)]
    arrived([o_swap])
    attended = jnp.concatenate([halves[h] + dot(b.oin[...], wo_rows(h, other)) for h in range(2)], 1)
    h1, n1, inv1 = norm_forward(b.x[own_rows].astype(F32) + attended, gains[0], biases[0])
    b.h1[...] = h1
    b.n1[...] = n1
    b.inv1[...] = inv1
    b.h1b[own_rows] = h1.astype(BF16)
    h_swap = remote(b.h1b.at[own_rows], b.h1b.at[own_rows], sibling)

    @pl.when(seg == 1)
    def _():
        b.xp[256:272] = dot(b.hopin[...], b.turn[...], NT).astype(BF16)

    for n in ("f1", "f2", "f0"):
        gather_done(n)

    def feed_weight(t, kind):
        cols = [256 * j + 128 * kind for j in range(3)]
        blocks = [b.wf[2 * t + i, :, :, :, c : c + 128].reshape(D, 128) for i in range(2) for c in cols]
        return jnp.concatenate(blocks, 1)

    def up_weight(t):
        return feed_weight(t, 0)

    def down_weight(t):
        return feed_weight(t, 1)

    def gelu_share(units):
        return 0.5 * (1.0 + lax.erf(units * INV_ROOT_TWO))

    early = pltpu.make_async_remote_copy(
        src_ref=b.es,
        dst_ref=b.er,
        send_sem=xsem.at[XBASE[6] + 3],
        recv_sem=xsem.at[XBASE[6] + 4],
        device_id=sibling,
        device_id_type=MESH,
    )
    row16 = lax.broadcasted_iota(jnp.int32, (16, D), 0)

    @pl.when(seg == 0)
    def _():
        arrived([h_swap])
        rows = b.h1b[OWN + 256 : OWN + 272]
        units = [dot(rows, up_weight(t)) for t in range(2)]
        part = sum(dot((units[t] * gelu_share(units[t])).astype(BF16), down_weight(t), NT) for t in range(2))

        @pl.when(core == 0)
        def _():
            b.es[...] = part
            early.start()

        @pl.when(core == 1)
        def _():
            early.wait_recv()
            whole = b.h1[256:272] + part + b.er[...]
            written = norm_forward(whole, gains[1], biases[1])[0]
            b.hop[...] = jnp.where(row16 % 8 < 5, written, 0.0).astype(BF16)
            hops[0].start()
            hops[1].start()

    def project_up(rows):
        for t in range(2):
            units = dot(b.h1b[rows], up_weight(t))
            b.ul[t, rows] = units
            b.gl[t, rows] = (units * gelu_share(units)).astype(BF16)

    @pl.loop(0, 2)
    def _(i):
        @pl.when((i == 1) & (seg == 1))
        def _():
            arrived([h_swap])

        project_up(pl.ds(pl.multiple_of(OWN * jnp.where(i == 0, core, other), 16), OWN))


    def partial_down(rows):
        return sum(dot(b.gl[t, rows], down_weight(t), NT) for t in range(2))

    b.fs[...] = partial_down(other_rows).astype(BF16)
    f_swap = remote(b.fs, b.fr, sibling)
    branch = partial_down(own_rows)
    arrived([f_swap])
    out, n2, inv2 = norm_forward(b.h1[...] + branch + b.fr[...].astype(F32), gains[1], biases[1])
    low = out.astype(BF16)
    b.yb[...] = low
    b.mo[...] = low[256:272].astype(F32).reshape(2, 8, D)
    for i in range(TP):
        to_device(
            b.yb.at[pl.ds(TOKENS * i, TOKENS)],
            hout.at[seg, pl.ds(pl.multiple_of(TOKENS * core, 16), TOKENS)],
            (i, chain),
            xsem.at[XBASE[3] + 2 * seg + core],
            3,
            i,
        )
    for i in range(2):
        to_device(b.mo.at[i], mout.at[seg], (2 * core + i, chain), xsem.at[XBASE[4] + seg], 4, i)

    for i in range(TP):
        from_device(b.gyt.at[pl.ds(TOKENS * i, TOKENS)], 1, i)
    for i in range(2):
        from_device(b.gm.at[i], 2, i)
    upstream = jnp.concatenate([b.gyt[...].astype(F32), b.gm[...].reshape(16, D)], 0)
    b.sg[...] = jnp.zeros((48, D), F32)
    b.sg[1:2] = column_sum(upstream * n2)
    b.sg[3:4] = column_sum(upstream)
    dz = norm_backward(upstream, n2, inv2, gains[1])
    b.dz[...] = dz
    b.dfb[own_rows] = dz.astype(BF16)
    df_swap = remote(b.dfb.at[own_rows], b.dfb.at[own_rows], sibling)

    def weight_grad(into, left, right, jobs_):
        @pl.loop(0, 2)
        def _(t):
            part = dot(left[...], right[t], TN).astype(BF16)
            for i in range(2):
                into[2 * t + i] = part[:, HALF * i : HALF * (i + 1)].reshape(nz, ny, br, HALF)

            for h in range(2):

                @pl.when(t == h)
                def _():
                    for n in jobs_:
                        if is_ring(n, 0) and scatters[n][1][0] != "x":
                            ring_send(n, h)
                        elif h == 1:
                            scatter_send(n, 0)

    scatters = {j[0]: j for j in scatter_jobs()}
    rs = {}

    def is_ring(name, step):
        _, order, cols, axes = scatters[name]
        return step == 0 and name in RINGS and size[order[0]] == 4

    def source_of(name, step):
        _, order, cols, axes = scatters[name]
        axis = order[step]
        left = [a for a in axes if a not in order[:step]]
        array = getattr(b, GRADS[name[0]]) if step == 0 else k[SUMMED, step - 1, name]
        tail = (slice(None), cols) if step == 0 else ()

        def part(place, half=None):
            where = []
            for a in left:
                if a == axis:
                    where.append(place)
                elif half is not None:
                    where.append(pl.ds(half * (size[a] // 2), size[a] // 2))
                    half = None
                else:
                    where.append(slice(None))
            return array.at[tuple(where) + tail]

        return part

    def ring_send(name, half):
        axis = scatters[name][1][0]
        n = size[axis]
        part = source_of(name, 0)
        landing, over = k[LANDED, 0, name], k[PASSED, 0, name]
        right, left, far = (near[axis][o] for o in (1, n - 1, 2))
        to = moved(axis, 1), moved(axis, n - 1)
        cut = size[[a for a in scatters[name][3] if a != axis][0]] // 2
        if name not in rs:
            rs[name] = ([None, None], Group(lambda: landing), cut, (right, left), to)
        rs[name][0][half] = remote(part(far, half), lambda: over.at[half], to[half])
        if half == 0:
            rs[name][1].add(part(left, 0), landing.at[1, :cut], to[1])
        else:
            rs[name][1].add(part(right, 1), landing.at[0, cut:], to[0])

    def scatter_send(name, step):
        axis = scatters[name][1][step]
        n = size[axis]
        part = source_of(name, step)
        landing = k[LANDED, step, name]
        if is_ring(name, step):
            ring_send(name, 0)
            ring_send(name, 1)
            return
        rs[name] = [Group(lambda: landing)] if n > 1 else []
        for o in range(1, n):
            rs[name][0].add(part(near[axis][o]), landing.at[o - 1], moved(axis, o))

    def scatter_pass(name):
        if not is_ring(name, 0):
            return
        passing, coming, half, places_, devices = rs[name]
        part = source_of(name, 0)
        landing, over, updated = k[LANDED, 0, name], k[PASSED, 0, name], k[UPDATED, 0, name]
        for i in range(2):
            arrived([passing[i]])
            updated[i] = (part(places_[i], i)[...].astype(F32) + over[i].astype(F32)).astype(BF16)
            where = landing.at[0, :half] if i == 0 else landing.at[1, half:]
            coming.add(updated.at[i], where, devices[i])

    def scatter_sum(name, step):
        _, order, cols, axes = scatters[name]
        axis = order[step]
        total = source_of(name, step)(at[axis])[...].astype(F32)
        ring = is_ring(name, step)
        arrived([rs[name][1]] if ring else rs[name])
        for o in range(2 if ring else size[axis] - 1):
            total = total + k[LANDED, step, name][o].astype(F32)
        if step < len(order) - 1:
            k[SUMMED, step, name][...] = total.astype(BF16)
        return total

    def scatter_on(names, step):
        for n in names:
            scatter_sum(n, step)
            scatter_send(n, step + 1)

    down_names, up_names = ("t0", "t1", "t2"), ("i0", "i1", "i2")
    arrived([df_swap])
    weight_grad(b.gt, b.dfb, b.gl, down_names)
    @pl.loop(0, 2)
    def _(i):
        rows = pl.ds(pl.multiple_of(OWN * i, 16), OWN)
        for t in range(2):
            units = b.ul[t, rows]
            slope = gelu_share(units) + units * jnp.exp(-0.5 * units * units) * INV_ROOT_TWOPI
            b.du[t, rows] = (dot(b.dfb[rows], down_weight(t)) * slope).astype(BF16)

    weight_grad(b.gi, b.h1b, b.du, up_names)
    for n in down_names:
        scatter_pass(n)

    def partial_up(rows):
        return sum(dot(b.du[t, rows], up_weight(t), NT) for t in range(2))

    dh_swap = Group(lambda: b.dhr)

    @pl.loop(0, 2)
    def _(i):
        part = partial_up(pl.ds(pl.multiple_of(OWN * jnp.where(i == 0, other, core), 16), OWN))

        @pl.when(i == 0)
        def _():
            b.dhs[...] = part.astype(BF16)
            dh_swap.add(b.dhs, b.dhr, sibling)

        @pl.when(i == 1)
        def _():
            b.dz[...] = b.dz[...] + part

    arrived([dh_swap])
    into_first = b.dz[...] + b.dhr[...].astype(F32)
    b.sg[0:1] = column_sum(into_first * b.n1[...])
    b.sg[2:3] = column_sum(into_first)
    dr = norm_backward(into_first, b.n1[...], b.inv1[...], gains[0])
    b.dr[...] = dr
    b.dab[own_rows] = dr.astype(BF16)
    da_swap = remote(b.dab.at[own_rows], b.dab.at[own_rows], sibling)

    def grad_mixed(rows):
        parts = [dot(b.dab[rows, HALF * h : HALF * (h + 1)], wo_rows(h, core), NT) for h in range(2)]
        for p in range(3):
            b.doc[p, rows] = (parts[0] + parts[1])[:, 128 * p : 128 * p + 128].astype(BF16)

    grad_mixed(own_rows)
    arrived([da_swap])
    grad_mixed(other_rows)

    mixed_t = b.ot[...].reshape(HALF, ROWS)

    def proj_grad(h):
        cols = pl.ds(pl.multiple_of(HALF * h, 128), HALF)
        return dot(mixed_t, b.dab[:, cols]).astype(BF16).reshape(b.gos.shape)

    def wo_part(c):
        return head_rows(b.ga.at[:, :, :, wo_cols], c)

    b.gos[...] = proj_grad(other)
    go_swap = remote(b.gos, wo_part(core), sibling)
    wo_part(core)[...] = proj_grad(core)

    def backward_pair(p):
        qp, kp, vp = (b.qkv[3 * p + i] for i in range(3))
        dop = b.doc[p]
        kt = kp.T
        dv = dk = 0.0
        dq = []
        for hh in range(2):
            inside, _, _ = head_masks(hh)
            zero = jnp.zeros_like(kp)
            grad_probs = dot(jnp.where(inside, vp, zero), dop, NT)
            low_probs = b.pt[2 * p + hh]
            probs = low_probs.astype(F32)
            row_term = jnp.sum(probs * grad_probs, 0, keepdims=True)
            ds = (probs * (grad_probs - row_term)).astype(BF16)
            dv = dv + dot(low_probs, jnp.where(inside, dop, zero))
            dk = dk + dot(ds, jnp.where(inside, qp, zero))
            dq.append(dot(kt[64 * hh : 64 * hh + 64], ds))
        b.dqkv[3 * p] = (jnp.concatenate(dq, 0) * 0.125).T.astype(BF16)
        b.dqkv[3 * p + 1] = (dk * 0.125).astype(BF16)
        b.dqkv[3 * p + 2] = dv.astype(BF16)

    def joined(rows, wanted):
        return jnp.concatenate([b.dqkv[i, rows] for i in wanted], 1)

    def attention_grad(p):
        grads = jnp.concatenate([b.dqkv[3 * p + i] for i in range(3)], 1)

        part = dot(b.both[jnp.minimum(p, 1)], grads, TN).astype(BF16)

        @pl.when(p == 0)
        def _():
            b.gx[...] = part.reshape(TP, nz, sh.xrows, HALF)

        @pl.when(p > 0)
        def _():
            cols = pl.ds(pl.multiple_of(HALF * p, 128), HALF)
            b.ga[:, :, :, cols] = part.reshape(nz, ny, br, HALF)

    @pl.loop(0, 3)
    def _(p):
        backward_pair(p)
        attention_grad(p)

        @pl.when(p == 0)
        def _():
            arrived([go_swap])
            scatter_send("aw", 0)
            scatter_send("x0", 0)
            for n in up_names:
                scatter_pass(n)

        @pl.when(p == 1)
        def _():
            scatter_send("a1", 0)
            scatter_on(down_names, 0)
            for n in ("aw", "x0"):
                scatter_pass(n)

        @pl.when(p == 2)
        def _():
            scatter_send("a2", 0)
            scatter_send("a3", 0)
            scatter_pass("a1")
            scatter_on(up_names, 0)


    def partial_input(rows):
        return dot(joined(rows, range(9)), attention_weight(), NT)

    b.dxs[...] = partial_input(other_rows).astype(BF16)
    dx_swap = remote(b.dxs, b.dxr, sibling)
    dx = partial_input(own_rows) + b.dr[...]
    arrived([dx_swap])
    dx = dx + b.dxr[...].astype(F32)
    b.dxb[...] = dx[:256].astype(BF16)
    for i in range(TP):
        to_device(
            b.dxb.at[pl.ds(TOKENS * i, TOKENS)],
            dxo.at[seg, pl.ds(pl.multiple_of(TOKENS * core, 16), TOKENS)],
            (i, chain),
            xsem.at[XBASE[5] + 2 * seg + core],
            5,
            i,
        )

    @pl.when((core == 0) & (seg == 0))
    def _():
        b.sg[16:32] = dx[256:272]

    @pl.when(core == 1)
    def _():
        b.sg[32:48] = dx[256:272]

    small_grads = dot(b.sg[...].astype(BF16), smallsel[...], TN).astype(BF16)
    b.ga[:, :, :, 4 * HALF :] = small_grads.reshape(nz, ny, br, SMALL)
    scatter_send("as", 0)
    attention_names = ("aw", "x0", "a1", "a2", "a3", "as")
    scatter_on(down_names, 1)
    scatter_on(attention_names, 0)
    scatter_on(up_names, 1)

    def last_rows(names, first_col):
        for j, n in enumerate(names):
            total = scatter_sum(n, 2)
            cols = slice(first_col + 128 * j, first_col + 128 * j + 128)
            b.sf[0, :, cols] = total[:wr]
            b.sf[1, :, cols] = total[wr:]

    for n in attention_names:
        cols = scatters[n][2]
        total = scatter_sum(n, 1).astype(BF16)
        if n == "x0":
            spread = dot(packy[...], total, TN).astype(BF16)
            b.e3y[...] = spread.reshape(ny, 2 * sh.pc, HALF)
            ysteps = [Group(lambda: b.r3y)] if ny > 1 else []
            for o in range(1, ny):
                ysteps[0].add(b.e3y.at[(y + o) % ny], b.r3y.at[o - 1], moved("y", o))
        else:
            spread = dot(packsel[...], total, TN).astype(BF16)
            b.e3[:, :, cols.start - HALF : cols.stop - HALF] = spread.reshape(TP, 2 * sh.pc, cols.stop - cols.start)
    steps = [Group(lambda: b.r3)]
    for o in range(1, TP):
        steps[0].add(b.e3.at[(x + o) % TP], b.r3.at[o - 1], moved("x", o))
    last_rows(down_names, HALF)
    last_rows(up_names, 0)
    sf_local = local(b.sf.at[core], gfo.at[core])
    sf_swap = remote(b.sf.at[other], gfo.at[core], sibling)

    arrived(steps)
    total = b.e3[x].astype(F32)
    for o in range(1, TP):
        total = total + b.r3[o - 1].astype(F32)
    b.s4[:, :, HALF:] = total.reshape(2, sh.pc, REST)
    arrived(ysteps)
    total = b.e3y[y].astype(F32)
    for o in range(1, ny):
        total = total + b.r3y[o - 1].astype(F32)
    b.s4[:, :, :HALF] = total.reshape(2, sh.pc, HALF)
    s4_local = local(b.s4.at[core], gao.at[core])
    s4_swap = remote(b.s4.at[other], gao.at[core], sibling)

    for kind, out_ref in ((3, hout), (5, dxo)):
        for s in range(2):
            for j in range(2):
                from_device(out_ref.at[s, pl.ds(TOKENS * j, TOKENS)], kind, 2 * s + j)
    for s in range(2):
        from_device(mout.at[s], 4, s)
    sf_local.wait()
    s4_local.wait()
    arrived([sf_swap, s4_swap])

    for group in sent[-SENDS:]:
        group.wait_send()
    for same, copy in conditional:

        @pl.when(jnp.logical_not(same))
        def _():
            copy.wait_send()

    @pl.when((seg == 0) & (core == 1))
    def _():
        hops[0].wait_send()
        hops[1].wait_send()

    @pl.when((seg == 0) & (core == 0))
    def _():
        early.wait_send()


def layer(sh, arrays):
    constants = [jnp.asarray(a, BF16) for a in selections(sh)]
    tables = scratch_of(sh)
    names = [list(table) for table in tables]
    anywhere = pl.BlockSpec(memory_space=pl.ANY)
    outs = [
        jax.ShapeDtypeStruct((2, 128, D), BF16),
        jax.ShapeDtypeStruct((2, 8, D), F32),
        jax.ShapeDtypeStruct((2, 128, D), BF16),
        jax.ShapeDtypeStruct((2, sh.pc, ACOLS), F32),
        jax.ShapeDtypeStruct((2, sh.wrows, D), F32),
    ]
    return pl.pallas_call(
        functools.partial(kernel, sh, names),
        name="layer",
        out_shape=outs,
        in_specs=[anywhere] * 15,
        out_specs=[anywhere] * len(outs),
        scratch_shapes=[pltpu.VMEM(*one) for table in tables for one in table.values()]
        + [
            pltpu.SemaphoreType.DMA((SENDS,)),
            pltpu.SemaphoreType.DMA((96,)),
            pltpu.SemaphoreType.DMA((45,)),
            pltpu.SemaphoreType.DMA((20,)),
        ],
        compiler_params=pltpu.CompilerParams(
            collective_id=0, has_side_effects=True, vmem_limit_bytes=64 * 2**20 - 2**17
        ),
    )(*arrays, *constants)


def unpack_kernel(sh, *refs):
    arrays, results, held, outs, sems = refs[:5], refs[5:15], refs[15:20], refs[20:30], refs[30]
    loads = [pltpu.make_async_copy(arrays[i], held[i], sems.at[i]) for i in range(5)]
    stores = [pltpu.make_async_copy(outs[i], results[i], sems.at[5 + i]) for i in range(10)]
    for copy in loads:
        copy.start()
    hout, mout, dxo, gao, gfo = held
    hidden, memory, grad_in, gq, gp, gains, biases, tokens, gi, gt = outs
    ar = sh.arows
    loads[0].wait()
    hidden[...] = hout[...]
    stores[0].start()
    loads[2].wait()
    grad_in[...] = dxo[...].astype(F32)
    stores[2].start()
    loads[1].wait()
    for i in range(2):
        memory[:, i] = mout[i, :5].astype(BF16)
    stores[1].start()
    loads[3].wait()
    for h in range(2):
        for p in range(3):
            for i in range(3):
                to = D * i + HALF * h + 128 * p
                first = HALF * p + 128 * i
                gq[:, to : to + 128] = gao[h, :ar, first : first + 128]
        gp[:, HALF * h : HALF * (h + 1)] = gao[h, :ar, WO : WO + HALF]
    small = gao[0, :, 4 * HALF :] + gao[1, :, 4 * HALF :]
    turned = small.T[:, :ar]
    gains[...] = turned[0:2]
    biases[...] = turned[2:4]
    for kind in range(2):
        tokens[:, kind] = small[:ar, 4 + MEM * kind : 4 + MEM * (kind + 1)]
    for i in range(3, 8):
        stores[i].start()
    loads[4].wait()
    for h in range(2):
        gi[:, HALF * h : HALF * (h + 1)] = gfo[h, :, :HALF]
        gt[:, HALF * h : HALF * (h + 1)] = gfo[h, :, HALF:]
    for i in range(8, 10):
        stores[i].start()
    for copy in stores:
        copy.wait()


def unpack(sh, *arrays):
    ar, wr = sh.arows, sh.wrows
    shapes = [
        ((2, 128, D), BF16),
        ((5, 2, D), BF16),
        ((2, 128, D), F32),
        ((ar, 3 * D), F32),
        ((ar, D), F32),
        ((2, ar), F32),
        ((2, ar), F32),
        ((ar, 2, MEM), F32),
        ((wr, D), F32),
        ((wr, D), F32),
    ]
    anywhere = pl.BlockSpec(memory_space=pl.ANY)
    return pl.pallas_call(
        functools.partial(unpack_kernel, sh),
        name="unpack",
        out_shape=[jax.ShapeDtypeStruct(*one) for one in shapes],
        in_specs=[anywhere] * 5,
        out_specs=[anywhere] * len(shapes),
        scratch_shapes=[pltpu.VMEM(a.shape, a.dtype) for a in arrays]
        + [pltpu.VMEM(*one) for one in shapes]
        + [pltpu.SemaphoreType.DMA((15,))],
        compiler_params=pltpu.CompilerParams(vmem_limit_bytes=64 * 2**20 - 2**17),
    )(*arrays)


def body(
    sh,
    hidden_in,
    reset,
    w_qkv,
    w_attn_out,
    norm_gains,
    norm_biases,
    memory_tokens,
    w_in,
    w_out,
    grad_hidden,
    grad_memory,
):
    arrays = (
        hidden_in,
        grad_hidden,
        grad_memory.transpose(1, 0, 2),
        w_qkv,
        w_attn_out,
        norm_gains,
        norm_biases,
        memory_tokens.transpose(2, 0, 1),
        w_in,
        w_out.T,
    )
    hidden, memory, *middle, tokens, gi, gt = unpack(sh, *layer(sh, arrays))
    return hidden, memory.transpose(1, 0, 2), *middle, tokens.transpose(1, 2, 0), gi, gt.T


def solution(mesh):
    sh = Shape(mesh.shape["dp"])
    return jax.shard_map(
        functools.partial(body, sh),
        mesh=mesh,
        in_specs=(
            P("dp", "tp", None),
            P("dp"),
            P(("dp", "tp"), None),
            P(("dp", "tp"), None),
            P(None, ("dp", "tp")),
            P(None, ("dp", "tp")),
            P(None, None, ("dp", "tp")),
            P("dp", "tp"),
            P("tp", "dp"),
            P("dp", "tp", None),
            P("dp", "tp", None),
        ),
        out_specs=(
            P("dp", "tp", None),
            P("dp", "tp", None),
            P("dp", "tp", None),
            P(("dp", "tp"), None),
            P(("dp", "tp"), None),
            P(None, ("dp", "tp")),
            P(None, ("dp", "tp")),
            P(None, None, ("dp", "tp")),
            P("dp", "tp"),
            P("tp", "dp"),
        ),
        check_vma=False,
    )
```

```python
import functools
import types

import jax
import jax.numpy as jnp
import numpy as np
from jax import lax
from jax.experimental import pallas as pl
from jax.experimental.pallas import tpu as pltpu
from jax.sharding import PartitionSpec as P

D = 768
HALF = 384
MEM = 10
TOKENS = 64
OWN = 272
ROWS = 2 * OWN
TP = 4
SMALL = 128
ACOLS = 4 * HALF + SMALL
REST = ACOLS - HALF
CUT = HALF + 640
WO = 3 * HALF
EPSILON = 1e-05
INV_ROOT_TWO = 0.7071067811865476
INV_ROOT_TWOPI = 0.3989422804014327
EXP_SCALE = 0.125 * 1.4426950408889634
MASKED = -1e30
F32 = jnp.float32
BF16 = jnp.bfloat16
MESH = pl.DeviceIdType.MESH
NN = (((1,), (0,)), ((), ()))
NT = (((1,), (1,)), ((), ()))
TN = (((0,), (0,)), ((), ()))


def dot(a, b, dims=NN):
    return lax.dot_general(a, b, dims, preferred_element_type=F32)


def up16(n):
    return -(-n // 16) * 16


class Shape:
    def __init__(self, dp):
        self.dp = dp
        planes = dp // 2
        self.ny = int(round(planes**0.5))
        self.nz = planes // self.ny
        self.wrows = D // dp
        self.arows = D // (dp * TP)
        self.brows = 2 * self.wrows
        self.pr = up16(self.arows)
        self.xrows = 2 * self.arows * self.ny
        self.pc = -(-self.arows // 8) * 8
        self.fr = up16(self.wrows)


def selections(sh):
    pack = np.zeros((sh.brows, TP * 2 * sh.pc), np.float32)
    for c in range(2):
        for x in range(TP):
            for i in range(sh.arows):
                pack[c * sh.wrows + x * sh.arows + i, (x * 2 + c) * sh.pc + i] = 1
    packy = np.zeros((sh.xrows, sh.ny * 2 * sh.pc), np.float32)
    turn = np.zeros((D, D), np.float32)
    ar = sh.arows
    for c in range(2):
        for y in range(sh.ny):
            for i in range(ar):
                row = (y * 2 + c) * ar + i
                packy[row, (y * 2 + c) * sh.pc + i] = 1
                for x in range(TP):
                    for z in range(sh.nz):
                        place = (z * sh.ny + y) * sh.brows + (c * TP + x) * ar + i
                        turn[(x * sh.nz + z) * sh.xrows + row, place] = 1
    small = np.zeros((48, SMALL), np.float32)
    for i in range(4):
        small[i, i] = 1
    for kind in range(2):
        for i in range(MEM):
            small[16 + 16 * kind + (i // 5) * 8 + i % 5, 4 + MEM * kind + i] = 1
    places = np.zeros((4, MEM, SMALL), np.float32)
    for kind, (rows, first) in enumerate(((2, 0), (2, 2), (MEM, 4), (MEM, 4 + MEM))):
        for i in range(rows):
            places[kind, i, first + i] = 1
    return pack, small, places, packy, turn


def norm_forward(inputs, gain, offset):
    centred = inputs - jnp.mean(inputs, -1, keepdims=True)
    spread = jnp.mean(centred * centred, -1, keepdims=True)
    inverse = lax.rsqrt(spread + EPSILON)
    normed = centred * inverse
    return normed * gain + offset, normed, inverse


def norm_backward(upstream, normed, inverse, gain):
    scaled = upstream * gain
    first_mean = jnp.mean(scaled, -1, keepdims=True)
    second_mean = jnp.mean(scaled * normed, -1, keepdims=True)
    return inverse * (scaled - first_mean - normed * second_mean)


def column_sum(a):
    return jnp.sum(a, 0, keepdims=True)


XBASE = (0, 4, 8, 10, 14, 16, 20)
SENDS = 40
STAGED, LANDED, SUMMED, PASSED, UPDATED = range(5)


def scratch_of(sh):
    nz, ny, br = sh.nz, sh.ny, sh.brows
    ar, wr = sh.arows, sh.wrows
    operands = [
        (5, 2, D),
        (ar, 3 * D),
        (ar, D),
        (2, ar),
        (2, ar),
        (ar, 2, MEM),
        (wr, D),
        (wr, D),
        (br, TP * 2 * sh.pc),
        (48, SMALL),
        (4, MEM, SMALL),
        (sh.xrows, ny * 2 * sh.pc),
    ]
    jobs = {(STAGED, i, 0): (dims, BF16) for i, dims in enumerate(operands)}
    s = dict(
        pk=((2, sh.pr, ACOLS), BF16),
        ff=((2, sh.fr, D), BF16),
        gms=((2, 8, D), F32),
        p1=((2, sh.pr, ACOLS), BF16),
        p2=((TP, 2 * sh.pc, REST), BF16),
        p2y=((ny, 2 * sh.pc, HALF), BF16),
        turn=((D, D), BF16),
        wx=((TP, nz, sh.xrows, HALF), BF16),
        gx=((TP, nz, sh.xrows, HALF), BF16),
        f1=((2, sh.fr, D), BF16),
        wa=((nz, ny, br, ACOLS), BF16),
        wf=((TP, nz, ny, br, D), BF16),
        wo=((2, nz, ny, br, HALF), BF16),
        par=((8, D), F32),
        both=((2, ROWS, D), BF16),
        gyt=((TP * TOKENS, D), BF16),
        gm=((2, 8, D), F32),
        qkv=((9, ROWS, 128), BF16),
        pt=((6, ROWS, ROWS), BF16),
        ot=((3, 128, ROWS), BF16),
        oc=((ROWS, HALF), BF16),
        oin=((OWN, HALF), BF16),
        h1=((OWN, D), F32),
        n1=((OWN, D), F32),
        inv1=((OWN, 1), F32),
        h1b=((ROWS, D), BF16),
        gl=((2, ROWS, D), BF16),
        ul=((2, ROWS, D), F32),
        fs=((OWN, D), BF16),
        fr=((OWN, D), BF16),
        n2=((OWN, D), F32),
        yb=((OWN, D), BF16),
        mo=((2, 8, D), F32),
        hop=((16, D), BF16),
        hopin=((16, D), BF16),
        es=((16, D), F32),
        er=((16, D), F32),
        dz=((OWN, D), F32),
        dfb=((ROWS, D), BF16),
        du=((2, ROWS, D), BF16),
        dhs=((OWN, D), BF16),
        dhr=((OWN, D), BF16),
        dr=((OWN, D), F32),
        dab=((ROWS, D), BF16),
        doc=((3, ROWS, 128), BF16),
        dqkv=((9, ROWS, 128), BF16),
        ga=((nz, ny, br, ACOLS), BF16),
        gi=((TP, nz, ny, br, HALF), BF16),
        gt=((TP, nz, ny, br, HALF), BF16),
        dxs=((OWN, D), BF16),
        dxr=((OWN, D), BF16),
        dxb=((TP * TOKENS, D), BF16),
        sg=((48, D), F32),
        ms=((16, D), F32),
        mr=((16, D), F32),
        tot=((br, REST), BF16),
        e3=((TP, 2 * sh.pc, REST), BF16),
        r3=((TP - 1, 2 * sh.pc, REST), BF16),
        e3y=((ny, 2 * sh.pc, HALF), BF16),
        r3y=((max(1, ny - 1), 2 * sh.pc, HALF), BF16),
        s4=((2, sh.pc, ACOLS), F32),
        sf=((2, sh.wrows, D), F32),
    )
    s.update(gos=((nz // 2, ny, br, HALF) if nz > 1 else (1, 1, HALF, HALF), BF16))
    sizes = {"x": TP, "z": nz, "y": ny}
    for name, order, cols, axes in scatter_jobs():
        left = [a for a in axes]
        block = (sh.xrows if name[0] == "x" else br, cols.stop - cols.start)
        for step, axis in enumerate(order):
            left = [a for a in left if a != axis]
            dims = tuple(sizes[a] for a in left)
            ring = step == 0 and name in RINGS and sizes[axis] == 4
            jobs[LANDED, step, name] = ((2 if ring else max(1, sizes[axis] - 1),) + dims + block, BF16)
            if step < len(order) - 1:
                jobs[SUMMED, step, name] = (dims + block, BF16)
            if ring:
                jobs[PASSED, 0, name] = ((2, dims[0] // 2) + dims[1:] + block, BF16)
                jobs[UPDATED, 0, name] = jobs[PASSED, 0, name]
    return s, jobs


def scatter_jobs():
    orders = [("z", "y", "x"), ("x", "z", "y"), ("y", "x", "z")]
    jobs = []
    for kind in ("t", "i"):
        for j in range(3):
            jobs.append((f"{kind}{j}", orders[j], slice(128 * j, 128 * j + 128), ("x", "z", "y")))
    zy, yz = ("z", "y"), ("y", "z")
    jobs.append(("aw", yz, slice(WO, WO + HALF), zy))
    jobs.append(("x0", ("x", "z"), slice(0, HALF), ("x", "z")))
    jobs.append(("a1", zy, slice(HALF, 2 * HALF), zy))
    jobs.append(("a2", yz, slice(2 * HALF, 2 * HALF + 256), zy))
    jobs.append(("a3", zy, slice(2 * HALF + 256, 3 * HALF), zy))
    jobs.append(("as", yz, slice(4 * HALF, ACOLS), zy))
    return jobs


def gather_jobs():
    orders = [("x", "y", "z"), ("y", "z", "x"), ("z", "x", "y")]
    jobs = [(f"f{j}", orders[j], slice(256 * j, 256 * j + 256), ("x", "z", "y")) for j in range(3)]
    jobs.append(("x0", ("z", "x"), slice(0, HALF), ("x", "z")))
    jobs.append(("a0", ("y", "z"), slice(HALF, CUT), ("z", "y")))
    jobs.append(("a1", ("z", "y"), slice(CUT, ACOLS), ("z", "y")))
    return jobs


RINGS = ("t0", "t1", "t2", "i0", "i1", "i2", "aw", "x0", "a1")
WEIGHTS = {"f": "wf", "a": "wa", "x": "wx"}
GRADS = {"t": "gt", "i": "gi", "a": "ga", "x": "gx"}


def kernel(sh, names, *refs):
    xin, gin = refs[:2]
    hout, mout, dxo, gao, gfo = refs[15:20]
    ssem, rsem, xsem, lsem = refs[-4:]
    count = len(names[0])
    b = types.SimpleNamespace(**dict(zip(names[0], refs[20 : 20 + count])))
    b.xp, b.x = b.both.at[0], b.both.at[1]
    k = dict(zip(names[1], refs[20 + count : -4]))
    staged = [k[STAGED, i, 0] for i in range(12)]
    gmem, wq, wp, gain_in, bias_in, token_in, up_in, down_in = staged[:8]
    packsel, smallsel, places, packy = staged[8:]
    turn = refs[14]
    nz, ny, br, wr, ar = sh.nz, sh.ny, sh.brows, sh.wrows, sh.arows
    pk, ff, gms = b.pk, b.ff, b.gms

    dp = lax.axis_index("dp")
    x = lax.axis_index("tp")
    core = dp % 2
    y = (dp // 2) % ny
    z = dp // (2 * ny)
    other = 1 - core
    chain = x // 2
    seg = jnp.where((x == 1) | (x == 2), 1, 0)
    at = {"x": x, "y": y, "z": z}
    size = {"x": TP, "y": ny, "z": nz}

    def device(x_=x, y_=y, z_=z, c_=core):
        return ((z_ * ny + y_) * 2 + c_, x_)

    near = {a: [(at[a] + o) % size[a] for o in range(size[a])] for a in at}

    def moved_to(axis, offset, core_=core):
        there = dict(at)
        there[axis] = near[axis][offset]
        return device(there["x"], there["y"], there["z"], core_)

    neighbours = {a: [moved_to(a, o) for o in range(size[a])] for a in at}

    def moved(axis, offset):
        return neighbours[axis][offset]

    sibling = device(c_=other)
    sent = []

    class Group:
        def __init__(self, like):
            if len(sent) >= SENDS:
                sent[-SENDS].wait_send()
            self.like = like
            self.number = len(sent)
            sent.append(self)

        def add(self, src, dst, to):
            pltpu.make_async_remote_copy(
                src_ref=src,
                dst_ref=dst,
                send_sem=ssem.at[self.number % SENDS],
                recv_sem=rsem.at[self.number],
                device_id=to,
                device_id_type=MESH,
            ).start()

        def wait_send(self):
            like = self.like()
            pltpu.make_async_copy(like, like, ssem.at[self.number % SENDS]).wait()

        def wait_recv(self):
            like = self.like()
            pltpu.make_async_copy(like, like, rsem.at[self.number]).wait()

    def remote(src, dst, to):
        where = dst if callable(dst) else lambda: dst
        group = Group(where)
        group.add(src, where(), to)
        return group

    def arrived(groups):
        for group in groups:
            group.wait_recv()

    locals_ = [0]

    def local(src, dst):
        copy = pltpu.make_async_copy(src, dst, lsem.at[locals_[0]])
        locals_[0] += 1
        copy.start()
        return copy

    staging = [local(refs[2 + i], staged[i]) for i in range(12)]
    turn_local = local(turn, b.turn)

    barrier = pltpu.get_barrier_semaphore()
    peers = [sibling]
    for o in range(1, TP):
        peers += [moved("x", o), moved_to("x", o, other)]
    for axis in ("y", "z"):
        for o in range(1, size[axis]):
            peers.append(moved(axis, o))
    for peer in peers:
        pl.semaphore_signal(barrier, inc=1, device_id=peer, device_id_type=MESH)

    pk[...] = jnp.zeros(pk.shape, BF16)
    ff[...] = jnp.zeros(ff.shape, BF16)
    gms[...] = jnp.zeros(gms.shape, F32)
    for copy in staging:
        copy.wait()
    small = dot(gain_in[...], places[0, :2], TN) + dot(bias_in[...], places[1, :2], TN)
    small = small + dot(token_in[:, 0], places[2]) + dot(token_in[:, 1], places[3])
    small = small.astype(BF16)
    for h in range(2):
        for p in range(3):
            for i in range(3):
                first = D * i + HALF * h + 128 * p
                pk[h, :ar, HALF * p + 128 * i : HALF * p + 128 * (i + 1)] = wq[:, first : first + 128]
        pk[h, :ar, WO : WO + HALF] = wp[:, HALF * h : HALF * (h + 1)]
        pk[h, :ar, 4 * HALF :] = small
        for j in range(3):
            cols = slice(HALF * h + 128 * j, HALF * h + 128 * (j + 1))
            ff[h, :wr, 256 * j : 256 * j + 128] = up_in[:, cols]
            ff[h, :wr, 256 * j + 128 : 256 * j + 256] = down_in[:, cols]
        gms[h, 0:5] = gmem[:, h].astype(F32)
    pl.semaphore_wait(barrier, len(peers))

    pk_local = local(pk.at[core], b.p1.at[core])
    ff_local = local(ff.at[core], b.f1.at[core])
    pk_swap = remote(pk.at[other], b.p1.at[core], sibling)
    ff_swap = remote(ff.at[other], b.f1.at[core], sibling)

    conditional = []

    def to_device(src, dst, place, here, kind, send_slot):
        copy = pltpu.make_async_remote_copy(
            src_ref=src,
            dst_ref=dst,
            send_sem=xsem.at[25 + XBASE[kind] + send_slot],
            recv_sem=here,
            device_id=device(x_=place[0], c_=place[1]),
            device_id_type=MESH,
        )
        same = (place[0] == x) & (place[1] == core)

        @pl.when(same)
        def _():
            pltpu.make_async_copy(src, dst, here).start()

        @pl.when(jnp.logical_not(same))
        def _():
            copy.start()

        conditional.append((same, copy))

    def from_device(dst, kind, slot):
        pltpu.make_async_copy(dst, dst, xsem.at[XBASE[kind] + slot]).wait()

    def chip_of(k, s):
        return s + k * (3 - 2 * s)

    def send_rows():
        for s in range(2):
            for j in range(2):
                to_device(
                    xin.at[s, pl.ds(TOKENS * j, TOKENS)],
                    b.x.at[pl.ds(pl.multiple_of(OWN * j + TOKENS * x, 16), TOKENS)],
                    (chip_of(core, s), j),
                    xsem.at[XBASE[0] + x],
                    0,
                    2 * s + j,
                )

    def send_upstream():
        for s in range(2):
            for j in range(2):
                to_device(
                    gin.at[s, pl.ds(TOKENS * j, TOKENS)],
                    b.gyt.at[pl.ds(pl.multiple_of(TOKENS * x, 16), TOKENS)],
                    (chip_of(core, s), j),
                    xsem.at[XBASE[1] + x],
                    1,
                    2 * s + j,
                )
            to_device(
                gms.at[s], b.gm.at[x % 2], (chip_of(core, s), x // 2), xsem.at[XBASE[2] + x % 2], 2, s
            )

    def part_of(job, step, place, half=None):
        name, order, cols, axes = job
        fixed = {a: at[a] for a in order[step:]}
        fixed[order[step]] = place
        where = []
        for a in axes:
            if a in fixed:
                where.append(fixed[a])
            elif half is not None:
                where.append(pl.ds(half * (size[a] // 2), size[a] // 2))
                half = None
            else:
                where.append(slice(None))
        return getattr(b, WEIGHTS[name[0]]).at[tuple(where) + (slice(None), cols)]

    def gather_start(name, step):
        job = gathers[name]
        axis = job[1][step]
        n = size[axis]
        own = part_of(job, step, at[axis])
        free = [a for a in job[3] if a not in job[1][step:]]
        relay = n == 4 and step == len(job[1]) - 1 and size[free[0]] % 2 == 0
        state = types.SimpleNamespace(step=step, relay=relay)
        if relay:
            first = [part_of(job, step, at[axis], h) for h in range(2)]
            right, left = moved(axis, 1), moved(axis, n - 1)
            state.right, state.left = (
                remote(first[h], lambda h=h: part_of(job, step, at[axis], h), to) for h, to in ((0, right), (1, left))
            )
            state.every = [Group(lambda: part_of(job, step, pl.ds(0, 2)))]
            state.every[0].add(first[1], first[1], right)
            state.every[0].add(first[0], first[0], left)
        else:
            state.every = [Group(lambda: part_of(job, step, pl.ds(0, n - 1)))] if n > 1 else []
            for o in range(1, n):
                state.every[0].add(own, own, moved(axis, o))
        flying[name] = state

    def gather_pass(name):
        job, state = gathers[name], flying[name]
        if not state.relay:
            return
        axis = job[1][state.step]
        n = size[axis]
        for copy, back, onward, half in ((state.right, n - 1, 1, 0), (state.left, 1, n - 1, 1)):
            arrived([copy])
            piece = part_of(job, state.step, near[axis][back], half)
            state.every[0].add(piece, piece, moved(axis, onward))

    def gather_done(name):
        arrived(flying[name].every)

    gathers = {j[0]: j for j in gather_jobs()}
    flying = {}

    pk_local.wait()
    arrived([pk_swap])
    packed = jnp.concatenate([b.p1[c].astype(F32)[: sh.pc] for c in range(2)], 0).astype(BF16)
    b.p2y[y] = packed[:, :HALF]
    b.p2[x] = packed[:, HALF:]
    mine = b.p2y.at[y]
    ysteps, xsteps = [], [Group(lambda: b.p2.at[: TP - 1])]
    if ny > 1:
        ysteps.append(Group(lambda: b.p2y.at[: ny - 1]))
    for o in range(1, ny):
        ysteps[0].add(mine, mine, moved("y", o))
    mine = b.p2.at[x]
    for o in range(1, TP):
        xsteps[0].add(mine, mine, moved("x", o))
    ff_local.wait()
    arrived([ff_swap])
    two = [b.f1[c].astype(F32)[:wr] for c in range(2)]
    b.wf[x, z, y] = jnp.concatenate(two, 0).astype(BF16)
    feed_names, first_names = ("f1", "f2", "f0"), ("x0", "a0", "a1")
    for n in feed_names:
        gather_start(n, 0)
    send_rows()
    arrived(ysteps)
    b.wx[x, z] = dot(packy[...], b.p2y[...].reshape(ny * 2 * sh.pc, HALF)).astype(BF16)
    gather_start("x0", 0)
    arrived(xsteps)
    b.wa[z, y, :, HALF:] = dot(packsel[...], b.p2[...].reshape(TP * 2 * sh.pc, REST)).astype(BF16)
    for n in ("a0", "a1"):
        gather_start(n, 0)
    for n in feed_names:
        gather_done(n)
        gather_start(n, 1)
    for n in first_names:
        gather_done(n)
        gather_start(n, 1)
    for n in first_names:
        gather_pass(n)
    for n in feed_names:
        gather_done(n)
        gather_start(n, 2)

    for i in range(TP):
        from_device(b.x.at[pl.ds(pl.multiple_of(OWN * core + TOKENS * i, 16), TOKENS)], 0, i)
    half = b.x.at[pl.ds(pl.multiple_of(OWN * core, 16), TP * TOKENS)]
    x_swap = remote(half, half, sibling)
    for first in (256, OWN + 256):
        b.x[first : first + 16] = jnp.zeros((16, D), BF16)
    turn_local.wait()
    arrived([x_swap])

    @pl.loop(0, 2)
    def _(i):
        rows = pl.ds(pl.multiple_of(OWN * i, 16), OWN)
        b.xp[rows] = dot(b.x[rows], b.turn[...], NT).astype(BF16)

    for n in first_names:
        gather_done(n)
    wo_cols = slice(WO, WO + HALF)
    wo_local = local(b.wa.at[:, :, :, wo_cols], b.wo.at[core])
    wo_swap = remote(b.wa.at[:, :, :, wo_cols], b.wo.at[core], sibling)
    gather_pass("f1")
    send_upstream()

    def attention_weight():
        return b.wa[:, :, :, :WO].reshape(D, WO)

    small = b.wa[:, :, :, 4 * HALF :].reshape(D, SMALL)
    chosen = dot(smallsel[...], small, NT)
    b.par[...] = chosen[0:8]
    memory = chosen[16:48].astype(BF16)
    b.x[OWN + 256 : OWN + 272] = memory[16:]
    turned = dot(memory, b.turn[...], NT).astype(BF16)
    b.xp[OWN + 256 : OWN + 272] = turned[16:]

    @pl.when(seg == 0)
    def _():
        b.x[256:272] = memory[:16]
        b.xp[256:272] = turned[:16]

    gains = [b.par[i : i + 1] for i in range(2)]
    biases = [b.par[2 + i : 3 + i] for i in range(2)]

    hop_to = jnp.where(x == 0, 1, 2)
    hops = []
    for j in range(2):
        hops.append(
            pltpu.make_async_remote_copy(
                src_ref=b.hop,
                dst_ref=b.hopin,
                send_sem=xsem.at[XBASE[6] + j],
                recv_sem=xsem.at[XBASE[6] + 2],
                device_id=device(x_=hop_to, c_=j),
                device_id_type=MESH,
            )
        )

    own_rows = pl.ds(pl.multiple_of(OWN * core, 16), OWN)
    other_rows = pl.ds(pl.multiple_of(OWN * other, 16), OWN)

    out = dot(b.xp[...], b.wx[...].reshape(D, HALF)).astype(BF16)
    for i in range(3):
        b.qkv[i] = out[:, 128 * i : 128 * i + 128]
    out = dot(b.x[...], b.wa[:, :, :, HALF:WO].reshape(D, 2 * HALF)).astype(BF16)
    for i in range(3, 9):
        b.qkv[i] = out[:, 128 * (i - 3) : 128 * (i - 2)]

    def head_masks(hh):
        lane = lax.broadcasted_iota(jnp.int32, (ROWS, 128), 1)
        row = lax.broadcasted_iota(jnp.int32, (ROWS, 128), 0)
        inside = (lane // 64) == hh
        spare = lane == 64 * (1 - hh)
        memory = ((row >= 256) & (row < 272)) | (row >= OWN + 256)
        invalid = memory & (row % 8 >= 5)
        return inside, spare, invalid

    def forward_pair(p):
        qp, kp, vp = (b.qkv[3 * p + i] for i in range(3))
        vt = vp.T
        for hh in range(2):
            inside, spare, invalid = head_masks(hh)
            zero = jnp.zeros_like(kp)
            kmask = jnp.where(spare & invalid, jnp.full_like(kp, MASKED), zero)
            km = jnp.where(inside, kp, kmask)
            qm = jnp.where(inside, qp, jnp.where(spare, jnp.ones_like(qp), zero))
            scores = dot(km, qm, NT)
            peak = jnp.max(scores, 0, keepdims=True)
            raised = jnp.exp2((scores - peak) * EXP_SCALE)
            total = jnp.sum(raised, 0, keepdims=True)
            probs = (raised * (1.0 / total)).astype(BF16)
            b.pt[2 * p + hh] = probs
            b.ot[p, 64 * hh : 64 * hh + 64] = dot(vt[64 * hh : 64 * hh + 64], probs).astype(BF16)
        b.oc[:, pl.ds(pl.multiple_of(128 * p, 128), 128)] = b.ot[p].T

    @pl.loop(0, 3)
    def _(j):
        cols = pl.ds(pl.multiple_of(128 * j, 128), 128)
        block = dot(b.turn[...], b.wx[:, :, :, cols].reshape(D, 128), TN).astype(BF16)
        b.wa[:, :, :, cols] = block.reshape(nz, ny, br, 128)

    @pl.loop(0, 2)
    def _(i):
        @pl.when((i == 1) & (seg == 1))
        def _():
            hops[0].wait_recv()
            b.x[256:272] = b.hopin[...]
            rows = dot(b.hopin[...], attention_weight()).astype(BF16)
            for j in range(9):
                b.qkv[j, 256:272] = rows[:, 128 * j : 128 * j + 128]

        @pl.when(i == seg)
        def _():
            for p in range(3):
                forward_pair(p)

        @pl.when(i == 0)
        def _():
            for n in ("f2", "f0"):
                gather_pass(n)

    def head_rows(ref, c):
        if nz > 1:
            return ref.at[pl.ds(c * (nz // 2), nz // 2)]
        return ref.at[:, :, pl.ds(pl.multiple_of(c * HALF, 16), HALF)]

    def wo_rows(h, c):
        return head_rows(b.wo.at[h], c)[...].reshape(HALF, HALF)

    o_swap = remote(b.oc.at[other_rows], b.oin, sibling)
    wo_local.wait()
    arrived([wo_swap])
    halves = [dot(b.oc[own_rows], wo_rows(h, core)) for h in range(2)]
    arrived([o_swap])
    attended = jnp.concatenate([halves[h] + dot(b.oin[...], wo_rows(h, other)) for h in range(2)], 1)
    h1, n1, inv1 = norm_forward(b.x[own_rows].astype(F32) + attended, gains[0], biases[0])
    b.h1[...] = h1
    b.n1[...] = n1
    b.inv1[...] = inv1
    b.h1b[own_rows] = h1.astype(BF16)
    h_swap = remote(b.h1b.at[own_rows], b.h1b.at[own_rows], sibling)

    @pl.when(seg == 1)
    def _():
        b.xp[256:272] = dot(b.hopin[...], b.turn[...], NT).astype(BF16)

    for n in ("f1", "f2", "f0"):
        gather_done(n)

    def feed_weight(t, kind):
        cols = [256 * j + 128 * kind for j in range(3)]
        blocks = [b.wf[2 * t + i, :, :, :, c : c + 128].reshape(D, 128) for i in range(2) for c in cols]
        return jnp.concatenate(blocks, 1)

    def up_weight(t):
        return feed_weight(t, 0)

    def down_weight(t):
        return feed_weight(t, 1)

    def gelu_share(units):
        return 0.5 * (1.0 + lax.erf(units * INV_ROOT_TWO))

    early = pltpu.make_async_remote_copy(
        src_ref=b.es,
        dst_ref=b.er,
        send_sem=xsem.at[XBASE[6] + 3],
        recv_sem=xsem.at[XBASE[6] + 4],
        device_id=sibling,
        device_id_type=MESH,
    )
    row16 = lax.broadcasted_iota(jnp.int32, (16, D), 0)

    @pl.when(seg == 0)
    def _():
        arrived([h_swap])
        rows = b.h1b[OWN + 256 : OWN + 272]
        units = [dot(rows, up_weight(t)) for t in range(2)]
        part = sum(dot((units[t] * gelu_share(units[t])).astype(BF16), down_weight(t), NT) for t in range(2))

        @pl.when(core == 0)
        def _():
            b.es[...] = part
            early.start()

        @pl.when(core == 1)
        def _():
            early.wait_recv()
            whole = b.h1[256:272] + part + b.er[...]
            written = norm_forward(whole, gains[1], biases[1])[0]
            b.hop[...] = jnp.where(row16 % 8 < 5, written, 0.0).astype(BF16)
            hops[0].start()
            hops[1].start()

    def project_up(rows):
        for t in range(2):
            units = dot(b.h1b[rows], up_weight(t))
            b.ul[t, rows] = units
            b.gl[t, rows] = (units * gelu_share(units)).astype(BF16)

    @pl.loop(0, 2)
    def _(i):
        @pl.when((i == 1) & (seg == 1))
        def _():
            arrived([h_swap])

        project_up(pl.ds(pl.multiple_of(OWN * jnp.where(i == 0, core, other), 16), OWN))


    def partial_down(rows):
        return sum(dot(b.gl[t, rows], down_weight(t), NT) for t in range(2))

    b.fs[...] = partial_down(other_rows).astype(BF16)
    f_swap = remote(b.fs, b.fr, sibling)
    branch = partial_down(own_rows)
    arrived([f_swap])
    out, n2, inv2 = norm_forward(b.h1[...] + branch + b.fr[...].astype(F32), gains[1], biases[1])
    low = out.astype(BF16)
    b.yb[...] = low
    b.mo[...] = low[256:272].astype(F32).reshape(2, 8, D)
    for i in range(TP):
        to_device(
            b.yb.at[pl.ds(TOKENS * i, TOKENS)],
            hout.at[seg, pl.ds(pl.multiple_of(TOKENS * core, 16), TOKENS)],
            (i, chain),
            xsem.at[XBASE[3] + 2 * seg + core],
            3,
            i,
        )
    for i in range(2):
        to_device(b.mo.at[i], mout.at[seg], (2 * core + i, chain), xsem.at[XBASE[4] + seg], 4, i)

    for i in range(TP):
        from_device(b.gyt.at[pl.ds(TOKENS * i, TOKENS)], 1, i)
    for i in range(2):
        from_device(b.gm.at[i], 2, i)
    upstream = jnp.concatenate([b.gyt[...].astype(F32), b.gm[...].reshape(16, D)], 0)
    b.sg[...] = jnp.zeros((48, D), F32)
    b.sg[1:2] = column_sum(upstream * n2)
    b.sg[3:4] = column_sum(upstream)
    dz = norm_backward(upstream, n2, inv2, gains[1])
    b.dz[...] = dz
    b.dfb[own_rows] = dz.astype(BF16)
    df_swap = remote(b.dfb.at[own_rows], b.dfb.at[own_rows], sibling)

    def weight_grad(into, left, right, jobs_):
        @pl.loop(0, 2)
        def _(t):
            part = dot(left[...], right[t], TN).astype(BF16)
            for i in range(2):
                into[2 * t + i] = part[:, HALF * i : HALF * (i + 1)].reshape(nz, ny, br, HALF)

            for h in range(2):

                @pl.when(t == h)
                def _():
                    for n in jobs_:
                        if is_ring(n, 0) and scatters[n][1][0] != "x":
                            ring_send(n, h)
                        elif h == 1:
                            scatter_send(n, 0)

    scatters = {j[0]: j for j in scatter_jobs()}
    rs = {}

    def is_ring(name, step):
        _, order, cols, axes = scatters[name]
        return step == 0 and name in RINGS and size[order[0]] == 4

    def source_of(name, step):
        _, order, cols, axes = scatters[name]
        axis = order[step]
        left = [a for a in axes if a not in order[:step]]
        array = getattr(b, GRADS[name[0]]) if step == 0 else k[SUMMED, step - 1, name]
        tail = (slice(None), cols) if step == 0 else ()

        def part(place, half=None):
            where = []
            for a in left:
                if a == axis:
                    where.append(place)
                elif half is not None:
                    where.append(pl.ds(half * (size[a] // 2), size[a] // 2))
                    half = None
                else:
                    where.append(slice(None))
            return array.at[tuple(where) + tail]

        return part

    def ring_send(name, half):
        axis = scatters[name][1][0]
        n = size[axis]
        part = source_of(name, 0)
        landing, over = k[LANDED, 0, name], k[PASSED, 0, name]
        right, left, far = (near[axis][o] for o in (1, n - 1, 2))
        to = moved(axis, 1), moved(axis, n - 1)
        cut = size[[a for a in scatters[name][3] if a != axis][0]] // 2
        if name not in rs:
            rs[name] = ([None, None], Group(lambda: landing), cut, (right, left), to)
        rs[name][0][half] = remote(part(far, half), lambda: over.at[half], to[half])
        if half == 0:
            rs[name][1].add(part(left, 0), landing.at[1, :cut], to[1])
        else:
            rs[name][1].add(part(right, 1), landing.at[0, cut:], to[0])

    def scatter_send(name, step):
        axis = scatters[name][1][step]
        n = size[axis]
        part = source_of(name, step)
        landing = k[LANDED, step, name]
        if is_ring(name, step):
            ring_send(name, 0)
            ring_send(name, 1)
            return
        rs[name] = [Group(lambda: landing)] if n > 1 else []
        for o in range(1, n):
            rs[name][0].add(part(near[axis][o]), landing.at[o - 1], moved(axis, o))

    def scatter_pass(name):
        if not is_ring(name, 0):
            return
        passing, coming, half, places_, devices = rs[name]
        part = source_of(name, 0)
        landing, over, updated = k[LANDED, 0, name], k[PASSED, 0, name], k[UPDATED, 0, name]
        for i in range(2):
            arrived([passing[i]])
            updated[i] = (part(places_[i], i)[...].astype(F32) + over[i].astype(F32)).astype(BF16)
            where = landing.at[0, :half] if i == 0 else landing.at[1, half:]
            coming.add(updated.at[i], where, devices[i])

    def scatter_sum(name, step):
        _, order, cols, axes = scatters[name]
        axis = order[step]
        total = source_of(name, step)(at[axis])[...].astype(F32)
        ring = is_ring(name, step)
        arrived([rs[name][1]] if ring else rs[name])
        for o in range(2 if ring else size[axis] - 1):
            total = total + k[LANDED, step, name][o].astype(F32)
        if step < len(order) - 1:
            k[SUMMED, step, name][...] = total.astype(BF16)
        return total

    def scatter_on(names, step):
        for n in names:
            scatter_sum(n, step)
            scatter_send(n, step + 1)

    down_names, up_names = ("t0", "t1", "t2"), ("i0", "i1", "i2")
    arrived([df_swap])
    weight_grad(b.gt, b.dfb, b.gl, down_names)
    @pl.loop(0, 2)
    def _(i):
        rows = pl.ds(pl.multiple_of(OWN * i, 16), OWN)
        for t in range(2):
            units = b.ul[t, rows]
            slope = gelu_share(units) + units * jnp.exp(-0.5 * units * units) * INV_ROOT_TWOPI
            b.du[t, rows] = (dot(b.dfb[rows], down_weight(t)) * slope).astype(BF16)


    def partial_up(rows):
        return sum(dot(b.du[t, rows], up_weight(t), NT) for t in range(2))

    dh_swap = Group(lambda: b.dhr)

    @pl.loop(0, 2)
    def _(i):
        part = partial_up(pl.ds(pl.multiple_of(OWN * jnp.where(i == 0, other, core), 16), OWN))

        @pl.when(i == 0)
        def _():
            b.dhs[...] = part.astype(BF16)
            dh_swap.add(b.dhs, b.dhr, sibling)

        @pl.when(i == 1)
        def _():
            b.dz[...] = b.dz[...] + part

    arrived([dh_swap])
    into_first = b.dz[...] + b.dhr[...].astype(F32)
    b.sg[0:1] = column_sum(into_first * b.n1[...])
    b.sg[2:3] = column_sum(into_first)
    dr = norm_backward(into_first, b.n1[...], b.inv1[...], gains[0])
    b.dr[...] = dr
    b.dab[own_rows] = dr.astype(BF16)
    da_swap = remote(b.dab.at[own_rows], b.dab.at[own_rows], sibling)

    def grad_mixed(rows):
        parts = [dot(b.dab[rows, HALF * h : HALF * (h + 1)], wo_rows(h, core), NT) for h in range(2)]
        for p in range(3):
            b.doc[p, rows] = (parts[0] + parts[1])[:, 128 * p : 128 * p + 128].astype(BF16)

    weight_grad(b.gi, b.h1b, b.du, up_names)
    for n in down_names:
        scatter_pass(n)
    arrived([da_swap])
    grad_mixed(slice(None))

    mixed_t = b.ot[...].reshape(HALF, ROWS)

    def proj_grad(h):
        cols = pl.ds(pl.multiple_of(HALF * h, 128), HALF)
        return dot(mixed_t, b.dab[:, cols]).astype(BF16).reshape(b.gos.shape)

    def wo_part(c):
        return head_rows(b.ga.at[:, :, :, wo_cols], c)

    b.gos[...] = proj_grad(other)
    go_swap = remote(b.gos, wo_part(core), sibling)
    wo_part(core)[...] = proj_grad(core)

    def backward_pair(p):
        qp, kp, vp = (b.qkv[3 * p + i] for i in range(3))
        dop = b.doc[p]
        kt = kp.T
        dv = dk = 0.0
        dq = []
        for hh in range(2):
            inside, _, _ = head_masks(hh)
            zero = jnp.zeros_like(kp)
            grad_probs = dot(jnp.where(inside, vp, zero), dop, NT)
            low_probs = b.pt[2 * p + hh]
            probs = low_probs.astype(F32)
            row_term = jnp.sum(probs * grad_probs, 0, keepdims=True)
            ds = (probs * (grad_probs - row_term)).astype(BF16)
            dv = dv + dot(low_probs, jnp.where(inside, dop, zero))
            dk = dk + dot(ds, jnp.where(inside, qp, zero))
            dq.append(dot(kt[64 * hh : 64 * hh + 64], ds))
        b.dqkv[3 * p] = (jnp.concatenate(dq, 0) * 0.125).T.astype(BF16)
        b.dqkv[3 * p + 1] = (dk * 0.125).astype(BF16)
        b.dqkv[3 * p + 2] = dv.astype(BF16)

    def joined(rows, wanted):
        return jnp.concatenate([b.dqkv[i, rows] for i in wanted], 1)

    def attention_grad(p):
        grads = jnp.concatenate([b.dqkv[3 * p + i] for i in range(3)], 1)

        part = dot(b.both[jnp.minimum(p, 1)], grads, TN).astype(BF16)

        @pl.when(p == 0)
        def _():
            b.gx[...] = part.reshape(TP, nz, sh.xrows, HALF)

        @pl.when(p > 0)
        def _():
            cols = pl.ds(pl.multiple_of(HALF * p, 128), HALF)
            b.ga[:, :, :, cols] = part.reshape(nz, ny, br, HALF)

    @pl.loop(0, 3)
    def _(p):
        backward_pair(p)
        attention_grad(p)

        @pl.when(p == 0)
        def _():
            arrived([go_swap])
            scatter_send("aw", 0)
            scatter_send("x0", 0)
            for n in up_names:
                scatter_pass(n)

        @pl.when(p == 1)
        def _():
            scatter_send("a1", 0)
            scatter_on(down_names, 0)
            for n in ("aw", "x0"):
                scatter_pass(n)

        @pl.when(p == 2)
        def _():
            scatter_send("a2", 0)
            scatter_send("a3", 0)
            scatter_pass("a1")


    def partial_input(rows):
        return dot(joined(rows, range(9)), attention_weight(), NT)

    memory_rows = [pl.ds(pl.multiple_of(OWN * c + 256, 16), 16) for c in (other, core)]
    part = dot(jnp.concatenate([joined(rows, range(9)) for rows in memory_rows], 0), attention_weight(), NT)
    b.ms[...] = part[:16]
    memory_swap = remote(b.ms, b.mr, sibling)
    b.dxs[...] = partial_input(other_rows).astype(BF16)
    dx_swap = remote(b.dxs, b.dxr, sibling)
    arrived([memory_swap])
    memory_grad = part[16:] + b.dr[256:272] + b.mr[...]

    @pl.when((core == 0) & (seg == 0))
    def _():
        b.sg[16:32] = memory_grad

    @pl.when(core == 1)
    def _():
        b.sg[32:48] = memory_grad

    small_grads = dot(b.sg[...].astype(BF16), smallsel[...], TN).astype(BF16)
    b.ga[:, :, :, 4 * HALF :] = small_grads.reshape(nz, ny, br, SMALL)
    scatter_send("as", 0)
    dx = partial_input(own_rows) + b.dr[...]
    scatter_on(up_names, 0)
    arrived([dx_swap])
    dx = dx + b.dxr[...].astype(F32)
    b.dxb[...] = dx[:256].astype(BF16)
    for i in range(TP):
        to_device(
            b.dxb.at[pl.ds(TOKENS * i, TOKENS)],
            dxo.at[seg, pl.ds(pl.multiple_of(TOKENS * core, 16), TOKENS)],
            (i, chain),
            xsem.at[XBASE[5] + 2 * seg + core],
            5,
            i,
        )
    scatter_on(("aw", "x0", "a1"), 0)
    scatter_on(down_names, 1)
    scatter_on(("a2", "a3", "as"), 0)
    spread = dot(packy[...], scatter_sum("x0", 1).astype(BF16), TN).astype(BF16)
    b.e3y[...] = spread.reshape(ny, 2 * sh.pc, HALF)
    ysteps = [Group(lambda: b.r3y)] if ny > 1 else []
    for o in range(1, ny):
        ysteps[0].add(b.e3y.at[near["y"][o]], b.r3y.at[o - 1], moved("y", o))
    scatter_on(up_names, 1)
    for n in ("aw", "a1", "a2", "a3", "as"):
        cols = scatters[n][2]
        b.tot[:, cols.start - HALF : cols.stop - HALF] = scatter_sum(n, 1).astype(BF16)
    spread = dot(packsel[...], b.tot[...], TN).astype(BF16)
    b.e3[...] = spread.reshape(TP, 2 * sh.pc, REST)
    steps = [Group(lambda: b.r3)]
    for o in range(1, TP):
        steps[0].add(b.e3.at[near["x"][o]], b.r3.at[o - 1], moved("x", o))

    def last_rows(wanted, first_col):
        for j, n in enumerate(wanted):
            total = scatter_sum(n, 2)
            cols = slice(first_col + 128 * j, first_col + 128 * j + 128)
            b.sf[0, :, cols] = total[:wr]
            b.sf[1, :, cols] = total[wr:]

    last_rows(down_names, HALF)
    last_rows(up_names, 0)
    sf_local = local(b.sf.at[core], gfo.at[core])
    sf_swap = remote(b.sf.at[other], gfo.at[core], sibling)

    arrived(steps)
    total = b.e3[x].astype(F32)
    for o in range(1, TP):
        total = total + b.r3[o - 1].astype(F32)
    b.s4[:, :, HALF:] = total.reshape(2, sh.pc, REST)
    arrived(ysteps)
    total = b.e3y[y].astype(F32)
    for o in range(1, ny):
        total = total + b.r3y[o - 1].astype(F32)
    b.s4[:, :, :HALF] = total.reshape(2, sh.pc, HALF)
    s4_local = local(b.s4.at[core], gao.at[core])
    s4_swap = remote(b.s4.at[other], gao.at[core], sibling)

    for kind, out_ref in ((3, hout), (5, dxo)):
        for s in range(2):
            for j in range(2):
                from_device(out_ref.at[s, pl.ds(TOKENS * j, TOKENS)], kind, 2 * s + j)
    for s in range(2):
        from_device(mout.at[s], 4, s)
    sf_local.wait()
    s4_local.wait()
    arrived([sf_swap, s4_swap])

    for group in sent[-SENDS:]:
        group.wait_send()
    for same, copy in conditional:

        @pl.when(jnp.logical_not(same))
        def _():
            copy.wait_send()

    @pl.when((seg == 0) & (core == 1))
    def _():
        hops[0].wait_send()
        hops[1].wait_send()

    @pl.when((seg == 0) & (core == 0))
    def _():
        early.wait_send()


def layer(sh, arrays):
    constants = [jnp.asarray(a, BF16) for a in selections(sh)]
    tables = scratch_of(sh)
    names = [list(table) for table in tables]
    anywhere = pl.BlockSpec(memory_space=pl.ANY)
    outs = [
        jax.ShapeDtypeStruct((2, 128, D), BF16),
        jax.ShapeDtypeStruct((2, 8, D), F32),
        jax.ShapeDtypeStruct((2, 128, D), BF16),
        jax.ShapeDtypeStruct((2, sh.pc, ACOLS), F32),
        jax.ShapeDtypeStruct((2, sh.wrows, D), F32),
    ]
    return pl.pallas_call(
        functools.partial(kernel, sh, names),
        name="layer",
        out_shape=outs,
        in_specs=[anywhere] * 15,
        out_specs=[anywhere] * len(outs),
        scratch_shapes=[pltpu.VMEM(*one) for table in tables for one in table.values()]
        + [
            pltpu.SemaphoreType.DMA((SENDS,)),
            pltpu.SemaphoreType.DMA((96,)),
            pltpu.SemaphoreType.DMA((45,)),
            pltpu.SemaphoreType.DMA((20,)),
        ],
        compiler_params=pltpu.CompilerParams(
            collective_id=0, has_side_effects=True, vmem_limit_bytes=64 * 2**20 - 2**17
        ),
    )(*arrays, *constants)


def unpack_kernel(sh, *refs):
    arrays, results, held, outs, sems = refs[:5], refs[5:15], refs[15:20], refs[20:30], refs[30]
    loads = [pltpu.make_async_copy(arrays[i], held[i], sems.at[i]) for i in range(5)]
    stores = [pltpu.make_async_copy(outs[i], results[i], sems.at[5 + i]) for i in range(10)]
    for copy in loads:
        copy.start()
    hout, mout, dxo, gao, gfo = held
    hidden, memory, grad_in, gq, gp, gains, biases, tokens, gi, gt = outs
    ar = sh.arows
    loads[0].wait()
    hidden[...] = hout[...]
    stores[0].start()
    loads[2].wait()
    grad_in[...] = dxo[...].astype(F32)
    stores[2].start()
    loads[1].wait()
    for i in range(2):
        memory[:, i] = mout[i, :5].astype(BF16)
    stores[1].start()
    loads[3].wait()
    for h in range(2):
        for p in range(3):
            for i in range(3):
                to = D * i + HALF * h + 128 * p
                first = HALF * p + 128 * i
                gq[:, to : to + 128] = gao[h, :ar, first : first + 128]
        gp[:, HALF * h : HALF * (h + 1)] = gao[h, :ar, WO : WO + HALF]
    small = gao[0, :, 4 * HALF :] + gao[1, :, 4 * HALF :]
    turned = small.T[:, :ar]
    gains[...] = turned[0:2]
    biases[...] = turned[2:4]
    for kind in range(2):
        tokens[:, kind] = small[:ar, 4 + MEM * kind : 4 + MEM * (kind + 1)]
    for i in range(3, 8):
        stores[i].start()
    loads[4].wait()
    for h in range(2):
        gi[:, HALF * h : HALF * (h + 1)] = gfo[h, :, :HALF]
        gt[:, HALF * h : HALF * (h + 1)] = gfo[h, :, HALF:]
    for i in range(8, 10):
        stores[i].start()
    for copy in stores:
        copy.wait()


def unpack(sh, *arrays):
    ar, wr = sh.arows, sh.wrows
    shapes = [
        ((2, 128, D), BF16),
        ((5, 2, D), BF16),
        ((2, 128, D), F32),
        ((ar, 3 * D), F32),
        ((ar, D), F32),
        ((2, ar), F32),
        ((2, ar), F32),
        ((ar, 2, MEM), F32),
        ((wr, D), F32),
        ((wr, D), F32),
    ]
    anywhere = pl.BlockSpec(memory_space=pl.ANY)
    return pl.pallas_call(
        functools.partial(unpack_kernel, sh),
        name="unpack",
        out_shape=[jax.ShapeDtypeStruct(*one) for one in shapes],
        in_specs=[anywhere] * 5,
        out_specs=[anywhere] * len(shapes),
        scratch_shapes=[pltpu.VMEM(a.shape, a.dtype) for a in arrays]
        + [pltpu.VMEM(*one) for one in shapes]
        + [pltpu.SemaphoreType.DMA((15,))],
        compiler_params=pltpu.CompilerParams(vmem_limit_bytes=64 * 2**20 - 2**17),
    )(*arrays)


def body(
    sh,
    hidden_in,
    reset,
    w_qkv,
    w_attn_out,
    norm_gains,
    norm_biases,
    memory_tokens,
    w_in,
    w_out,
    grad_hidden,
    grad_memory,
):
    arrays = (
        hidden_in,
        grad_hidden,
        grad_memory.transpose(1, 0, 2),
        w_qkv,
        w_attn_out,
        norm_gains,
        norm_biases,
        memory_tokens.transpose(2, 0, 1),
        w_in,
        w_out.T,
    )
    hidden, memory, *middle, tokens, gi, gt = unpack(sh, *layer(sh, arrays))
    return hidden, memory.transpose(1, 0, 2), *middle, tokens.transpose(1, 2, 0), gi, gt.T


def solution(mesh):
    sh = Shape(mesh.shape["dp"])
    return jax.shard_map(
        functools.partial(body, sh),
        mesh=mesh,
        in_specs=(
            P("dp", "tp", None),
            P("dp"),
            P(("dp", "tp"), None),
            P(("dp", "tp"), None),
            P(None, ("dp", "tp")),
            P(None, ("dp", "tp")),
            P(None, None, ("dp", "tp")),
            P("dp", "tp"),
            P("tp", "dp"),
            P("dp", "tp", None),
            P("dp", "tp", None),
        ),
        out_specs=(
            P("dp", "tp", None),
            P("dp", "tp", None),
            P("dp", "tp", None),
            P(("dp", "tp"), None),
            P(("dp", "tp"), None),
            P(None, ("dp", "tp")),
            P(None, ("dp", "tp")),
            P(None, None, ("dp", "tp")),
            P("dp", "tp"),
            P("tp", "dp"),
        ),
        check_vma=False,
    )
```

```python
import functools
import types

import jax
import jax.numpy as jnp
import numpy as np
from jax import lax
from jax.experimental import pallas as pl
from jax.experimental.pallas import tpu as pltpu
from jax.sharding import PartitionSpec as P

D = 768
HALF = 384
MEM = 10
TOKENS = 64
OWN = 272
ROWS = 2 * OWN
TP = 4
SMALL = 128
ACOLS = 4 * HALF + SMALL
REST = ACOLS - HALF
CUT = HALF + 640
WO = 3 * HALF
EPSILON = 1e-05
INV_ROOT_TWO = 0.7071067811865476
INV_ROOT_TWOPI = 0.3989422804014327
EXP_SCALE = 0.125 * 1.4426950408889634
MASKED = -1e30
F32 = jnp.float32
BF16 = jnp.bfloat16
MESH = pl.DeviceIdType.MESH
NN = (((1,), (0,)), ((), ()))
NT = (((1,), (1,)), ((), ()))
TN = (((0,), (0,)), ((), ()))


def dot(a, b, dims=NN):
    return lax.dot_general(a, b, dims, preferred_element_type=F32)


def up16(n):
    return -(-n // 16) * 16


class Shape:
    def __init__(self, dp):
        self.dp = dp
        planes = dp // 2
        self.ny = int(round(planes**0.5))
        self.nz = planes // self.ny
        self.wrows = D // dp
        self.arows = D // (dp * TP)
        self.brows = 2 * self.wrows
        self.pr = up16(self.arows)
        self.xrows = 2 * self.arows * self.ny
        self.pc = -(-self.arows // 8) * 8
        self.fr = up16(self.wrows)


def selections(sh):
    pack = np.zeros((sh.brows, TP * 2 * sh.pc), np.float32)
    for c in range(2):
        for x in range(TP):
            for i in range(sh.arows):
                pack[c * sh.wrows + x * sh.arows + i, (x * 2 + c) * sh.pc + i] = 1
    packy = np.zeros((sh.xrows, sh.ny * 2 * sh.pc), np.float32)
    turn = np.zeros((D, D), np.float32)
    ar = sh.arows
    for c in range(2):
        for y in range(sh.ny):
            for i in range(ar):
                row = (y * 2 + c) * ar + i
                packy[row, (y * 2 + c) * sh.pc + i] = 1
                for x in range(TP):
                    for z in range(sh.nz):
                        place = (z * sh.ny + y) * sh.brows + (c * TP + x) * ar + i
                        turn[(x * sh.nz + z) * sh.xrows + row, place] = 1
    small = np.zeros((48, SMALL), np.float32)
    for i in range(4):
        small[i, i] = 1
    for kind in range(2):
        for i in range(MEM):
            small[16 + 16 * kind + (i // 5) * 8 + i % 5, 4 + MEM * kind + i] = 1
    places = np.zeros((4, MEM, SMALL), np.float32)
    for kind, (rows, first) in enumerate(((2, 0), (2, 2), (MEM, 4), (MEM, 4 + MEM))):
        for i in range(rows):
            places[kind, i, first + i] = 1
    return pack, small, places, packy, turn


def norm_forward(inputs, gain, offset):
    centred = inputs - jnp.mean(inputs, -1, keepdims=True)
    spread = jnp.mean(centred * centred, -1, keepdims=True)
    inverse = lax.rsqrt(spread + EPSILON)
    normed = centred * inverse
    return normed * gain + offset, normed, inverse


def norm_backward(upstream, normed, inverse, gain):
    scaled = upstream * gain
    first_mean = jnp.mean(scaled, -1, keepdims=True)
    second_mean = jnp.mean(scaled * normed, -1, keepdims=True)
    return inverse * (scaled - first_mean - normed * second_mean)


def column_sum(a):
    return jnp.sum(a, 0, keepdims=True)


XBASE = (0, 4, 8, 10, 14, 16, 20)
SENDS = 40
STAGED, LANDED, SUMMED, PASSED, UPDATED = range(5)


def scratch_of(sh):
    nz, ny, br = sh.nz, sh.ny, sh.brows
    ar, wr = sh.arows, sh.wrows
    operands = [
        (5, 2, D),
        (ar, 3 * D),
        (ar, D),
        (2, ar),
        (2, ar),
        (ar, 2, MEM),
        (wr, D),
        (wr, D),
        (br, TP * 2 * sh.pc),
        (48, SMALL),
        (4, MEM, SMALL),
        (sh.xrows, ny * 2 * sh.pc),
    ]
    jobs = {(STAGED, i, 0): (dims, BF16) for i, dims in enumerate(operands)}
    s = dict(
        pk=((2, sh.pr, ACOLS), BF16),
        ff=((2, sh.fr, D), BF16),
        gms=((2, 8, D), F32),
        p1=((2, sh.pr, ACOLS), BF16),
        p2=((TP, 2 * sh.pc, REST), BF16),
        p2y=((ny, 2 * sh.pc, HALF), BF16),
        turn=((D, D), BF16),
        wx=((TP, nz, sh.xrows, HALF), BF16),
        gx=((TP, nz, sh.xrows, HALF), BF16),
        f1=((2, sh.fr, D), BF16),
        wa=((nz, ny, br, ACOLS), BF16),
        wf=((TP, nz, ny, br, D), BF16),
        wo=((2, nz, ny, br, HALF), BF16),
        par=((8, D), F32),
        both=((2, ROWS, D), BF16),
        gyt=((TP * TOKENS, D), BF16),
        gm=((2, 8, D), F32),
        qkv=((9, ROWS, 128), BF16),
        pt=((6, ROWS, ROWS), BF16),
        ot=((3, 128, ROWS), BF16),
        oc=((ROWS, HALF), BF16),
        oin=((OWN, HALF), BF16),
        h1=((OWN, D), F32),
        n1=((OWN, D), F32),
        inv1=((OWN, 1), F32),
        h1b=((ROWS, D), BF16),
        gl=((2, ROWS, D), BF16),
        ul=((2, ROWS, D), F32),
        fs=((OWN, D), BF16),
        fr=((OWN, D), BF16),
        n2=((OWN, D), F32),
        yb=((OWN, D), BF16),
        mo=((2, 8, D), F32),
        hop=((16, D), BF16),
        hopin=((16, D), BF16),
        es=((16, D), F32),
        er=((16, D), F32),
        dz=((OWN, D), F32),
        dfb=((ROWS, D), BF16),
        du=((2, ROWS, D), BF16),
        dhs=((OWN, D), BF16),
        dhr=((OWN, D), BF16),
        dr=((OWN, D), F32),
        dab=((ROWS, D), BF16),
        doc=((3, ROWS, 128), BF16),
        dqkv=((9, ROWS, 128), BF16),
        ga=((nz, ny, br, ACOLS), BF16),
        gi=((TP, nz, ny, br, HALF), BF16),
        gt=((TP, nz, ny, br, HALF), BF16),
        dxs=((OWN, D), BF16),
        dxr=((OWN, D), BF16),
        dxb=((TP * TOKENS, D), BF16),
        sg=((48, D), F32),
        ms=((16, D), F32),
        mr=((16, D), F32),
        tot=((br, REST), BF16),
        e3=((TP, 2 * sh.pc, REST), BF16),
        r3=((TP - 1, 2 * sh.pc, REST), BF16),
        e3y=((ny, 2 * sh.pc, HALF), BF16),
        r3y=((max(1, ny - 1), 2 * sh.pc, HALF), BF16),
        s4=((2, sh.pc, ACOLS), F32),
        sf=((2, sh.wrows, D), F32),
    )
    s.update(gos=((nz // 2, ny, br, HALF) if nz > 1 else (1, 1, HALF, HALF), BF16))
    sizes = {"x": TP, "z": nz, "y": ny}
    for name, order, cols, axes in scatter_jobs():
        left = [a for a in axes]
        block = (sh.xrows if name[0] == "x" else br, cols.stop - cols.start)
        for step, axis in enumerate(order):
            left = [a for a in left if a != axis]
            dims = tuple(sizes[a] for a in left)
            ring = step == 0 and name in RINGS and sizes[axis] == 4
            jobs[LANDED, step, name] = ((2 if ring else max(1, sizes[axis] - 1),) + dims + block, BF16)
            if step < len(order) - 1:
                jobs[SUMMED, step, name] = (dims + block, BF16)
            if ring:
                jobs[PASSED, 0, name] = ((2, dims[0] // 2) + dims[1:] + block, BF16)
                jobs[UPDATED, 0, name] = jobs[PASSED, 0, name]
    return s, jobs


def scatter_jobs():
    orders = [("z", "y", "x"), ("x", "z", "y"), ("y", "x", "z")]
    jobs = []
    for kind in ("t", "i"):
        for j in range(3):
            jobs.append((f"{kind}{j}", orders[j], slice(128 * j, 128 * j + 128), ("x", "z", "y")))
    zy, yz = ("z", "y"), ("y", "z")
    jobs.append(("aw", yz, slice(WO, WO + HALF), zy))
    jobs.append(("x0", ("x", "z"), slice(0, HALF), ("x", "z")))
    jobs.append(("a1", zy, slice(HALF, 2 * HALF), zy))
    jobs.append(("a2", yz, slice(2 * HALF, 2 * HALF + 256), zy))
    jobs.append(("a3", zy, slice(2 * HALF + 256, 3 * HALF), zy))
    jobs.append(("as", yz, slice(4 * HALF, ACOLS), zy))
    return jobs


def gather_jobs():
    orders = [("x", "y", "z"), ("y", "z", "x"), ("z", "x", "y")]
    jobs = [(f"f{j}", orders[j], slice(256 * j, 256 * j + 256), ("x", "z", "y")) for j in range(3)]
    jobs.append(("x0", ("z", "x"), slice(0, HALF), ("x", "z")))
    jobs.append(("a0", ("y", "z"), slice(HALF, CUT), ("z", "y")))
    jobs.append(("a1", ("z", "y"), slice(CUT, ACOLS), ("z", "y")))
    return jobs


RINGS = ("t0", "t1", "t2", "i0", "i1", "i2", "aw", "x0", "a1")
WEIGHTS = {"f": "wf", "a": "wa", "x": "wx"}
GRADS = {"t": "gt", "i": "gi", "a": "ga", "x": "gx"}


def kernel(sh, names, *refs):
    xin, gin = refs[:2]
    hout, mout, dxo, gao, gfo = refs[15:20]
    ssem, rsem, xsem, lsem = refs[-4:]
    count = len(names[0])
    b = types.SimpleNamespace(**dict(zip(names[0], refs[20 : 20 + count])))
    b.xp, b.x = b.both.at[0], b.both.at[1]
    k = dict(zip(names[1], refs[20 + count : -4]))
    staged = [k[STAGED, i, 0] for i in range(12)]
    gmem, wq, wp, gain_in, bias_in, token_in, up_in, down_in = staged[:8]
    packsel, smallsel, places, packy = staged[8:]
    turn = refs[14]
    nz, ny, br, wr, ar = sh.nz, sh.ny, sh.brows, sh.wrows, sh.arows
    pk, ff, gms = b.pk, b.ff, b.gms

    dp = lax.axis_index("dp")
    x = lax.axis_index("tp")
    core = dp % 2
    y = (dp // 2) % ny
    z = dp // (2 * ny)
    other = 1 - core
    chain = x // 2
    seg = jnp.where((x == 1) | (x == 2), 1, 0)
    at = {"x": x, "y": y, "z": z}
    size = {"x": TP, "y": ny, "z": nz}

    def device(x_=x, y_=y, z_=z, c_=core):
        return ((z_ * ny + y_) * 2 + c_, x_)

    near = {a: [(at[a] + o) % size[a] for o in range(size[a])] for a in at}

    def moved_to(axis, offset, core_=core):
        there = dict(at)
        there[axis] = near[axis][offset]
        return device(there["x"], there["y"], there["z"], core_)

    neighbours = {a: [moved_to(a, o) for o in range(size[a])] for a in at}

    def moved(axis, offset):
        return neighbours[axis][offset]

    sibling = device(c_=other)
    sent = []

    class Group:
        def __init__(self, like):
            if len(sent) >= SENDS:
                sent[-SENDS].wait_send()
            self.like = like
            self.number = len(sent)
            sent.append(self)

        def add(self, src, dst, to):
            pltpu.make_async_remote_copy(
                src_ref=src,
                dst_ref=dst,
                send_sem=ssem.at[self.number % SENDS],
                recv_sem=rsem.at[self.number],
                device_id=to,
                device_id_type=MESH,
            ).start()

        def wait_send(self):
            like = self.like()
            pltpu.make_async_copy(like, like, ssem.at[self.number % SENDS]).wait()

        def wait_recv(self):
            like = self.like()
            pltpu.make_async_copy(like, like, rsem.at[self.number]).wait()

    def remote(src, dst, to):
        where = dst if callable(dst) else lambda: dst
        group = Group(where)
        group.add(src, where(), to)
        return group

    def arrived(groups):
        for group in groups:
            group.wait_recv()

    locals_ = [0]

    def local(src, dst):
        copy = pltpu.make_async_copy(src, dst, lsem.at[locals_[0]])
        locals_[0] += 1
        copy.start()
        return copy

    staging = [local(refs[2 + i], staged[i]) for i in range(12)]
    turn_local = local(turn, b.turn)

    barrier = pltpu.get_barrier_semaphore()
    peers = [sibling]
    for o in range(1, TP):
        peers += [moved("x", o), moved_to("x", o, other)]
    for axis in ("y", "z"):
        for o in range(1, size[axis]):
            peers.append(moved(axis, o))
    for peer in peers:
        pl.semaphore_signal(barrier, inc=1, device_id=peer, device_id_type=MESH)

    pk[...] = jnp.zeros(pk.shape, BF16)
    ff[...] = jnp.zeros(ff.shape, BF16)
    gms[...] = jnp.zeros(gms.shape, F32)
    for copy in staging:
        copy.wait()
    small = dot(gain_in[...], places[0, :2], TN) + dot(bias_in[...], places[1, :2], TN)
    small = small + dot(token_in[:, 0], places[2]) + dot(token_in[:, 1], places[3])
    small = small.astype(BF16)
    for h in range(2):
        for p in range(3):
            for i in range(3):
                first = D * i + HALF * h + 128 * p
                pk[h, :ar, HALF * p + 128 * i : HALF * p + 128 * (i + 1)] = wq[:, first : first + 128]
        pk[h, :ar, WO : WO + HALF] = wp[:, HALF * h : HALF * (h + 1)]
        pk[h, :ar, 4 * HALF :] = small
        for j in range(3):
            cols = slice(HALF * h + 128 * j, HALF * h + 128 * (j + 1))
            ff[h, :wr, 256 * j : 256 * j + 128] = up_in[:, cols]
            ff[h, :wr, 256 * j + 128 : 256 * j + 256] = down_in[:, cols]
        gms[h, 0:5] = gmem[:, h].astype(F32)
    pl.semaphore_wait(barrier, len(peers))

    pk_local = local(pk.at[core], b.p1.at[core])
    ff_local = local(ff.at[core], b.f1.at[core])
    pk_swap = remote(pk.at[other], b.p1.at[core], sibling)
    ff_swap = remote(ff.at[other], b.f1.at[core], sibling)

    conditional = []

    def to_device(src, dst, place, here, kind, send_slot):
        copy = pltpu.make_async_remote_copy(
            src_ref=src,
            dst_ref=dst,
            send_sem=xsem.at[25 + XBASE[kind] + send_slot],
            recv_sem=here,
            device_id=device(x_=place[0], c_=place[1]),
            device_id_type=MESH,
        )
        same = (place[0] == x) & (place[1] == core)

        @pl.when(same)
        def _():
            pltpu.make_async_copy(src, dst, here).start()

        @pl.when(jnp.logical_not(same))
        def _():
            copy.start()

        conditional.append((same, copy))

    def from_device(dst, kind, slot):
        pltpu.make_async_copy(dst, dst, xsem.at[XBASE[kind] + slot]).wait()

    def chip_of(k, s):
        return s + k * (3 - 2 * s)

    def send_rows():
        for s in range(2):
            for j in range(2):
                to_device(
                    xin.at[s, pl.ds(TOKENS * j, TOKENS)],
                    b.x.at[pl.ds(pl.multiple_of(OWN * j + TOKENS * x, 16), TOKENS)],
                    (chip_of(core, s), j),
                    xsem.at[XBASE[0] + x],
                    0,
                    2 * s + j,
                )

    def send_upstream():
        for s in range(2):
            for j in range(2):
                to_device(
                    gin.at[s, pl.ds(TOKENS * j, TOKENS)],
                    b.gyt.at[pl.ds(pl.multiple_of(TOKENS * x, 16), TOKENS)],
                    (chip_of(core, s), j),
                    xsem.at[XBASE[1] + x],
                    1,
                    2 * s + j,
                )
            to_device(
                gms.at[s], b.gm.at[x % 2], (chip_of(core, s), x // 2), xsem.at[XBASE[2] + x % 2], 2, s
            )

    def part_of(job, step, place, half=None):
        name, order, cols, axes = job
        fixed = {a: at[a] for a in order[step:]}
        fixed[order[step]] = place
        where = []
        for a in axes:
            if a in fixed:
                where.append(fixed[a])
            elif half is not None:
                where.append(pl.ds(half * (size[a] // 2), size[a] // 2))
                half = None
            else:
                where.append(slice(None))
        return getattr(b, WEIGHTS[name[0]]).at[tuple(where) + (slice(None), cols)]

    def gather_start(name, step):
        job = gathers[name]
        axis = job[1][step]
        n = size[axis]
        own = part_of(job, step, at[axis])
        free = [a for a in job[3] if a not in job[1][step:]]
        relay = n == 4 and step == len(job[1]) - 1 and size[free[0]] % 2 == 0
        state = types.SimpleNamespace(step=step, relay=relay)
        if relay:
            first = [part_of(job, step, at[axis], h) for h in range(2)]
            right, left = moved(axis, 1), moved(axis, n - 1)
            state.right, state.left = (
                remote(first[h], lambda h=h: part_of(job, step, at[axis], h), to) for h, to in ((0, right), (1, left))
            )
            state.every = [Group(lambda: part_of(job, step, pl.ds(0, 2)))]
            state.every[0].add(first[1], first[1], right)
            state.every[0].add(first[0], first[0], left)
        else:
            state.every = [Group(lambda: part_of(job, step, pl.ds(0, n - 1)))] if n > 1 else []
            for o in range(1, n):
                state.every[0].add(own, own, moved(axis, o))
        flying[name] = state

    def gather_pass(name):
        job, state = gathers[name], flying[name]
        if not state.relay:
            return
        axis = job[1][state.step]
        n = size[axis]
        for copy, back, onward, half in ((state.right, n - 1, 1, 0), (state.left, 1, n - 1, 1)):
            arrived([copy])
            piece = part_of(job, state.step, near[axis][back], half)
            state.every[0].add(piece, piece, moved(axis, onward))

    def gather_done(name):
        arrived(flying[name].every)

    gathers = {j[0]: j for j in gather_jobs()}
    flying = {}

    pk_local.wait()
    arrived([pk_swap])
    packed = jnp.concatenate([b.p1[c].astype(F32)[: sh.pc] for c in range(2)], 0).astype(BF16)
    b.p2y[y] = packed[:, :HALF]
    b.p2[x] = packed[:, HALF:]
    mine = b.p2y.at[y]
    ysteps, xsteps = [], [Group(lambda: b.p2.at[: TP - 1])]
    if ny > 1:
        ysteps.append(Group(lambda: b.p2y.at[: ny - 1]))
    for o in range(1, ny):
        ysteps[0].add(mine, mine, moved("y", o))
    mine = b.p2.at[x]
    for o in range(1, TP):
        xsteps[0].add(mine, mine, moved("x", o))
    ff_local.wait()
    arrived([ff_swap])
    two = [b.f1[c].astype(F32)[:wr] for c in range(2)]
    b.wf[x, z, y] = jnp.concatenate(two, 0).astype(BF16)
    feed_names, first_names = ("f1", "f2", "f0"), ("x0", "a0", "a1")
    for n in feed_names:
        gather_start(n, 0)
    send_rows()
    arrived(ysteps)
    b.wx[x, z] = dot(packy[...], b.p2y[...].reshape(ny * 2 * sh.pc, HALF)).astype(BF16)
    gather_start("x0", 0)
    arrived(xsteps)
    b.wa[z, y, :, HALF:] = dot(packsel[...], b.p2[...].reshape(TP * 2 * sh.pc, REST)).astype(BF16)
    for n in ("a0", "a1"):
        gather_start(n, 0)
    for n in feed_names:
        gather_done(n)
        gather_start(n, 1)
    for n in first_names:
        gather_done(n)
        gather_start(n, 1)
    for n in first_names:
        gather_pass(n)
    for n in feed_names:
        gather_done(n)
        gather_start(n, 2)

    for i in range(TP):
        from_device(b.x.at[pl.ds(pl.multiple_of(OWN * core + TOKENS * i, 16), TOKENS)], 0, i)
    half = b.x.at[pl.ds(pl.multiple_of(OWN * core, 16), TP * TOKENS)]
    x_swap = remote(half, half, sibling)
    for first in (256, OWN + 256):
        b.x[first : first + 16] = jnp.zeros((16, D), BF16)
    turn_local.wait()
    arrived([x_swap])

    @pl.loop(0, 2)
    def _(i):
        rows = pl.ds(pl.multiple_of(OWN * i, 16), OWN)
        b.xp[rows] = dot(b.x[rows], b.turn[...], NT).astype(BF16)

    for n in first_names:
        gather_done(n)
    wo_cols = slice(WO, WO + HALF)
    wo_local = local(b.wa.at[:, :, :, wo_cols], b.wo.at[core])
    wo_swap = remote(b.wa.at[:, :, :, wo_cols], b.wo.at[core], sibling)
    gather_pass("f1")
    send_upstream()

    def attention_weight():
        return b.wa[:, :, :, :WO].reshape(D, WO)

    small = b.wa[:, :, :, 4 * HALF :].reshape(D, SMALL)
    chosen = dot(smallsel[...], small, NT)
    b.par[...] = chosen[0:8]
    memory = chosen[16:48].astype(BF16)
    b.x[OWN + 256 : OWN + 272] = memory[16:]
    turned = dot(memory, b.turn[...], NT).astype(BF16)
    b.xp[OWN + 256 : OWN + 272] = turned[16:]

    @pl.when(seg == 0)
    def _():
        b.x[256:272] = memory[:16]
        b.xp[256:272] = turned[:16]

    gains = [b.par[i : i + 1] for i in range(2)]
    biases = [b.par[2 + i : 3 + i] for i in range(2)]

    hop_to = jnp.where(x == 0, 1, 2)
    hops = []
    for j in range(2):
        hops.append(
            pltpu.make_async_remote_copy(
                src_ref=b.hop,
                dst_ref=b.hopin,
                send_sem=xsem.at[XBASE[6] + j],
                recv_sem=xsem.at[XBASE[6] + 2],
                device_id=device(x_=hop_to, c_=j),
                device_id_type=MESH,
            )
        )

    own_rows = pl.ds(pl.multiple_of(OWN * core, 16), OWN)
    other_rows = pl.ds(pl.multiple_of(OWN * other, 16), OWN)

    out = dot(b.xp[...], b.wx[...].reshape(D, HALF)).astype(BF16)
    for i in range(3):
        b.qkv[i] = out[:, 128 * i : 128 * i + 128]
    out = dot(b.x[...], b.wa[:, :, :, HALF:WO].reshape(D, 2 * HALF)).astype(BF16)
    for i in range(3, 9):
        b.qkv[i] = out[:, 128 * (i - 3) : 128 * (i - 2)]

    def head_masks(hh):
        lane = lax.broadcasted_iota(jnp.int32, (ROWS, 128), 1)
        row = lax.broadcasted_iota(jnp.int32, (ROWS, 128), 0)
        inside = (lane // 64) == hh
        spare = lane == 64 * (1 - hh)
        memory = ((row >= 256) & (row < 272)) | (row >= OWN + 256)
        invalid = memory & (row % 8 >= 5)
        return inside, spare, invalid

    def forward_pair(p):
        qp, kp, vp = (b.qkv[3 * p + i] for i in range(3))
        vt = vp.T
        for hh in range(2):
            inside, spare, invalid = head_masks(hh)
            zero = jnp.zeros_like(kp)
            kmask = jnp.where(spare & invalid, jnp.full_like(kp, MASKED), zero)
            km = jnp.where(inside, kp, kmask)
            qm = jnp.where(inside, qp, jnp.where(spare, jnp.ones_like(qp), zero))
            scores = dot(km, qm, NT)
            peak = jnp.max(scores, 0, keepdims=True)
            raised = jnp.exp2((scores - peak) * EXP_SCALE)
            total = jnp.sum(raised, 0, keepdims=True)
            probs = (raised * (1.0 / total)).astype(BF16)
            b.pt[2 * p + hh] = probs
            b.ot[p, 64 * hh : 64 * hh + 64] = dot(vt[64 * hh : 64 * hh + 64], probs).astype(BF16)
        b.oc[:, pl.ds(pl.multiple_of(128 * p, 128), 128)] = b.ot[p].T

    @pl.loop(0, 3)
    def _(j):
        cols = pl.ds(pl.multiple_of(128 * j, 128), 128)
        block = dot(b.turn[...], b.wx[:, :, :, cols].reshape(D, 128), TN).astype(BF16)
        b.wa[:, :, :, cols] = block.reshape(nz, ny, br, 128)

    @pl.loop(0, 2)
    def _(i):
        @pl.when((i == 1) & (seg == 1))
        def _():
            hops[0].wait_recv()
            b.x[256:272] = b.hopin[...]
            rows = dot(b.hopin[...], attention_weight()).astype(BF16)
            for j in range(9):
                b.qkv[j, 256:272] = rows[:, 128 * j : 128 * j + 128]

        @pl.when(i == seg)
        def _():
            for p in range(3):
                forward_pair(p)

        @pl.when(i == 0)
        def _():
            for n in ("f2", "f0"):
                gather_pass(n)

    def head_rows(ref, c):
        if nz > 1:
            return ref.at[pl.ds(c * (nz // 2), nz // 2)]
        return ref.at[:, :, pl.ds(pl.multiple_of(c * HALF, 16), HALF)]

    def wo_rows(h, c):
        return head_rows(b.wo.at[h], c)[...].reshape(HALF, HALF)

    o_swap = remote(b.oc.at[other_rows], b.oin, sibling)
    wo_local.wait()
    arrived([wo_swap])
    halves = [dot(b.oc[own_rows], wo_rows(h, core)) for h in range(2)]
    arrived([o_swap])
    attended = jnp.concatenate([halves[h] + dot(b.oin[...], wo_rows(h, other)) for h in range(2)], 1)
    h1, n1, inv1 = norm_forward(b.x[own_rows].astype(F32) + attended, gains[0], biases[0])
    b.h1[...] = h1
    b.n1[...] = n1
    b.inv1[...] = inv1
    b.h1b[own_rows] = h1.astype(BF16)
    h_swap = remote(b.h1b.at[own_rows], b.h1b.at[own_rows], sibling)

    @pl.when(seg == 1)
    def _():
        b.xp[256:272] = dot(b.hopin[...], b.turn[...], NT).astype(BF16)

    for n in ("f1", "f2", "f0"):
        gather_done(n)

    def feed_weight(t, kind):
        cols = [256 * j + 128 * kind for j in range(3)]
        blocks = [b.wf[2 * t + i, :, :, :, c : c + 128].reshape(D, 128) for i in range(2) for c in cols]
        return jnp.concatenate(blocks, 1)

    def up_weight(t):
        return feed_weight(t, 0)

    def down_weight(t):
        return feed_weight(t, 1)

    def gelu_share(units):
        return 0.5 * (1.0 + lax.erf(units * INV_ROOT_TWO))

    early = pltpu.make_async_remote_copy(
        src_ref=b.es,
        dst_ref=b.er,
        send_sem=xsem.at[XBASE[6] + 3],
        recv_sem=xsem.at[XBASE[6] + 4],
        device_id=sibling,
        device_id_type=MESH,
    )
    row16 = lax.broadcasted_iota(jnp.int32, (16, D), 0)

    @pl.when(seg == 0)
    def _():
        arrived([h_swap])
        rows = b.h1b[OWN + 256 : OWN + 272]
        units = [dot(rows, up_weight(t)) for t in range(2)]
        part = sum(dot((units[t] * gelu_share(units[t])).astype(BF16), down_weight(t), NT) for t in range(2))

        @pl.when(core == 0)
        def _():
            b.es[...] = part
            early.start()

        @pl.when(core == 1)
        def _():
            early.wait_recv()
            whole = b.h1[256:272] + part + b.er[...]
            written = norm_forward(whole, gains[1], biases[1])[0]
            b.hop[...] = jnp.where(row16 % 8 < 5, written, 0.0).astype(BF16)
            hops[0].start()
            hops[1].start()

    def project_up(rows):
        for t in range(2):
            units = dot(b.h1b[rows], up_weight(t))
            b.ul[t, rows] = units
            b.gl[t, rows] = (units * gelu_share(units)).astype(BF16)

    @pl.loop(0, 2)
    def _(i):
        @pl.when((i == 1) & (seg == 1))
        def _():
            arrived([h_swap])

        project_up(pl.ds(pl.multiple_of(OWN * jnp.where(i == 0, core, other), 16), OWN))


    def partial_down(rows):
        return sum(dot(b.gl[t, rows], down_weight(t), NT) for t in range(2))

    b.fs[...] = partial_down(other_rows).astype(BF16)
    f_swap = remote(b.fs, b.fr, sibling)
    branch = partial_down(own_rows)
    arrived([f_swap])
    out, n2, inv2 = norm_forward(b.h1[...] + branch + b.fr[...].astype(F32), gains[1], biases[1])
    low = out.astype(BF16)
    b.yb[...] = low
    b.mo[...] = low[256:272].astype(F32).reshape(2, 8, D)
    for i in range(TP):
        to_device(
            b.yb.at[pl.ds(TOKENS * i, TOKENS)],
            hout.at[seg, pl.ds(pl.multiple_of(TOKENS * core, 16), TOKENS)],
            (i, chain),
            xsem.at[XBASE[3] + 2 * seg + core],
            3,
            i,
        )
    for i in range(2):
        to_device(b.mo.at[i], mout.at[seg], (2 * core + i, chain), xsem.at[XBASE[4] + seg], 4, i)

    for i in range(TP):
        from_device(b.gyt.at[pl.ds(TOKENS * i, TOKENS)], 1, i)
    for i in range(2):
        from_device(b.gm.at[i], 2, i)
    upstream = jnp.concatenate([b.gyt[...].astype(F32), b.gm[...].reshape(16, D)], 0)
    b.sg[...] = jnp.zeros((48, D), F32)
    b.sg[1:2] = column_sum(upstream * n2)
    b.sg[3:4] = column_sum(upstream)
    dz = norm_backward(upstream, n2, inv2, gains[1])
    b.dz[...] = dz
    b.dfb[own_rows] = dz.astype(BF16)
    df_swap = remote(b.dfb.at[own_rows], b.dfb.at[own_rows], sibling)

    def weight_grad(into, left, right, jobs_):
        @pl.loop(0, 2)
        def _(t):
            part = dot(left[...], right[t], TN).astype(BF16)
            for i in range(2):
                into[2 * t + i] = part[:, HALF * i : HALF * (i + 1)].reshape(nz, ny, br, HALF)

            for h in range(2):

                @pl.when(t == h)
                def _():
                    for n in jobs_:
                        if is_ring(n, 0) and scatters[n][1][0] != "x":
                            ring_send(n, h)
                        elif h == 1:
                            scatter_send(n, 0)

    scatters = {j[0]: j for j in scatter_jobs()}
    rs = {}

    def is_ring(name, step):
        _, order, cols, axes = scatters[name]
        return step == 0 and name in RINGS and size[order[0]] == 4

    def source_of(name, step):
        _, order, cols, axes = scatters[name]
        axis = order[step]
        left = [a for a in axes if a not in order[:step]]
        array = getattr(b, GRADS[name[0]]) if step == 0 else k[SUMMED, step - 1, name]
        tail = (slice(None), cols) if step == 0 else ()

        def part(place, half=None):
            where = []
            for a in left:
                if a == axis:
                    where.append(place)
                elif half is not None:
                    where.append(pl.ds(half * (size[a] // 2), size[a] // 2))
                    half = None
                else:
                    where.append(slice(None))
            return array.at[tuple(where) + tail]

        return part

    def ring_send(name, half):
        axis = scatters[name][1][0]
        n = size[axis]
        part = source_of(name, 0)
        landing, over = k[LANDED, 0, name], k[PASSED, 0, name]
        right, left, far = (near[axis][o] for o in (1, n - 1, 2))
        to = moved(axis, 1), moved(axis, n - 1)
        cut = size[[a for a in scatters[name][3] if a != axis][0]] // 2
        if name not in rs:
            rs[name] = ([None, None], Group(lambda: landing), cut, (right, left), to)
        rs[name][0][half] = remote(part(far, half), lambda: over.at[half], to[half])
        if half == 0:
            rs[name][1].add(part(left, 0), landing.at[1, :cut], to[1])
        else:
            rs[name][1].add(part(right, 1), landing.at[0, cut:], to[0])

    def scatter_send(name, step):
        axis = scatters[name][1][step]
        n = size[axis]
        part = source_of(name, step)
        landing = k[LANDED, step, name]
        if is_ring(name, step):
            ring_send(name, 0)
            ring_send(name, 1)
            return
        rs[name] = [Group(lambda: landing)] if n > 1 else []
        for o in range(1, n):
            rs[name][0].add(part(near[axis][o]), landing.at[o - 1], moved(axis, o))

    def scatter_pass(name):
        if not is_ring(name, 0):
            return
        passing, coming, half, places_, devices = rs[name]
        part = source_of(name, 0)
        landing, over, updated = k[LANDED, 0, name], k[PASSED, 0, name], k[UPDATED, 0, name]
        for i in range(2):
            arrived([passing[i]])
            updated[i] = (part(places_[i], i)[...].astype(F32) + over[i].astype(F32)).astype(BF16)
            where = landing.at[0, :half] if i == 0 else landing.at[1, half:]
            coming.add(updated.at[i], where, devices[i])

    def scatter_sum(name, step):
        _, order, cols, axes = scatters[name]
        axis = order[step]
        total = source_of(name, step)(at[axis])[...].astype(F32)
        ring = is_ring(name, step)
        arrived([rs[name][1]] if ring else rs[name])
        for o in range(2 if ring else size[axis] - 1):
            total = total + k[LANDED, step, name][o].astype(F32)
        if step < len(order) - 1:
            k[SUMMED, step, name][...] = total.astype(BF16)
        return total

    def scatter_on(names, step):
        for n in names:
            scatter_sum(n, step)
            scatter_send(n, step + 1)

    down_names, up_names = ("t0", "t1", "t2"), ("i0", "i1", "i2")
    arrived([df_swap])
    weight_grad(b.gt, b.dfb, b.gl, down_names)
    @pl.loop(0, 2)
    def _(i):
        rows = pl.ds(pl.multiple_of(OWN * i, 16), OWN)
        for t in range(2):
            units = b.ul[t, rows]
            slope = gelu_share(units) + units * jnp.exp(-0.5 * units * units) * INV_ROOT_TWOPI
            b.du[t, rows] = (dot(b.dfb[rows], down_weight(t)) * slope).astype(BF16)


    def partial_up(rows):
        return sum(dot(b.du[t, rows], up_weight(t), NT) for t in range(2))

    dh_swap = Group(lambda: b.dhr)

    @pl.loop(0, 2)
    def _(i):
        part = partial_up(pl.ds(pl.multiple_of(OWN * jnp.where(i == 0, other, core), 16), OWN))

        @pl.when(i == 0)
        def _():
            b.dhs[...] = part.astype(BF16)
            dh_swap.add(b.dhs, b.dhr, sibling)

        @pl.when(i == 1)
        def _():
            b.dz[...] = b.dz[...] + part

    arrived([dh_swap])
    into_first = b.dz[...] + b.dhr[...].astype(F32)
    b.sg[0:1] = column_sum(into_first * b.n1[...])
    b.sg[2:3] = column_sum(into_first)
    dr = norm_backward(into_first, b.n1[...], b.inv1[...], gains[0])
    b.dr[...] = dr
    b.dab[own_rows] = dr.astype(BF16)
    da_swap = remote(b.dab.at[own_rows], b.dab.at[own_rows], sibling)

    def grad_mixed(rows):
        parts = [dot(b.dab[rows, HALF * h : HALF * (h + 1)], wo_rows(h, core), NT) for h in range(2)]
        for p in range(3):
            b.doc[p, rows] = (parts[0] + parts[1])[:, 128 * p : 128 * p + 128].astype(BF16)

    weight_grad(b.gi, b.h1b, b.du, up_names)
    for n in down_names:
        scatter_pass(n)
    arrived([da_swap])
    grad_mixed(slice(None))

    mixed_t = b.ot[...].reshape(HALF, ROWS)

    def proj_grad(h):
        cols = pl.ds(pl.multiple_of(HALF * h, 128), HALF)
        return dot(mixed_t, b.dab[:, cols]).astype(BF16).reshape(b.gos.shape)

    def wo_part(c):
        return head_rows(b.ga.at[:, :, :, wo_cols], c)

    b.gos[...] = proj_grad(other)
    go_swap = remote(b.gos, wo_part(core), sibling)
    wo_part(core)[...] = proj_grad(core)

    def backward_pair(p):
        qp, kp, vp = (b.qkv[3 * p + i] for i in range(3))
        dop = b.doc[p]
        kt = kp.T
        dv = dk = 0.0
        dq = []
        for hh in range(2):
            inside, _, _ = head_masks(hh)
            zero = jnp.zeros_like(kp)
            grad_probs = dot(jnp.where(inside, vp, zero), dop, NT)
            low_probs = b.pt[2 * p + hh]
            probs = low_probs.astype(F32)
            row_term = jnp.sum(probs * grad_probs, 0, keepdims=True)
            ds = (probs * (grad_probs - row_term)).astype(BF16)
            dv = dv + dot(low_probs, jnp.where(inside, dop, zero))
            dk = dk + dot(ds, jnp.where(inside, qp, zero))
            dq.append(dot(kt[64 * hh : 64 * hh + 64], ds))
        b.dqkv[3 * p] = (jnp.concatenate(dq, 0) * 0.125).T.astype(BF16)
        b.dqkv[3 * p + 1] = (dk * 0.125).astype(BF16)
        b.dqkv[3 * p + 2] = dv.astype(BF16)

    def joined(rows, wanted):
        return jnp.concatenate([b.dqkv[i, rows] for i in wanted], 1)

    def attention_grad(p):
        grads = jnp.concatenate([b.dqkv[3 * p + i] for i in range(3)], 1)

        part = dot(b.both[jnp.minimum(p, 1)], grads, TN).astype(BF16)

        @pl.when(p == 0)
        def _():
            b.gx[...] = part.reshape(TP, nz, sh.xrows, HALF)

        @pl.when(p > 0)
        def _():
            cols = pl.ds(pl.multiple_of(HALF * p, 128), HALF)
            b.ga[:, :, :, cols] = part.reshape(nz, ny, br, HALF)

    @pl.loop(0, 3)
    def _(p):
        backward_pair(p)
        attention_grad(p)

        @pl.when(p == 0)
        def _():
            arrived([go_swap])
            scatter_send("aw", 0)
            scatter_send("x0", 0)

        @pl.when(p == 1)
        def _():
            scatter_send("a1", 0)
            for n in up_names:
                scatter_pass(n)

        @pl.when(p == 2)
        def _():
            scatter_send("a2", 0)
            scatter_send("a3", 0)
            for n in ("aw", "x0"):
                scatter_pass(n)
            scatter_on(down_names, 0)


    def partial_input(rows):
        return dot(joined(rows, range(9)), attention_weight(), NT)

    memory_rows = [pl.ds(pl.multiple_of(OWN * c + 256, 16), 16) for c in (other, core)]
    part = dot(jnp.concatenate([joined(rows, range(9)) for rows in memory_rows], 0), attention_weight(), NT)
    b.ms[...] = part[:16]
    memory_swap = remote(b.ms, b.mr, sibling)
    b.dxs[...] = partial_input(other_rows).astype(BF16)
    dx_swap = remote(b.dxs, b.dxr, sibling)
    arrived([memory_swap])
    memory_grad = part[16:] + b.dr[256:272] + b.mr[...]

    @pl.when((core == 0) & (seg == 0))
    def _():
        b.sg[16:32] = memory_grad

    @pl.when(core == 1)
    def _():
        b.sg[32:48] = memory_grad

    small_grads = dot(b.sg[...].astype(BF16), smallsel[...], TN).astype(BF16)
    b.ga[:, :, :, 4 * HALF :] = small_grads.reshape(nz, ny, br, SMALL)
    scatter_send("as", 0)
    scatter_pass("a1")
    dx = partial_input(own_rows) + b.dr[...]
    scatter_on(up_names, 0)
    arrived([dx_swap])
    dx = dx + b.dxr[...].astype(F32)
    b.dxb[...] = dx[:256].astype(BF16)
    for i in range(TP):
        to_device(
            b.dxb.at[pl.ds(TOKENS * i, TOKENS)],
            dxo.at[seg, pl.ds(pl.multiple_of(TOKENS * core, 16), TOKENS)],
            (i, chain),
            xsem.at[XBASE[5] + 2 * seg + core],
            5,
            i,
        )
    scatter_on(("aw", "x0", "a1"), 0)
    scatter_on(down_names, 1)
    scatter_on(("a2", "a3", "as"), 0)
    spread = dot(packy[...], scatter_sum("x0", 1).astype(BF16), TN).astype(BF16)
    b.e3y[...] = spread.reshape(ny, 2 * sh.pc, HALF)
    ysteps = [Group(lambda: b.r3y)] if ny > 1 else []
    for o in range(1, ny):
        ysteps[0].add(b.e3y.at[near["y"][o]], b.r3y.at[o - 1], moved("y", o))
    scatter_on(up_names, 1)
    for n in ("aw", "a1", "a2", "a3", "as"):
        cols = scatters[n][2]
        b.tot[:, cols.start - HALF : cols.stop - HALF] = scatter_sum(n, 1).astype(BF16)
    spread = dot(packsel[...], b.tot[...], TN).astype(BF16)
    b.e3[...] = spread.reshape(TP, 2 * sh.pc, REST)
    steps = [Group(lambda: b.r3)]
    for o in range(1, TP):
        steps[0].add(b.e3.at[near["x"][o]], b.r3.at[o - 1], moved("x", o))

    def last_rows(wanted, first_col):
        for j, n in enumerate(wanted):
            total = scatter_sum(n, 2)
            cols = slice(first_col + 128 * j, first_col + 128 * j + 128)
            b.sf[0, :, cols] = total[:wr]
            b.sf[1, :, cols] = total[wr:]

    last_rows(down_names, HALF)
    last_rows(up_names, 0)
    sf_local = local(b.sf.at[core], gfo.at[core])
    sf_swap = remote(b.sf.at[other], gfo.at[core], sibling)

    arrived(steps)
    total = b.e3[x].astype(F32)
    for o in range(1, TP):
        total = total + b.r3[o - 1].astype(F32)
    b.s4[:, :, HALF:] = total.reshape(2, sh.pc, REST)
    arrived(ysteps)
    total = b.e3y[y].astype(F32)
    for o in range(1, ny):
        total = total + b.r3y[o - 1].astype(F32)
    b.s4[:, :, :HALF] = total.reshape(2, sh.pc, HALF)
    s4_local = local(b.s4.at[core], gao.at[core])
    s4_swap = remote(b.s4.at[other], gao.at[core], sibling)

    for kind, out_ref in ((3, hout), (5, dxo)):
        for s in range(2):
            for j in range(2):
                from_device(out_ref.at[s, pl.ds(TOKENS * j, TOKENS)], kind, 2 * s + j)
    for s in range(2):
        from_device(mout.at[s], 4, s)
    sf_local.wait()
    s4_local.wait()
    arrived([sf_swap, s4_swap])

    for group in sent[-SENDS:]:
        group.wait_send()
    for same, copy in conditional:

        @pl.when(jnp.logical_not(same))
        def _():
            copy.wait_send()

    @pl.when((seg == 0) & (core == 1))
    def _():
        hops[0].wait_send()
        hops[1].wait_send()

    @pl.when((seg == 0) & (core == 0))
    def _():
        early.wait_send()


def layer(sh, arrays):
    constants = [jnp.asarray(a, BF16) for a in selections(sh)]
    tables = scratch_of(sh)
    names = [list(table) for table in tables]
    anywhere = pl.BlockSpec(memory_space=pl.ANY)
    outs = [
        jax.ShapeDtypeStruct((2, 128, D), BF16),
        jax.ShapeDtypeStruct((2, 8, D), F32),
        jax.ShapeDtypeStruct((2, 128, D), BF16),
        jax.ShapeDtypeStruct((2, sh.pc, ACOLS), F32),
        jax.ShapeDtypeStruct((2, sh.wrows, D), F32),
    ]
    return pl.pallas_call(
        functools.partial(kernel, sh, names),
        name="layer",
        out_shape=outs,
        in_specs=[anywhere] * 15,
        out_specs=[anywhere] * len(outs),
        scratch_shapes=[pltpu.VMEM(*one) for table in tables for one in table.values()]
        + [
            pltpu.SemaphoreType.DMA((SENDS,)),
            pltpu.SemaphoreType.DMA((96,)),
            pltpu.SemaphoreType.DMA((45,)),
            pltpu.SemaphoreType.DMA((20,)),
        ],
        compiler_params=pltpu.CompilerParams(
            collective_id=0, has_side_effects=True, vmem_limit_bytes=64 * 2**20 - 2**17
        ),
    )(*arrays, *constants)


def unpack_kernel(sh, *refs):
    arrays, results, held, outs, sems = refs[:5], refs[5:15], refs[15:20], refs[20:30], refs[30]
    loads = [pltpu.make_async_copy(arrays[i], held[i], sems.at[i]) for i in range(5)]
    stores = [pltpu.make_async_copy(outs[i], results[i], sems.at[5 + i]) for i in range(10)]
    for copy in loads:
        copy.start()
    hout, mout, dxo, gao, gfo = held
    hidden, memory, grad_in, gq, gp, gains, biases, tokens, gi, gt = outs
    ar = sh.arows
    loads[0].wait()
    hidden[...] = hout[...]
    stores[0].start()
    loads[2].wait()
    grad_in[...] = dxo[...].astype(F32)
    stores[2].start()
    loads[1].wait()
    for i in range(2):
        memory[:, i] = mout[i, :5].astype(BF16)
    stores[1].start()
    loads[3].wait()
    for h in range(2):
        for p in range(3):
            for i in range(3):
                to = D * i + HALF * h + 128 * p
                first = HALF * p + 128 * i
                gq[:, to : to + 128] = gao[h, :ar, first : first + 128]
        gp[:, HALF * h : HALF * (h + 1)] = gao[h, :ar, WO : WO + HALF]
    small = gao[0, :, 4 * HALF :] + gao[1, :, 4 * HALF :]
    turned = small.T[:, :ar]
    gains[...] = turned[0:2]
    biases[...] = turned[2:4]
    for kind in range(2):
        tokens[:, kind] = small[:ar, 4 + MEM * kind : 4 + MEM * (kind + 1)]
    for i in range(3, 8):
        stores[i].start()
    loads[4].wait()
    for h in range(2):
        gi[:, HALF * h : HALF * (h + 1)] = gfo[h, :, :HALF]
        gt[:, HALF * h : HALF * (h + 1)] = gfo[h, :, HALF:]
    for i in range(8, 10):
        stores[i].start()
    for copy in stores:
        copy.wait()


def unpack(sh, *arrays):
    ar, wr = sh.arows, sh.wrows
    shapes = [
        ((2, 128, D), BF16),
        ((5, 2, D), BF16),
        ((2, 128, D), F32),
        ((ar, 3 * D), F32),
        ((ar, D), F32),
        ((2, ar), F32),
        ((2, ar), F32),
        ((ar, 2, MEM), F32),
        ((wr, D), F32),
        ((wr, D), F32),
    ]
    anywhere = pl.BlockSpec(memory_space=pl.ANY)
    return pl.pallas_call(
        functools.partial(unpack_kernel, sh),
        name="unpack",
        out_shape=[jax.ShapeDtypeStruct(*one) for one in shapes],
        in_specs=[anywhere] * 5,
        out_specs=[anywhere] * len(shapes),
        scratch_shapes=[pltpu.VMEM(a.shape, a.dtype) for a in arrays]
        + [pltpu.VMEM(*one) for one in shapes]
        + [pltpu.SemaphoreType.DMA((15,))],
        compiler_params=pltpu.CompilerParams(vmem_limit_bytes=64 * 2**20 - 2**17),
    )(*arrays)


def body(
    sh,
    hidden_in,
    reset,
    w_qkv,
    w_attn_out,
    norm_gains,
    norm_biases,
    memory_tokens,
    w_in,
    w_out,
    grad_hidden,
    grad_memory,
):
    arrays = (
        hidden_in,
        grad_hidden,
        grad_memory.transpose(1, 0, 2),
        w_qkv,
        w_attn_out,
        norm_gains,
        norm_biases,
        memory_tokens.transpose(2, 0, 1),
        w_in,
        w_out.T,
    )
    hidden, memory, *middle, tokens, gi, gt = unpack(sh, *layer(sh, arrays))
    return hidden, memory.transpose(1, 0, 2), *middle, tokens.transpose(1, 2, 0), gi, gt.T


def solution(mesh):
    sh = Shape(mesh.shape["dp"])
    return jax.shard_map(
        functools.partial(body, sh),
        mesh=mesh,
        in_specs=(
            P("dp", "tp", None),
            P("dp"),
            P(("dp", "tp"), None),
            P(("dp", "tp"), None),
            P(None, ("dp", "tp")),
            P(None, ("dp", "tp")),
            P(None, None, ("dp", "tp")),
            P("dp", "tp"),
            P("tp", "dp"),
            P("dp", "tp", None),
            P("dp", "tp", None),
        ),
        out_specs=(
            P("dp", "tp", None),
            P("dp", "tp", None),
            P("dp", "tp", None),
            P(("dp", "tp"), None),
            P(("dp", "tp"), None),
            P(None, ("dp", "tp")),
            P(None, ("dp", "tp")),
            P(None, None, ("dp", "tp")),
            P("dp", "tp"),
            P("tp", "dp"),
        ),
        check_vma=False,
    )
```

```python
import functools
import types

import jax
import jax.numpy as jnp
import numpy as np
from jax import lax
from jax.experimental import pallas as pl
from jax.experimental.pallas import tpu as pltpu
from jax.sharding import PartitionSpec as P

D = 768
HALF = 384
MEM = 10
TOKENS = 64
OWN = 272
ROWS = 2 * OWN
TP = 4
SMALL = 128
ACOLS = 4 * HALF + SMALL
REST = ACOLS - HALF
CUT = HALF + 640
WO = 3 * HALF
EPSILON = 1e-05
INV_ROOT_TWO = 0.7071067811865476
INV_ROOT_TWOPI = 0.3989422804014327
EXP_SCALE = 0.125 * 1.4426950408889634
MASKED = -1e30
F32 = jnp.float32
BF16 = jnp.bfloat16
MESH = pl.DeviceIdType.MESH
NN = (((1,), (0,)), ((), ()))
NT = (((1,), (1,)), ((), ()))
TN = (((0,), (0,)), ((), ()))


def dot(a, b, dims=NN):
    return lax.dot_general(a, b, dims, preferred_element_type=F32)


def up16(n):
    return -(-n // 16) * 16


class Shape:
    def __init__(self, dp):
        self.dp = dp
        planes = dp // 2
        self.ny = int(round(planes**0.5))
        self.nz = planes // self.ny
        self.wrows = D // dp
        self.arows = D // (dp * TP)
        self.brows = 2 * self.wrows
        self.pr = up16(self.arows)
        self.xrows = 2 * self.arows * self.ny
        self.pc = -(-self.arows // 8) * 8
        self.fr = up16(self.wrows)


def selections(sh):
    pack = np.zeros((sh.brows, TP * 2 * sh.pc), np.float32)
    for c in range(2):
        for x in range(TP):
            for i in range(sh.arows):
                pack[c * sh.wrows + x * sh.arows + i, (x * 2 + c) * sh.pc + i] = 1
    packy = np.zeros((sh.xrows, sh.ny * 2 * sh.pc), np.float32)
    turn = np.zeros((D, D), np.float32)
    ar = sh.arows
    for c in range(2):
        for y in range(sh.ny):
            for i in range(ar):
                row = (y * 2 + c) * ar + i
                packy[row, (y * 2 + c) * sh.pc + i] = 1
                for x in range(TP):
                    for z in range(sh.nz):
                        place = (z * sh.ny + y) * sh.brows + (c * TP + x) * ar + i
                        turn[(x * sh.nz + z) * sh.xrows + row, place] = 1
    small = np.zeros((48, SMALL), np.float32)
    for i in range(4):
        small[i, i] = 1
    for kind in range(2):
        for i in range(MEM):
            small[16 + 16 * kind + (i // 5) * 8 + i % 5, 4 + MEM * kind + i] = 1
    places = np.zeros((4, MEM, SMALL), np.float32)
    for kind, (rows, first) in enumerate(((2, 0), (2, 2), (MEM, 4), (MEM, 4 + MEM))):
        for i in range(rows):
            places[kind, i, first + i] = 1
    return pack, small, places, packy, turn


def norm_forward(inputs, gain, offset):
    centred = inputs - jnp.mean(inputs, -1, keepdims=True)
    spread = jnp.mean(centred * centred, -1, keepdims=True)
    inverse = lax.rsqrt(spread + EPSILON)
    normed = centred * inverse
    return normed * gain + offset, normed, inverse


def norm_backward(upstream, normed, inverse, gain):
    scaled = upstream * gain
    first_mean = jnp.mean(scaled, -1, keepdims=True)
    second_mean = jnp.mean(scaled * normed, -1, keepdims=True)
    return inverse * (scaled - first_mean - normed * second_mean)


def column_sum(a):
    return jnp.sum(a, 0, keepdims=True)


XBASE = (0, 4, 8, 10, 14, 16, 20)
SENDS = 40
STAGED, LANDED, SUMMED, PASSED, UPDATED = range(5)


def scratch_of(sh):
    nz, ny, br = sh.nz, sh.ny, sh.brows
    ar, wr = sh.arows, sh.wrows
    operands = [
        (5, 2, D),
        (ar, 3 * D),
        (ar, D),
        (2, ar),
        (2, ar),
        (ar, 2, MEM),
        (wr, D),
        (wr, D),
        (br, TP * 2 * sh.pc),
        (48, SMALL),
        (4, MEM, SMALL),
        (sh.xrows, ny * 2 * sh.pc),
    ]
    jobs = {(STAGED, i, 0): (dims, BF16) for i, dims in enumerate(operands)}
    s = dict(
        pk=((2, sh.pr, ACOLS), BF16),
        ff=((2, sh.fr, D), BF16),
        gms=((2, 8, D), F32),
        p1=((2, sh.pr, ACOLS), BF16),
        p2=((TP, 2 * sh.pc, REST), BF16),
        p2y=((ny, 2 * sh.pc, HALF), BF16),
        turn=((D, D), BF16),
        wx=((TP, nz, sh.xrows, HALF), BF16),
        gx=((TP, nz, sh.xrows, HALF), BF16),
        f1=((2, sh.fr, D), BF16),
        wa=((nz, ny, br, ACOLS), BF16),
        wf=((TP, nz, ny, br, D), BF16),
        wo=((2, nz, ny, br, HALF), BF16),
        par=((8, D), F32),
        both=((2, ROWS, D), BF16),
        gyt=((TP * TOKENS, D), BF16),
        gm=((2, 8, D), F32),
        qkv=((9, ROWS, 128), BF16),
        pt=((6, ROWS, ROWS), BF16),
        ot=((3, 128, ROWS), BF16),
        oc=((ROWS, HALF), BF16),
        oin=((OWN, HALF), BF16),
        h1=((OWN, D), F32),
        n1=((OWN, D), F32),
        inv1=((OWN, 1), F32),
        h1b=((ROWS, D), BF16),
        gl=((2, ROWS, D), BF16),
        ul=((2, ROWS, D), F32),
        fs=((OWN, D), BF16),
        fr=((OWN, D), BF16),
        n2=((OWN, D), F32),
        yb=((OWN, D), BF16),
        mo=((2, 8, D), F32),
        hop=((16, D), BF16),
        hopin=((16, D), BF16),
        es=((16, D), F32),
        er=((16, D), F32),
        dz=((OWN, D), F32),
        dfb=((ROWS, D), BF16),
        du=((2, ROWS, D), BF16),
        dhs=((OWN, D), BF16),
        dhr=((OWN, D), BF16),
        dr=((OWN, D), F32),
        dab=((ROWS, D), BF16),
        doc=((3, ROWS, 128), BF16),
        dqkv=((9, ROWS, 128), BF16),
        ga=((nz, ny, br, ACOLS), BF16),
        gi=((TP, nz, ny, br, HALF), BF16),
        gt=((TP, nz, ny, br, HALF), BF16),
        dxs=((OWN, D), BF16),
        dxr=((OWN, D), BF16),
        dxb=((TP * TOKENS, D), BF16),
        sg=((48, D), F32),
        ms=((16, D), F32),
        mr=((16, D), F32),
        tot=((br, 2 * HALF), BF16),
        e3=((TP, 2 * sh.pc, 2 * HALF), BF16),
        r3=((TP - 1, 2 * sh.pc, 2 * HALF), BF16),
        ez=((nz, TP, 2 * sh.pc, 256), BF16),
        rz=((nz * TP - 1, 2 * sh.pc, 256), BF16),
        ey=((ny, TP, 2 * sh.pc, 256), BF16),
        ry=((ny * TP - 1, 2 * sh.pc, 256), BF16),
        e3y=((ny, 2 * sh.pc, HALF), BF16),
        r3y=((max(1, ny - 1), 2 * sh.pc, HALF), BF16),
        s4=((2, sh.pc, ACOLS), F32),
        sf=((2, sh.wrows, D), F32),
    )
    s.update(gos=((nz // 2, ny, br, HALF) if nz > 1 else (1, 1, HALF, HALF), BF16))
    sizes = {"x": TP, "z": nz, "y": ny}
    for name, order, cols, axes in scatter_jobs():
        left = [a for a in axes]
        block = (sh.xrows if name[0] == "x" else br, cols.stop - cols.start)
        for step, axis in enumerate(order):
            left = [a for a in left if a != axis]
            dims = tuple(sizes[a] for a in left)
            ring = step == 0 and name in RINGS and sizes[axis] == 4
            jobs[LANDED, step, name] = ((2 if ring else max(1, sizes[axis] - 1),) + dims + block, BF16)
            if step < len(order) - 1:
                jobs[SUMMED, step, name] = (dims + block, BF16)
            if ring:
                jobs[PASSED, 0, name] = ((2, dims[0] // 2) + dims[1:] + block, BF16)
                jobs[UPDATED, 0, name] = jobs[PASSED, 0, name]
    return s, jobs


def scatter_jobs():
    orders = [("z", "y", "x"), ("x", "z", "y"), ("y", "x", "z")]
    jobs = []
    for kind in ("t", "i"):
        for j in range(3):
            jobs.append((f"{kind}{j}", orders[j], slice(128 * j, 128 * j + 128), ("x", "z", "y")))
    zy, yz = ("z", "y"), ("y", "z")
    jobs.append(("aw", yz, slice(WO, WO + HALF), zy))
    jobs.append(("x0", ("x", "z"), slice(0, HALF), ("x", "z")))
    jobs.append(("a1", zy, slice(HALF, 2 * HALF), zy))
    jobs.append(("a2", yz, slice(2 * HALF, 2 * HALF + 256), zy))
    jobs.append(("a3", zy, slice(2 * HALF + 256, 3 * HALF), zy))
    jobs.append(("as", zy, slice(4 * HALF, ACOLS), zy))
    return jobs


def gather_jobs():
    orders = [("x", "y", "z"), ("y", "z", "x"), ("z", "x", "y")]
    jobs = [(f"f{j}", orders[j], slice(256 * j, 256 * j + 256), ("x", "z", "y")) for j in range(3)]
    jobs.append(("x0", ("z", "x"), slice(0, HALF), ("x", "z")))
    jobs.append(("a0", ("y", "z"), slice(HALF, CUT), ("z", "y")))
    jobs.append(("a1", ("z", "y"), slice(CUT, ACOLS), ("z", "y")))
    return jobs


RINGS = ("t0", "t1", "t2", "i0", "i1", "i2", "aw", "x0", "a1")
WEIGHTS = {"f": "wf", "a": "wa", "x": "wx"}
GRADS = {"t": "gt", "i": "gi", "a": "ga", "x": "gx"}


def kernel(sh, names, *refs):
    xin, gin = refs[:2]
    hout, mout, dxo, gao, gfo = refs[15:20]
    ssem, rsem, xsem, lsem = refs[-4:]
    count = len(names[0])
    b = types.SimpleNamespace(**dict(zip(names[0], refs[20 : 20 + count])))
    b.xp, b.x = b.both.at[0], b.both.at[1]
    k = dict(zip(names[1], refs[20 + count : -4]))
    staged = [k[STAGED, i, 0] for i in range(12)]
    gmem, wq, wp, gain_in, bias_in, token_in, up_in, down_in = staged[:8]
    packsel, smallsel, places, packy = staged[8:]
    turn = refs[14]
    nz, ny, br, wr, ar = sh.nz, sh.ny, sh.brows, sh.wrows, sh.arows
    pk, ff, gms = b.pk, b.ff, b.gms

    dp = lax.axis_index("dp")
    x = lax.axis_index("tp")
    core = dp % 2
    y = (dp // 2) % ny
    z = dp // (2 * ny)
    other = 1 - core
    chain = x // 2
    seg = jnp.where((x == 1) | (x == 2), 1, 0)
    at = {"x": x, "y": y, "z": z}
    size = {"x": TP, "y": ny, "z": nz}

    def device(x_=x, y_=y, z_=z, c_=core):
        return ((z_ * ny + y_) * 2 + c_, x_)

    near = {a: [(at[a] + o) % size[a] for o in range(size[a])] for a in at}

    def moved_to(axis, offset, core_=core):
        there = dict(at)
        there[axis] = near[axis][offset]
        return device(there["x"], there["y"], there["z"], core_)

    def plane_device(axis, offset, x_offset):
        there = dict(at)
        there[axis], there["x"] = near[axis][offset], near["x"][x_offset]
        return device(there["x"], there["y"], there["z"])

    neighbours = {a: [moved_to(a, o) for o in range(size[a])] for a in at}

    def moved(axis, offset):
        return neighbours[axis][offset]

    sibling = device(c_=other)
    sent = []

    class Group:
        def __init__(self, like):
            if len(sent) >= SENDS:
                sent[-SENDS].wait_send()
            self.like = like
            self.number = len(sent)
            sent.append(self)

        def add(self, src, dst, to):
            pltpu.make_async_remote_copy(
                src_ref=src,
                dst_ref=dst,
                send_sem=ssem.at[self.number % SENDS],
                recv_sem=rsem.at[self.number],
                device_id=to,
                device_id_type=MESH,
            ).start()

        def wait_send(self):
            like = self.like()
            pltpu.make_async_copy(like, like, ssem.at[self.number % SENDS]).wait()

        def wait_recv(self):
            like = self.like()
            pltpu.make_async_copy(like, like, rsem.at[self.number]).wait()

    def remote(src, dst, to):
        where = dst if callable(dst) else lambda: dst
        group = Group(where)
        group.add(src, where(), to)
        return group

    def arrived(groups):
        for group in groups:
            group.wait_recv()

    locals_ = [0]

    def local(src, dst):
        copy = pltpu.make_async_copy(src, dst, lsem.at[locals_[0]])
        locals_[0] += 1
        copy.start()
        return copy

    staging = [local(refs[2 + i], staged[i]) for i in range(12)]
    turn_local = local(turn, b.turn)

    barrier = pltpu.get_barrier_semaphore()
    peers = [sibling]
    for o in range(1, TP):
        peers += [moved("x", o), moved_to("x", o, other)]
    for axis in ("y", "z"):
        for o in range(1, size[axis]):
            peers.append(moved(axis, o))
            peers += [plane_device(axis, o, o2) for o2 in range(1, TP)]
    for peer in peers:
        pl.semaphore_signal(barrier, inc=1, device_id=peer, device_id_type=MESH)

    pk[...] = jnp.zeros(pk.shape, BF16)
    ff[...] = jnp.zeros(ff.shape, BF16)
    gms[...] = jnp.zeros(gms.shape, F32)
    for copy in staging:
        copy.wait()
    small = dot(gain_in[...], places[0, :2], TN) + dot(bias_in[...], places[1, :2], TN)
    small = small + dot(token_in[:, 0], places[2]) + dot(token_in[:, 1], places[3])
    small = small.astype(BF16)
    for h in range(2):
        for p in range(3):
            for i in range(3):
                first = D * i + HALF * h + 128 * p
                pk[h, :ar, HALF * p + 128 * i : HALF * p + 128 * (i + 1)] = wq[:, first : first + 128]
        pk[h, :ar, WO : WO + HALF] = wp[:, HALF * h : HALF * (h + 1)]
        pk[h, :ar, 4 * HALF :] = small
        for j in range(3):
            cols = slice(HALF * h + 128 * j, HALF * h + 128 * (j + 1))
            ff[h, :wr, 256 * j : 256 * j + 128] = up_in[:, cols]
            ff[h, :wr, 256 * j + 128 : 256 * j + 256] = down_in[:, cols]
        gms[h, 0:5] = gmem[:, h].astype(F32)
    pl.semaphore_wait(barrier, len(peers))

    pk_local = local(pk.at[core], b.p1.at[core])
    ff_local = local(ff.at[core], b.f1.at[core])
    pk_swap = remote(pk.at[other], b.p1.at[core], sibling)
    ff_swap = remote(ff.at[other], b.f1.at[core], sibling)

    conditional = []

    def to_device(src, dst, place, here, kind, send_slot):
        copy = pltpu.make_async_remote_copy(
            src_ref=src,
            dst_ref=dst,
            send_sem=xsem.at[25 + XBASE[kind] + send_slot],
            recv_sem=here,
            device_id=device(x_=place[0], c_=place[1]),
            device_id_type=MESH,
        )
        same = (place[0] == x) & (place[1] == core)

        @pl.when(same)
        def _():
            pltpu.make_async_copy(src, dst, here).start()

        @pl.when(jnp.logical_not(same))
        def _():
            copy.start()

        conditional.append((same, copy))

    def from_device(dst, kind, slot):
        pltpu.make_async_copy(dst, dst, xsem.at[XBASE[kind] + slot]).wait()

    def chip_of(k, s):
        return s + k * (3 - 2 * s)

    def send_rows():
        for s in range(2):
            for j in range(2):
                to_device(
                    xin.at[s, pl.ds(TOKENS * j, TOKENS)],
                    b.x.at[pl.ds(pl.multiple_of(OWN * j + TOKENS * x, 16), TOKENS)],
                    (chip_of(core, s), j),
                    xsem.at[XBASE[0] + x],
                    0,
                    2 * s + j,
                )

    def send_upstream():
        for s in range(2):
            for j in range(2):
                to_device(
                    gin.at[s, pl.ds(TOKENS * j, TOKENS)],
                    b.gyt.at[pl.ds(pl.multiple_of(TOKENS * x, 16), TOKENS)],
                    (chip_of(core, s), j),
                    xsem.at[XBASE[1] + x],
                    1,
                    2 * s + j,
                )
            to_device(
                gms.at[s], b.gm.at[x % 2], (chip_of(core, s), x // 2), xsem.at[XBASE[2] + x % 2], 2, s
            )

    def part_of(job, step, place, half=None):
        name, order, cols, axes = job
        fixed = {a: at[a] for a in order[step:]}
        fixed[order[step]] = place
        where = []
        for a in axes:
            if a in fixed:
                where.append(fixed[a])
            elif half is not None:
                where.append(pl.ds(half * (size[a] // 2), size[a] // 2))
                half = None
            else:
                where.append(slice(None))
        return getattr(b, WEIGHTS[name[0]]).at[tuple(where) + (slice(None), cols)]

    def gather_start(name, step):
        job = gathers[name]
        axis = job[1][step]
        n = size[axis]
        own = part_of(job, step, at[axis])
        free = [a for a in job[3] if a not in job[1][step:]]
        relay = n == 4 and step == len(job[1]) - 1 and size[free[0]] % 2 == 0
        state = types.SimpleNamespace(step=step, relay=relay)
        if relay:
            first = [part_of(job, step, at[axis], h) for h in range(2)]
            right, left = moved(axis, 1), moved(axis, n - 1)
            state.right, state.left = (
                remote(first[h], lambda h=h: part_of(job, step, at[axis], h), to) for h, to in ((0, right), (1, left))
            )
            state.every = [Group(lambda: part_of(job, step, pl.ds(0, 2)))]
            state.every[0].add(first[1], first[1], right)
            state.every[0].add(first[0], first[0], left)
        else:
            state.every = [Group(lambda: part_of(job, step, pl.ds(0, n - 1)))] if n > 1 else []
            for o in range(1, n):
                state.every[0].add(own, own, moved(axis, o))
        flying[name] = state

    def gather_pass(name):
        job, state = gathers[name], flying[name]
        if not state.relay:
            return
        axis = job[1][state.step]
        n = size[axis]
        for copy, back, onward, half in ((state.right, n - 1, 1, 0), (state.left, 1, n - 1, 1)):
            arrived([copy])
            piece = part_of(job, state.step, near[axis][back], half)
            state.every[0].add(piece, piece, moved(axis, onward))

    def gather_done(name):
        arrived(flying[name].every)

    gathers = {j[0]: j for j in gather_jobs()}
    flying = {}

    pk_local.wait()
    arrived([pk_swap])
    packed = jnp.concatenate([b.p1[c].astype(F32)[: sh.pc] for c in range(2)], 0).astype(BF16)
    b.p2y[y] = packed[:, :HALF]
    b.p2[x] = packed[:, HALF:]
    mine = b.p2y.at[y]
    ysteps, xsteps = [], [Group(lambda: b.p2.at[: TP - 1])]
    if ny > 1:
        ysteps.append(Group(lambda: b.p2y.at[: ny - 1]))
    for o in range(1, ny):
        ysteps[0].add(mine, mine, moved("y", o))
    mine = b.p2.at[x]
    for o in range(1, TP):
        xsteps[0].add(mine, mine, moved("x", o))
    ff_local.wait()
    arrived([ff_swap])
    two = [b.f1[c].astype(F32)[:wr] for c in range(2)]
    b.wf[x, z, y] = jnp.concatenate(two, 0).astype(BF16)
    feed_names, first_names = ("f1", "f2", "f0"), ("x0", "a0", "a1")
    for n in feed_names:
        gather_start(n, 0)
    send_rows()
    arrived(ysteps)
    b.wx[x, z] = dot(packy[...], b.p2y[...].reshape(ny * 2 * sh.pc, HALF)).astype(BF16)
    gather_start("x0", 0)
    arrived(xsteps)
    b.wa[z, y, :, HALF:] = dot(packsel[...], b.p2[...].reshape(TP * 2 * sh.pc, REST)).astype(BF16)
    for n in ("a0", "a1"):
        gather_start(n, 0)
    for n in feed_names:
        gather_done(n)
        gather_start(n, 1)
    for n in first_names:
        gather_done(n)
        gather_start(n, 1)
    for n in first_names:
        gather_pass(n)
    for n in feed_names:
        gather_done(n)
        gather_start(n, 2)

    for i in range(TP):
        from_device(b.x.at[pl.ds(pl.multiple_of(OWN * core + TOKENS * i, 16), TOKENS)], 0, i)
    half = b.x.at[pl.ds(pl.multiple_of(OWN * core, 16), TP * TOKENS)]
    x_swap = remote(half, half, sibling)
    for first in (256, OWN + 256):
        b.x[first : first + 16] = jnp.zeros((16, D), BF16)
    turn_local.wait()
    arrived([x_swap])

    @pl.loop(0, 2)
    def _(i):
        rows = pl.ds(pl.multiple_of(OWN * i, 16), OWN)
        b.xp[rows] = dot(b.x[rows], b.turn[...], NT).astype(BF16)

    for n in first_names:
        gather_done(n)
    wo_cols = slice(WO, WO + HALF)
    wo_local = local(b.wa.at[:, :, :, wo_cols], b.wo.at[core])
    wo_swap = remote(b.wa.at[:, :, :, wo_cols], b.wo.at[core], sibling)
    gather_pass("f1")
    send_upstream()

    def attention_weight():
        return b.wa[:, :, :, :WO].reshape(D, WO)

    small = b.wa[:, :, :, 4 * HALF :].reshape(D, SMALL)
    chosen = dot(smallsel[...], small, NT)
    b.par[...] = chosen[0:8]
    memory = chosen[16:48].astype(BF16)
    b.x[OWN + 256 : OWN + 272] = memory[16:]
    turned = dot(memory, b.turn[...], NT).astype(BF16)
    b.xp[OWN + 256 : OWN + 272] = turned[16:]

    @pl.when(seg == 0)
    def _():
        b.x[256:272] = memory[:16]
        b.xp[256:272] = turned[:16]

    gains = [b.par[i : i + 1] for i in range(2)]
    biases = [b.par[2 + i : 3 + i] for i in range(2)]

    hop_to = jnp.where(x == 0, 1, 2)
    hops = []
    for j in range(2):
        hops.append(
            pltpu.make_async_remote_copy(
                src_ref=b.hop,
                dst_ref=b.hopin,
                send_sem=xsem.at[XBASE[6] + j],
                recv_sem=xsem.at[XBASE[6] + 2],
                device_id=device(x_=hop_to, c_=j),
                device_id_type=MESH,
            )
        )

    own_rows = pl.ds(pl.multiple_of(OWN * core, 16), OWN)
    other_rows = pl.ds(pl.multiple_of(OWN * other, 16), OWN)

    out = dot(b.xp[...], b.wx[...].reshape(D, HALF)).astype(BF16)
    for i in range(3):
        b.qkv[i] = out[:, 128 * i : 128 * i + 128]
    out = dot(b.x[...], b.wa[:, :, :, HALF:WO].reshape(D, 2 * HALF)).astype(BF16)
    for i in range(3, 9):
        b.qkv[i] = out[:, 128 * (i - 3) : 128 * (i - 2)]

    def head_masks(hh):
        lane = lax.broadcasted_iota(jnp.int32, (ROWS, 128), 1)
        row = lax.broadcasted_iota(jnp.int32, (ROWS, 128), 0)
        inside = (lane // 64) == hh
        spare = lane == 64 * (1 - hh)
        memory = ((row >= 256) & (row < 272)) | (row >= OWN + 256)
        invalid = memory & (row % 8 >= 5)
        return inside, spare, invalid

    def forward_pair(p):
        qp, kp, vp = (b.qkv[3 * p + i] for i in range(3))
        vt = vp.T
        for hh in range(2):
            inside, spare, invalid = head_masks(hh)
            zero = jnp.zeros_like(kp)
            kmask = jnp.where(spare & invalid, jnp.full_like(kp, MASKED), zero)
            km = jnp.where(inside, kp, kmask)
            qm = jnp.where(inside, qp, jnp.where(spare, jnp.ones_like(qp), zero))
            scores = dot(km, qm, NT)
            peak = jnp.max(scores, 0, keepdims=True)
            raised = jnp.exp2((scores - peak) * EXP_SCALE)
            total = jnp.sum(raised, 0, keepdims=True)
            probs = (raised * (1.0 / total)).astype(BF16)
            b.pt[2 * p + hh] = probs
            b.ot[p, 64 * hh : 64 * hh + 64] = dot(vt[64 * hh : 64 * hh + 64], probs).astype(BF16)
        b.oc[:, pl.ds(pl.multiple_of(128 * p, 128), 128)] = b.ot[p].T

    @pl.loop(0, 3)
    def _(j):
        cols = pl.ds(pl.multiple_of(128 * j, 128), 128)
        block = dot(b.turn[...], b.wx[:, :, :, cols].reshape(D, 128), TN).astype(BF16)
        b.wa[:, :, :, cols] = block.reshape(nz, ny, br, 128)

    @pl.loop(0, 2)
    def _(i):
        @pl.when((i == 1) & (seg == 1))
        def _():
            hops[0].wait_recv()
            b.x[256:272] = b.hopin[...]
            rows = dot(b.hopin[...], attention_weight()).astype(BF16)
            for j in range(9):
                b.qkv[j, 256:272] = rows[:, 128 * j : 128 * j + 128]

        @pl.when(i == seg)
        def _():
            for p in range(3):
                forward_pair(p)

        @pl.when(i == 0)
        def _():
            for n in ("f2", "f0"):
                gather_pass(n)

    def head_rows(ref, c):
        if nz > 1:
            return ref.at[pl.ds(c * (nz // 2), nz // 2)]
        return ref.at[:, :, pl.ds(pl.multiple_of(c * HALF, 16), HALF)]

    def wo_rows(h, c):
        return head_rows(b.wo.at[h], c)[...].reshape(HALF, HALF)

    o_swap = remote(b.oc.at[other_rows], b.oin, sibling)
    wo_local.wait()
    arrived([wo_swap])
    halves = [dot(b.oc[own_rows], wo_rows(h, core)) for h in range(2)]
    arrived([o_swap])
    attended = jnp.concatenate([halves[h] + dot(b.oin[...], wo_rows(h, other)) for h in range(2)], 1)
    h1, n1, inv1 = norm_forward(b.x[own_rows].astype(F32) + attended, gains[0], biases[0])
    b.h1[...] = h1
    b.n1[...] = n1
    b.inv1[...] = inv1
    b.h1b[own_rows] = h1.astype(BF16)
    h_swap = remote(b.h1b.at[own_rows], b.h1b.at[own_rows], sibling)

    @pl.when(seg == 1)
    def _():
        b.xp[256:272] = dot(b.hopin[...], b.turn[...], NT).astype(BF16)

    for n in ("f1", "f2", "f0"):
        gather_done(n)

    def feed_weight(t, kind):
        cols = [256 * j + 128 * kind for j in range(3)]
        blocks = [b.wf[2 * t + i, :, :, :, c : c + 128].reshape(D, 128) for i in range(2) for c in cols]
        return jnp.concatenate(blocks, 1)

    def up_weight(t):
        return feed_weight(t, 0)

    def down_weight(t):
        return feed_weight(t, 1)

    def gelu_share(units):
        return 0.5 * (1.0 + lax.erf(units * INV_ROOT_TWO))

    early = pltpu.make_async_remote_copy(
        src_ref=b.es,
        dst_ref=b.er,
        send_sem=xsem.at[XBASE[6] + 3],
        recv_sem=xsem.at[XBASE[6] + 4],
        device_id=sibling,
        device_id_type=MESH,
    )
    row16 = lax.broadcasted_iota(jnp.int32, (16, D), 0)

    @pl.when(seg == 0)
    def _():
        arrived([h_swap])
        rows = b.h1b[OWN + 256 : OWN + 272]
        units = [dot(rows, up_weight(t)) for t in range(2)]
        part = sum(dot((units[t] * gelu_share(units[t])).astype(BF16), down_weight(t), NT) for t in range(2))

        @pl.when(core == 0)
        def _():
            b.es[...] = part
            early.start()

        @pl.when(core == 1)
        def _():
            early.wait_recv()
            whole = b.h1[256:272] + part + b.er[...]
            written = norm_forward(whole, gains[1], biases[1])[0]
            b.hop[...] = jnp.where(row16 % 8 < 5, written, 0.0).astype(BF16)
            hops[0].start()
            hops[1].start()

    def project_up(rows):
        for t in range(2):
            units = dot(b.h1b[rows], up_weight(t))
            b.ul[t, rows] = units
            b.gl[t, rows] = (units * gelu_share(units)).astype(BF16)

    @pl.loop(0, 2)
    def _(i):
        @pl.when((i == 1) & (seg == 1))
        def _():
            arrived([h_swap])

        project_up(pl.ds(pl.multiple_of(OWN * jnp.where(i == 0, core, other), 16), OWN))


    def partial_down(rows):
        return sum(dot(b.gl[t, rows], down_weight(t), NT) for t in range(2))

    b.fs[...] = partial_down(other_rows).astype(BF16)
    f_swap = remote(b.fs, b.fr, sibling)
    branch = partial_down(own_rows)
    arrived([f_swap])
    out, n2, inv2 = norm_forward(b.h1[...] + branch + b.fr[...].astype(F32), gains[1], biases[1])
    low = out.astype(BF16)
    b.yb[...] = low
    b.mo[...] = low[256:272].astype(F32).reshape(2, 8, D)
    for i in range(TP):
        to_device(
            b.yb.at[pl.ds(TOKENS * i, TOKENS)],
            hout.at[seg, pl.ds(pl.multiple_of(TOKENS * core, 16), TOKENS)],
            (i, chain),
            xsem.at[XBASE[3] + 2 * seg + core],
            3,
            i,
        )
    for i in range(2):
        to_device(b.mo.at[i], mout.at[seg], (2 * core + i, chain), xsem.at[XBASE[4] + seg], 4, i)

    for i in range(TP):
        from_device(b.gyt.at[pl.ds(TOKENS * i, TOKENS)], 1, i)
    for i in range(2):
        from_device(b.gm.at[i], 2, i)
    upstream = jnp.concatenate([b.gyt[...].astype(F32), b.gm[...].reshape(16, D)], 0)
    b.sg[...] = jnp.zeros((48, D), F32)
    b.sg[1:2] = column_sum(upstream * n2)
    b.sg[3:4] = column_sum(upstream)
    dz = norm_backward(upstream, n2, inv2, gains[1])
    b.dz[...] = dz
    b.dfb[own_rows] = dz.astype(BF16)
    df_swap = remote(b.dfb.at[own_rows], b.dfb.at[own_rows], sibling)

    def weight_grad(into, left, right, jobs_):
        @pl.loop(0, 2)
        def _(t):
            part = dot(left[...], right[t], TN).astype(BF16)
            for i in range(2):
                into[2 * t + i] = part[:, HALF * i : HALF * (i + 1)].reshape(nz, ny, br, HALF)

            for h in range(2):

                @pl.when(t == h)
                def _():
                    for n in jobs_:
                        if is_ring(n, 0) and scatters[n][1][0] != "x":
                            ring_send(n, h)
                        elif h == 1:
                            scatter_send(n, 0)

    scatters = {j[0]: j for j in scatter_jobs()}
    rs = {}

    def is_ring(name, step):
        _, order, cols, axes = scatters[name]
        return step == 0 and name in RINGS and size[order[0]] == 4

    def source_of(name, step):
        _, order, cols, axes = scatters[name]
        axis = order[step]
        left = [a for a in axes if a not in order[:step]]
        array = getattr(b, GRADS[name[0]]) if step == 0 else k[SUMMED, step - 1, name]
        tail = (slice(None), cols) if step == 0 else ()

        def part(place, half=None):
            where = []
            for a in left:
                if a == axis:
                    where.append(place)
                elif half is not None:
                    where.append(pl.ds(half * (size[a] // 2), size[a] // 2))
                    half = None
                else:
                    where.append(slice(None))
            return array.at[tuple(where) + tail]

        return part

    def ring_send(name, half):
        axis = scatters[name][1][0]
        n = size[axis]
        part = source_of(name, 0)
        landing, over = k[LANDED, 0, name], k[PASSED, 0, name]
        right, left, far = (near[axis][o] for o in (1, n - 1, 2))
        to = moved(axis, 1), moved(axis, n - 1)
        cut = size[[a for a in scatters[name][3] if a != axis][0]] // 2
        if name not in rs:
            rs[name] = ([None, None], Group(lambda: landing), cut, (right, left), to)
        rs[name][0][half] = remote(part(far, half), lambda: over.at[half], to[half])
        if half == 0:
            rs[name][1].add(part(left, 0), landing.at[1, :cut], to[1])
        else:
            rs[name][1].add(part(right, 1), landing.at[0, cut:], to[0])

    def scatter_send(name, step):
        axis = scatters[name][1][step]
        n = size[axis]
        part = source_of(name, step)
        landing = k[LANDED, step, name]
        if is_ring(name, step):
            ring_send(name, 0)
            ring_send(name, 1)
            return
        rs[name] = [Group(lambda: landing)] if n > 1 else []
        for o in range(1, n):
            rs[name][0].add(part(near[axis][o]), landing.at[o - 1], moved(axis, o))

    def scatter_pass(name):
        if not is_ring(name, 0):
            return
        passing, coming, half, places_, devices = rs[name]
        part = source_of(name, 0)
        landing, over, updated = k[LANDED, 0, name], k[PASSED, 0, name], k[UPDATED, 0, name]
        for i in range(2):
            arrived([passing[i]])
            updated[i] = (part(places_[i], i)[...].astype(F32) + over[i].astype(F32)).astype(BF16)
            where = landing.at[0, :half] if i == 0 else landing.at[1, half:]
            coming.add(updated.at[i], where, devices[i])

    def scatter_sum(name, step):
        _, order, cols, axes = scatters[name]
        axis = order[step]
        total = source_of(name, step)(at[axis])[...].astype(F32)
        ring = is_ring(name, step)
        arrived([rs[name][1]] if ring else rs[name])
        for o in range(2 if ring else size[axis] - 1):
            total = total + k[LANDED, step, name][o].astype(F32)
        if step < len(order) - 1:
            k[SUMMED, step, name][...] = total.astype(BF16)
        return total

    def scatter_on(names, step):
        for n in names:
            scatter_sum(n, step)
            scatter_send(n, step + 1)

    down_names, up_names = ("t0", "t1", "t2"), ("i0", "i1", "i2")
    arrived([df_swap])
    weight_grad(b.gt, b.dfb, b.gl, down_names)
    @pl.loop(0, 2)
    def _(i):
        rows = pl.ds(pl.multiple_of(OWN * i, 16), OWN)
        for t in range(2):
            units = b.ul[t, rows]
            slope = gelu_share(units) + units * jnp.exp(-0.5 * units * units) * INV_ROOT_TWOPI
            b.du[t, rows] = (dot(b.dfb[rows], down_weight(t)) * slope).astype(BF16)


    def partial_up(rows):
        return sum(dot(b.du[t, rows], up_weight(t), NT) for t in range(2))

    dh_swap = Group(lambda: b.dhr)

    @pl.loop(0, 2)
    def _(i):
        part = partial_up(pl.ds(pl.multiple_of(OWN * jnp.where(i == 0, other, core), 16), OWN))

        @pl.when(i == 0)
        def _():
            b.dhs[...] = part.astype(BF16)
            dh_swap.add(b.dhs, b.dhr, sibling)

        @pl.when(i == 1)
        def _():
            b.dz[...] = b.dz[...] + part

    arrived([dh_swap])
    into_first = b.dz[...] + b.dhr[...].astype(F32)
    b.sg[0:1] = column_sum(into_first * b.n1[...])
    b.sg[2:3] = column_sum(into_first)
    dr = norm_backward(into_first, b.n1[...], b.inv1[...], gains[0])
    b.dr[...] = dr
    b.dab[own_rows] = dr.astype(BF16)
    da_swap = remote(b.dab.at[own_rows], b.dab.at[own_rows], sibling)

    def grad_mixed(rows):
        parts = [dot(b.dab[rows, HALF * h : HALF * (h + 1)], wo_rows(h, core), NT) for h in range(2)]
        for p in range(3):
            b.doc[p, rows] = (parts[0] + parts[1])[:, 128 * p : 128 * p + 128].astype(BF16)

    weight_grad(b.gi, b.h1b, b.du, up_names)
    for n in down_names:
        scatter_pass(n)
    arrived([da_swap])
    grad_mixed(slice(None))

    mixed_t = b.ot[...].reshape(HALF, ROWS)

    def proj_grad(h):
        cols = pl.ds(pl.multiple_of(HALF * h, 128), HALF)
        return dot(mixed_t, b.dab[:, cols]).astype(BF16).reshape(b.gos.shape)

    def wo_part(c):
        return head_rows(b.ga.at[:, :, :, wo_cols], c)

    b.gos[...] = proj_grad(other)
    go_swap = remote(b.gos, wo_part(core), sibling)
    wo_part(core)[...] = proj_grad(core)

    def backward_pair(p):
        qp, kp, vp = (b.qkv[3 * p + i] for i in range(3))
        dop = b.doc[p]
        kt = kp.T
        dv = dk = 0.0
        dq = []
        for hh in range(2):
            inside, _, _ = head_masks(hh)
            zero = jnp.zeros_like(kp)
            grad_probs = dot(jnp.where(inside, vp, zero), dop, NT)
            low_probs = b.pt[2 * p + hh]
            probs = low_probs.astype(F32)
            row_term = jnp.sum(probs * grad_probs, 0, keepdims=True)
            ds = (probs * (grad_probs - row_term)).astype(BF16)
            dv = dv + dot(low_probs, jnp.where(inside, dop, zero))
            dk = dk + dot(ds, jnp.where(inside, qp, zero))
            dq.append(dot(kt[64 * hh : 64 * hh + 64], ds))
        b.dqkv[3 * p] = (jnp.concatenate(dq, 0) * 0.125).T.astype(BF16)
        b.dqkv[3 * p + 1] = (dk * 0.125).astype(BF16)
        b.dqkv[3 * p + 2] = dv.astype(BF16)

    def joined(rows, wanted):
        return jnp.concatenate([b.dqkv[i, rows] for i in wanted], 1)

    def attention_grad(p):
        grads = jnp.concatenate([b.dqkv[3 * p + i] for i in range(3)], 1)

        part = dot(b.both[jnp.minimum(p, 1)], grads, TN).astype(BF16)

        @pl.when(p == 0)
        def _():
            b.gx[...] = part.reshape(TP, nz, sh.xrows, HALF)

        @pl.when(p > 0)
        def _():
            cols = pl.ds(pl.multiple_of(HALF * p, 128), HALF)
            b.ga[:, :, :, cols] = part.reshape(nz, ny, br, HALF)

    @pl.loop(0, 3)
    def _(p):
        backward_pair(p)
        attention_grad(p)

        @pl.when(p == 0)
        def _():
            arrived([go_swap])
            scatter_send("aw", 0)
            scatter_send("x0", 0)

        @pl.when(p == 1)
        def _():
            scatter_send("a1", 0)
            for n in up_names:
                scatter_pass(n)

        @pl.when(p == 2)
        def _():
            scatter_send("a2", 0)
            scatter_send("a3", 0)
            for n in ("aw", "x0"):
                scatter_pass(n)
            scatter_on(down_names, 0)


    def partial_input(rows):
        return dot(joined(rows, range(9)), attention_weight(), NT)

    memory_rows = [pl.ds(pl.multiple_of(OWN * c + 256, 16), 16) for c in (other, core)]
    part = dot(jnp.concatenate([joined(rows, range(9)) for rows in memory_rows], 0), attention_weight(), NT)
    b.ms[...] = part[:16]
    memory_swap = remote(b.ms, b.mr, sibling)
    b.dxs[...] = partial_input(other_rows).astype(BF16)
    dx_swap = remote(b.dxs, b.dxr, sibling)
    arrived([memory_swap])
    memory_grad = part[16:] + b.dr[256:272] + b.mr[...]

    @pl.when((core == 0) & (seg == 0))
    def _():
        b.sg[16:32] = memory_grad

    @pl.when(core == 1)
    def _():
        b.sg[32:48] = memory_grad

    small_grads = dot(b.sg[...].astype(BF16), smallsel[...], TN).astype(BF16)
    b.ga[:, :, :, 4 * HALF :] = small_grads.reshape(nz, ny, br, SMALL)
    scatter_send("as", 0)
    scatter_pass("a1")
    dx = partial_input(own_rows) + b.dr[...]
    scatter_on(up_names, 0)
    arrived([dx_swap])
    dx = dx + b.dxr[...].astype(F32)
    b.dxb[...] = dx[:256].astype(BF16)
    for i in range(TP):
        to_device(
            b.dxb.at[pl.ds(TOKENS * i, TOKENS)],
            dxo.at[seg, pl.ds(pl.multiple_of(TOKENS * core, 16), TOKENS)],
            (i, chain),
            xsem.at[XBASE[5] + 2 * seg + core],
            5,
            i,
        )
    scatter_on(("aw", "x0", "a1"), 0)
    scatter_on(down_names, 1)

    def plane_send(axis, wanted, spread_, landed):
        n = size[axis]
        for name in wanted:
            scatter_sum(name, 0)
        rows = jnp.concatenate([k[SUMMED, 0, name][i] for i in range(n) for name in wanted], 1)
        part = dot(packsel[...], rows, TN).astype(BF16)
        for i in range(n):
            spread_[i] = part[:, 256 * i : 256 * (i + 1)].reshape(TP, 2 * sh.pc, 256)
        group = Group(lambda: landed)
        for o in range(n):
            for o2 in range(TP):
                if o + o2 > 0:
                    source = spread_.at[near[axis][o], near["x"][o2]]
                    group.add(source, landed.at[o * TP + o2 - 1], plane_device(axis, o, o2))
        return group

    def plane_total(axis, spread_, landed, group):
        arrived([group])
        total = spread_[at[axis], x].astype(F32)
        for i in range(size[axis] * TP - 1):
            total = total + landed[i].astype(F32)
        return total.reshape(2, sh.pc, 256)

    plane_z = plane_send("z", ("a2",), b.ez, b.rz)
    plane_y = plane_send("y", ("a3", "as"), b.ey, b.ry)
    spread = dot(packy[...], scatter_sum("x0", 1).astype(BF16), TN).astype(BF16)
    b.e3y[...] = spread.reshape(ny, 2 * sh.pc, HALF)
    ysteps = [Group(lambda: b.r3y)] if ny > 1 else []
    for o in range(1, ny):
        ysteps[0].add(b.e3y.at[near["y"][o]], b.r3y.at[o - 1], moved("y", o))
    for i, n in enumerate(("a1", "aw")):
        b.tot[:, HALF * i : HALF * (i + 1)] = scatter_sum(n, 1).astype(BF16)
    spread = dot(packsel[...], b.tot[...], TN).astype(BF16)
    b.e3[...] = spread.reshape(TP, 2 * sh.pc, 2 * HALF)
    steps = [Group(lambda: b.r3)]
    for o in range(1, TP):
        steps[0].add(b.e3.at[near["x"][o]], b.r3.at[o - 1], moved("x", o))
    scatter_on(up_names, 1)

    def last_rows(wanted, first_col):
        for j, n in enumerate(wanted):
            total = scatter_sum(n, 2)
            cols = slice(first_col + 128 * j, first_col + 128 * j + 128)
            b.sf[0, :, cols] = total[:wr]
            b.sf[1, :, cols] = total[wr:]

    last_rows(down_names, HALF)
    last_rows(up_names, 0)
    sf_local = local(b.sf.at[core], gfo.at[core])
    sf_swap = remote(b.sf.at[other], gfo.at[core], sibling)

    arrived(steps)
    total = b.e3[x].astype(F32)
    for o in range(1, TP):
        total = total + b.r3[o - 1].astype(F32)
    total = total.reshape(2, sh.pc, 2 * HALF)
    b.s4[:, :, HALF : 2 * HALF] = total[:, :, :HALF]
    b.s4[:, :, WO : WO + HALF] = total[:, :, HALF:]
    arrived(ysteps)
    total = b.e3y[y].astype(F32)
    for o in range(1, ny):
        total = total + b.r3y[o - 1].astype(F32)
    b.s4[:, :, :HALF] = total.reshape(2, sh.pc, HALF)
    b.s4[:, :, 2 * HALF : 2 * HALF + 256] = plane_total("z", b.ez, b.rz, plane_z)
    total = plane_total("y", b.ey, b.ry, plane_y)
    b.s4[:, :, 2 * HALF + 256 : 3 * HALF] = total[:, :, :128]
    b.s4[:, :, 4 * HALF :] = total[:, :, 128:]
    s4_local = local(b.s4.at[core], gao.at[core])
    s4_swap = remote(b.s4.at[other], gao.at[core], sibling)

    for kind, out_ref in ((3, hout), (5, dxo)):
        for s in range(2):
            for j in range(2):
                from_device(out_ref.at[s, pl.ds(TOKENS * j, TOKENS)], kind, 2 * s + j)
    for s in range(2):
        from_device(mout.at[s], 4, s)
    sf_local.wait()
    s4_local.wait()
    arrived([sf_swap, s4_swap])

    for group in sent[-SENDS:]:
        group.wait_send()
    for same, copy in conditional:

        @pl.when(jnp.logical_not(same))
        def _():
            copy.wait_send()

    @pl.when((seg == 0) & (core == 1))
    def _():
        hops[0].wait_send()
        hops[1].wait_send()

    @pl.when((seg == 0) & (core == 0))
    def _():
        early.wait_send()


def layer(sh, arrays):
    constants = [jnp.asarray(a, BF16) for a in selections(sh)]
    tables = scratch_of(sh)
    names = [list(table) for table in tables]
    anywhere = pl.BlockSpec(memory_space=pl.ANY)
    outs = [
        jax.ShapeDtypeStruct((2, 128, D), BF16),
        jax.ShapeDtypeStruct((2, 8, D), F32),
        jax.ShapeDtypeStruct((2, 128, D), BF16),
        jax.ShapeDtypeStruct((2, sh.pc, ACOLS), F32),
        jax.ShapeDtypeStruct((2, sh.wrows, D), F32),
    ]
    return pl.pallas_call(
        functools.partial(kernel, sh, names),
        name="layer",
        out_shape=outs,
        in_specs=[anywhere] * 15,
        out_specs=[anywhere] * len(outs),
        scratch_shapes=[pltpu.VMEM(*one) for table in tables for one in table.values()]
        + [
            pltpu.SemaphoreType.DMA((SENDS,)),
            pltpu.SemaphoreType.DMA((96,)),
            pltpu.SemaphoreType.DMA((45,)),
            pltpu.SemaphoreType.DMA((20,)),
        ],
        compiler_params=pltpu.CompilerParams(
            collective_id=0, has_side_effects=True, vmem_limit_bytes=64 * 2**20 - 2**17
        ),
    )(*arrays, *constants)


def unpack_kernel(sh, *refs):
    arrays, results, held, outs, sems = refs[:5], refs[5:15], refs[15:20], refs[20:30], refs[30]
    loads = [pltpu.make_async_copy(arrays[i], held[i], sems.at[i]) for i in range(5)]
    stores = [pltpu.make_async_copy(outs[i], results[i], sems.at[5 + i]) for i in range(10)]
    for copy in loads:
        copy.start()
    hout, mout, dxo, gao, gfo = held
    hidden, memory, grad_in, gq, gp, gains, biases, tokens, gi, gt = outs
    ar = sh.arows
    loads[0].wait()
    hidden[...] = hout[...]
    stores[0].start()
    loads[2].wait()
    grad_in[...] = dxo[...].astype(F32)
    stores[2].start()
    loads[1].wait()
    for i in range(2):
        memory[:, i] = mout[i, :5].astype(BF16)
    stores[1].start()
    loads[3].wait()
    for h in range(2):
        for p in range(3):
            for i in range(3):
                to = D * i + HALF * h + 128 * p
                first = HALF * p + 128 * i
                gq[:, to : to + 128] = gao[h, :ar, first : first + 128]
        gp[:, HALF * h : HALF * (h + 1)] = gao[h, :ar, WO : WO + HALF]
    small = gao[0, :, 4 * HALF :] + gao[1, :, 4 * HALF :]
    turned = small.T[:, :ar]
    gains[...] = turned[0:2]
    biases[...] = turned[2:4]
    for kind in range(2):
        tokens[:, kind] = small[:ar, 4 + MEM * kind : 4 + MEM * (kind + 1)]
    for i in range(3, 8):
        stores[i].start()
    loads[4].wait()
    for h in range(2):
        gi[:, HALF * h : HALF * (h + 1)] = gfo[h, :, :HALF]
        gt[:, HALF * h : HALF * (h + 1)] = gfo[h, :, HALF:]
    for i in range(8, 10):
        stores[i].start()
    for copy in stores:
        copy.wait()


def unpack(sh, *arrays):
    ar, wr = sh.arows, sh.wrows
    shapes = [
        ((2, 128, D), BF16),
        ((5, 2, D), BF16),
        ((2, 128, D), F32),
        ((ar, 3 * D), F32),
        ((ar, D), F32),
        ((2, ar), F32),
        ((2, ar), F32),
        ((ar, 2, MEM), F32),
        ((wr, D), F32),
        ((wr, D), F32),
    ]
    anywhere = pl.BlockSpec(memory_space=pl.ANY)
    return pl.pallas_call(
        functools.partial(unpack_kernel, sh),
        name="unpack",
        out_shape=[jax.ShapeDtypeStruct(*one) for one in shapes],
        in_specs=[anywhere] * 5,
        out_specs=[anywhere] * len(shapes),
        scratch_shapes=[pltpu.VMEM(a.shape, a.dtype) for a in arrays]
        + [pltpu.VMEM(*one) for one in shapes]
        + [pltpu.SemaphoreType.DMA((15,))],
        compiler_params=pltpu.CompilerParams(vmem_limit_bytes=64 * 2**20 - 2**17),
    )(*arrays)


def body(
    sh,
    hidden_in,
    reset,
    w_qkv,
    w_attn_out,
    norm_gains,
    norm_biases,
    memory_tokens,
    w_in,
    w_out,
    grad_hidden,
    grad_memory,
):
    arrays = (
        hidden_in,
        grad_hidden,
        grad_memory.transpose(1, 0, 2),
        w_qkv,
        w_attn_out,
        norm_gains,
        norm_biases,
        memory_tokens.transpose(2, 0, 1),
        w_in,
        w_out.T,
    )
    hidden, memory, *middle, tokens, gi, gt = unpack(sh, *layer(sh, arrays))
    return hidden, memory.transpose(1, 0, 2), *middle, tokens.transpose(1, 2, 0), gi, gt.T


def solution(mesh):
    sh = Shape(mesh.shape["dp"])
    return jax.shard_map(
        functools.partial(body, sh),
        mesh=mesh,
        in_specs=(
            P("dp", "tp", None),
            P("dp"),
            P(("dp", "tp"), None),
            P(("dp", "tp"), None),
            P(None, ("dp", "tp")),
            P(None, ("dp", "tp")),
            P(None, None, ("dp", "tp")),
            P("dp", "tp"),
            P("tp", "dp"),
            P("dp", "tp", None),
            P("dp", "tp", None),
        ),
        out_specs=(
            P("dp", "tp", None),
            P("dp", "tp", None),
            P("dp", "tp", None),
            P(("dp", "tp"), None),
            P(("dp", "tp"), None),
            P(None, ("dp", "tp")),
            P(None, ("dp", "tp")),
            P(None, None, ("dp", "tp")),
            P("dp", "tp"),
            P("tp", "dp"),
        ),
        check_vma=False,
    )
```

```python
import functools
import types

import jax
import jax.numpy as jnp
import numpy as np
from jax import lax
from jax.experimental import pallas as pl
from jax.experimental.pallas import tpu as pltpu
from jax.sharding import PartitionSpec as P

D = 768
HALF = 384
MEM = 10
TOKENS = 64
OWN = 272
ROWS = 2 * OWN
TP = 4
SMALL = 128
ACOLS = 4 * HALF + SMALL
REST = ACOLS - HALF
CUT = HALF + 640
WO = 3 * HALF
EPSILON = 1e-05
INV_ROOT_TWO = 0.7071067811865476
INV_ROOT_TWOPI = 0.3989422804014327
EXP_SCALE = 0.125 * 1.4426950408889634
MASKED = -1e30
F32 = jnp.float32
BF16 = jnp.bfloat16
MESH = pl.DeviceIdType.MESH
NN = (((1,), (0,)), ((), ()))
NT = (((1,), (1,)), ((), ()))
TN = (((0,), (0,)), ((), ()))


def dot(a, b, dims=NN):
    return lax.dot_general(a, b, dims, preferred_element_type=F32)


def up16(n):
    return -(-n // 16) * 16


class Shape:
    def __init__(self, dp):
        self.dp = dp
        planes = dp // 2
        self.ny = int(round(planes**0.5))
        self.nz = planes // self.ny
        self.wrows = D // dp
        self.arows = D // (dp * TP)
        self.brows = 2 * self.wrows
        self.pr = up16(self.arows)
        self.xrows = 2 * self.arows * self.ny
        self.pc = -(-self.arows // 8) * 8
        self.fr = up16(self.wrows)


def selections(sh):
    pack = np.zeros((sh.brows, TP * 2 * sh.pc), np.float32)
    for c in range(2):
        for x in range(TP):
            for i in range(sh.arows):
                pack[c * sh.wrows + x * sh.arows + i, (x * 2 + c) * sh.pc + i] = 1
    packy = np.zeros((sh.xrows, sh.ny * 2 * sh.pc), np.float32)
    turn = np.zeros((D, D), np.float32)
    ar = sh.arows
    for c in range(2):
        for y in range(sh.ny):
            for i in range(ar):
                row = (y * 2 + c) * ar + i
                packy[row, (y * 2 + c) * sh.pc + i] = 1
                for x in range(TP):
                    for z in range(sh.nz):
                        place = (z * sh.ny + y) * sh.brows + (c * TP + x) * ar + i
                        turn[(x * sh.nz + z) * sh.xrows + row, place] = 1
    small = np.zeros((48, SMALL), np.float32)
    for i in range(4):
        small[i, i] = 1
    for kind in range(2):
        for i in range(MEM):
            small[16 + 16 * kind + (i // 5) * 8 + i % 5, 4 + MEM * kind + i] = 1
    places = np.zeros((4, MEM, SMALL), np.float32)
    for kind, (rows, first) in enumerate(((2, 0), (2, 2), (MEM, 4), (MEM, 4 + MEM))):
        for i in range(rows):
            places[kind, i, first + i] = 1
    return pack, small, places, packy, turn


def norm_forward(inputs, gain, offset):
    centred = inputs - jnp.mean(inputs, -1, keepdims=True)
    spread = jnp.mean(centred * centred, -1, keepdims=True)
    inverse = lax.rsqrt(spread + EPSILON)
    normed = centred * inverse
    return normed * gain + offset, normed, inverse


def norm_backward(upstream, normed, inverse, gain):
    scaled = upstream * gain
    first_mean = jnp.mean(scaled, -1, keepdims=True)
    second_mean = jnp.mean(scaled * normed, -1, keepdims=True)
    return inverse * (scaled - first_mean - normed * second_mean)


def column_sum(a):
    return jnp.sum(a, 0, keepdims=True)


XBASE = (0, 4, 8, 10, 14, 16, 20)
SENDS = 40
STAGED, LANDED, SUMMED, PASSED, UPDATED = range(5)


def scratch_of(sh):
    nz, ny, br = sh.nz, sh.ny, sh.brows
    ar, wr = sh.arows, sh.wrows
    operands = [
        (5, 2, D),
        (ar, 3 * D),
        (ar, D),
        (2, ar),
        (2, ar),
        (ar, 2, MEM),
        (wr, D),
        (wr, D),
        (br, TP * 2 * sh.pc),
        (48, SMALL),
        (4, MEM, SMALL),
        (sh.xrows, ny * 2 * sh.pc),
    ]
    jobs = {(STAGED, i, 0): (dims, BF16) for i, dims in enumerate(operands)}
    s = dict(
        pk=((2, sh.pr, ACOLS), BF16),
        ff=((2, sh.fr, D), BF16),
        gms=((2, 8, D), F32),
        p1=((2, sh.pr, ACOLS), BF16),
        p2=((TP, 2 * sh.pc, REST), BF16),
        p2y=((ny, 2 * sh.pc, HALF), BF16),
        turn=((D, D), BF16),
        wx=((TP, nz, sh.xrows, HALF), BF16),
        gx=((TP, nz, sh.xrows, HALF), BF16),
        f1=((2, sh.fr, D), BF16),
        wa=((nz, ny, br, ACOLS), BF16),
        wf=((TP, nz, ny, br, D), BF16),
        wo=((2, nz, ny, br, HALF), BF16),
        par=((8, D), F32),
        both=((2, ROWS, D), BF16),
        gyt=((TP * TOKENS, D), BF16),
        gm=((2, 8, D), F32),
        qkv=((9, ROWS, 128), BF16),
        pt=((6, ROWS, ROWS), BF16),
        ot=((3, 128, ROWS), BF16),
        oc=((ROWS, HALF), BF16),
        oin=((OWN, HALF), BF16),
        h1=((OWN, D), F32),
        n1=((OWN, D), F32),
        inv1=((OWN, 1), F32),
        h1b=((ROWS, D), BF16),
        gl=((2, ROWS, D), BF16),
        ul=((2, ROWS, D), F32),
        fs=((OWN, D), BF16),
        fr=((OWN, D), BF16),
        n2=((OWN, D), F32),
        yb=((OWN, D), BF16),
        mo=((2, 8, D), F32),
        hop=((16, D), BF16),
        hopin=((16, D), BF16),
        es=((16, D), F32),
        er=((16, D), F32),
        dz=((OWN, D), F32),
        dfb=((ROWS, D), BF16),
        du=((2, ROWS, D), BF16),
        dhs=((OWN, D), BF16),
        dhr=((OWN, D), BF16),
        dr=((OWN, D), F32),
        dab=((ROWS, D), BF16),
        doc=((3, ROWS, 128), BF16),
        dqkv=((9, ROWS, 128), BF16),
        ga=((nz, ny, br, ACOLS), BF16),
        gi=((TP, nz, ny, br, HALF), BF16),
        gt=((TP, nz, ny, br, HALF), BF16),
        dxs=((OWN, D), BF16),
        dxr=((OWN, D), BF16),
        dxb=((TP * TOKENS, D), BF16),
        sg=((48, D), F32),
        ms=((16, D), F32),
        mr=((16, D), F32),
        tot=((br, REST), BF16),
        e3=((TP, 2 * sh.pc, REST), BF16),
        r3=((TP - 1, 2 * sh.pc, REST), BF16),
        e3y=((ny, 2 * sh.pc, HALF), BF16),
        r3y=((max(1, ny - 1), 2 * sh.pc, HALF), BF16),
        s4=((2, sh.pc, ACOLS), F32),
        sf=((2, sh.wrows, D), F32),
    )
    s.update(gos=((nz // 2, ny, br, HALF) if nz > 1 else (1, 1, HALF, HALF), BF16))
    sizes = {"x": TP, "z": nz, "y": ny}
    for name, order, cols, axes in scatter_jobs():
        left = [a for a in axes]
        block = (sh.xrows if name[0] == "x" else br, cols.stop - cols.start)
        for step, axis in enumerate(order):
            left = [a for a in left if a != axis]
            dims = tuple(sizes[a] for a in left)
            ring = step == 0 and name in RINGS and sizes[axis] == 4
            jobs[LANDED, step, name] = ((2 if ring else max(1, sizes[axis] - 1),) + dims + block, BF16)
            if step < len(order) - 1:
                jobs[SUMMED, step, name] = (dims + block, BF16)
            if ring:
                jobs[PASSED, 0, name] = ((2, dims[0] // 2) + dims[1:] + block, BF16)
                jobs[UPDATED, 0, name] = jobs[PASSED, 0, name]
    return s, jobs


def scatter_jobs():
    orders = [("z", "y", "x"), ("x", "z", "y"), ("y", "x", "z")]
    jobs = []
    for kind in ("t", "i"):
        for j in range(3):
            jobs.append((f"{kind}{j}", orders[j], slice(128 * j, 128 * j + 128), ("x", "z", "y")))
    zy, yz = ("z", "y"), ("y", "z")
    jobs.append(("aw", yz, slice(WO, WO + HALF), zy))
    jobs.append(("x0", ("x", "z"), slice(0, HALF), ("x", "z")))
    jobs.append(("a1", zy, slice(HALF, 2 * HALF), zy))
    jobs.append(("a2", yz, slice(2 * HALF, 2 * HALF + 256), zy))
    jobs.append(("a3", zy, slice(2 * HALF + 256, 3 * HALF), zy))
    jobs.append(("as", yz, slice(4 * HALF, ACOLS), zy))
    return jobs


def gather_jobs():
    orders = [("x", "y", "z"), ("y", "z", "x"), ("z", "x", "y")]
    jobs = [(f"f{j}", orders[j], slice(256 * j, 256 * j + 256), ("x", "z", "y")) for j in range(3)]
    jobs.append(("x0", ("z", "x"), slice(0, HALF), ("x", "z")))
    jobs.append(("a0", ("y", "z"), slice(HALF, CUT), ("z", "y")))
    jobs.append(("a1", ("z", "y"), slice(CUT, ACOLS), ("z", "y")))
    return jobs


RINGS = ("t0", "t1", "t2", "i0", "i1", "i2", "aw", "x0", "a1")
WEIGHTS = {"f": "wf", "a": "wa", "x": "wx"}
GRADS = {"t": "gt", "i": "gi", "a": "ga", "x": "gx"}


def kernel(sh, names, *refs):
    xin, gin = refs[:2]
    hout, mout, dxo, gao, gfo = refs[15:20]
    ssem, rsem, xsem, lsem = refs[-4:]
    count = len(names[0])
    b = types.SimpleNamespace(**dict(zip(names[0], refs[20 : 20 + count])))
    b.xp, b.x = b.both.at[0], b.both.at[1]
    k = dict(zip(names[1], refs[20 + count : -4]))
    staged = [k[STAGED, i, 0] for i in range(12)]
    gmem, wq, wp, gain_in, bias_in, token_in, up_in, down_in = staged[:8]
    packsel, smallsel, places, packy = staged[8:]
    turn = refs[14]
    nz, ny, br, wr, ar = sh.nz, sh.ny, sh.brows, sh.wrows, sh.arows
    pk, ff, gms = b.pk, b.ff, b.gms

    dp = lax.axis_index("dp")
    x = lax.axis_index("tp")
    core = dp % 2
    y = (dp // 2) % ny
    z = dp // (2 * ny)
    other = 1 - core
    chain = x // 2
    seg = jnp.where((x == 1) | (x == 2), 1, 0)
    at = {"x": x, "y": y, "z": z}
    size = {"x": TP, "y": ny, "z": nz}

    def device(x_=x, y_=y, z_=z, c_=core):
        return ((z_ * ny + y_) * 2 + c_, x_)

    near = {a: [(at[a] + o) % size[a] for o in range(size[a])] for a in at}

    def moved_to(axis, offset, core_=core):
        there = dict(at)
        there[axis] = near[axis][offset]
        return device(there["x"], there["y"], there["z"], core_)

    neighbours = {a: [moved_to(a, o) for o in range(size[a])] for a in at}

    def moved(axis, offset):
        return neighbours[axis][offset]

    sibling = device(c_=other)
    sent = []

    class Group:
        def __init__(self, like):
            if len(sent) >= SENDS:
                sent[-SENDS].wait_send()
            self.like = like
            self.number = len(sent)
            sent.append(self)

        def add(self, src, dst, to):
            pltpu.make_async_remote_copy(
                src_ref=src,
                dst_ref=dst,
                send_sem=ssem.at[self.number % SENDS],
                recv_sem=rsem.at[self.number],
                device_id=to,
                device_id_type=MESH,
            ).start()

        def wait_send(self):
            like = self.like()
            pltpu.make_async_copy(like, like, ssem.at[self.number % SENDS]).wait()

        def wait_recv(self):
            like = self.like()
            pltpu.make_async_copy(like, like, rsem.at[self.number]).wait()

    def remote(src, dst, to):
        where = dst if callable(dst) else lambda: dst
        group = Group(where)
        group.add(src, where(), to)
        return group

    def arrived(groups):
        for group in groups:
            group.wait_recv()

    locals_ = [0]

    def local(src, dst):
        copy = pltpu.make_async_copy(src, dst, lsem.at[locals_[0]])
        locals_[0] += 1
        copy.start()
        return copy

    staging = [local(refs[2 + i], staged[i]) for i in range(12)]
    turn_local = local(turn, b.turn)

    barrier = pltpu.get_barrier_semaphore()
    peers = [sibling]
    for o in range(1, TP):
        peers += [moved("x", o), moved_to("x", o, other)]
    for axis in ("y", "z"):
        for o in range(1, size[axis]):
            peers.append(moved(axis, o))
    for peer in peers:
        pl.semaphore_signal(barrier, inc=1, device_id=peer, device_id_type=MESH)

    pk[...] = jnp.zeros(pk.shape, BF16)
    ff[...] = jnp.zeros(ff.shape, BF16)
    gms[...] = jnp.zeros(gms.shape, F32)
    for copy in staging:
        copy.wait()
    small = dot(gain_in[...], places[0, :2], TN) + dot(bias_in[...], places[1, :2], TN)
    small = small + dot(token_in[:, 0], places[2]) + dot(token_in[:, 1], places[3])
    small = small.astype(BF16)
    for h in range(2):
        for p in range(3):
            for i in range(3):
                first = D * i + HALF * h + 128 * p
                pk[h, :ar, HALF * p + 128 * i : HALF * p + 128 * (i + 1)] = wq[:, first : first + 128]
        pk[h, :ar, WO : WO + HALF] = wp[:, HALF * h : HALF * (h + 1)]
        pk[h, :ar, 4 * HALF :] = small
        for j in range(3):
            cols = slice(HALF * h + 128 * j, HALF * h + 128 * (j + 1))
            ff[h, :wr, 256 * j : 256 * j + 128] = up_in[:, cols]
            ff[h, :wr, 256 * j + 128 : 256 * j + 256] = down_in[:, cols]
        gms[h, 0:5] = gmem[:, h].astype(F32)
    pl.semaphore_wait(barrier, len(peers))

    pk_local = local(pk.at[core], b.p1.at[core])
    ff_local = local(ff.at[core], b.f1.at[core])
    pk_swap = remote(pk.at[other], b.p1.at[core], sibling)
    ff_swap = remote(ff.at[other], b.f1.at[core], sibling)

    conditional = []

    def to_device(src, dst, place, here, kind, send_slot):
        copy = pltpu.make_async_remote_copy(
            src_ref=src,
            dst_ref=dst,
            send_sem=xsem.at[25 + XBASE[kind] + send_slot],
            recv_sem=here,
            device_id=device(x_=place[0], c_=place[1]),
            device_id_type=MESH,
        )
        same = (place[0] == x) & (place[1] == core)

        @pl.when(same)
        def _():
            pltpu.make_async_copy(src, dst, here).start()

        @pl.when(jnp.logical_not(same))
        def _():
            copy.start()

        conditional.append((same, copy))

    def from_device(dst, kind, slot):
        pltpu.make_async_copy(dst, dst, xsem.at[XBASE[kind] + slot]).wait()

    def chip_of(k, s):
        return s + k * (3 - 2 * s)

    def send_rows():
        for s in range(2):
            for j in range(2):
                to_device(
                    xin.at[s, pl.ds(TOKENS * j, TOKENS)],
                    b.x.at[pl.ds(pl.multiple_of(OWN * j + TOKENS * x, 16), TOKENS)],
                    (chip_of(core, s), j),
                    xsem.at[XBASE[0] + x],
                    0,
                    2 * s + j,
                )

    def send_upstream():
        for s in range(2):
            for j in range(2):
                to_device(
                    gin.at[s, pl.ds(TOKENS * j, TOKENS)],
                    b.gyt.at[pl.ds(pl.multiple_of(TOKENS * x, 16), TOKENS)],
                    (chip_of(core, s), j),
                    xsem.at[XBASE[1] + x],
                    1,
                    2 * s + j,
                )
            to_device(
                gms.at[s], b.gm.at[x % 2], (chip_of(core, s), x // 2), xsem.at[XBASE[2] + x % 2], 2, s
            )

    def part_of(job, step, place, half=None):
        name, order, cols, axes = job
        fixed = {a: at[a] for a in order[step:]}
        fixed[order[step]] = place
        where = []
        for a in axes:
            if a in fixed:
                where.append(fixed[a])
            elif half is not None:
                where.append(pl.ds(half * (size[a] // 2), size[a] // 2))
                half = None
            else:
                where.append(slice(None))
        return getattr(b, WEIGHTS[name[0]]).at[tuple(where) + (slice(None), cols)]

    def gather_start(name, step):
        job = gathers[name]
        axis = job[1][step]
        n = size[axis]
        own = part_of(job, step, at[axis])
        free = [a for a in job[3] if a not in job[1][step:]]
        relay = n == 4 and step == len(job[1]) - 1 and size[free[0]] % 2 == 0
        state = types.SimpleNamespace(step=step, relay=relay)
        if relay:
            first = [part_of(job, step, at[axis], h) for h in range(2)]
            right, left = moved(axis, 1), moved(axis, n - 1)
            state.right, state.left = (
                remote(first[h], lambda h=h: part_of(job, step, at[axis], h), to) for h, to in ((0, right), (1, left))
            )
            state.every = [Group(lambda: part_of(job, step, pl.ds(0, 2)))]
            state.every[0].add(first[1], first[1], right)
            state.every[0].add(first[0], first[0], left)
        else:
            state.every = [Group(lambda: part_of(job, step, pl.ds(0, n - 1)))] if n > 1 else []
            for o in range(1, n):
                state.every[0].add(own, own, moved(axis, o))
        flying[name] = state

    def gather_pass(name):
        job, state = gathers[name], flying[name]
        if not state.relay:
            return
        axis = job[1][state.step]
        n = size[axis]
        for copy, back, onward, half in ((state.right, n - 1, 1, 0), (state.left, 1, n - 1, 1)):
            arrived([copy])
            piece = part_of(job, state.step, near[axis][back], half)
            state.every[0].add(piece, piece, moved(axis, onward))

    def gather_done(name):
        arrived(flying[name].every)

    gathers = {j[0]: j for j in gather_jobs()}
    flying = {}

    pk_local.wait()
    arrived([pk_swap])
    packed = jnp.concatenate([b.p1[c].astype(F32)[: sh.pc] for c in range(2)], 0).astype(BF16)
    b.p2y[y] = packed[:, :HALF]
    b.p2[x] = packed[:, HALF:]
    mine = b.p2y.at[y]
    ysteps, xsteps = [], [Group(lambda: b.p2.at[: TP - 1])]
    if ny > 1:
        ysteps.append(Group(lambda: b.p2y.at[: ny - 1]))
    for o in range(1, ny):
        ysteps[0].add(mine, mine, moved("y", o))
    mine = b.p2.at[x]
    for o in range(1, TP):
        xsteps[0].add(mine, mine, moved("x", o))
    ff_local.wait()
    arrived([ff_swap])
    two = [b.f1[c].astype(F32)[:wr] for c in range(2)]
    b.wf[x, z, y] = jnp.concatenate(two, 0).astype(BF16)
    feed_names, first_names = ("f1", "f2", "f0"), ("x0", "a0", "a1")
    for n in feed_names:
        gather_start(n, 0)
    send_rows()
    arrived(ysteps)
    b.wx[x, z] = dot(packy[...], b.p2y[...].reshape(ny * 2 * sh.pc, HALF)).astype(BF16)
    gather_start("x0", 0)
    arrived(xsteps)
    b.wa[z, y, :, HALF:] = dot(packsel[...], b.p2[...].reshape(TP * 2 * sh.pc, REST)).astype(BF16)
    for n in ("a0", "a1"):
        gather_start(n, 0)
    for n in first_names:
        gather_done(n)
        gather_start(n, 1)
    for n in feed_names:
        gather_done(n)
        gather_start(n, 1)
    for n in first_names:
        gather_pass(n)
    for n in feed_names:
        gather_done(n)
        gather_start(n, 2)

    for i in range(TP):
        from_device(b.x.at[pl.ds(pl.multiple_of(OWN * core + TOKENS * i, 16), TOKENS)], 0, i)
    half = b.x.at[pl.ds(pl.multiple_of(OWN * core, 16), TP * TOKENS)]
    x_swap = remote(half, half, sibling)
    for first in (256, OWN + 256):
        b.x[first : first + 16] = jnp.zeros((16, D), BF16)
    turn_local.wait()
    arrived([x_swap])

    @pl.loop(0, 2)
    def _(i):
        rows = pl.ds(pl.multiple_of(OWN * i, 16), OWN)
        b.xp[rows] = dot(b.x[rows], b.turn[...], NT).astype(BF16)

    for n in first_names:
        gather_done(n)
    wo_cols = slice(WO, WO + HALF)
    wo_local = local(b.wa.at[:, :, :, wo_cols], b.wo.at[core])
    wo_swap = remote(b.wa.at[:, :, :, wo_cols], b.wo.at[core], sibling)
    gather_pass("f1")
    send_upstream()

    def attention_weight():
        return b.wa[:, :, :, :WO].reshape(D, WO)

    small = b.wa[:, :, :, 4 * HALF :].reshape(D, SMALL)
    chosen = dot(smallsel[...], small, NT)
    b.par[...] = chosen[0:8]
    memory = chosen[16:48].astype(BF16)
    b.x[OWN + 256 : OWN + 272] = memory[16:]
    turned = dot(memory, b.turn[...], NT).astype(BF16)
    b.xp[OWN + 256 : OWN + 272] = turned[16:]

    @pl.when(seg == 0)
    def _():
        b.x[256:272] = memory[:16]
        b.xp[256:272] = turned[:16]

    gains = [b.par[i : i + 1] for i in range(2)]
    biases = [b.par[2 + i : 3 + i] for i in range(2)]

    hop_to = jnp.where(x == 0, 1, 2)
    hops = []
    for j in range(2):
        hops.append(
            pltpu.make_async_remote_copy(
                src_ref=b.hop,
                dst_ref=b.hopin,
                send_sem=xsem.at[XBASE[6] + j],
                recv_sem=xsem.at[XBASE[6] + 2],
                device_id=device(x_=hop_to, c_=j),
                device_id_type=MESH,
            )
        )

    own_rows = pl.ds(pl.multiple_of(OWN * core, 16), OWN)
    other_rows = pl.ds(pl.multiple_of(OWN * other, 16), OWN)

    out = dot(b.xp[...], b.wx[...].reshape(D, HALF)).astype(BF16)
    for i in range(3):
        b.qkv[i] = out[:, 128 * i : 128 * i + 128]
    out = dot(b.x[...], b.wa[:, :, :, HALF:WO].reshape(D, 2 * HALF)).astype(BF16)
    for i in range(3, 9):
        b.qkv[i] = out[:, 128 * (i - 3) : 128 * (i - 2)]

    def head_masks(hh):
        lane = lax.broadcasted_iota(jnp.int32, (ROWS, 128), 1)
        row = lax.broadcasted_iota(jnp.int32, (ROWS, 128), 0)
        inside = (lane // 64) == hh
        spare = lane == 64 * (1 - hh)
        memory = ((row >= 256) & (row < 272)) | (row >= OWN + 256)
        invalid = memory & (row % 8 >= 5)
        return inside, spare, invalid

    def forward_pair(p):
        qp, kp, vp = (b.qkv[3 * p + i] for i in range(3))
        vt = vp.T
        for hh in range(2):
            inside, spare, invalid = head_masks(hh)
            zero = jnp.zeros_like(kp)
            kmask = jnp.where(spare & invalid, jnp.full_like(kp, MASKED), zero)
            km = jnp.where(inside, kp, kmask)
            qm = jnp.where(inside, qp, jnp.where(spare, jnp.ones_like(qp), zero))
            scores = dot(km, qm, NT)
            peak = jnp.max(scores, 0, keepdims=True)
            raised = jnp.exp2((scores - peak) * EXP_SCALE)
            total = jnp.sum(raised, 0, keepdims=True)
            probs = (raised * (1.0 / total)).astype(BF16)
            b.pt[2 * p + hh] = probs
            b.ot[p, 64 * hh : 64 * hh + 64] = dot(vt[64 * hh : 64 * hh + 64], probs).astype(BF16)
        b.oc[:, pl.ds(pl.multiple_of(128 * p, 128), 128)] = b.ot[p].T

    @pl.loop(0, 3)
    def _(j):
        cols = pl.ds(pl.multiple_of(128 * j, 128), 128)
        block = dot(b.turn[...], b.wx[:, :, :, cols].reshape(D, 128), TN).astype(BF16)
        b.wa[:, :, :, cols] = block.reshape(nz, ny, br, 128)

    @pl.loop(0, 2)
    def _(i):
        @pl.when((i == 1) & (seg == 1))
        def _():
            hops[0].wait_recv()
            b.x[256:272] = b.hopin[...]
            rows = dot(b.hopin[...], attention_weight()).astype(BF16)
            for j in range(9):
                b.qkv[j, 256:272] = rows[:, 128 * j : 128 * j + 128]

        @pl.when(i == seg)
        def _():
            for p in range(3):
                forward_pair(p)

        @pl.when(i == 0)
        def _():
            for n in ("f2", "f0"):
                gather_pass(n)

    def head_rows(ref, c):
        if nz > 1:
            return ref.at[pl.ds(c * (nz // 2), nz // 2)]
        return ref.at[:, :, pl.ds(pl.multiple_of(c * HALF, 16), HALF)]

    def wo_rows(h, c):
        return head_rows(b.wo.at[h], c)[...].reshape(HALF, HALF)

    o_swap = remote(b.oc.at[other_rows], b.oin, sibling)
    wo_local.wait()
    arrived([wo_swap])
    halves = [dot(b.oc[own_rows], wo_rows(h, core)) for h in range(2)]
    arrived([o_swap])
    attended = jnp.concatenate([halves[h] + dot(b.oin[...], wo_rows(h, other)) for h in range(2)], 1)
    h1, n1, inv1 = norm_forward(b.x[own_rows].astype(F32) + attended, gains[0], biases[0])
    b.h1[...] = h1
    b.n1[...] = n1
    b.inv1[...] = inv1
    b.h1b[own_rows] = h1.astype(BF16)
    h_swap = remote(b.h1b.at[own_rows], b.h1b.at[own_rows], sibling)

    @pl.when(seg == 1)
    def _():
        b.xp[256:272] = dot(b.hopin[...], b.turn[...], NT).astype(BF16)

    for n in ("f1", "f2", "f0"):
        gather_done(n)

    def feed_weight(t, kind):
        cols = [256 * j + 128 * kind for j in range(3)]
        blocks = [b.wf[2 * t + i, :, :, :, c : c + 128].reshape(D, 128) for i in range(2) for c in cols]
        return jnp.concatenate(blocks, 1)

    def up_weight(t):
        return feed_weight(t, 0)

    def down_weight(t):
        return feed_weight(t, 1)

    def gelu_share(units):
        return 0.5 * (1.0 + lax.erf(units * INV_ROOT_TWO))

    early = pltpu.make_async_remote_copy(
        src_ref=b.es,
        dst_ref=b.er,
        send_sem=xsem.at[XBASE[6] + 3],
        recv_sem=xsem.at[XBASE[6] + 4],
        device_id=sibling,
        device_id_type=MESH,
    )
    row16 = lax.broadcasted_iota(jnp.int32, (16, D), 0)

    @pl.when(seg == 0)
    def _():
        arrived([h_swap])
        rows = b.h1b[OWN + 256 : OWN + 272]
        units = [dot(rows, up_weight(t)) for t in range(2)]
        part = sum(dot((units[t] * gelu_share(units[t])).astype(BF16), down_weight(t), NT) for t in range(2))

        @pl.when(core == 0)
        def _():
            b.es[...] = part
            early.start()

        @pl.when(core == 1)
        def _():
            early.wait_recv()
            whole = b.h1[256:272] + part + b.er[...]
            written = norm_forward(whole, gains[1], biases[1])[0]
            b.hop[...] = jnp.where(row16 % 8 < 5, written, 0.0).astype(BF16)
            hops[0].start()
            hops[1].start()

    def project_up(rows):
        for t in range(2):
            units = dot(b.h1b[rows], up_weight(t))
            b.ul[t, rows] = units
            b.gl[t, rows] = (units * gelu_share(units)).astype(BF16)

    @pl.loop(0, 2)
    def _(i):
        @pl.when((i == 1) & (seg == 1))
        def _():
            arrived([h_swap])

        project_up(pl.ds(pl.multiple_of(OWN * jnp.where(i == 0, core, other), 16), OWN))


    def partial_down(rows):
        return sum(dot(b.gl[t, rows], down_weight(t), NT) for t in range(2))

    b.fs[...] = partial_down(other_rows).astype(BF16)
    f_swap = remote(b.fs, b.fr, sibling)
    branch = partial_down(own_rows)
    arrived([f_swap])
    out, n2, inv2 = norm_forward(b.h1[...] + branch + b.fr[...].astype(F32), gains[1], biases[1])
    low = out.astype(BF16)
    b.yb[...] = low
    b.mo[...] = low[256:272].astype(F32).reshape(2, 8, D)
    for i in range(TP):
        to_device(
            b.yb.at[pl.ds(TOKENS * i, TOKENS)],
            hout.at[seg, pl.ds(pl.multiple_of(TOKENS * core, 16), TOKENS)],
            (i, chain),
            xsem.at[XBASE[3] + 2 * seg + core],
            3,
            i,
        )
    for i in range(2):
        to_device(b.mo.at[i], mout.at[seg], (2 * core + i, chain), xsem.at[XBASE[4] + seg], 4, i)

    for i in range(TP):
        from_device(b.gyt.at[pl.ds(TOKENS * i, TOKENS)], 1, i)
    for i in range(2):
        from_device(b.gm.at[i], 2, i)
    upstream = jnp.concatenate([b.gyt[...].astype(F32), b.gm[...].reshape(16, D)], 0)
    b.sg[...] = jnp.zeros((48, D), F32)
    b.sg[1:2] = column_sum(upstream * n2)
    b.sg[3:4] = column_sum(upstream)
    dz = norm_backward(upstream, n2, inv2, gains[1])
    b.dz[...] = dz
    b.dfb[own_rows] = dz.astype(BF16)
    df_swap = remote(b.dfb.at[own_rows], b.dfb.at[own_rows], sibling)

    def weight_grad(into, left, right, jobs_):
        @pl.loop(0, 2)
        def _(t):
            part = dot(left[...], right[t], TN).astype(BF16)
            for i in range(2):
                into[2 * t + i] = part[:, HALF * i : HALF * (i + 1)].reshape(nz, ny, br, HALF)

            for h in range(2):

                @pl.when(t == h)
                def _():
                    for n in jobs_:
                        if is_ring(n, 0) and scatters[n][1][0] != "x":
                            ring_send(n, h)
                        elif h == 1:
                            scatter_send(n, 0)

    scatters = {j[0]: j for j in scatter_jobs()}
    rs = {}

    def is_ring(name, step):
        _, order, cols, axes = scatters[name]
        return step == 0 and name in RINGS and size[order[0]] == 4

    def source_of(name, step):
        _, order, cols, axes = scatters[name]
        axis = order[step]
        left = [a for a in axes if a not in order[:step]]
        array = getattr(b, GRADS[name[0]]) if step == 0 else k[SUMMED, step - 1, name]
        tail = (slice(None), cols) if step == 0 else ()

        def part(place, half=None):
            where = []
            for a in left:
                if a == axis:
                    where.append(place)
                elif half is not None:
                    where.append(pl.ds(half * (size[a] // 2), size[a] // 2))
                    half = None
                else:
                    where.append(slice(None))
            return array.at[tuple(where) + tail]

        return part

    def ring_send(name, half):
        axis = scatters[name][1][0]
        n = size[axis]
        part = source_of(name, 0)
        landing, over = k[LANDED, 0, name], k[PASSED, 0, name]
        right, left, far = (near[axis][o] for o in (1, n - 1, 2))
        to = moved(axis, 1), moved(axis, n - 1)
        cut = size[[a for a in scatters[name][3] if a != axis][0]] // 2
        if name not in rs:
            rs[name] = ([None, None], Group(lambda: landing), cut, (right, left), to)
        rs[name][0][half] = remote(part(far, half), lambda: over.at[half], to[half])
        if half == 0:
            rs[name][1].add(part(left, 0), landing.at[1, :cut], to[1])
        else:
            rs[name][1].add(part(right, 1), landing.at[0, cut:], to[0])

    def scatter_send(name, step):
        axis = scatters[name][1][step]
        n = size[axis]
        part = source_of(name, step)
        landing = k[LANDED, step, name]
        if is_ring(name, step):
            ring_send(name, 0)
            ring_send(name, 1)
            return
        rs[name] = [Group(lambda: landing)] if n > 1 else []
        for o in range(1, n):
            rs[name][0].add(part(near[axis][o]), landing.at[o - 1], moved(axis, o))

    def scatter_pass(name):
        if not is_ring(name, 0):
            return
        passing, coming, half, places_, devices = rs[name]
        part = source_of(name, 0)
        landing, over, updated = k[LANDED, 0, name], k[PASSED, 0, name], k[UPDATED, 0, name]
        for i in range(2):
            arrived([passing[i]])
            updated[i] = (part(places_[i], i)[...].astype(F32) + over[i].astype(F32)).astype(BF16)
            where = landing.at[0, :half] if i == 0 else landing.at[1, half:]
            coming.add(updated.at[i], where, devices[i])

    def scatter_sum(name, step):
        _, order, cols, axes = scatters[name]
        axis = order[step]
        total = source_of(name, step)(at[axis])[...].astype(F32)
        ring = is_ring(name, step)
        arrived([rs[name][1]] if ring else rs[name])
        for o in range(2 if ring else size[axis] - 1):
            total = total + k[LANDED, step, name][o].astype(F32)
        if step < len(order) - 1:
            k[SUMMED, step, name][...] = total.astype(BF16)
        return total

    def scatter_on(names, step):
        for n in names:
            scatter_sum(n, step)
            scatter_send(n, step + 1)

    down_names, up_names = ("t0", "t1", "t2"), ("i0", "i1", "i2")
    arrived([df_swap])
    weight_grad(b.gt, b.dfb, b.gl, down_names)
    @pl.loop(0, 2)
    def _(i):
        rows = pl.ds(pl.multiple_of(OWN * i, 16), OWN)
        for t in range(2):
            units = b.ul[t, rows]
            slope = gelu_share(units) + units * jnp.exp(-0.5 * units * units) * INV_ROOT_TWOPI
            b.du[t, rows] = (dot(b.dfb[rows], down_weight(t)) * slope).astype(BF16)


    def partial_up(rows):
        return sum(dot(b.du[t, rows], up_weight(t), NT) for t in range(2))

    dh_swap = Group(lambda: b.dhr)

    @pl.loop(0, 2)
    def _(i):
        part = partial_up(pl.ds(pl.multiple_of(OWN * jnp.where(i == 0, other, core), 16), OWN))

        @pl.when(i == 0)
        def _():
            b.dhs[...] = part.astype(BF16)
            dh_swap.add(b.dhs, b.dhr, sibling)

        @pl.when(i == 1)
        def _():
            b.dz[...] = b.dz[...] + part

    arrived([dh_swap])
    into_first = b.dz[...] + b.dhr[...].astype(F32)
    b.sg[0:1] = column_sum(into_first * b.n1[...])
    b.sg[2:3] = column_sum(into_first)
    dr = norm_backward(into_first, b.n1[...], b.inv1[...], gains[0])
    b.dr[...] = dr
    b.dab[own_rows] = dr.astype(BF16)
    da_swap = remote(b.dab.at[own_rows], b.dab.at[own_rows], sibling)

    def grad_mixed(rows):
        parts = [dot(b.dab[rows, HALF * h : HALF * (h + 1)], wo_rows(h, core), NT) for h in range(2)]
        for p in range(3):
            b.doc[p, rows] = (parts[0] + parts[1])[:, 128 * p : 128 * p + 128].astype(BF16)

    weight_grad(b.gi, b.h1b, b.du, up_names)
    for n in down_names:
        scatter_pass(n)
    arrived([da_swap])
    grad_mixed(slice(None))

    mixed_t = b.ot[...].reshape(HALF, ROWS)

    def proj_grad(h):
        cols = pl.ds(pl.multiple_of(HALF * h, 128), HALF)
        return dot(mixed_t, b.dab[:, cols]).astype(BF16).reshape(b.gos.shape)

    def wo_part(c):
        return head_rows(b.ga.at[:, :, :, wo_cols], c)

    b.gos[...] = proj_grad(other)
    go_swap = remote(b.gos, wo_part(core), sibling)
    wo_part(core)[...] = proj_grad(core)

    def backward_pair(p):
        qp, kp, vp = (b.qkv[3 * p + i] for i in range(3))
        dop = b.doc[p]
        kt = kp.T
        dv = dk = 0.0
        dq = []
        for hh in range(2):
            inside, _, _ = head_masks(hh)
            zero = jnp.zeros_like(kp)
            grad_probs = dot(jnp.where(inside, vp, zero), dop, NT)
            low_probs = b.pt[2 * p + hh]
            probs = low_probs.astype(F32)
            row_term = jnp.sum(probs * grad_probs, 0, keepdims=True)
            ds = (probs * (grad_probs - row_term)).astype(BF16)
            dv = dv + dot(low_probs, jnp.where(inside, dop, zero))
            dk = dk + dot(ds, jnp.where(inside, qp, zero))
            dq.append(dot(kt[64 * hh : 64 * hh + 64], ds))
        b.dqkv[3 * p] = (jnp.concatenate(dq, 0) * 0.125).T.astype(BF16)
        b.dqkv[3 * p + 1] = (dk * 0.125).astype(BF16)
        b.dqkv[3 * p + 2] = dv.astype(BF16)

    def joined(rows, wanted):
        return jnp.concatenate([b.dqkv[i, rows] for i in wanted], 1)

    def attention_grad(p):
        grads = jnp.concatenate([b.dqkv[3 * p + i] for i in range(3)], 1)

        part = dot(b.both[jnp.minimum(p, 1)], grads, TN).astype(BF16)

        @pl.when(p == 0)
        def _():
            b.gx[...] = part.reshape(TP, nz, sh.xrows, HALF)

        @pl.when(p > 0)
        def _():
            cols = pl.ds(pl.multiple_of(HALF * p, 128), HALF)
            b.ga[:, :, :, cols] = part.reshape(nz, ny, br, HALF)

    @pl.loop(0, 3)
    def _(p):
        backward_pair(p)
        attention_grad(p)

        @pl.when(p == 0)
        def _():
            arrived([go_swap])
            scatter_send("aw", 0)
            scatter_send("x0", 0)

        @pl.when(p == 1)
        def _():
            scatter_send("a1", 0)
            for n in up_names:
                scatter_pass(n)

        @pl.when(p == 2)
        def _():
            scatter_send("a2", 0)
            scatter_send("a3", 0)
            for n in ("aw", "x0"):
                scatter_pass(n)
            scatter_on(down_names, 0)


    def partial_input(rows):
        return dot(joined(rows, range(9)), attention_weight(), NT)

    memory_rows = [pl.ds(pl.multiple_of(OWN * c + 256, 16), 16) for c in (other, core)]
    part = dot(jnp.concatenate([joined(rows, range(9)) for rows in memory_rows], 0), attention_weight(), NT)
    b.ms[...] = part[:16]
    memory_swap = remote(b.ms, b.mr, sibling)
    b.dxs[...] = partial_input(other_rows).astype(BF16)
    dx_swap = remote(b.dxs, b.dxr, sibling)
    arrived([memory_swap])
    memory_grad = part[16:] + b.dr[256:272] + b.mr[...]

    @pl.when((core == 0) & (seg == 0))
    def _():
        b.sg[16:32] = memory_grad

    @pl.when(core == 1)
    def _():
        b.sg[32:48] = memory_grad

    small_grads = dot(b.sg[...].astype(BF16), smallsel[...], TN).astype(BF16)
    b.ga[:, :, :, 4 * HALF :] = small_grads.reshape(nz, ny, br, SMALL)
    scatter_send("as", 0)
    scatter_pass("a1")
    dx = partial_input(own_rows) + b.dr[...]
    scatter_on(up_names, 0)
    arrived([dx_swap])
    dx = dx + b.dxr[...].astype(F32)
    b.dxb[...] = dx[:256].astype(BF16)
    for i in range(TP):
        to_device(
            b.dxb.at[pl.ds(TOKENS * i, TOKENS)],
            dxo.at[seg, pl.ds(pl.multiple_of(TOKENS * core, 16), TOKENS)],
            (i, chain),
            xsem.at[XBASE[5] + 2 * seg + core],
            5,
            i,
        )
    scatter_on(("aw", "x0", "a1"), 0)
    scatter_on(down_names, 1)
    scatter_on(("a2", "a3", "as"), 0)
    spread = dot(packy[...], scatter_sum("x0", 1).astype(BF16), TN).astype(BF16)
    b.e3y[...] = spread.reshape(ny, 2 * sh.pc, HALF)
    ysteps = [Group(lambda: b.r3y)] if ny > 1 else []
    for o in range(1, ny):
        ysteps[0].add(b.e3y.at[near["y"][o]], b.r3y.at[o - 1], moved("y", o))
    scatter_on(up_names, 1)
    for n in ("aw", "a1", "a2", "a3", "as"):
        cols = scatters[n][2]
        b.tot[:, cols.start - HALF : cols.stop - HALF] = scatter_sum(n, 1).astype(BF16)
    spread = dot(packsel[...], b.tot[...], TN).astype(BF16)
    b.e3[...] = spread.reshape(TP, 2 * sh.pc, REST)
    steps = [Group(lambda: b.r3)]
    for o in range(1, TP):
        steps[0].add(b.e3.at[near["x"][o]], b.r3.at[o - 1], moved("x", o))

    def last_rows(wanted, first_col):
        for j, n in enumerate(wanted):
            total = scatter_sum(n, 2)
            cols = slice(first_col + 128 * j, first_col + 128 * j + 128)
            b.sf[0, :, cols] = total[:wr]
            b.sf[1, :, cols] = total[wr:]

    last_rows(down_names, HALF)
    last_rows(up_names, 0)
    sf_local = local(b.sf.at[core], gfo.at[core])
    sf_swap = remote(b.sf.at[other], gfo.at[core], sibling)

    arrived(steps)
    total = b.e3[x].astype(F32)
    for o in range(1, TP):
        total = total + b.r3[o - 1].astype(F32)
    b.s4[:, :, HALF:] = total.reshape(2, sh.pc, REST)
    arrived(ysteps)
    total = b.e3y[y].astype(F32)
    for o in range(1, ny):
        total = total + b.r3y[o - 1].astype(F32)
    b.s4[:, :, :HALF] = total.reshape(2, sh.pc, HALF)
    s4_local = local(b.s4.at[core], gao.at[core])
    s4_swap = remote(b.s4.at[other], gao.at[core], sibling)

    for kind, out_ref in ((3, hout), (5, dxo)):
        for s in range(2):
            for j in range(2):
                from_device(out_ref.at[s, pl.ds(TOKENS * j, TOKENS)], kind, 2 * s + j)
    for s in range(2):
        from_device(mout.at[s], 4, s)
    sf_local.wait()
    s4_local.wait()
    arrived([sf_swap, s4_swap])

    for group in sent[-SENDS:]:
        group.wait_send()
    for same, copy in conditional:

        @pl.when(jnp.logical_not(same))
        def _():
            copy.wait_send()

    @pl.when((seg == 0) & (core == 1))
    def _():
        hops[0].wait_send()
        hops[1].wait_send()

    @pl.when((seg == 0) & (core == 0))
    def _():
        early.wait_send()


def layer(sh, arrays):
    constants = [jnp.asarray(a, BF16) for a in selections(sh)]
    tables = scratch_of(sh)
    names = [list(table) for table in tables]
    anywhere = pl.BlockSpec(memory_space=pl.ANY)
    outs = [
        jax.ShapeDtypeStruct((2, 128, D), BF16),
        jax.ShapeDtypeStruct((2, 8, D), F32),
        jax.ShapeDtypeStruct((2, 128, D), BF16),
        jax.ShapeDtypeStruct((2, sh.pc, ACOLS), F32),
        jax.ShapeDtypeStruct((2, sh.wrows, D), F32),
    ]
    return pl.pallas_call(
        functools.partial(kernel, sh, names),
        name="layer",
        out_shape=outs,
        in_specs=[anywhere] * 15,
        out_specs=[anywhere] * len(outs),
        scratch_shapes=[pltpu.VMEM(*one) for table in tables for one in table.values()]
        + [
            pltpu.SemaphoreType.DMA((SENDS,)),
            pltpu.SemaphoreType.DMA((96,)),
            pltpu.SemaphoreType.DMA((45,)),
            pltpu.SemaphoreType.DMA((20,)),
        ],
        compiler_params=pltpu.CompilerParams(
            collective_id=0, has_side_effects=True, vmem_limit_bytes=64 * 2**20 - 2**17
        ),
    )(*arrays, *constants)


def unpack_kernel(sh, *refs):
    arrays, results, held, outs, sems = refs[:5], refs[5:15], refs[15:20], refs[20:30], refs[30]
    loads = [pltpu.make_async_copy(arrays[i], held[i], sems.at[i]) for i in range(5)]
    stores = [pltpu.make_async_copy(outs[i], results[i], sems.at[5 + i]) for i in range(10)]
    for copy in loads:
        copy.start()
    hout, mout, dxo, gao, gfo = held
    hidden, memory, grad_in, gq, gp, gains, biases, tokens, gi, gt = outs
    ar = sh.arows
    loads[0].wait()
    hidden[...] = hout[...]
    stores[0].start()
    loads[2].wait()
    grad_in[...] = dxo[...].astype(F32)
    stores[2].start()
    loads[1].wait()
    for i in range(2):
        memory[:, i] = mout[i, :5].astype(BF16)
    stores[1].start()
    loads[3].wait()
    for h in range(2):
        for p in range(3):
            for i in range(3):
                to = D * i + HALF * h + 128 * p
                first = HALF * p + 128 * i
                gq[:, to : to + 128] = gao[h, :ar, first : first + 128]
        gp[:, HALF * h : HALF * (h + 1)] = gao[h, :ar, WO : WO + HALF]
    small = gao[0, :, 4 * HALF :] + gao[1, :, 4 * HALF :]
    turned = small.T[:, :ar]
    gains[...] = turned[0:2]
    biases[...] = turned[2:4]
    for kind in range(2):
        tokens[:, kind] = small[:ar, 4 + MEM * kind : 4 + MEM * (kind + 1)]
    for i in range(3, 8):
        stores[i].start()
    loads[4].wait()
    for h in range(2):
        gi[:, HALF * h : HALF * (h + 1)] = gfo[h, :, :HALF]
        gt[:, HALF * h : HALF * (h + 1)] = gfo[h, :, HALF:]
    for i in range(8, 10):
        stores[i].start()
    for copy in stores:
        copy.wait()


def unpack(sh, *arrays):
    ar, wr = sh.arows, sh.wrows
    shapes = [
        ((2, 128, D), BF16),
        ((5, 2, D), BF16),
        ((2, 128, D), F32),
        ((ar, 3 * D), F32),
        ((ar, D), F32),
        ((2, ar), F32),
        ((2, ar), F32),
        ((ar, 2, MEM), F32),
        ((wr, D), F32),
        ((wr, D), F32),
    ]
    anywhere = pl.BlockSpec(memory_space=pl.ANY)
    return pl.pallas_call(
        functools.partial(unpack_kernel, sh),
        name="unpack",
        out_shape=[jax.ShapeDtypeStruct(*one) for one in shapes],
        in_specs=[anywhere] * 5,
        out_specs=[anywhere] * len(shapes),
        scratch_shapes=[pltpu.VMEM(a.shape, a.dtype) for a in arrays]
        + [pltpu.VMEM(*one) for one in shapes]
        + [pltpu.SemaphoreType.DMA((15,))],
        compiler_params=pltpu.CompilerParams(vmem_limit_bytes=64 * 2**20 - 2**17),
    )(*arrays)


def body(
    sh,
    hidden_in,
    reset,
    w_qkv,
    w_attn_out,
    norm_gains,
    norm_biases,
    memory_tokens,
    w_in,
    w_out,
    grad_hidden,
    grad_memory,
):
    arrays = (
        hidden_in,
        grad_hidden,
        grad_memory.transpose(1, 0, 2),
        w_qkv,
        w_attn_out,
        norm_gains,
        norm_biases,
        memory_tokens.transpose(2, 0, 1),
        w_in,
        w_out.T,
    )
    hidden, memory, *middle, tokens, gi, gt = unpack(sh, *layer(sh, arrays))
    return hidden, memory.transpose(1, 0, 2), *middle, tokens.transpose(1, 2, 0), gi, gt.T


def solution(mesh):
    sh = Shape(mesh.shape["dp"])
    return jax.shard_map(
        functools.partial(body, sh),
        mesh=mesh,
        in_specs=(
            P("dp", "tp", None),
            P("dp"),
            P(("dp", "tp"), None),
            P(("dp", "tp"), None),
            P(None, ("dp", "tp")),
            P(None, ("dp", "tp")),
            P(None, None, ("dp", "tp")),
            P("dp", "tp"),
            P("tp", "dp"),
            P("dp", "tp", None),
            P("dp", "tp", None),
        ),
        out_specs=(
            P("dp", "tp", None),
            P("dp", "tp", None),
            P("dp", "tp", None),
            P(("dp", "tp"), None),
            P(("dp", "tp"), None),
            P(None, ("dp", "tp")),
            P(None, ("dp", "tp")),
            P(None, None, ("dp", "tp")),
            P("dp", "tp"),
            P("tp", "dp"),
        ),
        check_vma=False,
    )
```
